32 devices in a mesh: gy: 4 (over y, x), gx: 8 (over z, core).
Axes of the slice: x: 2, y: 2, z: 4, core: 2. Of those that a mesh axis runs over, the one named last changes fastest.
Arguments:
- features: bfloat16 [128, 1024, 256], P('gy', 'gx'), may hold values from -8 to 8
- tissue: int32 [8, 64], P('gy', 'gx'), may hold values 0 or 1
- owner_map: int32 [4, 8, 16, 1], P('gy', 'gx'), may hold values from 0 to 7; in each aligned block of 16 rows (0 to 15, 16 to 31, ..., all dimensions but the last counted through in order) at most 2 rows name the same one
- w_conv: bfloat16 [9, 256, 256], replicated, may hold values from -0.125 to 0.125
- w_stride: bfloat16 [4, 256, 256], replicated, may hold values from -0.1875 to 0.1875
- w_query: float32 [256, 256], replicated, may hold values from -0.375 to 0.375
- w_key: float32 [256, 256], replicated, may hold values from -0.375 to 0.375
- w_value: float32 [256, 256], replicated, may hold values from -0.375 to 0.375
- cotangent: float32 [256], replicated, may hold values from -6 to 6
Outputs:
- embedding: float32 [256], replicated
- input_grad: bfloat16 [128, 1024, 256], P('gy', 'gx')
- conv_grad: float32 [9, 256, 256], replicated
The draws below stay inside these ranges and needn't reach their ends.
Inputs may be any that keep to these rules, and one draw needn't show every extreme that they name: `owner_map`: among the tiles of one device, no owner index is named more than 2 times.
All inputs are finite; a program needn't handle non-finite values. No bound on the sum of `tissue` on one device may be relied on, other than what follows from the above.
Results may differ from the reference program's by a relative error of at most 0.017.
Values may be sent and summed in bfloat16 or wider, within the bound.
No kernel may reach another device: no remote copies, remote signals or barrier semaphores. Data moves between devices by JAX's collectives and lax.ppermute only.
A program may use at most 128 MiB of HBM per device.

```python
import math
from functools import partial
import jax
import jax.numpy as jnp
import numpy as np
from jax import lax

C = 256
HEADS = 4
TILE = 8
TYD = 2
TXD = 8
CAP = 2
TILES_DEV = 16
NH = 128
NW = 1024
NTY = 8
NTX = 64
ALL_TILES = 512
N_GY = 4
N_GX = 8


def draw_features(key, part):
    first = jax.random.fold_in(jax.random.fold_in(key, 11), 0)
    values = jax.random.normal(first, (NH, NW, C), jnp.float32)
    return jnp.clip(values, -8.0, 8.0).astype(jnp.bfloat16)


def set_ends(array, key, low, top_value):
    shape = array.shape
    spot = [jax.random.randint(jax.random.fold_in(key, axis), (), 0, shape[axis]) for axis in range(len(shape))]
    array = array.at[tuple(spot)].set(low)
    longest = shape.index(max(shape))
    spot[longest] = (spot[longest] + 1) % shape[longest]
    return array.at[tuple(spot)].set(top_value)


def shared_out(own_key, own, number, rows, count, top, reach, lean):
    ranking = jax.random.permutation(own_key, count)
    heavy_load, usual = shares(count, rows * top, reach, lean, True), shares(count, rows * top, reach, lean, False)
    places = jnp.arange(count)

    def named(sizes, rotation):
        used = int((sizes > 0).sum())
        fixed = max(1, used // 4)
        moved = fixed + (places - fixed + rotation * (used - fixed)) % max(1, count - fixed)
        return jnp.zeros((count,), jnp.int32).at[ranking[jnp.where(places < fixed, places, moved)]].set(jnp.asarray(sizes, jnp.int32))

    sizes = jnp.where(number % 4 == 0, named(heavy_load, number // 4), named(usual, number - number // 4 - 1))
    mixed = jax.random.permutation(jax.random.fold_in(own, 3), count)
    source_of, sink = mixed[0:count // 2 * 2:2], mixed[1:count // 2 * 2:2]
    margin = jnp.minimum(sizes[source_of] - 1, reach - sizes[sink]) // 2
    margin = jnp.where((source_of == ranking[0]) | (sink == ranking[0]) | (sizes[sink] == 0), 0, jnp.maximum(margin, 0))
    moved = jax.random.randint(jax.random.fold_in(own, 4), (count // 2,), 0, 1 << 20) % (margin + 1)
    sizes = sizes.at[source_of].add(-moved).at[sink].add(moved)
    items = jnp.searchsorted(jnp.cumsum(sizes), jnp.arange(rows * top), side="right").astype(jnp.int32)
    table = items.reshape(top, rows).T
    table = table[jax.random.permutation(jax.random.fold_in(own, 1), rows)]
    rotation = jax.random.randint(jax.random.fold_in(own, 2), (rows, 1), 0, top)
    return jnp.take_along_axis(table, (jnp.arange(top)[None, :] + rotation) % top, axis=1)


def shares(number_of, total, bound, skew, full):
    weights = [(1 << 20) // math.isqrt(standing ** skew) + 1 for standing in range(1, number_of + 1)]
    largest = bound if full else min(bound, max(-(-total // number_of), total * weights[0] // sum(weights)))
    least = 1 if total - largest >= number_of - 1 else 0
    given, surplus = [largest] + [least] * (number_of - 1), total - largest - least * (number_of - 1)
    while surplus > 0:
        movable = [i for i in range(1, number_of) if given[i] < largest] or [i for i in range(1, number_of) if given[i] < bound]
        pool, remaining = sum([weights[i] for i in movable]), surplus
        for i in movable:
            extra = min(bound - given[i], max(1, remaining * weights[i] // pool), surplus)
            given[i] = given[i] + extra
            surplus = surplus - extra
    return np.array(given)


def gaussian(stream_key, shape, scale, most, held_as=jnp.bfloat16):
    return jnp.clip(scale * jax.random.normal(stream_key, shape, jnp.float32), -most, most).astype(held_as)


def setup_inputs(seed: int = 0) -> dict:
    key_of = jax.random.split(jax.random.key(seed), 10)
    features = draw_features(jax.random.fold_in(key_of[9], 71), 0)
    tissue = set_ends((jax.random.randint(key_of[1], (NTY, NTX), 0, 3) < 2).astype(jnp.int32), jax.random.fold_in(key_of[1], 1), 0, 1)
    owner_map_keys = jax.random.split(jax.random.fold_in(key_of[2], 1), N_GY * N_GX * TILES_DEV // TILES_DEV)
    owner_map_turns = jax.random.permutation(jax.random.fold_in(key_of[2], 3), N_GY * N_GX * TILES_DEV // TILES_DEV)
    owner_map = jax.vmap(lambda own, number: shared_out(jax.random.fold_in(key_of[2], 2), own, number, TILES_DEV, N_GX, 1, CAP, 2))(owner_map_keys, owner_map_turns).reshape((N_GY, N_GX, TILES_DEV, 1))
    w_conv = gaussian(key_of[3], (9, C, C), (9 * C) ** -0.5, 0.125)
    w_stride = gaussian(key_of[4], (4, C, C), (4 * C) ** -0.5, 0.1875)
    w_query = gaussian(key_of[5], (C, C), C ** -0.5, 0.375, jnp.float32)
    w_key = gaussian(key_of[6], (C, C), C ** -0.5, 0.375, jnp.float32)
    w_value = gaussian(key_of[7], (C, C), C ** -0.5, 0.375, jnp.float32)
    cotangent = gaussian(key_of[8], (C,), 1.0, 6.0, jnp.float32)
    return dict(features=features, tissue=tissue, owner_map=owner_map, w_conv=w_conv, w_stride=w_stride, w_query=w_query, w_key=w_key, w_value=w_value, cotangent=cotangent)


attention_bias = -1.0
loss_scale = 512.0

def forward_taps(padded, weight, pix_rows, pix_cols):
    channels = padded.shape[2]
    running = jnp.zeros((pix_rows * pix_cols, weight.shape[2]), jnp.float32)
    for tap_index in range(9):
        row_off, col_off = (tap_index // 3, tap_index % 3)
        window = padded[row_off:row_off + pix_rows, col_off:col_off + pix_cols].reshape(pix_rows * pix_cols, channels)
        running = running + jnp.dot(window, weight[tap_index], preferred_element_type=jnp.float32)
    return running.reshape(pix_rows, pix_cols, weight.shape[2])

def backward_taps(padded, weight, pix_rows, pix_cols):
    channels = padded.shape[2]
    running = jnp.zeros((pix_rows * pix_cols, weight.shape[1]), jnp.float32)
    for tap_index in range(9):
        row_off, col_off = (tap_index // 3, tap_index % 3)
        window = padded[2 - row_off:2 - row_off + pix_rows, 2 - col_off:2 - col_off + pix_cols].reshape(pix_rows * pix_cols, channels)
        running = running + lax.dot_general(window, weight[tap_index], (((1,), (1,)), ((), ())), preferred_element_type=jnp.float32)
    return running.reshape(pix_rows, pix_cols, weight.shape[1])

def weight_taps(padded, upstream, pix_rows, pix_cols):
    channels = padded.shape[2]
    flat_up = upstream.reshape(pix_rows * pix_cols, upstream.shape[2])
    pieces = []
    for tap_index in range(9):
        row_off, col_off = (tap_index // 3, tap_index % 3)
        window = padded[row_off:row_off + pix_rows, col_off:col_off + pix_cols].reshape(pix_rows * pix_cols, channels)
        pieces.append(lax.dot_general(window, flat_up, (((0,), (0,)), ((), ())), preferred_element_type=jnp.float32))
    return jnp.stack(pieces)

def strided_forward(field, weight):
    pix_rows, pix_cols, channels = field.shape
    running = jnp.zeros((pix_rows // 2 * (pix_cols // 2), weight.shape[2]), jnp.float32)
    for tap_index in range(4):
        row_off, col_off = (tap_index // 2, tap_index % 2)
        window = field[row_off::2, col_off::2].reshape(-1, channels)
        running = running + jnp.dot(window, weight[tap_index], preferred_element_type=jnp.float32)
    return running.reshape(pix_rows // 2, pix_cols // 2, weight.shape[2])

def strided_backward(upstream, weight):
    half_rows, half_cols, channels = upstream.shape
    flat_up = upstream.reshape(half_rows * half_cols, channels)
    tap_parts = []
    for tap_index in range(4):
        tap_parts.append(lax.dot_general(flat_up, weight[tap_index], (((1,), (1,)), ((), ())), preferred_element_type=jnp.float32).reshape(half_rows, half_cols, -1))
    upper_rows = jnp.stack([tap_parts[0], tap_parts[1]], axis=2)
    bottom = jnp.stack([tap_parts[2], tap_parts[3]], axis=2)
    stacked = jnp.stack([upper_rows, bottom], axis=1)
    return stacked.reshape(2 * half_rows, 2 * half_cols, -1)

def rms_normed(tokens_in):
    return tokens_in * lax.rsqrt(lax.optimization_barrier(jnp.mean(tokens_in * tokens_in, axis=-1, keepdims=True)) + 1e-05)

def silu_slope(values):
    gate_sig = jax.nn.sigmoid(values)
    return gate_sig * (1.0 + values * (1.0 - gate_sig))

def attend(query_tokens, query_flags, query_groups, key_tokens, key_flags, key_groups, w_query, w_key, w_value, head_count):
    highest = lax.Precision.HIGHEST
    query_count = query_tokens.shape[0]
    key_count = key_tokens.shape[0]
    query_rows = jnp.dot(query_tokens, w_query, precision=highest).reshape(query_count, head_count, -1)
    key_rows = jnp.dot(key_tokens, w_key, precision=highest).reshape(key_count, head_count, -1)
    value_rows = jnp.dot(key_tokens, w_value, precision=highest).reshape(key_count, head_count, -1)
    scores = jnp.einsum('qhd,khd->hqk', query_rows, key_rows, precision=highest) / math.sqrt(query_rows.shape[2])
    allowed = (query_groups[:, None] == key_groups[None, :]).astype(jnp.float32) * key_flags[None, :]
    weights = jax.nn.sigmoid(scores + attention_bias) * allowed[None]
    mixed_rows = jnp.einsum('hqk,khd->qhd', weights, value_rows, precision=highest).reshape(query_count, -1)
    return jnp.dot(query_flags, mixed_rows, precision=highest)

def self_attend(tokens_in, tile_flags, tile_groups, w_query, w_key, w_value, head_count):
    return attend(tokens_in, tile_flags, tile_groups, tokens_in, tile_flags, tile_groups, w_query, w_key, w_value, head_count)

def reference(features, tissue, owner_map, w_conv, w_stride, w_query, w_key, w_value, cotangent):
    channels = features.shape[2]
    padded = jnp.pad(features, ((1, 1), (1, 1), (0, 0)))
    pre_act = forward_taps(padded, w_conv, NH, NW)
    pixel_mask = jnp.repeat(jnp.repeat(tissue.astype(jnp.float32), 2 * TILE, axis=0), 2 * TILE, axis=1)[:, :, None]
    summed = (features.astype(jnp.float32) + jax.nn.silu(pre_act) * pixel_mask).astype(jnp.bfloat16)
    reduced = strided_forward(summed, w_stride)
    pooled = reduced.reshape(NTY, TILE, NTX, TILE, channels).mean(axis=(1, 3))
    normed = rms_normed(pooled).astype(jnp.bfloat16)
    group_owner = owner_map.reshape(N_GY, N_GX, TYD, TXD).transpose(0, 2, 1, 3).reshape(NTY, NTX)
    tile_flags = tissue.astype(jnp.float32)
    norm_scale = 1.0 / math.sqrt(ALL_TILES)
    seed_grad = cotangent * (loss_scale * norm_scale)
    partial_sums = []
    band_grads = []
    for band_index in range(N_GY):
        first_row = band_index * TYD
        band_tokens = normed[first_row:first_row + TYD].reshape(-1, channels).astype(jnp.float32)
        band_flags = tile_flags[first_row:first_row + TYD].reshape(-1)
        band_groups = group_owner[first_row:first_row + TYD].reshape(-1)
        band_fn = partial(self_attend, tile_flags=band_flags, tile_groups=band_groups, w_query=w_query, w_key=w_key, w_value=w_value, head_count=HEADS)
        band_sum, pull_band = jax.vjp(band_fn, band_tokens)
        partial_sums.append(band_sum)
        band_grads.append(pull_band(seed_grad)[0].reshape(TYD, NTX, channels))
    embedding = lax.optimization_barrier(jnp.sum(jnp.stack(partial_sums), axis=0)) * norm_scale
    token_grad = jnp.concatenate(band_grads, axis=0).astype(jnp.bfloat16)
    token_grad = lax.optimization_barrier(token_grad).astype(jnp.float32)
    pooled_grad = jax.vjp(rms_normed, pooled)[1](token_grad)[0]
    cell_grad = (pooled_grad / (TILE * TILE)).astype(jnp.bfloat16)
    cell_grad = jnp.broadcast_to(cell_grad[:, None, :, None, :], (NTY, TILE, NTX, TILE, channels)).reshape(NH // 2, NW // 2, channels)
    sum_grad = strided_backward(cell_grad, w_stride)
    pre_grad = (sum_grad * pixel_mask * silu_slope(pre_act)).astype(jnp.bfloat16)
    grad_pad = jnp.pad(pre_grad, ((1, 1), (1, 1), (0, 0)))
    input_grad = (sum_grad + backward_taps(grad_pad, w_conv, NH, NW)).astype(jnp.bfloat16)
    conv_grad = weight_taps(padded, pre_grad, NH, NW) / loss_scale
    return (embedding, input_grad, conv_grad)
```

```python
import math

import jax
import jax.numpy as jnp
from jax import lax
from jax.experimental import pallas as pl
from jax.experimental.pallas import tpu as pltpu
from jax.sharding import Mesh, PartitionSpec as P

HEADS = 4
F32 = jnp.float32
BF16 = jnp.bfloat16
HIGH = lax.Precision.HIGHEST

attention_bias = -1.0
loss_scale = 512.0

ROWS = 32
COLS = 128
CH = 256
HALO = 48
LANES = 128


def shape(dims, dtype):
    return jax.ShapeDtypeStruct(dims, dtype)


def nt(left, right, precision=None):
    return lax.dot_general(
        left, right, (((1,), (1,)), ((), ())), precision=precision, preferred_element_type=F32
    )


def tn(left, right, precision=None):
    return lax.dot_general(
        left, right, (((0,), (0,)), ((), ())), precision=precision, preferred_element_type=F32
    )


def dot(left, right, precision=None):
    return jnp.dot(left, right, precision=precision, preferred_element_type=F32)


def iota(dims, axis):
    return lax.broadcasted_iota(jnp.int32, dims, axis)


def columns_body(first_ref, last_ref, top_first, top_last, bot_first, bot_last, left_ref, right_ref, buf):
    row, spot = iota((HALO, (ROWS + 2) * 16), 0), iota((HALO, (ROWS + 2) * 16), 1)
    for block, top, bot, out, place in (
        (first_ref, top_first, bot_first, left_ref, 0),
        (last_ref, top_last, bot_last, right_ref, 15),
    ):
        buf[0:16] = top[0]
        buf[16 : 16 + ROWS * 16] = block[...].reshape(ROWS * 16, CH)
        buf[16 + ROWS * 16 :] = bot[0]
        pick = (spot == row * 16 + place).astype(BF16)
        out[...] = dot(pick, buf[...]).astype(BF16)


def outer_columns(block, top, bot):
    side = COLS // 16 - 1
    whole = pl.BlockSpec((HALO, CH), lambda i: (0, 0))
    tall = lambda at: pl.BlockSpec((ROWS, 16, CH), lambda i: (0, at, 0))
    flat = lambda at: pl.BlockSpec((1, 16, CH), lambda i: (0, at, 0))
    return pl.pallas_call(
        columns_body,
        grid=(1,),
        in_specs=[tall(0), tall(side), flat(0), flat(side), flat(0), flat(side)],
        out_specs=[whole, whole],
        out_shape=[shape((HALO, CH), BF16)] * 2,
        scratch_shapes=[pltpu.VMEM(((ROWS + 2) * 16, CH), BF16)],
        compiler_params=pltpu.CompilerParams(vmem_limit_bytes=8 << 20),
        cost_estimate=pl.CostEstimate(flops=1 << 20, bytes_accessed=1 << 20, transcendentals=0),
    )(block, block, top, top, bot, bot)


def shifted(value, amount, edge):
    wide = value.astype(F32)
    place = iota(wide.shape, 0)
    at = 0 if amount == 1 else COLS - 1
    return jnp.where(place == at, edge, pltpu.roll(wide, amount % COLS, 0)).astype(BF16)


def forward_body(
    flags_ref, feat, top, bot, left, right, weight, strided, owner_col, flag_col,
    slope_ref, turned_ref, pooled_ref, token_ref, wide, left32, right32, mask, sums,
):
    left32[...] = left[...].astype(F32)
    right32[...] = right[...].astype(F32)
    for tile in range(2 * COLS // 16):
        mask[16 * tile : 16 * tile + 16] = jnp.full((16, CH), flags_ref[tile], F32)

    def place(at, value):
        here = pl.multiple_of(at * COLS, COLS)
        wide[pl.ds(here, COLS), 0:CH] = shifted(value, 1, left32[pl.ds(at, 1)])
        wide[pl.ds(here, COLS), CH : 2 * CH] = value
        wide[pl.ds(here, COLS), 2 * CH :] = shifted(value, -1, right32[pl.ds(at, 1)])
        turned_ref[:, pl.ds(here, COLS)] = value.T

    place(0, top[0])
    place(ROWS + 1, bot[0])

    @pl.loop(0, ROWS)
    def _(r):
        place(r + 1, feat[r])

    sums[...] = jnp.zeros_like(sums)

    @pl.loop(0, ROWS // 4)
    def _(i):
        here = pl.multiple_of(i * 4 * COLS, COLS)
        act = dot(wide[pl.ds(here, 4 * COLS)], weight[0 : 3 * CH])
        act += dot(wide[pl.ds(here + COLS, 4 * COLS)], weight[3 * CH : 6 * CH])
        act += dot(wide[pl.ds(here + 2 * COLS, 4 * COLS)], weight[6 * CH :])
        band = i // 4
        keep = mask[pl.ds(pl.multiple_of(band * COLS, COLS), COLS)]
        for half in range(2):
            total = sums[band * 2 + half]
            for j in (half, half + 2):
                value = act[j * COLS : (j + 1) * COLS]
                gate = 0.5 * jnp.tanh(0.5 * value) + 0.5
                kept = gate * keep
                summed = (feat[4 * i + j].astype(F32) + value * kept).astype(BF16)
                slope_ref[4 * i + j] = (kept * (1.0 + value * (1.0 - gate))).astype(BF16)
                total += summed.astype(F32)
            sums[band * 2 + half] = total

    row, pix = iota((16, COLS), 0), iota((16, COLS), 1)
    pick = ((pix // 16 == row % 8) & (pix % 2 == row // 8)).astype(F32)
    pooled = jnp.zeros((16, CH), F32)
    for a in range(2):
        parts = [dot(pick, sums[band * 2 + a], HIGH) for band in range(2)]
        for b in range(2):
            taken = jnp.concatenate([part[8 * b : 8 * b + 8] for part in parts], axis=0)
            pooled += dot(taken, strided[2 * a + b].astype(F32), HIGH)
    pooled = pooled * (1.0 / 64.0)
    pooled_ref[...] = pooled
    normed = pooled * lax.rsqrt(jnp.mean(pooled * pooled, axis=-1, keepdims=True) + 1e-05)
    token_ref[:, 0:CH] = normed.astype(BF16)
    one = (owner_col[...] == iota((16, LANES), 1)) & (flag_col[...] != 0)
    token_ref[:, CH:] = one.astype(F32).astype(BF16)


def attention_body(
    place_ref, got, pooled_ref, w_query, w_key, w_value, cot, strided,
    spread_ref, emb_ref, dq, dk, dv, *, seed_scale,
):
    count = got.shape[0]
    tokens = got[:, 0:CH].astype(F32)
    group = got[:, CH:]
    pair = nt(group, group)
    query, key, value = (dot(tokens, w[...], HIGH) for w in (w_query, w_key, w_value))
    seed = cot[...] * seed_scale
    lane = iota((1, CH), 1) // (CH // HEADS)
    grad_q = jnp.zeros((count, CH), F32)
    grad_k = jnp.zeros((count, CH), F32)
    columns, seeds = [], []
    scale = 1.0 / math.sqrt(CH // HEADS)
    for h in range(HEADS):
        mine = lane == h
        q_h = jnp.where(mine, query, 0.0)
        k_h = jnp.where(mine, key, 0.0)
        seed_h = jnp.where(mine, seed, 0.0)
        gate = jax.nn.sigmoid(nt(q_h, key, HIGH) * scale + attention_bias)
        weights = gate * pair
        columns.append(jnp.sum(weights, axis=0, keepdims=True))
        seeds.append(seed_h)
        along = nt(jnp.broadcast_to(seed_h, (8, CH)), value, HIGH)[0:1]
        grad_s = weights * (1.0 - gate) * along * scale
        grad_q += dot(grad_s, k_h, HIGH)
        grad_k += tn(grad_s, q_h, HIGH)
    columns = jnp.concatenate(columns + [jnp.zeros((8 - HEADS, count), F32)], axis=0)
    seeds = jnp.concatenate(seeds + [jnp.zeros((8 - HEADS, CH), F32)], axis=0)
    grad_v = tn(columns, seeds, HIGH)
    mixed = dot(columns, value, HIGH)
    mixed = jnp.sum(jnp.where(lane == iota((8, CH), 0), mixed, 0.0), axis=0, keepdims=True)
    high = mixed.astype(BF16).astype(F32)
    low = mixed - high
    rows = iota((16, LANES), 0)
    packed = jnp.zeros((16, LANES), F32)
    for i, part in enumerate((high[:, :LANES], high[:, LANES:], low[:, :LANES], low[:, LANES:])):
        packed = jnp.where(rows == i, part, packed)
    emb_ref[...] = packed.astype(BF16)

    dq[...] = grad_q
    dk[...] = grad_k
    dv[...] = grad_v
    own = pl.ds(pl.multiple_of(place_ref[0] * 16, 16), 16)
    grad = nt(dq[own], w_query[...], HIGH) + nt(dk[own], w_key[...], HIGH) + nt(dv[own], w_value[...], HIGH)
    grad = grad.astype(BF16).astype(F32)
    pooled = pooled_ref[...]
    inv = lax.rsqrt(jnp.mean(pooled * pooled, axis=-1, keepdims=True) + 1e-05)
    unit = pooled * inv
    back = inv * (grad - unit * jnp.mean(grad * unit, axis=-1, keepdims=True))
    cell = (back * (1.0 / 64.0)).astype(BF16)
    pix, row = iota((COLS, 16), 0), iota((COLS, 16), 1)
    expand = ((pix // 16 == row % 8) & (pix % 2 == row // 8)).astype(F32)
    for a in range(2):
        even, odd = nt(cell, strided[2 * a]), nt(cell, strided[2 * a + 1])
        for band in range(2):
            both = jnp.concatenate([even[8 * band : 8 * band + 8], odd[8 * band : 8 * band + 8]], axis=0)
            spread_ref[band * 2 + a] = dot(expand, both, HIGH)


def weight_body(
    core_ref, spread, slope, turned, left, right, pre_ref, keep_ref, give_ref, wide, first, last,
):
    zero = jnp.zeros((1, CH), F32)
    first[...] = jnp.zeros_like(first)
    last[...] = jnp.zeros_like(last)

    @pl.loop(0, ROWS)
    def _(r):
        here = pl.ds(pl.multiple_of(r * COLS, COLS), COLS)
        grad = (spread[(r // 16) * 2 + r % 2] * slope[r].astype(F32)).astype(BF16)
        pre_ref[r] = grad
        wide[here, CH : 2 * CH] = grad
        wide[here, 0:CH] = shifted(grad, -1, zero)
        wide[here, 2 * CH :] = shifted(grad, 1, zero)
        full = grad.astype(F32)
        for a in range(3):
            first[a, pl.ds(r + a, 1)] = full[0:1]
            last[a, pl.ds(r + a, 1)] = full[COLS - 1 : COLS]

    is_one = core_ref[0] == 1

    @pl.loop(0, 3)
    def _(a):
        rows = pl.ds(pl.multiple_of(a * COLS, COLS), ROWS * COLS)
        result = dot(turned[:, rows], wide[...])
        parts = [result[:, 0:CH], result[:, CH : 2 * CH], result[:, 2 * CH :]]
        parts[0] += tn(left[...], first[a].astype(BF16))
        parts[2] += tn(right[...], last[a].astype(BF16))
        for b in range(3):
            low, high = parts[b][:, :LANES], parts[b][:, LANES:]
            at = pl.ds(pl.multiple_of((3 * a + b) * CH, CH), CH)
            keep_ref[at] = jnp.where(is_one, high, low).astype(BF16)
            give_ref[at] = jnp.where(is_one, low, high).astype(BF16)


def input_body(pre, top, bot, left, right, spread, weight, out_ref, wide, left32, right32):
    left32[...] = left[...].astype(F32)
    right32[...] = right[...].astype(F32)

    def place(at, value):
        here = pl.multiple_of(at * COLS, COLS)
        wide[pl.ds(here, COLS), 0:CH] = shifted(value, -1, right32[pl.ds(at, 1)])
        wide[pl.ds(here, COLS), CH : 2 * CH] = value
        wide[pl.ds(here, COLS), 2 * CH :] = shifted(value, 1, left32[pl.ds(at, 1)])

    place(0, top[0])
    place(ROWS + 1, bot[0])

    @pl.loop(0, ROWS)
    def _(r):
        place(r + 1, pre[r])

    @pl.loop(0, ROWS // 4)
    def _(i):
        total = jnp.zeros((4 * COLS, CH), F32)
        for a in range(3):
            here = pl.multiple_of((4 * i + 2 - a) * COLS, COLS)
            taps = jnp.concatenate([weight[3 * a + b] for b in range(3)], axis=1)
            total += nt(wide[pl.ds(here, 4 * COLS)], taps)
        for j in range(4):
            out_ref[4 * i + j] = (spread[(i // 4) * 2 + j % 2] + total[j * COLS : (j + 1) * COLS]).astype(BF16)


def add_body(one, two, out_ref):
    out_ref[...] = (one[...].astype(F32) + two[...].astype(F32)).astype(BF16)


def sum_body(got, emb, out_ref):
    share = got.shape[1]
    total = got[0].astype(F32)
    for i in range(1, got.shape[0]):
        total += got[i].astype(F32)
    total = total.astype(BF16)
    for i in range(out_ref.shape[0]):
        out_ref[i, 0:share] = total
        out_ref[i, share:] = emb[...]


def final_body(core_ref, mine, other, grad_ref, emb_ref, *, share, bands, norm_scale):
    is_one = core_ref[0] == 1
    chips = mine.shape[0]
    rows = grad_ref.shape[0]
    for i in range(chips):
        start = i * share
        size = min(share, rows - start)
        if size <= 0:
            break
        here, there = mine[i, 0:size].astype(F32), other[i, 0:size].astype(F32)
        grad_ref[start : start + size, 0:LANES] = jnp.where(is_one, there, here) * (1.0 / loss_scale)
        grad_ref[start : start + size, LANES:] = jnp.where(is_one, here, there) * (1.0 / loss_scale)
    total = jnp.zeros((16, LANES), F32)
    for band in range(bands):
        total += mine[band * (chips // bands), share : share + 16].astype(F32)
    both = total[0:2] + total[2:4]
    emb_ref[...] = jnp.concatenate([both, jnp.zeros((6, LANES), F32)], axis=0) * norm_scale


def per_device(features, tissue, owner_map, w_conv, w_stride, w_query, w_key, w_value, cotangent):
    gy_count, gz_count, cores = lax.axis_size("gy"), lax.axis_size("gz"), lax.axis_size("core")
    gx_count, chips = gz_count * cores, gy_count * gz_count
    across = ("gz", "core")
    core = lax.axis_index("core").astype(jnp.int32).reshape(1)
    place = (lax.axis_index("gz") * cores + lax.axis_index("core")).astype(jnp.int32).reshape(1)
    tiles_all = 16 * gy_count * gx_count
    norm_scale = 1.0 / math.sqrt(tiles_all)

    def to_next(value, axis, count):
        return lax.ppermute(value, axis, [(i, i + 1) for i in range(count - 1)])

    def to_last(value, axis, count):
        return lax.ppermute(value, axis, [(i + 1, i) for i in range(count - 1)])

    def halos(block):
        top = to_next(block[ROWS - 1 :], "gy", gy_count)
        bot = to_last(block[:1], "gy", gy_count)
        first, last = outer_columns(block, top, bot)
        return top, bot, to_next(last, across, gx_count), to_last(first, across, gx_count)

    smem = pl.BlockSpec(memory_space=pltpu.SMEM)
    vmem = pl.BlockSpec(memory_space=pltpu.VMEM)

    def run(body, args, outs, scratch=(), flops=0, mib=24):
        specs = [smem if a.dtype == jnp.int32 and a.ndim == 1 else vmem for a in args]
        return pl.pallas_call(
            body,
            in_specs=specs,
            out_shape=outs,
            scratch_shapes=list(scratch),
            compiler_params=pltpu.CompilerParams(vmem_limit_bytes=mib << 20),
            cost_estimate=pl.CostEstimate(flops=flops, bytes_accessed=4 << 20, transcendentals=0),
        )(*args)

    edge32 = pltpu.VMEM((HALO, CH), F32)
    wide = pltpu.VMEM(((ROWS + 2) * COLS, 3 * CH), BF16)
    conv_flops = 2 * ROWS * COLS * 9 * CH * CH

    top, bot, left, right = halos(features)
    slope, turned, pooled, token = run(
        forward_body,
        (
            tissue.reshape(-1), features, top, bot, left, right, w_conv.reshape(9 * CH, CH), w_stride,
            owner_map.reshape(16, 1), tissue.reshape(16, 1),
        ),
        [
            shape((ROWS, COLS, CH), BF16),
            shape((CH, (ROWS + 2) * COLS), BF16),
            shape((16, CH), F32),
            shape((16, CH + LANES), BF16),
        ],
        [wide, edge32, edge32, pltpu.VMEM((2 * COLS, CH), F32), pltpu.VMEM((4, COLS, CH), F32)],
        flops=conv_flops,
        mib=32,
    )
    got = lax.all_to_all(
        jnp.broadcast_to(token[None], (gx_count,) + token.shape), across, split_axis=0, concat_axis=0, tiled=True
    ).reshape(gx_count * 16, CH + LANES)
    count = gx_count * 16
    spread, emb = run(
        lambda *refs: attention_body(*refs, seed_scale=loss_scale * norm_scale),
        (place, got, pooled, w_query, w_key, w_value, cotangent.reshape(1, CH), w_stride),
        [shape((4, COLS, CH), F32), shape((16, LANES), BF16)],
        [pltpu.VMEM((count, CH), F32)] * 3,
        flops=1 << 30,
    )
    pre, keep, give = run(
        weight_body,
        (core, spread, slope, turned, left, right),
        [shape((ROWS, COLS, CH), BF16), shape((9 * CH, LANES), BF16), shape((9 * CH, LANES), BF16)],
        [pltpu.VMEM((ROWS * COLS, 3 * CH), BF16), pltpu.VMEM((3, HALO, CH), F32), pltpu.VMEM((3, HALO, CH), F32)],
        flops=conv_flops,
        mib=32,
    )
    swap = [(i, i ^ 1) for i in range(cores)]
    taken = lax.ppermute(give, "core", swap)
    share = -(-9 * CH // (16 * chips)) * 16
    chip_sum = run(add_body, (keep, taken), shape((9 * CH, LANES), BF16), flops=1 << 20)
    chip_sum = jnp.pad(chip_sum, ((0, share * chips - 9 * CH), (0, 0)))
    parts = lax.all_to_all(
        chip_sum.reshape(chips, share, LANES), ("gy", "gz"), split_axis=0, concat_axis=0, tiled=True
    )
    pre_top, pre_bot, pre_left, pre_right = halos(pre)
    input_grad = run(
        input_body,
        (pre, pre_top, pre_bot, pre_left, pre_right, spread, w_conv),
        shape((ROWS, COLS, CH), BF16),
        [wide, edge32, edge32],
        flops=conv_flops,
        mib=32,
    )
    spread_sum = run(sum_body, (parts, emb), shape((chips, share + 16, LANES), BF16), flops=1 << 20)
    mine = lax.all_to_all(spread_sum, ("gy", "gz"), split_axis=0, concat_axis=0, tiled=True)
    other = lax.ppermute(mine, "core", swap)
    conv_grad, embedding = run(
        lambda *refs: final_body(*refs, share=share, bands=gy_count, norm_scale=norm_scale),
        (core, mine, other),
        [shape((9 * CH, CH), F32), shape((8, LANES), F32)],
        flops=1 << 20,
    )
    return embedding[0:2].reshape(CH), input_grad, conv_grad.reshape(9, CH, CH)


def solution(mesh):
    sizes = mesh.devices.shape
    split = Mesh(mesh.devices.reshape(sizes[0], sizes[1] // 2, 2), ("gy", "gz", "core"))
    gx = ("gz", "core")
    in_specs = (P("gy", gx, None), P("gy", gx), P("gy", gx, None, None), P(), P(), P(), P(), P(), P())
    out_specs = (P(), P("gy", gx, None), P())
    return jax.shard_map(per_device, mesh=split, in_specs=in_specs, out_specs=out_specs, check_vma=False)
```

```python
import math

import jax
import jax.numpy as jnp
from jax import lax
from jax.experimental import pallas as pl
from jax.experimental.pallas import tpu as pltpu
from jax.sharding import Mesh, PartitionSpec as P

HEADS = 4
F32 = jnp.float32
BF16 = jnp.bfloat16

attention_bias = -1.0
loss_scale = 512.0

ROWS = 32
COLS = 128
CH = 256
HALO = 48
LANES = 128
STEP = 3
BLOCKS = (ROWS - 2) // STEP
TILE_CELLS = 64


def shape(dims, dtype):
    return jax.ShapeDtypeStruct(dims, dtype)


def nt(left, right):
    return lax.dot_general(left, right, (((1,), (1,)), ((), ())), preferred_element_type=F32)


def tn(left, right):
    return lax.dot_general(left, right, (((0,), (0,)), ((), ())), preferred_element_type=F32)


def nn(left, right):
    return jnp.dot(left, right, preferred_element_type=F32)


def halves(value):
    high = value.astype(BF16)
    return high, (value - high.astype(F32)).astype(BF16)


def wide_product(product, left, right):
    (a, b), (c, d) = left, right
    return product(a, c) + (product(a, d) + product(b, c))


def iota(dims, axis):
    return lax.broadcasted_iota(jnp.int32, dims, axis)


def gate_of(value):
    return 0.5 * jnp.tanh(0.5 * value) + 0.5


def copies(pairs, sems):
    started = [pltpu.make_async_copy(a, b, sems.at[i]) for i, (a, b) in enumerate(pairs)]
    for one in started:
        one.start()
    return started


def columns_body(block, top, bot, left_ref, right_ref, buf, sems):
    count = ROWS + 2
    started = []
    for side, at in enumerate((0, COLS - 16)):
        started += copies(
            [(block.at[:, at : at + 16], buf.at[side, 1 : ROWS + 1])], sems.at[side : side + 1]
        )
        buf[side, 0] = top[0, at : at + 16]
        buf[side, ROWS + 1] = bot[0, at : at + 16]
    for one in started:
        one.wait()
    row, spot = iota((HALO, count * 16), 0), iota((HALO, count * 16), 1)
    for side, (out, place) in enumerate(((left_ref, 0), (right_ref, 15))):
        pick = (spot == row * 16 + place).astype(F32).astype(BF16)
        out[...] = nn(pick, buf[side].reshape(count * 16, CH)).astype(BF16)


def forward_taps(weight, b):
    return jnp.concatenate([weight[3 * a + b] for a in range(3)], axis=0)


def forward_body(
    flags_ref, feat_in, weight_in, feat, weight, slope_ref, sums, cols, prod_a, prod_b, mask, sems
):
    started = copies([(weight_in, weight), (feat_in, feat)], sems)
    for tile in range(2 * COLS // 16):
        mask[16 * tile : 16 * tile + 16] = jnp.full((16, CH), flags_ref[tile], jnp.int32).astype(F32)
    sums[...] = jnp.zeros_like(sums)
    for one in started:
        one.wait()

    def products(block, out):
        first = 1 + STEP * block
        taken = [feat[pl.ds(first + a - 1, STEP)].reshape(STEP * COLS, CH) for a in range(3)]
        taken = jnp.concatenate(taken, axis=1)
        for b in range(3):
            out[b] = nn(taken, forward_taps(weight, b))

    def finish(block, prod, parity):
        band = block // (BLOCKS // 2)
        keep = mask[pl.ds(pl.multiple_of(band * COLS, COLS), COLS)]
        for j in range(STEP):
            r = 1 + STEP * block + j
            low, mid, high = (prod[b, j * COLS : (j + 1) * COLS] for b in range(3))
            value = mid + pltpu.roll(low, 1, 0) + pltpu.roll(high, COLS - 1, 0)
            gate = gate_of(value)
            kept = gate * keep
            pixel = feat[r].astype(F32)
            summed = (pixel + value * kept).astype(BF16).astype(F32)
            slope_ref[r] = (kept * (1.0 + value * (1.0 - gate))).astype(BF16)
            sums[band * 2 + (parity + j) % 2] += summed
            one = pl.ds(r, 1)
            cols[0, one] = mid[0:1] + high[1:2]
            cols[1, one] = mid[COLS - 1 :] + low[COLS - 2 : COLS - 1]
            cols[2, one] = summed[0:1]
            cols[3, one] = summed[COLS - 1 :]
            cols[4, one] = pixel[0:1]
            cols[5, one] = pixel[COLS - 1 :]

    products(0, prod_a)

    @pl.loop(0, BLOCKS // 2)
    def _(k):
        products(2 * k + 1, prod_b)
        finish(2 * k, prod_a, 1)
        products(jnp.minimum(2 * k + 2, BLOCKS - 1), prod_a)
        finish(2 * k + 1, prod_b, 0)


def border_body(
    flags_ref, feat, weight, sums, cols, top, bot, left, right, strided, owner_col, flag_col,
    pooled_ref, token_ref, edge_ref, side_ref, side32,
):
    added = []
    for i, side in enumerate((left, right)):
        side32[...] = side[...].astype(F32)
        near = [side32[a : a + ROWS].astype(BF16) for a in range(3)]
        added.append(nn(jnp.concatenate(near, axis=1), forward_taps(weight, 2 * i)))

    def pair(one, two):
        return jnp.concatenate([one, two], axis=0)

    taken = jnp.concatenate(
        [pair(top[0], feat[ROWS - 2]), pair(feat[0], feat[ROWS - 1]), pair(feat[1], bot[0])], axis=1
    )
    low, mid, high = (nn(taken, forward_taps(weight, b)) for b in range(3))
    pix = iota((COLS, CH), 0)
    rows = []
    for i, r in enumerate((0, ROWS - 1)):
        part = slice(i * COLS, (i + 1) * COLS)
        before = jnp.where(pix == 0, added[0][r : r + 1], pltpu.roll(low[part], 1, 0))
        after = jnp.where(pix == COLS - 1, added[1][r : r + 1], pltpu.roll(high[part], COLS - 1, 0))
        value = mid[part] + before + after
        gate = gate_of(value)
        keep = jnp.concatenate(
            [jnp.full((16, CH), flags_ref[8 * i + t], jnp.int32).astype(F32) for t in range(8)], axis=0
        )
        kept = gate * keep
        edge_ref[i] = (kept * (1.0 + value * (1.0 - gate))).astype(BF16)
        rows.append((feat[r].astype(F32) + value * kept).astype(BF16).astype(F32))

    line = iota((ROWS, CH), 0)
    deltas = []
    for i in range(2):
        value = cols[i] + added[i]
        gate = gate_of(value)
        tile = 7 * i
        keep = jnp.where(line < ROWS // 2, flags_ref[tile], flags_ref[8 + tile]).astype(F32)
        kept = gate * keep
        side_ref[i] = kept * (1.0 + value * (1.0 - gate))
        summed = (cols[4 + i] + value * kept).astype(BF16).astype(F32)
        inside = (line > 0) & (line < ROWS - 1)
        deltas.append(jnp.where(inside, summed - cols[2 + i], 0.0))

    row, spot = iota((16, COLS), 0), iota((16, COLS), 1)
    pick = ((spot // 16 == row % 8) & (spot % 2 == row // 8)).astype(F32).astype(BF16)
    place = iota((16, CH), 0)
    parts = {}
    for band in range(2):
        for a in range(2):
            total = sums[2 * band + a]
            if band == a:
                total += rows[band]
            high, low = halves(total)
            part = nn(pick, high) + nn(pick, low)
            mine = (line // 16 == band) & (line % 2 == a)
            for i in range(2):
                delta = jnp.sum(jnp.where(mine, deltas[i], 0.0), axis=0, keepdims=True)
                part += jnp.where(place == 15 * i, delta, 0.0)
            parts[band, a] = part
    taken = [
        jnp.concatenate([parts[band, a][8 * b : 8 * b + 8] for band in range(2)], axis=0)
        for a in range(2)
        for b in range(2)
    ]
    high, low = halves(jnp.concatenate(taken, axis=1))
    flat = strided[...].reshape(4 * CH, CH)
    pooled = (nn(high, flat) + nn(low, flat)) * (1.0 / TILE_CELLS)
    pooled_ref[...] = pooled
    normed = pooled * lax.rsqrt(jnp.mean(pooled * pooled, axis=-1, keepdims=True) + 1e-05)
    token_ref[:, 0:CH] = normed.astype(BF16)
    one = (owner_col[...] == iota((16, LANES), 1)) & (flag_col[...] != 0)
    token_ref[:, CH:] = one.astype(F32).astype(BF16)


def turn_body(feat, top, bot, w_query, w_key, w_value, token, turned_ref, high_ref, low_ref, buf, sems):
    started = copies([(w, buf.at[i]) for i, w in enumerate((w_query, w_key, w_value))], sems)
    turned_ref[:, 0:COLS] = top[0].T
    turned_ref[:, (ROWS + 1) * COLS :] = bot[0].T

    @pl.loop(0, ROWS // 4)
    def _(i):
        for j in range(4):
            here = pl.multiple_of((4 * i + j + 1) * COLS, COLS)
            turned_ref[:, pl.ds(here, COLS)] = feat[4 * i + j].T

    for i, one in enumerate(started):
        one.wait()
        high, low = halves(buf[i])
        high_ref[:, i * CH : (i + 1) * CH] = high
        low_ref[:, i * CH : (i + 1) * CH] = low


def pair_body(one, two, out_ref):
    out_ref[0:16] = one[...]
    out_ref[16:32] = two[...]


def attention_body(*refs, seed_scale, pieces):
    got = refs[:pieces]
    pooled_ref, high_w, low_w, cot, strided, spread_ref, emb_ref = refs[pieces:]
    got = jnp.concatenate([piece[...] for piece in got], axis=0)
    count = got.shape[0]
    tokens, group = got[:, 0:CH], got[:, CH:]
    pair = nt(group, group)
    pairs = jnp.concatenate([pair] * HEADS, axis=0)
    projected = nn(tokens, high_w[...]) + nn(tokens, low_w[...])
    query, key, value = (projected[:, i * CH : (i + 1) * CH] for i in range(3))
    lane = iota((1, CH), 1) // (CH // HEADS)
    scale = 1.0 / math.sqrt(CH // HEADS)

    def by_head(array):
        return jnp.concatenate([jnp.where(lane == h, array, 0.0) for h in range(HEADS)], axis=0)

    queries, keys = halves(by_head(query)), halves(by_head(key))
    gate = gate_of(wide_product(nt, queries, halves(key)) * scale + attention_bias)
    weights = gate * pairs
    seed = cot[...] * seed_scale
    seeds = jnp.where(lane == iota((8, CH), 0), seed, 0.0)
    values = halves(value)
    along = wide_product(nt, halves(seeds), values)
    columns, grads = [], []
    for h in range(HEADS):
        part = slice(h * count, (h + 1) * count)
        columns.append(jnp.sum(weights[part], axis=0, keepdims=True))
        grads.append(weights[part] * (1.0 - gate[part]) * (along[h : h + 1] * scale))
    columns = halves(jnp.concatenate(columns + [jnp.zeros((8 - HEADS, count), F32)], axis=0))
    grad_q = wide_product(nn, halves(jnp.concatenate([g[0:16] for g in grads], axis=1)), keys)
    narrow = halves(jnp.concatenate([g[:, 0:LANES] for g in grads], axis=0))
    grad_k = wide_product(tn, narrow, queries)[0:16]
    grad_v = wide_product(tn, columns, halves(seeds))[0:16]
    mixed = wide_product(nn, columns, values)
    mixed = jnp.sum(jnp.where(lane == iota((8, CH), 0), mixed, 0.0), axis=0, keepdims=True)
    high = mixed.astype(BF16).astype(F32)
    low = mixed - high
    rows = iota((16, LANES), 0)
    packed = jnp.zeros((16, LANES), F32)
    for i, part in enumerate((high[:, :LANES], high[:, LANES:], low[:, :LANES], low[:, LANES:])):
        packed = jnp.where(rows == i, part, packed)
    emb_ref[...] = packed.astype(BF16)

    grads = halves(jnp.concatenate([grad_q, grad_k, grad_v], axis=1))
    grad = wide_product(nt, grads, (high_w[...], low_w[...]))
    grad = grad.astype(BF16).astype(F32)
    pooled = pooled_ref[...]
    inv = lax.rsqrt(jnp.mean(pooled * pooled, axis=-1, keepdims=True) + 1e-05)
    unit = pooled * inv
    back = inv * (grad - unit * jnp.mean(grad * unit, axis=-1, keepdims=True))
    cell = (back * (1.0 / TILE_CELLS)).astype(BF16)
    spot, row = iota((COLS, 16), 0), iota((COLS, 16), 1)
    expand = ((spot // 16 == row % 8) & (spot % 2 == row // 8)).astype(F32).astype(BF16)
    taps = nt(cell, strided[...].reshape(4 * CH, CH))
    for band in range(2):
        here = taps[8 * band : 8 * band + 8]
        both = [
            jnp.concatenate([here[:, (2 * a + b) * CH : (2 * a + b + 1) * CH] for a in range(2)], axis=1)
            for b in range(2)
        ]
        high, low = halves(jnp.concatenate(both, axis=0))
        spread = nn(expand, high) + nn(expand, low)
        for a in range(2):
            spread_ref[band * 2 + a] = spread[:, a * CH : (a + 1) * CH]


GROUP = 8


def weight_body(
    core_ref, spread, slope, edge, side, turned, left, right,
    pre_ref, keep_ref, give_ref, wide_a, wide_b, total, first, last,
):
    first[...] = jnp.zeros_like(first)
    last[...] = jnp.zeros_like(last)
    pix = iota((COLS, CH), 0)

    def put(r, j, grad, wide):
        low = grad.astype(BF16)
        full = low.astype(F32)
        pre_ref[r] = low
        here = slice(j * COLS, (j + 1) * COLS)
        wide[here, CH : 2 * CH] = low
        wide[here, 0:CH] = jnp.where(pix == COLS - 1, 0.0, pltpu.roll(full, COLS - 1, 0)).astype(BF16)
        wide[here, 2 * CH :] = jnp.where(pix == 0, 0.0, pltpu.roll(full, 1, 0)).astype(BF16)
        for a in range(3):
            first[a, pl.ds(r + a, 1)] = full[0:1]
            last[a, pl.ds(r + a, 1)] = full[COLS - 1 : COLS]

    def build(group, wide):
        for j in range(GROUP):
            r = group * GROUP + j
            here = slope[r].astype(F32)
            here = jnp.where(pix == 0, side[0, pl.ds(r, 1)], here)
            here = jnp.where(pix == COLS - 1, side[1, pl.ds(r, 1)], here)
            if j == 0:
                here = jnp.where(r == 0, edge[0].astype(F32), here)
            if j == GROUP - 1:
                here = jnp.where(r == ROWS - 1, edge[1].astype(F32), here)
            put(r, j, spread[(r // 16) * 2 + j % 2] * here, wide)

    def products(group, wide):
        def near(a):
            return turned[:, pl.ds(pl.multiple_of((group * GROUP + a) * COLS, COLS), GROUP * COLS)]

        taken = jnp.concatenate([near(a) for a in range(3)], axis=0)
        return nn(taken, wide[...])

    groups = ROWS // GROUP
    total[...] = jnp.zeros_like(total)
    build(0, wide_a)

    @pl.loop(0, groups // 2)
    def _(k):
        build(2 * k + 1, wide_b)
        total[...] += products(2 * k, wide_a)
        build(jnp.minimum(2 * k + 2, groups - 1), wide_a)
        total[...] += products(2 * k + 1, wide_b)

    is_one = core_ref[0] == 1
    for a in range(3):
        for b in range(3):
            part = total[a * CH : (a + 1) * CH, b * CH : (b + 1) * CH]
            if b == 0:
                part += tn(left[...], first[a].astype(BF16))
            if b == 2:
                part += tn(right[...], last[a].astype(BF16))
            low, high = part[:, :LANES], part[:, LANES:]
            at = slice((3 * a + b) * CH, (3 * a + b + 1) * CH)
            keep_ref[at] = jnp.where(is_one, high, low).astype(BF16)
            give_ref[at] = jnp.where(is_one, low, high).astype(BF16)


def input_body(pre, top, bot, left, right, spread, weight, out_ref, prod_a, prod_b, side32, added):
    def taps(b):
        return jnp.concatenate([weight[3 * a + b] for a in range(3)], axis=1)

    for i, side in enumerate((left, right)):
        side32[...] = side[...].astype(F32)
        near = [side32[2 - a : 2 - a + ROWS].astype(BF16) for a in range(3)]
        added[i] = nt(jnp.concatenate(near, axis=1), taps(2 - 2 * i))

    pix = iota((COLS, CH), 0)

    def finish(r, parity, band, low, mid, high):
        after = jnp.where(pix == COLS - 1, added[1, pl.ds(r, 1)], pltpu.roll(low, COLS - 1, 0))
        before = jnp.where(pix == 0, added[0, pl.ds(r, 1)], pltpu.roll(high, 1, 0))
        out_ref[r] = (spread[band * 2 + parity] + (mid + after + before)).astype(BF16)

    def pair(one, two):
        return jnp.concatenate([one, two], axis=0)

    taken = jnp.concatenate(
        [pair(pre[1], bot[0]), pair(pre[0], pre[ROWS - 1]), pair(top[0], pre[ROWS - 2])], axis=1
    )
    edges = [nt(taken, taps(b)) for b in range(3)]
    for i, r in enumerate((0, ROWS - 1)):
        finish(r, i, i, *(part[i * COLS : (i + 1) * COLS] for part in edges))

    def products(block, out):
        first = 1 + STEP * block
        rows = [pre[pl.ds(first + 1 - a, STEP)].reshape(STEP * COLS, CH) for a in range(3)]
        rows = jnp.concatenate(rows, axis=1)
        for b in range(3):
            out[b] = nt(rows, taps(b))

    def close(block, prod, parity):
        band = block // (BLOCKS // 2)
        for j in range(STEP):
            parts = (prod[b, j * COLS : (j + 1) * COLS] for b in range(3))
            finish(1 + STEP * block + j, (parity + j) % 2, band, *parts)

    products(0, prod_a)

    @pl.loop(0, BLOCKS // 2)
    def _(k):
        products(2 * k + 1, prod_b)
        close(2 * k, prod_a, 1)
        products(jnp.minimum(2 * k + 2, BLOCKS - 1), prod_a)
        close(2 * k + 1, prod_b, 0)


def sum_body(place_ref, *refs, terms):
    outs, total_ref = refs[terms:-1], refs[-1]
    total = refs[0][...].astype(F32)
    for one in refs[1:terms]:
        total += one[...].astype(F32)
    total_ref[...] = total.astype(BF16)
    count, size = len(outs), outs[0].shape[0]
    for k, out in enumerate(outs):
        at = lax.rem(place_ref[0] + k, count) * size
        out[...] = total_ref[pl.ds(pl.multiple_of(at, 16), size)]


def last_sum_body(*refs):
    emb, out = refs[-2:]
    total = refs[0][...].astype(F32)
    for one in refs[1:-2]:
        total += one[...].astype(F32)
    out[0 : total.shape[0]] = total.astype(BF16)
    out[total.shape[0] :] = emb[...]


def stack_body(*refs):
    for i, one in enumerate(refs[:-1]):
        refs[-1][i] = one[...]


def final_body(place_ref, mine, other, grad_ref, emb_ref, *, share, norm_scale):
    gy, gz, core = place_ref[0], place_ref[1], place_ref[2]
    is_one = core == 1
    bands, depth = mine.shape[0], mine.shape[1]
    for k in range(bands):
        band = lax.rem(gy + bands - k, bands)
        for j in range(depth):
            at = (band * depth + lax.rem(gz + depth - j, depth)) * share
            here = pl.ds(pl.multiple_of(at, 16), share)
            one = mine[k, j, 0:share].astype(F32) * (1.0 / loss_scale)
            two = other[k, j, 0:share].astype(F32) * (1.0 / loss_scale)
            grad_ref[here, 0:LANES] = jnp.where(is_one, two, one)
            grad_ref[here, LANES:] = jnp.where(is_one, one, two)
    total = jnp.zeros((16, LANES), F32)
    for band in range(bands):
        k = lax.rem(gy + bands - band, bands)
        one, two = (array[k, gz, share : share + 16].astype(F32) for array in (mine, other))
        total += jnp.where(is_one, two, one)
    both = total[0:2] + total[2:4]
    emb_ref[...] = jnp.concatenate([both, jnp.zeros((6, LANES), F32)], axis=0) * norm_scale


SMEM = pl.BlockSpec(memory_space=pltpu.SMEM)
VMEM = pl.BlockSpec(memory_space=pltpu.VMEM)
HBM = pl.BlockSpec(memory_space=pltpu.HBM)


def run(body, args, outs, scratch=(), flops=1 << 20, mib=8, far=()):
    specs = [HBM if i in far else SMEM if a.dtype == jnp.int32 and a.ndim == 1 else VMEM for i, a in enumerate(args)]
    return pl.pallas_call(
        body,
        in_specs=specs,
        out_shape=outs,
        scratch_shapes=list(scratch),
        compiler_params=pltpu.CompilerParams(vmem_limit_bytes=mib << 20),
        cost_estimate=pl.CostEstimate(flops=flops, bytes_accessed=1 << 20, transcendentals=0),
    )(*args)


def per_device(features, tissue, owner_map, w_conv, w_stride, w_query, w_key, w_value, cotangent):
    gy_count, gz_count, cores = lax.axis_size("gy"), lax.axis_size("gz"), lax.axis_size("core")
    gx_count, chips = gz_count * cores, gy_count * gz_count
    across = ("gz", "core")
    gy, gz, core = (lax.axis_index(name).astype(jnp.int32) for name in ("gy", "gz", "core"))
    place = jnp.stack([gy, gz, core])
    norm_scale = 1.0 / math.sqrt(16 * gy_count * gx_count)
    swap = [(i, i ^ 1) for i in range(cores)]

    def to_next(value, axis, count):
        return lax.ppermute(value, axis, [(i, i + 1) for i in range(count - 1)])

    def to_last(value, axis, count):
        return lax.ppermute(value, axis, [(i + 1, i) for i in range(count - 1)])

    def around(value, axis, count, by):
        return lax.ppermute(value, axis, [(i, (i + by) % count) for i in range(count)])

    def halos(block):
        top = to_next(block[ROWS - 1 :], "gy", gy_count)
        bot = to_last(block[:1], "gy", gy_count)
        first, last = run(
            columns_body,
            (block, top, bot),
            [shape((HALO, CH), BF16)] * 2,
            [pltpu.VMEM((2, ROWS + 2, 16, CH), BF16), pltpu.SemaphoreType.DMA((2,))],
            far=(0,),
        )
        return top, bot, to_next(last, across, gx_count), to_last(first, across, gx_count)

    conv_flops = 2 * ROWS * COLS * 9 * CH * CH
    prod = pltpu.VMEM((3, STEP * COLS, CH), F32)
    side32 = pltpu.VMEM((HALO, CH), F32)
    flags = tissue.reshape(-1)

    top, bot, left, right = halos(features)
    feat, weight, slope, sums, cols = run(
        forward_body,
        (flags, features, w_conv),
        [
            shape((ROWS, COLS, CH), BF16),
            shape((9, CH, CH), BF16),
            shape((ROWS, COLS, CH), BF16),
            shape((4, COLS, CH), F32),
            shape((6, ROWS, CH), F32),
        ],
        [prod, prod, pltpu.VMEM((2 * COLS, CH), F32), pltpu.SemaphoreType.DMA((2,))],
        flops=conv_flops,
        mib=20,
        far=(1, 2),
    )
    pooled, token, edge, side = run(
        border_body,
        (
            flags, feat, weight, sums, cols, top, bot, left, right, w_stride,
            owner_map.reshape(16, 1), tissue.reshape(16, 1),
        ),
        [
            shape((16, CH), F32),
            shape((16, CH + LANES), BF16),
            shape((2, COLS, CH), BF16),
            shape((2, ROWS, CH), F32),
        ],
        [side32],
        flops=conv_flops // 8,
        mib=16,
    )
    both = run(
        pair_body, (token, lax.ppermute(token, "core", swap)), shape((32, CH + LANES), BF16), mib=1
    )
    pieces = [both] + [around(both, "gz", gz_count, k) for k in range(1, gz_count)]
    turned, high_w, low_w = run(
        turn_body,
        (feat, top, bot, w_query, w_key, w_value, token),
        [shape((CH, (ROWS + 2) * COLS), BF16), shape((CH, 3 * CH), BF16), shape((CH, 3 * CH), BF16)],
        [pltpu.VMEM((3, CH, CH), F32), pltpu.SemaphoreType.DMA((3,))],
        flops=conv_flops // 4,
        mib=16,
        far=(3, 4, 5),
    )
    spread, emb = run(
        lambda *refs: attention_body(*refs, seed_scale=loss_scale * norm_scale, pieces=gz_count),
        (*pieces, pooled, high_w, low_w, cotangent.reshape(1, CH), w_stride),
        [shape((4, COLS, CH), F32), shape((16, LANES), BF16)],
        flops=1 << 30,
        mib=16,
    )
    wide = pltpu.VMEM((GROUP * COLS, 3 * CH), BF16)
    border = pltpu.VMEM((3, HALO, CH), F32)
    pre, keep, give = run(
        weight_body,
        (core.reshape(1), spread, slope, edge, side, turned, left, right),
        [shape((ROWS, COLS, CH), BF16), shape((9 * CH, LANES), BF16), shape((9 * CH, LANES), BF16)],
        [wide, wide, pltpu.VMEM((3 * CH, 3 * CH), F32), border, border],
        flops=conv_flops,
        mib=28,
    )

    share = -(-9 * CH // (16 * chips)) * 16
    spare = share * chips - 9 * CH
    taken = lax.ppermute(give, "core", swap)
    if spare:
        keep, taken = (jnp.pad(a, ((0, spare), (0, 0))) for a in (keep, taken))

    def summed(at, terms, count):
        rows = terms[0].shape[0]
        outs = run(
            lambda *refs: sum_body(*refs, terms=len(terms)),
            (at.reshape(1), *terms),
            [shape((rows // count, LANES), BF16)] * count,
            [pltpu.VMEM((rows, LANES), BF16)],
        )
        return outs

    parts = summed(gy, [keep, taken], gy_count)
    parts = [parts[0]] + [around(parts[k], "gy", gy_count, k) for k in range(1, gy_count)]
    parts = summed(gz, parts, gz_count)
    parts = [parts[0]] + [around(parts[k], "gz", gz_count, k) for k in range(1, gz_count)]
    mine = run(last_sum_body, (*parts, emb), shape((share + 16, LANES), BF16))
    lines = [mine] + [around(mine, "gz", gz_count, k) for k in range(1, gz_count)]
    line = run(stack_body, tuple(lines), shape((gz_count, share + 16, LANES), BF16))
    planes = [line] + [around(line, "gy", gy_count, k) for k in range(1, gy_count)]
    plane = run(stack_body, tuple(planes), shape((gy_count, gz_count, share + 16, LANES), BF16))
    other = lax.ppermute(plane, "core", swap)
    conv_grad, embedding = run(
        lambda *refs: final_body(*refs, share=share, norm_scale=norm_scale),
        (place, plane, other),
        [shape((share * chips, CH), F32), shape((8, LANES), F32)],
        mib=16,
    )

    pre_top, pre_bot, pre_left, pre_right = halos(pre)
    input_grad = run(
        input_body,
        (pre, pre_top, pre_bot, pre_left, pre_right, spread, weight),
        shape((ROWS, COLS, CH), BF16),
        [prod, prod, side32, pltpu.VMEM((2, ROWS, CH), F32)],
        flops=conv_flops,
        mib=20,
    )
    return embedding[0:2].reshape(CH), input_grad, conv_grad[: 9 * CH].reshape(9, CH, CH)


def solution(mesh):
    sizes = mesh.devices.shape
    split = Mesh(mesh.devices.reshape(sizes[0], sizes[1] // 2, 2), ("gy", "gz", "core"))
    gx = ("gz", "core")
    in_specs = (P("gy", gx, None), P("gy", gx), P("gy", gx, None, None), P(), P(), P(), P(), P(), P())
    out_specs = (P(), P("gy", gx, None), P())
    return jax.shard_map(per_device, mesh=split, in_specs=in_specs, out_specs=out_specs, check_vma=False)
```

```python
import math

import jax
import jax.numpy as jnp
from jax import lax
from jax.experimental import pallas as pl
from jax.experimental.pallas import tpu as pltpu
from jax.sharding import Mesh, PartitionSpec as P

HEADS = 4
F32 = jnp.float32
BF16 = jnp.bfloat16

attention_bias = -1.0
loss_scale = 512.0

ROWS = 32
COLS = 128
CH = 256
HALO = 48
LANES = 128
STEP = 5
BLOCKS = (ROWS - 2) // STEP
TILE_CELLS = 64


def shape(dims, dtype):
    return jax.ShapeDtypeStruct(dims, dtype)


def nt(left, right):
    return lax.dot_general(left, right, (((1,), (1,)), ((), ())), preferred_element_type=F32)


def tn(left, right):
    return lax.dot_general(left, right, (((0,), (0,)), ((), ())), preferred_element_type=F32)


def nn(left, right):
    return jnp.dot(left, right, preferred_element_type=F32)


def halves(value):
    high = value.astype(BF16)
    return high, (value - high.astype(F32)).astype(BF16)


def wide_product(product, left, right):
    (a, b), (c, d) = left, right
    return product(a, c) + (product(a, d) + product(b, c))


def iota(dims, axis):
    return lax.broadcasted_iota(jnp.int32, dims, axis)


def gate_of(value):
    return 0.5 * jnp.tanh(0.5 * value) + 0.5


def copies(pairs, sems):
    started = [pltpu.make_async_copy(a, b, sems.at[i]) for i, (a, b) in enumerate(pairs)]
    for one in started:
        one.start()
    return started


def outer_body(block, first_ref, last_ref, left_ref, right_ref, buf, sems):
    started = copies(
        [
            (block.at[0:1], first_ref),
            (block.at[ROWS - 1 : ROWS], last_ref),
            (block.at[:, 0:16], buf.at[0]),
            (block.at[:, COLS - 16 : COLS], buf.at[1]),
        ],
        sems,
    )
    for one in started:
        one.wait()
    row, spot = iota((HALO, ROWS * 16), 0), iota((HALO, ROWS * 16), 1)
    for side, (out, place) in enumerate(((left_ref, 0), (right_ref, 15))):
        pick = (spot == (row - 1) * 16 + place).astype(F32).astype(BF16)
        out[...] = nn(pick, buf[side].reshape(ROWS * 16, CH)).astype(BF16)


def corner_body(left, right, top, bot, left_ref, right_ref):
    row = iota((HALO, CH), 0)
    for side, out, at in ((left, left_ref, 0), (right, right_ref, COLS - 16)):
        part = slice(0, 1) if at == 0 else slice(15, 16)
        above = top[0, at : at + 16].astype(F32)[part]
        below = bot[0, at : at + 16].astype(F32)[part]
        whole = jnp.where(row == 0, above, jnp.where(row == ROWS + 1, below, side[...].astype(F32)))
        out[...] = whole.astype(BF16)


def forward_taps(weight, b):
    return jnp.concatenate([weight[3 * a + b] for a in range(3)], axis=0)


def taken_rows(array, first, steps):
    rows = [array[pl.ds(first + step, STEP)].reshape(STEP * COLS, CH) for step in steps]
    return jnp.concatenate(rows, axis=1)


BESIDE = ((0, 1), (2, 3), (4,))


def forward_body(flags_ref, feat, weight, slope_ref, sums, cols, prod_a, prod_b, mask):
    for band in range(2):
        for tile in range(8):
            at = band * COLS + 16 * tile
            mask[at : at + 16] = jnp.full((16, CH), flags_ref[band, tile], jnp.int32).astype(F32)
    sums[...] = jnp.zeros_like(sums)

    def finish(block, j, prod, parity):
        band = block // (BLOCKS // 2)
        keep = mask[pl.ds(pl.multiple_of(band * COLS, COLS), COLS)]
        r = 1 + STEP * block + j
        low, mid, high = (prod[b, j * COLS : (j + 1) * COLS] for b in range(3))
        value = mid + pltpu.roll(low, 1, 0) + pltpu.roll(high, COLS - 1, 0)
        gate = gate_of(value)
        kept = gate * keep
        pixel = feat[r].astype(F32)
        summed = (pixel + value * kept).astype(BF16).astype(F32)
        slope_ref[r] = (kept * (1.0 + value * (1.0 - gate))).astype(BF16)
        sums[band * 2 + (parity + j) % 2] += summed
        one = pl.ds(r, 1)
        cols[0, one] = mid[0:1] + high[1:2]
        cols[1, one] = mid[COLS - 1 :] + low[COLS - 2 : COLS - 1]
        cols[2, one] = summed[0:1]
        cols[3, one] = summed[COLS - 1 :]
        cols[4, one] = pixel[0:1]
        cols[5, one] = pixel[COLS - 1 :]

    def step(block, out, done, prod, parity):
        taken = taken_rows(feat, 1 + STEP * block, (-1, 0, 1))
        for b in range(3):
            out[b] = nn(taken, forward_taps(weight, b))
            for j in BESIDE[b] if prod is not None else ():
                finish(done, j, prod, parity)

    step(0, prod_a, None, None, None)

    @pl.loop(0, BLOCKS // 2)
    def _(k):
        step(2 * k + 1, prod_b, 2 * k, prod_a, 1)
        step(jnp.minimum(2 * k + 2, BLOCKS - 1), prod_a, 2 * k + 1, prod_b, 0)


def border_body(
    flags_ref, feat, weight, sums, cols, top, bot, left, right, strided, owner_ref,
    pooled_ref, token_ref, edge_ref, side_ref, side32,
):
    added = []
    for i, side in enumerate((left, right)):
        side32[...] = side[...].astype(F32)
        near = [side32[a : a + ROWS].astype(BF16) for a in range(3)]
        added.append(nn(jnp.concatenate(near, axis=1), forward_taps(weight, 2 * i)))

    def pair(one, two):
        return jnp.concatenate([one, two], axis=0)

    taken = jnp.concatenate(
        [pair(top[0], feat[ROWS - 2]), pair(feat[0], feat[ROWS - 1]), pair(feat[1], bot[0])], axis=1
    )
    low, mid, high = (nn(taken, forward_taps(weight, b)) for b in range(3))
    pix = iota((COLS, CH), 0)
    rows = []
    for i, r in enumerate((0, ROWS - 1)):
        part = slice(i * COLS, (i + 1) * COLS)
        before = jnp.where(pix == 0, added[0][r : r + 1], pltpu.roll(low[part], 1, 0))
        after = jnp.where(pix == COLS - 1, added[1][r : r + 1], pltpu.roll(high[part], COLS - 1, 0))
        value = mid[part] + before + after
        gate = gate_of(value)
        keep = jnp.concatenate(
            [jnp.full((16, CH), flags_ref[i, t], jnp.int32).astype(F32) for t in range(8)], axis=0
        )
        kept = gate * keep
        edge_ref[i] = (kept * (1.0 + value * (1.0 - gate))).astype(BF16)
        rows.append((feat[r].astype(F32) + value * kept).astype(BF16).astype(F32))

    line = iota((ROWS, CH), 0)
    deltas = []
    for i in range(2):
        value = cols[i] + added[i]
        gate = gate_of(value)
        tile = 7 * i
        keep = jnp.where(line < ROWS // 2, flags_ref[0, tile], flags_ref[1, tile]).astype(F32)
        kept = gate * keep
        side_ref[i] = kept * (1.0 + value * (1.0 - gate))
        summed = (cols[4 + i] + value * kept).astype(BF16).astype(F32)
        inside = (line > 0) & (line < ROWS - 1)
        deltas.append(jnp.where(inside, summed - cols[2 + i], 0.0))

    row, spot = iota((16, COLS), 0), iota((16, COLS), 1)
    pick = ((spot // 16 == row % 8) & (spot % 2 == row // 8)).astype(F32).astype(BF16)
    place = iota((16, CH), 0)
    parts = {}
    for band in range(2):
        for a in range(2):
            total = sums[2 * band + a]
            if band == a:
                total += rows[band]
            high, low = halves(total)
            part = nn(pick, high) + nn(pick, low)
            mine = (line // 16 == band) & (line % 2 == a)
            for i in range(2):
                delta = jnp.sum(jnp.where(mine, deltas[i], 0.0), axis=0, keepdims=True)
                part += jnp.where(place == 15 * i, delta, 0.0)
            parts[band, a] = part
    taken = [
        jnp.concatenate([parts[band, a][8 * b : 8 * b + 8] for band in range(2)], axis=0)
        for a in range(2)
        for b in range(2)
    ]
    high, low = halves(jnp.concatenate(taken, axis=1))
    flat = strided[...].reshape(4 * CH, CH)
    pooled = (nn(high, flat) + nn(low, flat)) * (1.0 / TILE_CELLS)
    pooled_ref[...] = pooled
    normed = pooled * lax.rsqrt(jnp.mean(pooled * pooled, axis=-1, keepdims=True) + 1e-05)
    token_ref[:, 0:CH] = normed.astype(BF16)
    owner = jnp.full((16, LANES), -1, jnp.int32)
    for tile in range(16):
        named = jnp.where(flags_ref[tile // 8, tile % 8] != 0, owner_ref[tile], -1)
        owner = jnp.where(iota((16, LANES), 0) == tile, named, owner)
    token_ref[:, CH:] = (owner == iota((16, LANES), 1)).astype(F32).astype(BF16)


def turn_body(feat, top, bot, w_query, w_key, w_value, token, turned_ref, high_ref, low_ref):
    turned_ref[:, 0:COLS] = top[0].T
    turned_ref[:, (ROWS + 1) * COLS :] = bot[0].T

    @pl.loop(0, ROWS // 4)
    def _(i):
        for j in range(4):
            here = pl.multiple_of((4 * i + j + 1) * COLS, COLS)
            turned_ref[:, pl.ds(here, COLS)] = feat[4 * i + j].T

    for i, one in enumerate((w_query, w_key, w_value)):
        high, low = halves(one[...])
        high_ref[:, i * CH : (i + 1) * CH] = high
        low_ref[:, i * CH : (i + 1) * CH] = low


def pair_body(one, two, out_ref):
    out_ref[0:16] = one[...]
    out_ref[16:32] = two[...]


def attention_body(*refs, seed_scale, pieces):
    got = refs[:pieces]
    pooled_ref, high_w, low_w, cot, strided, spread_ref, emb_ref = refs[pieces:]
    got = jnp.concatenate([piece[...] for piece in got], axis=0)
    count = got.shape[0]
    tokens, group = got[:, 0:CH], got[:, CH:]
    pair = nt(group, group)
    pairs = jnp.concatenate([pair] * HEADS, axis=0)
    projected = nn(tokens, high_w[...]) + nn(tokens, low_w[...])
    query, key, value = (projected[:, i * CH : (i + 1) * CH] for i in range(3))
    lane = iota((1, CH), 1) // (CH // HEADS)
    scale = 1.0 / math.sqrt(CH // HEADS)

    def by_head(array):
        return jnp.concatenate([jnp.where(lane == h, array, 0.0) for h in range(HEADS)], axis=0)

    queries, keys = halves(by_head(query)), halves(by_head(key))
    gate = gate_of(wide_product(nt, queries, halves(key)) * scale + attention_bias)
    weights = gate * pairs
    seed = cot[...] * seed_scale
    seeds = jnp.where(lane == iota((8, CH), 0), seed, 0.0)
    values = halves(value)
    along = wide_product(nt, halves(seeds), values)
    columns, grads = [], []
    for h in range(HEADS):
        part = slice(h * count, (h + 1) * count)
        columns.append(jnp.sum(weights[part], axis=0, keepdims=True))
        grads.append(weights[part] * (1.0 - gate[part]) * (along[h : h + 1] * scale))
    columns = halves(jnp.concatenate(columns + [jnp.zeros((8 - HEADS, count), F32)], axis=0))
    grad_q = wide_product(nn, halves(jnp.concatenate([g[0:16] for g in grads], axis=1)), keys)
    narrow = halves(jnp.concatenate([g[:, 0:LANES] for g in grads], axis=0))
    grad_k = wide_product(tn, narrow, queries)[0:16]
    grad_v = wide_product(tn, columns, halves(seeds))[0:16]
    mixed = wide_product(nn, columns, values)
    mixed = jnp.sum(jnp.where(lane == iota((8, CH), 0), mixed, 0.0), axis=0, keepdims=True)
    high = mixed.astype(BF16).astype(F32)
    low = mixed - high
    rows = iota((16, LANES), 0)
    packed = jnp.zeros((16, LANES), F32)
    for i, part in enumerate((high[:, :LANES], high[:, LANES:], low[:, :LANES], low[:, LANES:])):
        packed = jnp.where(rows == i, part, packed)
    emb_ref[...] = packed.astype(BF16)

    grads = halves(jnp.concatenate([grad_q, grad_k, grad_v], axis=1))
    grad = wide_product(nt, grads, (high_w[...], low_w[...]))
    grad = grad.astype(BF16).astype(F32)
    pooled = pooled_ref[...]
    inv = lax.rsqrt(jnp.mean(pooled * pooled, axis=-1, keepdims=True) + 1e-05)
    unit = pooled * inv
    back = inv * (grad - unit * jnp.mean(grad * unit, axis=-1, keepdims=True))
    cell = (back * (1.0 / TILE_CELLS)).astype(BF16)
    spot, row = iota((COLS, 16), 0), iota((COLS, 16), 1)
    expand = ((spot // 16 == row % 8) & (spot % 2 == row // 8)).astype(F32).astype(BF16)
    taps = nt(cell, strided[...].reshape(4 * CH, CH))
    for band in range(2):
        here = taps[8 * band : 8 * band + 8]
        both = [
            jnp.concatenate([here[:, (2 * a + b) * CH : (2 * a + b + 1) * CH] for a in range(2)], axis=1)
            for b in range(2)
        ]
        high, low = halves(jnp.concatenate(both, axis=0))
        spread = nn(expand, high) + nn(expand, low)
        for a in range(2):
            spread_ref[band * 2 + a] = spread[:, a * CH : (a + 1) * CH]


GROUP = 8


def weight_body(
    spread, slope, edge, side, turned, left, right,
    pre_ref, keep_ref, give_ref, top_ref, bot_ref, left_ref, right_ref,
    wide_a, wide_b, total, first, last,
):
    first[...] = jnp.zeros_like(first)
    last[...] = jnp.zeros_like(last)
    pix = iota((COLS, CH), 0)

    def put(r, j, grad, wide):
        low = grad.astype(BF16)
        full = low.astype(F32)
        pre_ref[r] = low
        here = slice(j * COLS, (j + 1) * COLS)
        wide[here, CH : 2 * CH] = low
        wide[here, 0:CH] = jnp.where(pix == COLS - 1, 0.0, pltpu.roll(full, COLS - 1, 0)).astype(BF16)
        wide[here, 2 * CH :] = jnp.where(pix == 0, 0.0, pltpu.roll(full, 1, 0)).astype(BF16)
        for a in range(3):
            first[a, pl.ds(r + a, 1)] = full[0:1]
            last[a, pl.ds(r + a, 1)] = full[COLS - 1 : COLS]

    def build(group, wide, j):
        r = group * GROUP + j
        here = slope[r].astype(F32)
        here = jnp.where(pix == 0, side[0, pl.ds(r, 1)], here)
        here = jnp.where(pix == COLS - 1, side[1, pl.ds(r, 1)], here)
        if j == 0:
            here = jnp.where(r == 0, edge[0].astype(F32), here)
        if j == GROUP - 1:
            here = jnp.where(r == ROWS - 1, edge[1].astype(F32), here)
        put(r, j, spread[(r // 16) * 2 + j % 2] * here, wide)

    def step(group, wide, ahead, out):
        def near(a):
            return turned[:, pl.ds(pl.multiple_of((group * GROUP + a) * COLS, COLS), GROUP * COLS)]

        taken = jnp.concatenate([near(a) for a in range(3)], axis=0)
        for b in range(3):
            part = slice(b * CH, (b + 1) * CH)
            total[:, part] += nn(taken, wide[:, part])
            for j in range(GROUP * b // 3, GROUP * (b + 1) // 3):
                build(ahead, out, j)

    groups = ROWS // GROUP
    total[...] = jnp.zeros_like(total)
    for j in range(GROUP):
        build(0, wide_a, j)

    @pl.loop(0, groups // 2)
    def _(k):
        step(2 * k, wide_a, 2 * k + 1, wide_b)
        step(2 * k + 1, wide_b, jnp.minimum(2 * k + 2, groups - 1), wide_a)

    top_ref[...] = pre_ref[0:1]
    bot_ref[...] = pre_ref[ROWS - 1 : ROWS]
    left_ref[...] = first[1].astype(BF16)
    right_ref[...] = last[1].astype(BF16)
    is_one = lax.axis_index("core") == 1
    for a in range(3):
        for b in range(3):
            part = total[a * CH : (a + 1) * CH, b * CH : (b + 1) * CH]
            if b == 0:
                part += tn(left[...], first[a].astype(BF16))
            if b == 2:
                part += tn(right[...], last[a].astype(BF16))
            low, high = part[:, :LANES], part[:, LANES:]
            at = slice((3 * a + b) * CH, (3 * a + b + 1) * CH)
            keep_ref[at] = jnp.where(is_one, high, low).astype(BF16)
            give_ref[at] = jnp.where(is_one, low, high).astype(BF16)


def input_body(pre, top, bot, left, right, spread, weight, *refs, band):
    out, tag_ref, prod_a, prod_b, side32, added, done, sems = refs[-8:]
    half = ROWS // 2

    def taps(b):
        return jnp.concatenate([weight[3 * a + b] for a in range(3)], axis=1)

    for i, side in enumerate((left, right)):
        side32[...] = side[...].astype(F32)
        near = [side32[band * half + 2 - a : band * half + 2 - a + half].astype(BF16) for a in range(3)]
        added[i] = nt(jnp.concatenate(near, axis=1), taps(2 - 2 * i))

    pix = iota((COLS, CH), 0)

    def finish(r, prod, j):
        low, mid, high = (prod[b, j * COLS : (j + 1) * COLS] for b in range(3))
        at = r - band * half
        after = jnp.where(pix == COLS - 1, added[1, at : at + 1], pltpu.roll(low, COLS - 1, 0))
        before = jnp.where(pix == 0, added[0, at : at + 1], pltpu.roll(high, 1, 0))
        done[at] = (spread[band * 2 + r % 2] + (mid + after + before)).astype(BF16)

    if band == 0:
        rows = jnp.concatenate([pre[1], pre[0], top[0]], axis=1)
    else:
        rows = jnp.concatenate([bot[0], pre[ROWS - 1], pre[ROWS - 2]], axis=1)
    count = BLOCKS // 2
    started = []

    def send(first, last):
        sem = sems.at[len(started)]
        one = pltpu.make_async_copy(
            done.at[first : last], out.at[band * half + first : band * half + last], sem
        )
        one.start()
        started.append(one)

    def step(block, out, before, prod):
        if block == count:
            taken, size = rows, COLS
        else:
            taken, size = taken_rows(pre, 1 + STEP * (count * band + block), (1, 0, -1)), STEP * COLS
        for b in range(3):
            out[b, 0:size] = nt(taken, taps(b))
            if prod is not None:
                for j in BESIDE[b]:
                    finish(1 + STEP * (count * band + before) + j, prod, j)
        if prod is not None:
            first = STEP * before + 1 - band
            send(first, first + STEP)

    prods = (prod_a, prod_b)
    for block in range(count + 1):
        last = None if block == 0 else prods[(block - 1) % 2]
        step(block, prods[block % 2], block - 1, last)
    edge = 0 if band == 0 else ROWS - 1
    finish(edge, prods[count % 2], 0)
    send(edge - band * half, edge - band * half + 1)
    tag_ref[...] = jnp.zeros_like(tag_ref)
    for one in started:
        one.wait()


def sum_body(*refs, terms, axis, extra):
    outs, total_ref = refs[terms + extra : -1], refs[-1]
    total = refs[0][...].astype(F32)
    for one in refs[1:terms]:
        total += one[...].astype(F32)
    total_ref[...] = total.astype(BF16)
    count, size = len(outs), outs[0].shape[0]
    for k, out in enumerate(outs):
        at = lax.rem(lax.axis_index(axis) + k, count) * size
        out[...] = total_ref[pl.ds(pl.multiple_of(at, 16), size)]


def last_sum_body(*refs):
    emb, out = refs[-2:]
    total = refs[0][...].astype(F32)
    for one in refs[1:-2]:
        total += one[...].astype(F32)
    out[0 : total.shape[0]] = total.astype(BF16)
    out[total.shape[0] :] = emb[...]


def stack_body(*refs, terms):
    for i, one in enumerate(refs[:terms]):
        refs[-1][i] = one[...]


def final_body(mine, other, grad_ref, emb_ref, *, share, norm_scale):
    gy, gz = lax.axis_index("gy"), lax.axis_index("gz")
    is_one = lax.axis_index("core") == 1
    bands, depth = mine.shape[0], mine.shape[1]
    for k in range(bands):
        band = lax.rem(gy + bands - k, bands)
        for j in range(depth):
            at = (band * depth + lax.rem(gz + depth - j, depth)) * share
            here = pl.ds(pl.multiple_of(at, 16), share)
            one = mine[k, j, 0:share].astype(F32) * (1.0 / loss_scale)
            two = other[k, j, 0:share].astype(F32) * (1.0 / loss_scale)
            grad_ref[here, 0:LANES] = jnp.where(is_one, two, one)
            grad_ref[here, LANES:] = jnp.where(is_one, one, two)
    total = jnp.zeros((16, LANES), F32)
    for band in range(bands):
        k = lax.rem(gy + bands - band, bands)
        one, two = (array[k, gz, share : share + 16].astype(F32) for array in (mine, other))
        total += jnp.where(is_one, two, one)
    total = total * norm_scale
    emb_ref[:, 0:LANES] = total[0:1] + total[2:3]
    emb_ref[:, LANES:] = total[1:2] + total[3:4]


SMEM = pl.BlockSpec(memory_space=pltpu.SMEM)
VMEM = pl.BlockSpec(memory_space=pltpu.VMEM)
HBM = pl.BlockSpec(memory_space=pltpu.HBM)


def run(body, args, outs, scratch=(), flops=1 << 20, mib=8, far=(), **rest):
    specs = [HBM if i in far else SMEM if a.dtype == jnp.int32 else VMEM for i, a in enumerate(args)]
    return pl.pallas_call(
        body,
        in_specs=specs,
        out_shape=outs,
        scratch_shapes=list(scratch),
        compiler_params=pltpu.CompilerParams(vmem_limit_bytes=mib << 20),
        cost_estimate=pl.CostEstimate(flops=flops, bytes_accessed=1 << 20, transcendentals=0),
        **rest,
    )(*args)


def per_device(features, tissue, owner_map, w_conv, w_stride, w_query, w_key, w_value, cotangent):
    gy_count, gz_count, cores = lax.axis_size("gy"), lax.axis_size("gz"), lax.axis_size("core")
    gx_count, chips = gz_count * cores, gy_count * gz_count
    across = ("gz", "core")
    norm_scale = 1.0 / math.sqrt(16 * gy_count * gx_count)
    swap = [(i, i ^ 1) for i in range(cores)]

    def to_next(value, axis, count):
        return lax.ppermute(value, axis, [(i, i + 1) for i in range(count - 1)])

    def to_last(value, axis, count):
        return lax.ppermute(value, axis, [(i + 1, i) for i in range(count - 1)])

    def around(value, axis, count, by):
        return lax.ppermute(value, axis, [(i, (i + by) % count) for i in range(count)])

    column = shape((HALO, CH), BF16)
    line = shape((1, COLS, CH), BF16)

    def halos(first, last, left, right):
        top, bot = to_next(last, "gy", gy_count), to_last(first, "gy", gy_count)
        left, right = run(corner_body, (left, right, top, bot), [column] * 2, mib=1)
        return top, bot, to_next(right, across, gx_count), to_last(left, across, gx_count)

    conv_flops = 2 * ROWS * COLS * 9 * CH * CH
    prod = pltpu.VMEM((3, STEP * COLS, CH), F32)
    side32 = pltpu.VMEM((HALO, CH), F32)

    outer = run(
        outer_body,
        (features,),
        [line, line, column, column],
        [pltpu.VMEM((2, ROWS, 16, CH), BF16), pltpu.SemaphoreType.DMA((4,))],
        mib=56,
        far=(0,),
    )
    top, bot, left, right = halos(*outer)
    slope, sums, cols = run(
        forward_body,
        (tissue, features, w_conv),
        [shape((ROWS, COLS, CH), BF16), shape((4, COLS, CH), F32), shape((6, ROWS, CH), F32)],
        [prod, prod, pltpu.VMEM((2 * COLS, CH), F32)],
        flops=conv_flops,
        mib=20,
    )
    pooled, token, edge, side = run(
        border_body,
        (tissue, features, w_conv, sums, cols, top, bot, left, right, w_stride, owner_map.reshape(16)),
        [
            shape((16, CH), F32),
            shape((16, CH + LANES), BF16),
            shape((2, COLS, CH), BF16),
            shape((2, ROWS, CH), F32),
        ],
        [side32],
        flops=conv_flops // 8,
        mib=12,
    )
    both = run(
        pair_body, (token, lax.ppermute(token, "core", swap)), shape((32, CH + LANES), BF16), mib=1
    )
    pieces = [both] + [around(both, "gz", gz_count, k) for k in range(1, gz_count)]
    turned, high_w, low_w = run(
        turn_body,
        (features, top, bot, w_query, w_key, w_value, token),
        [shape((CH, (ROWS + 2) * COLS), BF16), shape((CH, 3 * CH), BF16), shape((CH, 3 * CH), BF16)],
        flops=conv_flops // 4,
        mib=12,
    )
    spread, emb = run(
        lambda *refs: attention_body(*refs, seed_scale=loss_scale * norm_scale, pieces=gz_count),
        (*pieces, pooled, high_w, low_w, cotangent.reshape(1, CH), w_stride),
        [shape((4, COLS, CH), F32), shape((16, LANES), BF16)],
        flops=1 << 30,
        mib=12,
    )
    wide = pltpu.VMEM((GROUP * COLS, 3 * CH), BF16)
    border = pltpu.VMEM((3, HALO, CH), F32)
    pre, keep, give, *outer = run(
        weight_body,
        (spread, slope, edge, side, turned, left, right),
        [
            shape((ROWS, COLS, CH), BF16),
            shape((9 * CH, LANES), BF16),
            shape((9 * CH, LANES), BF16),
            line,
            line,
            column,
            column,
        ],
        [wide, wide, pltpu.VMEM((3 * CH, 3 * CH), F32), border, border],
        flops=conv_flops,
        mib=20,
    )

    share = -(-9 * CH // (16 * chips)) * 16
    spare = share * chips - 9 * CH
    taken = lax.ppermute(give, "core", swap)
    pre_top, pre_bot, pre_left, pre_right = halos(*outer)
    if spare:
        keep, taken = (jnp.pad(a, ((0, spare), (0, 0))) for a in (keep, taken))

    def summed(axis, terms, count, *after):
        rows = terms[0].shape[0]
        return run(
            lambda *refs: sum_body(*refs, terms=len(terms), axis=axis, extra=len(after)),
            (*terms, *after),
            [shape((rows // count, LANES), BF16)] * count,
            [pltpu.VMEM((rows, LANES), BF16)],
            mib=6,
        )

    def band_of_input(band, *after):
        return run(
            lambda *refs: input_body(*refs, band=band),
            (pre, pre_top, pre_bot, pre_left, pre_right, spread, w_conv, *after),
            [shape((ROWS, COLS, CH), BF16), shape((8, LANES), F32)],
            [
                prod,
                prod,
                side32,
                pltpu.VMEM((2, ROWS // 2, CH), F32),
                pltpu.VMEM((ROWS // 2, COLS, CH), BF16),
                pltpu.SemaphoreType.DMA((BLOCKS,)),
            ],
            flops=conv_flops // 2,
            mib=20,
            far=(8,),
            out_specs=[HBM, VMEM],
            input_output_aliases={8: 0} if len(after) == 2 else {},
        )

    parts = summed("gy", [keep, taken], gy_count)
    upper, tag = band_of_input(0, parts[0])
    parts = [parts[0]] + [around(parts[k], "gy", gy_count, k) for k in range(1, gy_count)]
    parts = summed("gz", parts, gz_count, tag)
    parts = [parts[0]] + [around(parts[k], "gz", gz_count, k) for k in range(1, gz_count)]
    mine = run(last_sum_body, (*parts, emb), shape((share + 16, LANES), BF16), mib=2)
    lines = [mine] + [around(mine, "gz", gz_count, k) for k in range(1, gz_count)]

    def stacked(terms, *after):
        return run(
            lambda *refs: stack_body(*refs, terms=len(terms)),
            (*terms, *after),
            shape((len(terms),) + terms[0].shape, BF16),
            mib=4,
        )

    row = stacked(lines)
    input_grad, tag = band_of_input(1, row, upper)
    plane = stacked([row] + [around(row, "gy", gy_count, k) for k in range(1, gy_count)], tag)
    other = lax.ppermute(plane, "core", swap)
    conv_grad, embedding = run(
        lambda *refs: final_body(*refs, share=share, norm_scale=norm_scale),
        (plane, other),
        [shape((share * chips, CH), F32), shape((1, CH), F32)],
        mib=8,
    )
    return embedding.reshape(CH), input_grad, conv_grad[: 9 * CH].reshape(9, CH, CH)


def solution(mesh):
    sizes = mesh.devices.shape
    split = Mesh(mesh.devices.reshape(sizes[0], sizes[1] // 2, 2), ("gy", "gz", "core"))
    gx = ("gz", "core")
    in_specs = (P("gy", gx, None), P("gy", gx), P("gy", gx, None, None), P(), P(), P(), P(), P(), P())
    out_specs = (P(), P("gy", gx, None), P())
    return jax.shard_map(per_device, mesh=split, in_specs=in_specs, out_specs=out_specs, check_vma=False)
```

```python
import math

import jax
import jax.numpy as jnp
from jax import lax
from jax.experimental import pallas as pl
from jax.experimental.pallas import tpu as pltpu
from jax.sharding import Mesh, PartitionSpec as P

HEADS = 4
F32 = jnp.float32
BF16 = jnp.bfloat16

attention_bias = -1.0
loss_scale = 512.0

ROWS = 32
COLS = 128
CH = 256
HALO = 48
LANES = 128
STEP = 5
BLOCKS = (ROWS - 2) // STEP
TILE_CELLS = 64


def shape(dims, dtype):
    return jax.ShapeDtypeStruct(dims, dtype)


def nt(left, right):
    return lax.dot_general(left, right, (((1,), (1,)), ((), ())), preferred_element_type=F32)


def tn(left, right):
    return lax.dot_general(left, right, (((0,), (0,)), ((), ())), preferred_element_type=F32)


def nn(left, right):
    return jnp.dot(left, right, preferred_element_type=F32)


def halves(value):
    high = value.astype(BF16)
    return high, (value - high.astype(F32)).astype(BF16)


def wide_product(product, left, right):
    (a, b), (c, d) = left, right
    return product(a, c) + (product(a, d) + product(b, c))


def iota(dims, axis):
    return lax.broadcasted_iota(jnp.int32, dims, axis)


def gate_of(value):
    return 0.5 * jnp.tanh(0.5 * value) + 0.5


def copies(pairs, sems):
    started = [pltpu.make_async_copy(a, b, sems.at[i]) for i, (a, b) in enumerate(pairs)]
    for one in started:
        one.start()
    return started


def is_odd(axis):
    return lax.axis_index(axis) % 2 == 1


def rows_body(block, even_ref, odd_ref, buf, sems):
    started = copies([(block.at[0:1], buf.at[0:1]), (block.at[ROWS - 1 : ROWS], buf.at[1:2])], sems)
    for one in started:
        one.wait()
    order_rows(buf[0], buf[1], even_ref, odd_ref)


def order_rows(first, last, even_ref, odd_ref):
    odd = is_odd("gy")
    even_ref[0] = jnp.where(odd, first, last)
    odd_ref[0] = jnp.where(odd, last, first)


def columns_body(block, left_ref, right_ref):
    row, spot = iota((HALO, ROWS * 16), 0), iota((HALO, ROWS * 16), 1)
    for out, at, place in ((left_ref, 0, 0), (right_ref, COLS - 16, 15)):
        pick = (spot == (row - 1) * 16 + place).astype(F32).astype(BF16)
        out[...] = nn(pick, block[:, at : at + 16].reshape(ROWS * 16, CH)).astype(BF16)


def corner_body(left, right, even, odd, top_ref, bot_ref, even_ref, odd_ref):
    low = is_odd("gy")
    top_ref[0] = jnp.where(low, even[0], odd[0])
    bot_ref[0] = jnp.where(low, odd[0], even[0])
    row = iota((HALO, CH), 0)
    whole = []
    for side, at in ((left, 0), (right, COLS - 16)):
        part = slice(0, 1) if at == 0 else slice(15, 16)
        above = top_ref[0, at : at + 16].astype(F32)[part]
        below = bot_ref[0, at : at + 16].astype(F32)[part]
        whole.append(jnp.where(row == 0, above, jnp.where(row == ROWS + 1, below, side[...].astype(F32))))
    high = is_odd("core")
    even_ref[...] = jnp.where(high, whole[0], whole[1]).astype(BF16)
    odd_ref[...] = jnp.where(high, whole[1], whole[0]).astype(BF16)


def sides(even, odd):
    high = is_odd("core")
    one, two = even[...].astype(F32), odd[...].astype(F32)
    return jnp.where(high, one, two), jnp.where(high, two, one)


def forward_taps(weight, b):
    return jnp.concatenate([weight[3 * a + b] for a in range(3)], axis=0)


def taken_rows(array, first, steps):
    rows = [array[pl.ds(first + step, STEP)].reshape(STEP * COLS, CH) for step in steps]
    return jnp.concatenate(rows, axis=1)


BESIDE = ((0, 1), (2, 3), (4,))


def forward_body(flags_ref, feat, weight, slope_ref, sums, cols, prod_a, prod_b, mask):
    for band in range(2):
        for tile in range(8):
            at = band * COLS + 16 * tile
            mask[at : at + 16] = jnp.full((16, CH), flags_ref[band, tile], jnp.int32).astype(F32)
    sums[...] = jnp.zeros_like(sums)

    def finish(block, j, prod, parity):
        band = block // (BLOCKS // 2)
        keep = mask[pl.ds(pl.multiple_of(band * COLS, COLS), COLS)]
        r = 1 + STEP * block + j
        low, mid, high = (prod[b, j * COLS : (j + 1) * COLS] for b in range(3))
        value = mid + pltpu.roll(low, 1, 0) + pltpu.roll(high, COLS - 1, 0)
        gate = gate_of(value)
        kept = gate * keep
        pixel = feat[r].astype(F32)
        summed = (pixel + value * kept).astype(BF16).astype(F32)
        slope_ref[r] = (kept * (1.0 + value * (1.0 - gate))).astype(BF16)
        sums[band * 2 + (parity + j) % 2] += summed
        one = pl.ds(r, 1)
        cols[0, one] = mid[0:1] + high[1:2]
        cols[1, one] = mid[COLS - 1 :] + low[COLS - 2 : COLS - 1]
        cols[2, one] = summed[0:1]
        cols[3, one] = summed[COLS - 1 :]
        cols[4, one] = pixel[0:1]
        cols[5, one] = pixel[COLS - 1 :]

    def step(block, out, done, prod, parity):
        taken = taken_rows(feat, 1 + STEP * block, (-1, 0, 1))
        for b in range(3):
            out[b] = nn(taken, forward_taps(weight, b))
            for j in BESIDE[b] if prod is not None else ():
                finish(done, j, prod, parity)

    step(0, prod_a, None, None, None)

    @pl.loop(0, BLOCKS // 2)
    def _(k):
        step(2 * k + 1, prod_b, 2 * k, prod_a, 1)
        step(jnp.minimum(2 * k + 2, BLOCKS - 1), prod_a, 2 * k + 1, prod_b, 0)


def border_body(
    flags_ref, feat, weight, sums, cols, top, bot, even, odd, strided, owner_ref,
    pooled_ref, token_ref, edge_ref, side_ref, side32,
):
    added = []
    for i, whole in enumerate(sides(even, odd)):
        side32[...] = whole
        near = [side32[a : a + ROWS].astype(BF16) for a in range(3)]
        added.append(nn(jnp.concatenate(near, axis=1), forward_taps(weight, 2 * i)))

    def pair(one, two):
        return jnp.concatenate([one, two], axis=0)

    taken = jnp.concatenate(
        [pair(top[0], feat[ROWS - 2]), pair(feat[0], feat[ROWS - 1]), pair(feat[1], bot[0])], axis=1
    )
    low, mid, high = (nn(taken, forward_taps(weight, b)) for b in range(3))
    pix = iota((COLS, CH), 0)
    rows = []
    for i, r in enumerate((0, ROWS - 1)):
        part = slice(i * COLS, (i + 1) * COLS)
        before = jnp.where(pix == 0, added[0][r : r + 1], pltpu.roll(low[part], 1, 0))
        after = jnp.where(pix == COLS - 1, added[1][r : r + 1], pltpu.roll(high[part], COLS - 1, 0))
        value = mid[part] + before + after
        gate = gate_of(value)
        keep = jnp.concatenate(
            [jnp.full((16, CH), flags_ref[i, t], jnp.int32).astype(F32) for t in range(8)], axis=0
        )
        kept = gate * keep
        edge_ref[i] = (kept * (1.0 + value * (1.0 - gate))).astype(BF16)
        rows.append((feat[r].astype(F32) + value * kept).astype(BF16).astype(F32))

    line = iota((ROWS, CH), 0)
    deltas = []
    for i in range(2):
        value = cols[i] + added[i]
        gate = gate_of(value)
        tile = 7 * i
        keep = jnp.where(line < ROWS // 2, flags_ref[0, tile], flags_ref[1, tile]).astype(F32)
        kept = gate * keep
        side_ref[i] = kept * (1.0 + value * (1.0 - gate))
        summed = (cols[4 + i] + value * kept).astype(BF16).astype(F32)
        inside = (line > 0) & (line < ROWS - 1)
        deltas.append(jnp.where(inside, summed - cols[2 + i], 0.0))

    row, spot = iota((16, COLS), 0), iota((16, COLS), 1)
    pick = ((spot // 16 == row % 8) & (spot % 2 == row // 8)).astype(F32).astype(BF16)
    place = iota((16, CH), 0)
    parts = {}
    for band in range(2):
        for a in range(2):
            total = sums[2 * band + a]
            if band == a:
                total += rows[band]
            high, low = halves(total)
            part = nn(pick, high) + nn(pick, low)
            mine = (line // 16 == band) & (line % 2 == a)
            for i in range(2):
                delta = jnp.sum(jnp.where(mine, deltas[i], 0.0), axis=0, keepdims=True)
                part += jnp.where(place == 15 * i, delta, 0.0)
            parts[band, a] = part
    taken = [
        jnp.concatenate([parts[band, a][8 * b : 8 * b + 8] for band in range(2)], axis=0)
        for a in range(2)
        for b in range(2)
    ]
    high, low = halves(jnp.concatenate(taken, axis=1))
    flat = strided[...].reshape(4 * CH, CH)
    pooled = (nn(high, flat) + nn(low, flat)) * (1.0 / TILE_CELLS)
    pooled_ref[...] = pooled
    normed = pooled * lax.rsqrt(jnp.mean(pooled * pooled, axis=-1, keepdims=True) + 1e-05)
    token_ref[:, 0:CH] = normed.astype(BF16)
    owner = jnp.full((16, LANES), -1, jnp.int32)
    for tile in range(16):
        named = jnp.where(flags_ref[tile // 8, tile % 8] != 0, owner_ref[tile], -1)
        owner = jnp.where(iota((16, LANES), 0) == tile, named, owner)
    token_ref[:, CH:] = (owner == iota((16, LANES), 1)).astype(F32).astype(BF16)


def turn_body(feat, top, bot, w_query, w_key, w_value, token, turned_ref, high_ref, low_ref):
    turned_ref[:, 0:COLS] = top[0].T
    turned_ref[:, (ROWS + 1) * COLS :] = bot[0].T

    @pl.loop(0, ROWS // 4)
    def _(i):
        for j in range(4):
            here = pl.multiple_of((4 * i + j + 1) * COLS, COLS)
            turned_ref[:, pl.ds(here, COLS)] = feat[4 * i + j].T

    for i, one in enumerate((w_query, w_key, w_value)):
        high, low = halves(one[...])
        high_ref[:, i * CH : (i + 1) * CH] = high
        low_ref[:, i * CH : (i + 1) * CH] = low


def pair_body(one, two, out_ref):
    out_ref[0:16] = one[...]
    out_ref[16:32] = two[...]


def attention_body(*refs, seed_scale, pieces):
    got = refs[:pieces]
    pooled_ref, high_w, low_w, cot, strided, spread_ref, emb_ref = refs[pieces:]
    got = jnp.concatenate([piece[...] for piece in got], axis=0)
    count = got.shape[0]
    tokens, group = got[:, 0:CH], got[:, CH:]
    pair = nt(group, group)
    pairs = jnp.concatenate([pair] * HEADS, axis=0)
    projected = nn(tokens, high_w[...]) + nn(tokens, low_w[...])
    query, key, value = (projected[:, i * CH : (i + 1) * CH] for i in range(3))
    lane = iota((1, CH), 1) // (CH // HEADS)
    scale = 1.0 / math.sqrt(CH // HEADS)

    def by_head(array):
        return jnp.concatenate([jnp.where(lane == h, array, 0.0) for h in range(HEADS)], axis=0)

    queries, keys = halves(by_head(query)), halves(by_head(key))
    gate = gate_of(wide_product(nt, queries, halves(key)) * scale + attention_bias)
    weights = gate * pairs
    seed = cot[...] * seed_scale
    seeds = jnp.where(lane == iota((8, CH), 0), seed, 0.0)
    values = halves(value)
    along = wide_product(nt, halves(seeds), values)
    columns, grads = [], []
    for h in range(HEADS):
        part = slice(h * count, (h + 1) * count)
        columns.append(jnp.sum(weights[part], axis=0, keepdims=True))
        grads.append(weights[part] * (1.0 - gate[part]) * (along[h : h + 1] * scale))
    columns = halves(jnp.concatenate(columns + [jnp.zeros((8 - HEADS, count), F32)], axis=0))
    grad_q = wide_product(nn, halves(jnp.concatenate([g[0:16] for g in grads], axis=1)), keys)
    narrow = halves(jnp.concatenate([g[:, 0:LANES] for g in grads], axis=0))
    grad_k = wide_product(tn, narrow, queries)[0:16]
    grad_v = wide_product(tn, columns, halves(seeds))[0:16]
    mixed = wide_product(nn, columns, values)
    mixed = jnp.sum(jnp.where(lane == iota((8, CH), 0), mixed, 0.0), axis=0, keepdims=True)
    high = mixed.astype(BF16).astype(F32)
    low = mixed - high
    rows = iota((16, LANES), 0)
    packed = jnp.zeros((16, LANES), F32)
    for i, part in enumerate((high[:, :LANES], high[:, LANES:], low[:, :LANES], low[:, LANES:])):
        packed = jnp.where(rows == i, part, packed)
    emb_ref[...] = packed.astype(BF16)

    grads = halves(jnp.concatenate([grad_q, grad_k, grad_v], axis=1))
    grad = wide_product(nt, grads, (high_w[...], low_w[...]))
    grad = grad.astype(BF16).astype(F32)
    pooled = pooled_ref[...]
    inv = lax.rsqrt(jnp.mean(pooled * pooled, axis=-1, keepdims=True) + 1e-05)
    unit = pooled * inv
    back = inv * (grad - unit * jnp.mean(grad * unit, axis=-1, keepdims=True))
    cell = (back * (1.0 / TILE_CELLS)).astype(BF16)
    spot, row = iota((COLS, 16), 0), iota((COLS, 16), 1)
    expand = ((spot // 16 == row % 8) & (spot % 2 == row // 8)).astype(F32).astype(BF16)
    taps = nt(cell, strided[...].reshape(4 * CH, CH))
    for band in range(2):
        here = taps[8 * band : 8 * band + 8]
        both = [
            jnp.concatenate([here[:, (2 * a + b) * CH : (2 * a + b + 1) * CH] for a in range(2)], axis=1)
            for b in range(2)
        ]
        high, low = halves(jnp.concatenate(both, axis=0))
        spread = nn(expand, high) + nn(expand, low)
        for a in range(2):
            spread_ref[band * 2 + a] = spread[:, a * CH : (a + 1) * CH]


GROUP = 8


def weight_body(
    spread, slope, edge, side, turned, even, odd,
    pre_ref, keep_ref, give_ref, even_ref, odd_ref, left_ref, right_ref,
    wide_a, wide_b, total, first, last,
):
    first[...] = jnp.zeros_like(first)
    last[...] = jnp.zeros_like(last)
    pix = iota((COLS, CH), 0)

    def put(r, j, grad, wide):
        low = grad.astype(BF16)
        full = low.astype(F32)
        pre_ref[r] = low
        here = slice(j * COLS, (j + 1) * COLS)
        wide[here, CH : 2 * CH] = low
        wide[here, 0:CH] = jnp.where(pix == COLS - 1, 0.0, pltpu.roll(full, COLS - 1, 0)).astype(BF16)
        wide[here, 2 * CH :] = jnp.where(pix == 0, 0.0, pltpu.roll(full, 1, 0)).astype(BF16)
        for a in range(3):
            first[a, pl.ds(r + a, 1)] = full[0:1]
            last[a, pl.ds(r + a, 1)] = full[COLS - 1 : COLS]

    def build(group, wide, j):
        r = group * GROUP + j
        here = slope[r].astype(F32)
        here = jnp.where(pix == 0, side[0, pl.ds(r, 1)], here)
        here = jnp.where(pix == COLS - 1, side[1, pl.ds(r, 1)], here)
        if j == 0:
            here = jnp.where(r == 0, edge[0].astype(F32), here)
        if j == GROUP - 1:
            here = jnp.where(r == ROWS - 1, edge[1].astype(F32), here)
        put(r, j, spread[(r // 16) * 2 + j % 2] * here, wide)

    def step(group, wide, ahead, out):
        def near(a):
            return turned[:, pl.ds(pl.multiple_of((group * GROUP + a) * COLS, COLS), GROUP * COLS)]

        taken = jnp.concatenate([near(a) for a in range(3)], axis=0)
        for b in range(3):
            part = slice(b * CH, (b + 1) * CH)
            total[:, part] += nn(taken, wide[:, part])
            for j in range(GROUP * b // 3, GROUP * (b + 1) // 3):
                build(ahead, out, j)

    groups = ROWS // GROUP
    total[...] = jnp.zeros_like(total)
    for j in range(GROUP):
        build(0, wide_a, j)

    @pl.loop(0, groups // 2)
    def _(k):
        step(2 * k, wide_a, 2 * k + 1, wide_b)
        step(2 * k + 1, wide_b, jnp.minimum(2 * k + 2, groups - 1), wide_a)

    order_rows(pre_ref[0], pre_ref[ROWS - 1], even_ref, odd_ref)
    left_ref[...] = first[1].astype(BF16)
    right_ref[...] = last[1].astype(BF16)
    is_one = is_odd("core")
    left, right = (part.astype(BF16) for part in sides(even, odd))
    for a in range(3):
        for b in range(3):
            part = total[a * CH : (a + 1) * CH, b * CH : (b + 1) * CH]
            if b == 0:
                part += tn(left, first[a].astype(BF16))
            if b == 2:
                part += tn(right, last[a].astype(BF16))
            low, high = part[:, :LANES], part[:, LANES:]
            at = slice((3 * a + b) * CH, (3 * a + b + 1) * CH)
            keep_ref[at] = jnp.where(is_one, high, low).astype(BF16)
            give_ref[at] = jnp.where(is_one, low, high).astype(BF16)


def input_body(pre, top, bot, even, odd, spread, weight, out, prod_a, prod_b, side32, added, done, sems):
    def taps(b):
        return jnp.concatenate([weight[3 * a + b] for a in range(3)], axis=1)

    for i, whole in enumerate(sides(even, odd)):
        side32[...] = whole
        near = [side32[2 - a : 2 - a + ROWS].astype(BF16) for a in range(3)]
        added[i] = nt(jnp.concatenate(near, axis=1), taps(2 - 2 * i))

    pix = iota((COLS, CH), 0)

    def finish(r, band, parity, prod, j):
        low, mid, high = (prod[b, j * COLS : (j + 1) * COLS] for b in range(3))
        after = jnp.where(pix == COLS - 1, added[1, pl.ds(r, 1)], pltpu.roll(low, COLS - 1, 0))
        before = jnp.where(pix == 0, added[0, pl.ds(r, 1)], pltpu.roll(high, 1, 0))
        done[r] = (spread[band * 2 + parity] + (mid + after + before)).astype(BF16)

    def send(first, count, sem):
        return pltpu.make_async_copy(done.at[pl.ds(first, count)], out.at[pl.ds(first, count)], sem)

    def step(block, store, before, prod, parity):
        taken = taken_rows(pre, 1 + STEP * block, (1, 0, -1))
        for b in range(3):
            store[b] = nt(taken, taps(b))
            for j in BESIDE[b] if prod is not None else ():
                finish(1 + STEP * before + j, before // (BLOCKS // 2), (parity + j) % 2, prod, j)
        if prod is not None:
            send(1 + STEP * before, STEP, sems.at[before]).start()

    step(0, prod_a, None, None, None)

    @pl.loop(0, BLOCKS // 2)
    def _(k):
        step(2 * k + 1, prod_b, 2 * k, prod_a, 1)
        step(jnp.minimum(2 * k + 2, BLOCKS - 1), prod_a, 2 * k + 1, prod_b, 0)

    def pair(one, two):
        return jnp.concatenate([one, two], axis=0)

    rows = jnp.concatenate(
        [pair(pre[1], bot[0]), pair(pre[0], pre[ROWS - 1]), pair(top[0], pre[ROWS - 2])], axis=1
    )
    for b in range(3):
        prod_b[b, 0 : 2 * COLS] = nt(rows, taps(b))
    for i, r in enumerate((0, ROWS - 1)):
        finish(r, i, i, prod_b, i)
        send(r, 1, sems.at[BLOCKS + i]).start()
    for block in range(BLOCKS):
        send(1 + STEP * block, STEP, sems.at[block]).wait()
    for i, r in enumerate((0, ROWS - 1)):
        send(r, 1, sems.at[BLOCKS + i]).wait()


def add_body(one, two, out):
    out[...] = (one[...].astype(F32) + two[...].astype(F32)).astype(BF16)


def stack_body(one, two, out):
    out[0 : one.shape[0]] = one[...]
    out[one.shape[0] :] = two[...]


def final_body(mine, other, grad_ref, emb_ref, *, share, depth, norm_scale):
    is_one = is_odd("core")
    for i in range(mine.shape[0]):
        here = slice(i * share, (i + 1) * share)
        one = mine[i, 0:share].astype(F32) * (1.0 / loss_scale)
        two = other[i, 0:share].astype(F32) * (1.0 / loss_scale)
        grad_ref[here, 0:LANES] = jnp.where(is_one, two, one)
        grad_ref[here, LANES:] = jnp.where(is_one, one, two)
    total = jnp.zeros((16, LANES), F32)
    for i in range(0, mine.shape[0], depth):
        one, two = (array[i, share : share + 16].astype(F32) for array in (mine, other))
        total += jnp.where(is_one, two, one)
    total = total * norm_scale
    emb_ref[:, 0:LANES] = total[0:1] + total[2:3]
    emb_ref[:, LANES:] = total[1:2] + total[3:4]


SMEM = pl.BlockSpec(memory_space=pltpu.SMEM)
VMEM = pl.BlockSpec(memory_space=pltpu.VMEM)
HBM = pl.BlockSpec(memory_space=pltpu.HBM)


def run(body, args, outs, scratch=(), flops=1 << 20, mib=8, far=(), **rest):
    specs = [HBM if i in far else SMEM if a.dtype == jnp.int32 else VMEM for i, a in enumerate(args)]
    return pl.pallas_call(
        body,
        in_specs=specs,
        out_shape=outs,
        scratch_shapes=list(scratch),
        compiler_params=pltpu.CompilerParams(vmem_limit_bytes=mib << 20),
        cost_estimate=pl.CostEstimate(flops=flops, bytes_accessed=1 << 20, transcendentals=0),
        **rest,
    )(*args)


def per_device(features, tissue, owner_map, w_conv, w_stride, w_query, w_key, w_value, cotangent):
    gy_count, gz_count, cores = lax.axis_size("gy"), lax.axis_size("gz"), lax.axis_size("core")
    gx_count, chips = gz_count * cores, gy_count * gz_count
    across = ("gz", "core")
    norm_scale = 1.0 / math.sqrt(16 * gy_count * gx_count)
    swap = [(i, i ^ 1) for i in range(cores)]

    def pairs(value, axis, count, odd):
        low = range(odd, count - 1, 2)
        return lax.ppermute(value, axis, [(i, i + 1) for i in low] + [(i + 1, i) for i in low])

    def around(value, axis, count, by):
        return lax.ppermute(value, axis, [(i, (i + by) % count) for i in range(count)])

    column = shape((HALO, CH), BF16)
    line = shape((1, COLS, CH), BF16)

    def halos(even, odd, left, right):
        even, odd = pairs(even, "gy", gy_count, 0), pairs(odd, "gy", gy_count, 1)
        top, bot, even, odd = run(
            corner_body, (left, right, even, odd), [line, line, column, column], mib=1
        )
        return top, bot, pairs(even, across, gx_count, 0), pairs(odd, across, gx_count, 1)

    conv_flops = 2 * ROWS * COLS * 9 * CH * CH
    prod = pltpu.VMEM((3, STEP * COLS, CH), F32)
    side32 = pltpu.VMEM((HALO, CH), F32)

    rows = run(
        rows_body,
        (features,),
        [line, line],
        [pltpu.VMEM((2, COLS, CH), BF16), pltpu.SemaphoreType.DMA((2,))],
        mib=56,
        far=(0,),
    )
    outer = run(columns_body, (features,), [column, column], mib=2)
    top, bot, even, odd = halos(*rows, *outer)
    slope, sums, cols = run(
        forward_body,
        (tissue, features, w_conv),
        [shape((ROWS, COLS, CH), BF16), shape((4, COLS, CH), F32), shape((6, ROWS, CH), F32)],
        [prod, prod, pltpu.VMEM((2 * COLS, CH), F32)],
        flops=conv_flops,
        mib=20,
    )
    pooled, token, edge, side = run(
        border_body,
        (tissue, features, w_conv, sums, cols, top, bot, even, odd, w_stride, owner_map.reshape(16)),
        [
            shape((16, CH), F32),
            shape((16, CH + LANES), BF16),
            shape((2, COLS, CH), BF16),
            shape((2, ROWS, CH), F32),
        ],
        [side32],
        flops=conv_flops // 8,
        mib=12,
    )
    both = run(
        pair_body, (token, lax.ppermute(token, "core", swap)), shape((32, CH + LANES), BF16), mib=1
    )
    pieces = [both] + [around(both, "gz", gz_count, k) for k in range(1, gz_count)]
    turned, high_w, low_w = run(
        turn_body,
        (features, top, bot, w_query, w_key, w_value, token),
        [shape((CH, (ROWS + 2) * COLS), BF16), shape((CH, 3 * CH), BF16), shape((CH, 3 * CH), BF16)],
        flops=conv_flops // 4,
        mib=12,
    )
    spread, emb = run(
        lambda *refs: attention_body(*refs, seed_scale=loss_scale * norm_scale, pieces=gz_count),
        (*pieces, pooled, high_w, low_w, cotangent.reshape(1, CH), w_stride),
        [shape((4, COLS, CH), F32), shape((16, LANES), BF16)],
        flops=1 << 30,
        mib=12,
    )
    wide = pltpu.VMEM((GROUP * COLS, 3 * CH), BF16)
    border = pltpu.VMEM((3, HALO, CH), F32)
    pre, keep, give, *outer = run(
        weight_body,
        (spread, slope, edge, side, turned, even, odd),
        [
            shape((ROWS, COLS, CH), BF16),
            shape((9 * CH, LANES), BF16),
            shape((9 * CH, LANES), BF16),
            line,
            line,
            column,
            column,
        ],
        [wide, wide, pltpu.VMEM((3 * CH, 3 * CH), F32), border, border],
        flops=conv_flops,
        mib=20,
    )

    share = -(-9 * CH // (16 * chips)) * 16
    spare = share * chips - 9 * CH
    taken = lax.ppermute(give, "core", swap)
    chip_sum = run(add_body, (keep, taken), shape((9 * CH, LANES), BF16), mib=6)
    if spare:
        chip_sum = jnp.pad(chip_sum, ((0, spare), (0, 0)))
    mine = lax.psum_scatter(chip_sum, ("gy", "gz"), scatter_dimension=0, tiled=True)
    pre_halos = halos(*outer)
    mine, *pre_halos = lax.optimization_barrier((mine, *pre_halos))
    mine = run(stack_body, (mine, emb), shape((share + 16, LANES), BF16), mib=2)
    plane = lax.all_gather(mine, ("gy", "gz"), axis=0, tiled=False)
    input_grad = run(
        input_body,
        (pre, *pre_halos, spread, w_conv),
        shape((ROWS, COLS, CH), BF16),
        [
            prod,
            prod,
            side32,
            pltpu.VMEM((2, ROWS, CH), F32),
            pltpu.VMEM((ROWS, COLS, CH), BF16),
            pltpu.SemaphoreType.DMA((BLOCKS + 2,)),
        ],
        flops=conv_flops,
        mib=20,
        out_specs=HBM,
    )
    plane, input_grad = lax.optimization_barrier((plane, input_grad))
    other = lax.ppermute(plane, "core", swap)
    conv_grad, embedding = run(
        lambda *refs: final_body(*refs, share=share, depth=gz_count, norm_scale=norm_scale),
        (plane, other),
        [shape((share * chips, CH), F32), shape((1, CH), F32)],
        mib=8,
    )
    return embedding.reshape(CH), input_grad, conv_grad[: 9 * CH].reshape(9, CH, CH)


def solution(mesh):
    sizes = mesh.devices.shape
    split = Mesh(mesh.devices.reshape(sizes[0], sizes[1] // 2, 2), ("gy", "gz", "core"))
    gx = ("gz", "core")
    in_specs = (P("gy", gx, None), P("gy", gx), P("gy", gx, None, None), P(), P(), P(), P(), P(), P())
    out_specs = (P(), P("gy", gx, None), P())
    return jax.shard_map(per_device, mesh=split, in_specs=in_specs, out_specs=out_specs, check_vma=False)
```

```python
import math

import jax
import jax.numpy as jnp
from jax import lax
from jax.experimental import pallas as pl
from jax.experimental.pallas import tpu as pltpu
from jax.sharding import Mesh, PartitionSpec as P

HEADS = 4
F32 = jnp.float32
BF16 = jnp.bfloat16

attention_bias = -1.0
loss_scale = 512.0

ROWS = 32
COLS = 128
CH = 256
HALO = 48
LANES = 128
STEP = 5
BLOCKS = (ROWS - 2) // STEP
TILE_CELLS = 64


def shape(dims, dtype):
    return jax.ShapeDtypeStruct(dims, dtype)


def nt(left, right):
    return lax.dot_general(left, right, (((1,), (1,)), ((), ())), preferred_element_type=F32)


def tn(left, right):
    return lax.dot_general(left, right, (((0,), (0,)), ((), ())), preferred_element_type=F32)


def nn(left, right):
    return jnp.dot(left, right, preferred_element_type=F32)


def halves(value):
    high = value.astype(BF16)
    return high, (value - high.astype(F32)).astype(BF16)


def wide_product(product, left, right):
    (a, b), (c, d) = left, right
    return product(a, c) + (product(a, d) + product(b, c))


def iota(dims, axis):
    return lax.broadcasted_iota(jnp.int32, dims, axis)


def gate_of(value):
    return 0.5 * jnp.tanh(0.5 * value) + 0.5


def copies(pairs, sems):
    started = [pltpu.make_async_copy(a, b, sems.at[i]) for i, (a, b) in enumerate(pairs)]
    for one in started:
        one.start()
    return started


def is_odd(axis):
    return lax.axis_index(axis) % 2 == 1


def rows_body(block, even_ref, odd_ref, buf, sems):
    started = copies([(block.at[0:1], buf.at[0:1]), (block.at[ROWS - 1 : ROWS], buf.at[1:2])], sems)
    for one in started:
        one.wait()
    order_rows(buf[0], buf[1], even_ref, odd_ref)


def order_rows(first, last, even_ref, odd_ref):
    odd = is_odd("gy")
    even_ref[0] = jnp.where(odd, first, last)
    odd_ref[0] = jnp.where(odd, last, first)


def columns_body(block, left_ref, right_ref):
    row, spot = iota((HALO, ROWS * 16), 0), iota((HALO, ROWS * 16), 1)
    for out, at, place in ((left_ref, 0, 0), (right_ref, COLS - 16, 15)):
        pick = (spot == (row - 1) * 16 + place).astype(F32).astype(BF16)
        out[...] = nn(pick, block[:, at : at + 16].reshape(ROWS * 16, CH)).astype(BF16)


def corner_body(left, right, even, odd, top_ref, bot_ref, even_ref, odd_ref):
    low = is_odd("gy")
    top_ref[0] = jnp.where(low, even[0], odd[0])
    bot_ref[0] = jnp.where(low, odd[0], even[0])
    row = iota((HALO, CH), 0)
    whole = []
    for side, at in ((left, 0), (right, COLS - 16)):
        part = slice(0, 1) if at == 0 else slice(15, 16)
        above = top_ref[0, at : at + 16].astype(F32)[part]
        below = bot_ref[0, at : at + 16].astype(F32)[part]
        whole.append(jnp.where(row == 0, above, jnp.where(row == ROWS + 1, below, side[...].astype(F32))))
    high = is_odd("core")
    even_ref[...] = jnp.where(high, whole[0], whole[1]).astype(BF16)
    odd_ref[...] = jnp.where(high, whole[1], whole[0]).astype(BF16)


def sides(even, odd):
    high = is_odd("core")
    one, two = even[...].astype(F32), odd[...].astype(F32)
    return jnp.where(high, one, two), jnp.where(high, two, one)


def forward_taps(weight, b):
    return jnp.concatenate([weight[3 * a + b] for a in range(3)], axis=0)


def taken_rows(array, first, steps):
    rows = [array[pl.ds(first + step, STEP)].reshape(STEP * COLS, CH) for step in steps]
    return jnp.concatenate(rows, axis=1)


BESIDE = ((0, 1), (2, 3), (4,))


def forward_body(flags_ref, feat, weight, slope_ref, sums, cols, wide, prod_a, prod_b, mask):
    for band in range(2):
        for tile in range(8):
            at = band * COLS + 16 * tile
            mask[at : at + 16] = jnp.full((16, CH), flags_ref[band, tile], jnp.int32).astype(F32)
    sums[...] = jnp.zeros_like(sums)
    pix = iota((COLS, CH), 0)
    taps = weight[...].reshape(9 * CH, CH)

    def build(r):
        here = slice(r * COLS, (r + 1) * COLS)
        pixel = feat[r].astype(F32)
        wide[here, 0:CH] = jnp.where(pix == 0, 0.0, pltpu.roll(pixel, 1, 0)).astype(BF16)
        wide[here, CH : 2 * CH] = feat[r]
        wide[here, 2 * CH :] = jnp.where(pix == COLS - 1, 0.0, pltpu.roll(pixel, COLS - 1, 0)).astype(BF16)

    def finish(r, value):
        band = r // 16
        gate = gate_of(value)
        kept = gate * mask[band * COLS : (band + 1) * COLS]
        pixel = feat[r].astype(F32)
        summed = (pixel + value * kept).astype(BF16).astype(F32)
        slope_ref[r] = (kept * (1.0 + value * (1.0 - gate))).astype(BF16)
        sums[band * 2 + r % 2] += summed
        for i, part in enumerate((value, summed, pixel)):
            cols[2 * i, r : r + 1] = part[0:1]
            cols[2 * i + 1, r : r + 1] = part[COLS - 1 :]

    prods = (prod_a, prod_b)
    for r in range(STEP + 2):
        build(r)
    for block in range(BLOCKS + 1):
        if block < BLOCKS:
            near = [slice((STEP * block + a) * COLS, (STEP * (block + 1) + a) * COLS) for a in range(3)]
            prods[block % 2][...] = nn(jnp.concatenate([wide[part] for part in near], axis=1), taps)
        for j in range(STEP):
            if block > 0:
                finish(1 + STEP * (block - 1) + j, prods[(block - 1) % 2][j * COLS : (j + 1) * COLS])
            ahead = STEP * (block + 1) + 2 + j
            if ahead < ROWS:
                build(ahead)


def border_body(
    flags_ref, feat, weight, sums, cols, top, bot, even, odd, strided, owner_ref,
    pooled_ref, token_ref, edge_ref, side_ref, side32,
):
    added = []
    for i, whole in enumerate(sides(even, odd)):
        side32[...] = whole
        near = [side32[a : a + ROWS].astype(BF16) for a in range(3)]
        added.append(nn(jnp.concatenate(near, axis=1), forward_taps(weight, 2 * i)))

    def pair(one, two):
        return jnp.concatenate([one, two], axis=0)

    taken = jnp.concatenate(
        [pair(top[0], feat[ROWS - 2]), pair(feat[0], feat[ROWS - 1]), pair(feat[1], bot[0])], axis=1
    )
    low, mid, high = (nn(taken, forward_taps(weight, b)) for b in range(3))
    pix = iota((COLS, CH), 0)
    rows = []
    for i, r in enumerate((0, ROWS - 1)):
        part = slice(i * COLS, (i + 1) * COLS)
        before = jnp.where(pix == 0, added[0][r : r + 1], pltpu.roll(low[part], 1, 0))
        after = jnp.where(pix == COLS - 1, added[1][r : r + 1], pltpu.roll(high[part], COLS - 1, 0))
        value = mid[part] + before + after
        gate = gate_of(value)
        keep = jnp.concatenate(
            [jnp.full((16, CH), flags_ref[i, t], jnp.int32).astype(F32) for t in range(8)], axis=0
        )
        kept = gate * keep
        edge_ref[i] = (kept * (1.0 + value * (1.0 - gate))).astype(BF16)
        rows.append((feat[r].astype(F32) + value * kept).astype(BF16).astype(F32))

    line = iota((ROWS, CH), 0)
    deltas = []
    for i in range(2):
        value = cols[i] + added[i]
        gate = gate_of(value)
        tile = 7 * i
        keep = jnp.where(line < ROWS // 2, flags_ref[0, tile], flags_ref[1, tile]).astype(F32)
        kept = gate * keep
        side_ref[i] = kept * (1.0 + value * (1.0 - gate))
        summed = (cols[4 + i] + value * kept).astype(BF16).astype(F32)
        inside = (line > 0) & (line < ROWS - 1)
        deltas.append(jnp.where(inside, summed - cols[2 + i], 0.0))

    row, spot = iota((16, COLS), 0), iota((16, COLS), 1)
    pick = ((spot // 16 == row % 8) & (spot % 2 == row // 8)).astype(F32).astype(BF16)
    place = iota((16, CH), 0)
    parts = {}
    for band in range(2):
        for a in range(2):
            total = sums[2 * band + a]
            if band == a:
                total += rows[band]
            high, low = halves(total)
            part = nn(pick, high) + nn(pick, low)
            mine = (line // 16 == band) & (line % 2 == a)
            for i in range(2):
                delta = jnp.sum(jnp.where(mine, deltas[i], 0.0), axis=0, keepdims=True)
                part += jnp.where(place == 15 * i, delta, 0.0)
            parts[band, a] = part
    taken = [
        jnp.concatenate([parts[band, a][8 * b : 8 * b + 8] for band in range(2)], axis=0)
        for a in range(2)
        for b in range(2)
    ]
    high, low = halves(jnp.concatenate(taken, axis=1))
    flat = strided[...].reshape(4 * CH, CH)
    pooled = (nn(high, flat) + nn(low, flat)) * (1.0 / TILE_CELLS)
    pooled_ref[...] = pooled
    normed = pooled * lax.rsqrt(jnp.mean(pooled * pooled, axis=-1, keepdims=True) + 1e-05)
    token_ref[:, 0:CH] = normed.astype(BF16)
    owner = jnp.full((16, LANES), -1, jnp.int32)
    for tile in range(16):
        named = jnp.where(flags_ref[tile // 8, tile % 8] != 0, owner_ref[tile], -1)
        owner = jnp.where(iota((16, LANES), 0) == tile, named, owner)
    token_ref[:, CH:] = (owner == iota((16, LANES), 1)).astype(F32).astype(BF16)


def turn_body(feat, top, bot, w_query, w_key, w_value, token, turned_ref, high_ref, low_ref):
    turned_ref[:, 0:COLS] = top[0].T
    turned_ref[:, (ROWS + 1) * COLS :] = bot[0].T

    @pl.loop(0, ROWS // 4)
    def _(i):
        for j in range(4):
            here = pl.multiple_of((4 * i + j + 1) * COLS, COLS)
            turned_ref[:, pl.ds(here, COLS)] = feat[4 * i + j].T

    for i, one in enumerate((w_query, w_key, w_value)):
        high, low = halves(one[...])
        high_ref[:, i * CH : (i + 1) * CH] = high
        low_ref[:, i * CH : (i + 1) * CH] = low


def pair_body(one, two, out_ref):
    out_ref[0:16] = one[...]
    out_ref[16:32] = two[...]


def attention_body(*refs, seed_scale, pieces):
    got = refs[:pieces]
    pooled_ref, high_w, low_w, cot, strided, spread_ref, emb_ref = refs[pieces:]
    got = jnp.concatenate([piece[...] for piece in got], axis=0)
    count = got.shape[0]
    tokens, group = got[:, 0:CH], got[:, CH:]
    pair = nt(group, group)
    pairs = jnp.concatenate([pair] * HEADS, axis=0)
    projected = nn(tokens, high_w[...]) + nn(tokens, low_w[...])
    query, key, value = (projected[:, i * CH : (i + 1) * CH] for i in range(3))
    lane = iota((1, CH), 1) // (CH // HEADS)
    scale = 1.0 / math.sqrt(CH // HEADS)

    def by_head(array):
        return jnp.concatenate([jnp.where(lane == h, array, 0.0) for h in range(HEADS)], axis=0)

    queries, keys = halves(by_head(query)), halves(by_head(key))
    gate = gate_of(wide_product(nt, queries, halves(key)) * scale + attention_bias)
    weights = gate * pairs
    seed = cot[...] * seed_scale
    seeds = jnp.where(lane == iota((8, CH), 0), seed, 0.0)
    values = halves(value)
    along = wide_product(nt, halves(seeds), values)
    columns, grads = [], []
    for h in range(HEADS):
        part = slice(h * count, (h + 1) * count)
        columns.append(jnp.sum(weights[part], axis=0, keepdims=True))
        grads.append(weights[part] * (1.0 - gate[part]) * (along[h : h + 1] * scale))
    columns = halves(jnp.concatenate(columns + [jnp.zeros((8 - HEADS, count), F32)], axis=0))
    grad_q = wide_product(nn, halves(jnp.concatenate([g[0:16] for g in grads], axis=1)), keys)
    narrow = halves(jnp.concatenate([g[:, 0:LANES] for g in grads], axis=0))
    grad_k = wide_product(tn, narrow, queries)[0:16]
    grad_v = wide_product(tn, columns, halves(seeds))[0:16]
    mixed = wide_product(nn, columns, values)
    mixed = jnp.sum(jnp.where(lane == iota((8, CH), 0), mixed, 0.0), axis=0, keepdims=True)
    high = mixed.astype(BF16).astype(F32)
    low = mixed - high
    rows = iota((16, LANES), 0)
    packed = jnp.zeros((16, LANES), F32)
    for i, part in enumerate((high[:, :LANES], high[:, LANES:], low[:, :LANES], low[:, LANES:])):
        packed = jnp.where(rows == i, part, packed)
    emb_ref[...] = packed.astype(BF16)

    grads = halves(jnp.concatenate([grad_q, grad_k, grad_v], axis=1))
    grad = wide_product(nt, grads, (high_w[...], low_w[...]))
    grad = grad.astype(BF16).astype(F32)
    pooled = pooled_ref[...]
    inv = lax.rsqrt(jnp.mean(pooled * pooled, axis=-1, keepdims=True) + 1e-05)
    unit = pooled * inv
    back = inv * (grad - unit * jnp.mean(grad * unit, axis=-1, keepdims=True))
    cell = (back * (1.0 / TILE_CELLS)).astype(BF16)
    spot, row = iota((COLS, 16), 0), iota((COLS, 16), 1)
    expand = ((spot // 16 == row % 8) & (spot % 2 == row // 8)).astype(F32).astype(BF16)
    taps = nt(cell, strided[...].reshape(4 * CH, CH))
    for band in range(2):
        here = taps[8 * band : 8 * band + 8]
        both = [
            jnp.concatenate([here[:, (2 * a + b) * CH : (2 * a + b + 1) * CH] for a in range(2)], axis=1)
            for b in range(2)
        ]
        high, low = halves(jnp.concatenate(both, axis=0))
        spread = nn(expand, high) + nn(expand, low)
        for a in range(2):
            spread_ref[band * 2 + a] = spread[:, a * CH : (a + 1) * CH]


GROUP = 8


def weight_body(
    spread, slope, edge, side, turned, even, odd,
    pre_ref, keep_ref, give_ref, even_ref, odd_ref, left_ref, right_ref,
    wide_a, wide_b, total, first, last,
):
    first[...] = jnp.zeros_like(first)
    last[...] = jnp.zeros_like(last)
    pix = iota((COLS, CH), 0)

    def put(r, j, grad, wide):
        low = grad.astype(BF16)
        full = low.astype(F32)
        pre_ref[r] = low
        here = slice(j * COLS, (j + 1) * COLS)
        wide[here, CH : 2 * CH] = low
        wide[here, 0:CH] = jnp.where(pix == COLS - 1, 0.0, pltpu.roll(full, COLS - 1, 0)).astype(BF16)
        wide[here, 2 * CH :] = jnp.where(pix == 0, 0.0, pltpu.roll(full, 1, 0)).astype(BF16)
        for a in range(3):
            first[a, pl.ds(r + a, 1)] = full[0:1]
            last[a, pl.ds(r + a, 1)] = full[COLS - 1 : COLS]

    def build(group, wide, j):
        r = group * GROUP + j
        here = slope[r].astype(F32)
        here = jnp.where(pix == 0, side[0, pl.ds(r, 1)], here)
        here = jnp.where(pix == COLS - 1, side[1, pl.ds(r, 1)], here)
        if j == 0:
            here = jnp.where(r == 0, edge[0].astype(F32), here)
        if j == GROUP - 1:
            here = jnp.where(r == ROWS - 1, edge[1].astype(F32), here)
        put(r, j, spread[(r // 16) * 2 + j % 2] * here, wide)

    def step(group, wide, ahead, out):
        def near(a):
            return turned[:, pl.ds(pl.multiple_of((group * GROUP + a) * COLS, COLS), GROUP * COLS)]

        taken = jnp.concatenate([near(a) for a in range(3)], axis=0)
        for b in range(3):
            part = slice(b * CH, (b + 1) * CH)
            total[:, part] += nn(taken, wide[:, part])
            for j in range(GROUP * b // 3, GROUP * (b + 1) // 3):
                build(ahead, out, j)

    groups = ROWS // GROUP
    total[...] = jnp.zeros_like(total)
    for j in range(GROUP):
        build(0, wide_a, j)

    @pl.loop(0, groups // 2)
    def _(k):
        step(2 * k, wide_a, 2 * k + 1, wide_b)
        step(2 * k + 1, wide_b, jnp.minimum(2 * k + 2, groups - 1), wide_a)

    order_rows(pre_ref[0], pre_ref[ROWS - 1], even_ref, odd_ref)
    left_ref[...] = first[1].astype(BF16)
    right_ref[...] = last[1].astype(BF16)
    is_one = is_odd("core")
    left, right = (part.astype(BF16) for part in sides(even, odd))
    for a in range(3):
        for b in range(3):
            part = total[a * CH : (a + 1) * CH, b * CH : (b + 1) * CH]
            if b == 0:
                part += tn(left, first[a].astype(BF16))
            if b == 2:
                part += tn(right, last[a].astype(BF16))
            low, high = part[:, :LANES], part[:, LANES:]
            at = slice((3 * a + b) * CH, (3 * a + b + 1) * CH)
            keep_ref[at] = jnp.where(is_one, high, low).astype(BF16)
            give_ref[at] = jnp.where(is_one, low, high).astype(BF16)


def back_taps(weight, b):
    return jnp.concatenate([weight[3 * a + b] for a in range(3)], axis=1)


def input_blocks(pre, weight, first, count, prods, finish, send):
    for block in range(count + 1):
        if block < count:
            taken = taken_rows(pre, first + STEP * block, (1, 0, -1))
        for b in range(3):
            if block < count:
                prods[block % 2][b] = nt(taken, back_taps(weight, b))
            for j in BESIDE[b] if block > 0 else ():
                finish(first + STEP * (block - 1) + j, prods[(block - 1) % 2], j)
        if block > 0:
            send(first + STEP * (block - 1), STEP)


HALF = ROWS // 2


def upper_body(pre, spread, weight, out, kept_ref, raw_ref, prod_a, prod_b, done, sems):
    pix = iota((COLS, CH), 0)
    started = []

    def finish(r, prod, j):
        low, mid, high = (prod[b, j * COLS : (j + 1) * COLS] for b in range(3))
        after = jnp.where(pix == COLS - 1, 0.0, pltpu.roll(low, COLS - 1, 0))
        before = jnp.where(pix == 0, 0.0, pltpu.roll(high, 1, 0))
        value = spread[r % 2] + (mid + after + before)
        done[r] = value.astype(BF16)
        raw_ref[0, r : r + 1] = value[0:1]
        raw_ref[1, r : r + 1] = value[COLS - 1 :]
        kept_ref[0, r] = done[r, 0:16]
        kept_ref[1, r] = done[r, COLS - 16 :]

    def send(first, count):
        here = slice(first, first + count)
        started.append(pltpu.make_async_copy(done.at[here], out.at[here], sems.at[len(started)]))
        started[-1].start()

    input_blocks(pre, weight, 1, BLOCKS // 2, (prod_a, prod_b), finish, send)
    for one in started:
        one.wait()


def lower_body(
    pre, top, bot, even, odd, spread, weight, kept, raw, _, out, prod_a, prod_b, side32, added, done, fixed, sems
):
    for i, whole in enumerate(sides(even, odd)):
        side32[...] = whole
        near = [side32[2 - a : 2 - a + ROWS].astype(BF16) for a in range(3)]
        added[i] = nt(jnp.concatenate(near, axis=1), back_taps(weight, 2 - 2 * i))
    started = []

    def start(source, target):
        started.append(pltpu.make_async_copy(source, target, sems.at[len(started)]))
        started[-1].start()

    small = iota((16, CH), 0)
    for i in range(2):
        for r in range(1, HALF):
            value = raw[i, r : r + 1] + added[i, r : r + 1]
            fixed[i, r] = jnp.where(small == 15 * i, value, kept[i, r].astype(F32)).astype(BF16)
        at = (COLS - 16) * i
        start(fixed.at[i, 1:HALF], out.at[1:HALF, at : at + 16])

    pix = iota((COLS, CH), 0)

    def finish(r, prod, j):
        low, mid, high = (prod[b, j * COLS : (j + 1) * COLS] for b in range(3))
        after = jnp.where(pix == COLS - 1, added[1, r : r + 1], pltpu.roll(low, COLS - 1, 0))
        before = jnp.where(pix == 0, added[0, r : r + 1], pltpu.roll(high, 1, 0))
        at = r - HALF if r >= HALF else HALF
        done[at] = (spread[(r // HALF) * 2 + r % 2] + (mid + after + before)).astype(BF16)

    def send(first, count):
        at = first - HALF if first >= HALF else HALF
        start(done.at[at : at + count], out.at[first : first + count])

    input_blocks(pre, weight, HALF, BLOCKS // 2, (prod_a, prod_b), finish, send)

    def pair(one, two):
        return jnp.concatenate([one, two], axis=0)

    rows = jnp.concatenate(
        [pair(pre[1], bot[0]), pair(pre[0], pre[ROWS - 1]), pair(top[0], pre[ROWS - 2])], axis=1
    )
    for b in range(3):
        prod_b[b, 0 : 2 * COLS] = nt(rows, back_taps(weight, b))
    for i, r in enumerate((0, ROWS - 1)):
        finish(r, prod_b, i)
        send(r, 1)
    for one in started:
        one.wait()


def sum_body(*refs, terms, axis):
    outs, total_ref = refs[terms:-1], refs[-1]
    total = refs[0][...].astype(F32)
    for one in refs[1:terms]:
        total += one[...].astype(F32)
    total_ref[...] = total.astype(BF16)
    size = outs[0].shape[0]
    for k, out in enumerate(outs):
        at = lax.bitwise_xor(lax.axis_index(axis), k) * size
        out[...] = total_ref[pl.ds(pl.multiple_of(at, 16), size)]


def last_sum_body(*refs):
    emb, out = refs[-2:]
    total = refs[0][...].astype(F32)
    for one in refs[1:-2]:
        total += one[...].astype(F32)
    out[0 : total.shape[0]] = total.astype(BF16)
    out[total.shape[0] :] = emb[...]


def stack_body(*refs):
    for i, one in enumerate(refs[:-1]):
        refs[-1][i] = one[...]


def final_body(mine, other, grad_ref, emb_ref, buf, sems, *, share, norm_scale):
    gy, gz = lax.axis_index("gy"), lax.axis_index("gz")
    is_one = is_odd("core")
    bands, depth = mine.shape[0], mine.shape[1]

    def send(i, at):
        here = pl.ds(pl.multiple_of(at, 16), share)
        return pltpu.make_async_copy(buf.at[i], grad_ref.at[here], sems.at[i])

    sent = []
    for k in range(bands):
        for j in range(depth):
            i = k * depth + j
            at = (lax.bitwise_xor(gy, k) * depth + lax.bitwise_xor(gz, j)) * share
            one = mine[k, j, 0:share].astype(F32) * (1.0 / loss_scale)
            two = other[k, j, 0:share].astype(F32) * (1.0 / loss_scale)
            buf[i, :, 0:LANES] = jnp.where(is_one, two, one)
            buf[i, :, LANES:] = jnp.where(is_one, one, two)
            sent.append(send(i, at))
            sent[-1].start()
    total = jnp.zeros((16, LANES), F32)
    for band in range(bands):
        k = lax.bitwise_xor(gy, band)
        one, two = (array[k, gz, share : share + 16].astype(F32) for array in (mine, other))
        total += jnp.where(is_one, two, one)
    total = total * norm_scale
    emb_ref[:, 0:LANES] = total[0:1] + total[2:3]
    emb_ref[:, LANES:] = total[1:2] + total[3:4]
    for one in sent:
        one.wait()


SMEM = pl.BlockSpec(memory_space=pltpu.SMEM)
VMEM = pl.BlockSpec(memory_space=pltpu.VMEM)
HBM = pl.BlockSpec(memory_space=pltpu.HBM)


def run(body, args, outs, scratch=(), flops=1 << 20, mib=8, far=(), **rest):
    specs = [HBM if i in far else SMEM if a.dtype == jnp.int32 else VMEM for i, a in enumerate(args)]
    return pl.pallas_call(
        body,
        in_specs=specs,
        out_shape=outs,
        scratch_shapes=list(scratch),
        compiler_params=pltpu.CompilerParams(vmem_limit_bytes=mib << 20),
        cost_estimate=pl.CostEstimate(flops=flops, bytes_accessed=1 << 20, transcendentals=0),
        **rest,
    )(*args)


def per_device(features, tissue, owner_map, w_conv, w_stride, w_query, w_key, w_value, cotangent):
    gy_count, gz_count, cores = lax.axis_size("gy"), lax.axis_size("gz"), lax.axis_size("core")
    gx_count, chips = gz_count * cores, gy_count * gz_count
    across = ("gz", "core")
    norm_scale = 1.0 / math.sqrt(16 * gy_count * gx_count)
    swap = [(i, i ^ 1) for i in range(cores)]

    def pairs(value, axis, count, odd):
        low = range(odd, count - 1, 2)
        return lax.ppermute(value, axis, [(i, i + 1) for i in low] + [(i + 1, i) for i in low])

    def others(values, axis, count):
        return [
            lax.ppermute(value, axis, [(i, i ^ k) for i in range(count)])
            for k, value in enumerate(values, 1)
        ]

    column = shape((HALO, CH), BF16)
    line = shape((1, COLS, CH), BF16)

    def halos(even, odd, left, right):
        even, odd = pairs(even, "gy", gy_count, 0), pairs(odd, "gy", gy_count, 1)
        top, bot, even, odd = run(
            corner_body, (left, right, even, odd), [line, line, column, column], mib=1
        )
        return top, bot, pairs(even, across, gx_count, 0), pairs(odd, across, gx_count, 1)

    conv_flops = 2 * ROWS * COLS * 9 * CH * CH
    prod = pltpu.VMEM((3, STEP * COLS, CH), F32)
    side32 = pltpu.VMEM((HALO, CH), F32)

    rows = run(
        rows_body,
        (features,),
        [line, line],
        [pltpu.VMEM((2, COLS, CH), BF16), pltpu.SemaphoreType.DMA((2,))],
        mib=56,
        far=(0,),
    )
    outer = run(columns_body, (features,), [column, column], mib=2)
    top, bot, even, odd = halos(*rows, *outer)
    slope, sums, cols = run(
        forward_body,
        (tissue, features, w_conv),
        [shape((ROWS, COLS, CH), BF16), shape((4, COLS, CH), F32), shape((6, ROWS, CH), F32)],
        [
            pltpu.VMEM((ROWS * COLS, 3 * CH), BF16),
            pltpu.VMEM((STEP * COLS, CH), F32),
            pltpu.VMEM((STEP * COLS, CH), F32),
            pltpu.VMEM((2 * COLS, CH), F32),
        ],
        flops=conv_flops,
        mib=24,
    )
    pooled, token, edge, side = run(
        border_body,
        (tissue, features, w_conv, sums, cols, top, bot, even, odd, w_stride, owner_map.reshape(16)),
        [
            shape((16, CH), F32),
            shape((16, CH + LANES), BF16),
            shape((2, COLS, CH), BF16),
            shape((2, ROWS, CH), F32),
        ],
        [side32],
        flops=conv_flops // 8,
        mib=12,
    )
    both = run(
        pair_body, (token, lax.ppermute(token, "core", swap)), shape((32, CH + LANES), BF16), mib=1
    )
    pieces = [both] + others([both] * (gz_count - 1), "gz", gz_count)
    turned, high_w, low_w = run(
        turn_body,
        (features, top, bot, w_query, w_key, w_value, token),
        [shape((CH, (ROWS + 2) * COLS), BF16), shape((CH, 3 * CH), BF16), shape((CH, 3 * CH), BF16)],
        flops=conv_flops // 4,
        mib=12,
    )
    spread, emb = run(
        lambda *refs: attention_body(*refs, seed_scale=loss_scale * norm_scale, pieces=gz_count),
        (*pieces, pooled, high_w, low_w, cotangent.reshape(1, CH), w_stride),
        [shape((4, COLS, CH), F32), shape((16, LANES), BF16)],
        flops=1 << 30,
        mib=12,
    )
    wide = pltpu.VMEM((GROUP * COLS, 3 * CH), BF16)
    border = pltpu.VMEM((3, HALO, CH), F32)
    pre, keep, give, *outer = run(
        weight_body,
        (spread, slope, edge, side, turned, even, odd),
        [
            shape((ROWS, COLS, CH), BF16),
            shape((9 * CH, LANES), BF16),
            shape((9 * CH, LANES), BF16),
            line,
            line,
            column,
            column,
        ],
        [wide, wide, pltpu.VMEM((3 * CH, 3 * CH), F32), border, border],
        flops=conv_flops,
        mib=20,
    )

    share = -(-9 * CH // (16 * chips)) * 16
    spare = share * chips - 9 * CH
    taken = lax.ppermute(give, "core", swap)
    if spare:
        keep, taken = (jnp.pad(a, ((0, spare), (0, 0))) for a in (keep, taken))

    def summed(axis, terms, count):
        rows = terms[0].shape[0]
        return run(
            lambda *refs: sum_body(*refs, terms=len(terms), axis=axis),
            terms,
            [shape((rows // count, LANES), BF16)] * count,
            [pltpu.VMEM((rows, LANES), BF16)],
            mib=6,
        )

    def stacked(terms):
        return run(stack_body, terms, shape((len(terms),) + terms[0].shape, BF16), mib=4)

    block = shape((ROWS, COLS, CH), BF16)
    parts = summed("gy", [keep, taken], gy_count)
    *parts, pre_upper = lax.optimization_barrier((*parts, pre))
    upper, kept, raw = run(
        upper_body,
        (pre_upper, spread, w_conv),
        [block, shape((2, HALF, 16, CH), BF16), shape((2, HALF, CH), F32)],
        [prod, prod, pltpu.VMEM((HALF, COLS, CH), BF16), pltpu.SemaphoreType.DMA((BLOCKS,))],
        flops=conv_flops // 2,
        mib=20,
        out_specs=[HBM, VMEM, VMEM],
    )
    raw, *outer = lax.optimization_barrier((raw, *outer))
    parts = [parts[0]] + others(parts[1:], "gy", gy_count)
    pre_halos = halos(*outer)
    *parts, raw = lax.optimization_barrier((*parts, raw))
    parts = summed("gz", parts, gz_count)
    parts = [parts[0]] + others(parts[1:], "gz", gz_count)
    mine = run(last_sum_body, (*parts, emb), shape((share + 16, LANES), BF16), mib=2)
    row = stacked([mine] + others([mine] * (gz_count - 1), "gz", gz_count))
    row, pre_lower = lax.optimization_barrier((row, pre))
    input_grad = run(
        lower_body,
        (pre_lower, *pre_halos, spread, w_conv, kept, raw, upper),
        block,
        [
            prod,
            prod,
            side32,
            pltpu.VMEM((2, ROWS, CH), F32),
            pltpu.VMEM((HALF + 1, COLS, CH), BF16),
            pltpu.VMEM((2, HALF, 16, CH), BF16),
            pltpu.SemaphoreType.DMA((BLOCKS + 2,)),
        ],
        flops=conv_flops // 2,
        mib=20,
        far=(9,),
        out_specs=HBM,
        input_output_aliases={9: 0},
    )
    planes = [row] + others([row] * (gy_count - 1), "gy", gy_count)
    *planes, input_grad = lax.optimization_barrier((*planes, input_grad))
    plane = stacked(planes)
    other = lax.ppermute(plane, "core", swap)
    conv_grad, embedding = run(
        lambda *refs: final_body(*refs, share=share, norm_scale=norm_scale),
        (plane, other),
        [shape((share * chips, CH), F32), shape((1, CH), F32)],
        [pltpu.VMEM((chips, share, CH), F32), pltpu.SemaphoreType.DMA((chips,))],
        mib=8,
        out_specs=[HBM, VMEM],
    )
    return embedding.reshape(CH), input_grad, conv_grad[: 9 * CH].reshape(9, CH, CH)


def solution(mesh):
    sizes = mesh.devices.shape
    split = Mesh(mesh.devices.reshape(sizes[0], sizes[1] // 2, 2), ("gy", "gz", "core"))
    gx = ("gz", "core")
    in_specs = (P("gy", gx, None), P("gy", gx), P("gy", gx, None, None), P(), P(), P(), P(), P(), P())
    out_specs = (P(), P("gy", gx, None), P())
    return jax.shard_map(per_device, mesh=split, in_specs=in_specs, out_specs=out_specs, check_vma=False)
```

```python
import math

import jax
import jax.numpy as jnp
from jax import lax
from jax.experimental import pallas as pl
from jax.experimental.pallas import tpu as pltpu
from jax.sharding import Mesh, PartitionSpec as P

HEADS = 4
F32 = jnp.float32
BF16 = jnp.bfloat16

attention_bias = -1.0
loss_scale = 512.0

ROWS = 32
COLS = 128
CH = 256
HALO = 48
LANES = 128
STEP = 5
TILE_CELLS = 64


def shape(dims, dtype):
    return jax.ShapeDtypeStruct(dims, dtype)


def nt(left, right):
    return lax.dot_general(left, right, (((1,), (1,)), ((), ())), preferred_element_type=F32)


def tn(left, right):
    return lax.dot_general(left, right, (((0,), (0,)), ((), ())), preferred_element_type=F32)


def nn(left, right):
    return jnp.dot(left, right, preferred_element_type=F32)


def halves(value):
    high = value.astype(BF16)
    return high, (value - high.astype(F32)).astype(BF16)


def wide_product(product, left, right):
    (a, b), (c, d) = left, right
    return product(a, c) + (product(a, d) + product(b, c))


def iota(dims, axis):
    return lax.broadcasted_iota(jnp.int32, dims, axis)


def gate_of(value):
    return 0.5 * jnp.tanh(0.5 * value) + 0.5


def copies(pairs, sems):
    started = [pltpu.make_async_copy(a, b, sems.at[i]) for i, (a, b) in enumerate(pairs)]
    for one in started:
        one.start()
    return started


def is_odd(axis):
    return lax.axis_index(axis) % 2 == 1


def rows_body(block, even_ref, odd_ref, sems):
    odd = is_odd("gy")
    first, last = jnp.where(odd, 0, ROWS - 1), jnp.where(odd, ROWS - 1, 0)
    started = copies([(block.at[pl.ds(first, 1)], even_ref), (block.at[pl.ds(last, 1)], odd_ref)], sems)
    for one in started:
        one.wait()


def columns_body(block, left_ref, right_ref):
    row, spot = iota((HALO, ROWS * 16), 0), iota((HALO, ROWS * 16), 1)
    for out, at, place in ((left_ref, 0, 0), (right_ref, COLS - 16, 15)):
        pick = (spot == (row - 1) * 16 + place).astype(F32).astype(BF16)
        out[...] = nn(pick, block[:, at : at + 16].reshape(ROWS * 16, CH)).astype(BF16)


def corner_body(left, right, even, odd, top_ref, bot_ref, even_ref, odd_ref):
    low = is_odd("gy")
    top_ref[0] = jnp.where(low, even[0], odd[0])
    bot_ref[0] = jnp.where(low, odd[0], even[0])
    row = iota((HALO, CH), 0)
    whole = []
    for side, at in ((left, 0), (right, COLS - 16)):
        part = slice(0, 1) if at == 0 else slice(15, 16)
        above = top_ref[0, at : at + 16].astype(F32)[part]
        below = bot_ref[0, at : at + 16].astype(F32)[part]
        whole.append(jnp.where(row == 0, above, jnp.where(row == ROWS + 1, below, side[...].astype(F32))))
    high = is_odd("core")
    even_ref[...] = jnp.where(high, whole[0], whole[1]).astype(BF16)
    odd_ref[...] = jnp.where(high, whole[1], whole[0]).astype(BF16)


def sides(even, odd):
    high = is_odd("core")
    one, two = even[...].astype(F32), odd[...].astype(F32)
    return jnp.where(high, one, two), jnp.where(high, two, one)


def forward_taps(weight, b):
    return jnp.concatenate([weight[3 * a + b] for a in range(3)], axis=0)


HALF = ROWS // 2
BLOCKS = (HALF - 1) // STEP


def neighbours(row):
    pix = iota((COLS, CH), 0)
    wide = row.astype(F32)
    left = jnp.where(pix == 0, 0.0, pltpu.roll(wide, 1, 0)).astype(BF16)
    right = jnp.where(pix == COLS - 1, 0.0, pltpu.roll(wide, COLS - 1, 0)).astype(BF16)
    return left, right


def forward_body(flags_ref, feat, weight, slope_ref, sums, cols, wide, prod_a, prod_b, mask, *, band):
    for tile in range(8):
        mask[16 * tile : 16 * tile + 16] = jnp.full((16, CH), flags_ref[band, tile], jnp.int32).astype(F32)
    sums[...] = jnp.zeros_like(sums)
    taps = weight[...].reshape(9 * CH, CH)
    base = (HALF - 1) * band

    def build(i):
        here = slice(i * COLS, (i + 1) * COLS)
        row = feat[base + i]
        wide[here, 0:CH], wide[here, 2 * CH :] = neighbours(row)
        wide[here, CH : 2 * CH] = row

    def finish(r, value):
        at = r - HALF * band
        gate = gate_of(value)
        kept = gate * mask[...]
        pixel = feat[r].astype(F32)
        summed = (pixel + value * kept).astype(BF16).astype(F32)
        slope_ref[at] = (kept * (1.0 + value * (1.0 - gate))).astype(BF16)
        sums[r % 2] += summed
        for i, part in enumerate((value, summed, pixel)):
            cols[2 * i, at : at + 1] = part[0:1]
            cols[2 * i + 1, at : at + 1] = part[COLS - 1 :]

    prods = (prod_a, prod_b)
    for i in range(STEP + 2):
        build(i)
    for block in range(BLOCKS + 1):
        if block < BLOCKS:
            near = [slice((STEP * block + a) * COLS, (STEP * (block + 1) + a) * COLS) for a in range(3)]
            prods[block % 2][...] = nn(jnp.concatenate([wide[part] for part in near], axis=1), taps)
        for j in range(STEP):
            if block > 0:
                row = base + 1 + STEP * (block - 1) + j
                finish(row, prods[(block - 1) % 2][j * COLS : (j + 1) * COLS])
            ahead = STEP * (block + 1) + 2 + j
            if ahead < HALF + 1:
                build(ahead)


def border_body(
    flags_ref, feat, weight, sums_a, sums_b, cols_a, cols_b, top, bot, even, odd, strided, owner_ref,
    pooled_ref, token_ref, edge_ref, side_ref, side32,
):
    added = []
    cols = [jnp.concatenate([cols_a[i], cols_b[i]], axis=0) for i in range(6)]
    for i, whole in enumerate(sides(even, odd)):
        side32[...] = whole
        near = [side32[a : a + ROWS].astype(BF16) for a in range(3)]
        added.append(nn(jnp.concatenate(near, axis=1), forward_taps(weight, 2 * i)))

    def pair(one, two):
        return jnp.concatenate([one, two], axis=0)

    taken = jnp.concatenate(
        [pair(top[0], feat[ROWS - 2]), pair(feat[0], feat[ROWS - 1]), pair(feat[1], bot[0])], axis=1
    )
    low, mid, high = (nn(taken, forward_taps(weight, b)) for b in range(3))
    pix = iota((COLS, CH), 0)
    rows = []
    for i, r in enumerate((0, ROWS - 1)):
        part = slice(i * COLS, (i + 1) * COLS)
        before = jnp.where(pix == 0, added[0][r : r + 1], pltpu.roll(low[part], 1, 0))
        after = jnp.where(pix == COLS - 1, added[1][r : r + 1], pltpu.roll(high[part], COLS - 1, 0))
        value = mid[part] + before + after
        gate = gate_of(value)
        keep = jnp.concatenate(
            [jnp.full((16, CH), flags_ref[i, t], jnp.int32).astype(F32) for t in range(8)], axis=0
        )
        kept = gate * keep
        edge_ref[i] = (kept * (1.0 + value * (1.0 - gate))).astype(BF16)
        rows.append((feat[r].astype(F32) + value * kept).astype(BF16).astype(F32))

    line = iota((ROWS, CH), 0)
    deltas = []
    for i in range(2):
        value = cols[i] + added[i]
        gate = gate_of(value)
        tile = 7 * i
        keep = jnp.where(line < ROWS // 2, flags_ref[0, tile], flags_ref[1, tile]).astype(F32)
        kept = gate * keep
        side_ref[i] = kept * (1.0 + value * (1.0 - gate))
        summed = (cols[4 + i] + value * kept).astype(BF16).astype(F32)
        inside = (line > 0) & (line < ROWS - 1)
        deltas.append(jnp.where(inside, summed - cols[2 + i], 0.0))

    row, spot = iota((16, COLS), 0), iota((16, COLS), 1)
    pick = ((spot // 16 == row % 8) & (spot % 2 == row // 8)).astype(F32).astype(BF16)
    place = iota((16, CH), 0)
    parts = {}
    for band in range(2):
        for a in range(2):
            total = (sums_a, sums_b)[band][a]
            if band == a:
                total += rows[band]
            high, low = halves(total)
            part = nn(pick, high) + nn(pick, low)
            mine = (line // 16 == band) & (line % 2 == a)
            for i in range(2):
                delta = jnp.sum(jnp.where(mine, deltas[i], 0.0), axis=0, keepdims=True)
                part += jnp.where(place == 15 * i, delta, 0.0)
            parts[band, a] = part
    taken = [
        jnp.concatenate([parts[band, a][8 * b : 8 * b + 8] for band in range(2)], axis=0)
        for a in range(2)
        for b in range(2)
    ]
    high, low = halves(jnp.concatenate(taken, axis=1))
    flat = strided[...].reshape(4 * CH, CH)
    pooled = (nn(high, flat) + nn(low, flat)) * (1.0 / TILE_CELLS)
    pooled_ref[...] = pooled
    normed = pooled * lax.rsqrt(jnp.mean(pooled * pooled, axis=-1, keepdims=True) + 1e-05)
    token_ref[:, 0:CH] = normed.astype(BF16)
    owner = jnp.full((16, LANES), -1, jnp.int32)
    for tile in range(16):
        named = jnp.where(flags_ref[tile // 8, tile % 8] != 0, owner_ref[tile], -1)
        owner = jnp.where(iota((16, LANES), 0) == tile, named, owner)
    token_ref[:, CH:] = (owner == iota((16, LANES), 1)).astype(F32).astype(BF16)


def turn_body(feat, top, bot, w_query, w_key, w_value, token, turned_ref, high_ref, low_ref):
    turned_ref[:, 0:COLS] = top[0].T
    turned_ref[:, (ROWS + 1) * COLS :] = bot[0].T

    @pl.loop(0, ROWS // 4)
    def _(i):
        for j in range(4):
            here = pl.multiple_of((4 * i + j + 1) * COLS, COLS)
            turned_ref[:, pl.ds(here, COLS)] = feat[4 * i + j].T

    for i, one in enumerate((w_query, w_key, w_value)):
        high, low = halves(one[...])
        high_ref[:, i * CH : (i + 1) * CH] = high
        low_ref[:, i * CH : (i + 1) * CH] = low


def pair_body(one, two, out_ref):
    out_ref[0 : one.shape[0]] = one[...]
    out_ref[one.shape[0] :] = two[...]


def attention_body(*refs, seed_scale, pieces):
    got = refs[:pieces]
    pooled_ref, high_w, low_w, cot, strided, spread_ref, emb_ref = refs[pieces:]
    got = jnp.concatenate([piece[...] for piece in got], axis=0)
    count = got.shape[0]
    tokens, group = got[:, 0:CH], got[:, CH:]
    pair = nt(group, group)
    pairs = jnp.concatenate([pair] * HEADS, axis=0)
    projected = nn(tokens, high_w[...]) + nn(tokens, low_w[...])
    query, key, value = (projected[:, i * CH : (i + 1) * CH] for i in range(3))
    lane = iota((1, CH), 1) // (CH // HEADS)
    scale = 1.0 / math.sqrt(CH // HEADS)

    def by_head(array):
        return jnp.concatenate([jnp.where(lane == h, array, 0.0) for h in range(HEADS)], axis=0)

    queries, keys = halves(by_head(query)), halves(by_head(key))
    gate = gate_of(wide_product(nt, queries, halves(key)) * scale + attention_bias)
    weights = gate * pairs
    seed = cot[...] * seed_scale
    seeds = jnp.where(lane == iota((8, CH), 0), seed, 0.0)
    values = halves(value)
    along = wide_product(nt, halves(seeds), values)
    columns, grads = [], []
    for h in range(HEADS):
        part = slice(h * count, (h + 1) * count)
        columns.append(jnp.sum(weights[part], axis=0, keepdims=True))
        grads.append(weights[part] * (1.0 - gate[part]) * (along[h : h + 1] * scale))
    columns = halves(jnp.concatenate(columns + [jnp.zeros((8 - HEADS, count), F32)], axis=0))
    grad_q = wide_product(nn, halves(jnp.concatenate([g[0:16] for g in grads], axis=1)), keys)
    narrow = halves(jnp.concatenate([g[:, 0:LANES] for g in grads], axis=0))
    grad_k = wide_product(tn, narrow, queries)[0:16]
    grad_v = wide_product(tn, columns, halves(seeds))[0:16]
    mixed = wide_product(nn, columns, values)
    mixed = jnp.sum(jnp.where(lane == iota((8, CH), 0), mixed, 0.0), axis=0, keepdims=True)
    high = mixed.astype(BF16).astype(F32)
    low = mixed - high
    rows = iota((16, LANES), 0)
    packed = jnp.zeros((16, LANES), F32)
    for i, part in enumerate((high[:, :LANES], high[:, LANES:], low[:, :LANES], low[:, LANES:])):
        packed = jnp.where(rows == i, part, packed)
    emb_ref[...] = packed.astype(BF16)

    grads = halves(jnp.concatenate([grad_q, grad_k, grad_v], axis=1))
    grad = wide_product(nt, grads, (high_w[...], low_w[...]))
    grad = grad.astype(BF16).astype(F32)
    pooled = pooled_ref[...]
    inv = lax.rsqrt(jnp.mean(pooled * pooled, axis=-1, keepdims=True) + 1e-05)
    unit = pooled * inv
    back = inv * (grad - unit * jnp.mean(grad * unit, axis=-1, keepdims=True))
    cell = (back * (1.0 / TILE_CELLS)).astype(BF16)
    spot, row = iota((COLS, 16), 0), iota((COLS, 16), 1)
    expand = ((spot // 16 == row % 8) & (spot % 2 == row // 8)).astype(F32).astype(BF16)
    taps = nt(cell, strided[...].reshape(4 * CH, CH))
    for band in range(2):
        here = taps[8 * band : 8 * band + 8]
        both = [
            jnp.concatenate([here[:, (2 * a + b) * CH : (2 * a + b + 1) * CH] for a in range(2)], axis=1)
            for b in range(2)
        ]
        high, low = halves(jnp.concatenate(both, axis=0))
        spread = nn(expand, high) + nn(expand, low)
        for a in range(2):
            spread_ref[band * 2 + a] = spread[:, a * CH : (a + 1) * CH]


GROUPS = (6, 10, 16)


def weight_body(
    spread, slope_a, slope_b, edge, side, turned, even, odd,
    wide, keep_ref, give_ref, even_ref, odd_ref, left_ref, right_ref, total, first, last,
):
    first[...] = jnp.zeros_like(first)
    last[...] = jnp.zeros_like(last)
    pix = iota((COLS, CH), 0)

    def build(r):
        if r in (0, ROWS - 1):
            slope = edge[r // HALF].astype(F32)
        else:
            slope = (slope_a, slope_b)[r // HALF][r % HALF].astype(F32)
            slope = jnp.where(pix == 0, side[0, r : r + 1], slope)
            slope = jnp.where(pix == COLS - 1, side[1, r : r + 1], slope)
        grad = (spread[(r // HALF) * 2 + r % 2] * slope).astype(BF16)
        here = slice(r * COLS, (r + 1) * COLS)
        wide[here, 2 * CH :], wide[here, 0:CH] = neighbours(grad)
        wide[here, CH : 2 * CH] = grad
        full = grad.astype(F32)
        for a in range(3):
            first[a, r + a : r + a + 1] = full[0:1]
            last[a, r + a : r + a + 1] = full[COLS - 1 :]

    is_one = is_odd("core")
    left, right = (part.astype(BF16) for part in sides(even, odd))

    def put(part, a, b):
        if b == 0:
            part += tn(left, first[a].astype(BF16))
        if b == 2:
            part += tn(right, last[a].astype(BF16))
        low, high = part[:, :LANES], part[:, LANES:]
        at = slice((3 * a + b) * CH, (3 * a + b + 1) * CH)
        keep_ref[at] = jnp.where(is_one, high, low).astype(BF16)
        give_ref[at] = jnp.where(is_one, low, high).astype(BF16)

    for r in range(GROUPS[0]):
        build(r)
    start = 0
    for g, count in enumerate(GROUPS):
        here = slice(start * COLS, (start + count) * COLS)
        near = [turned[:, (start + a) * COLS : (start + a + count) * COLS] for a in range(3)]
        near = jnp.concatenate(near, axis=0)
        start += count
        ahead = GROUPS[g + 1] if g + 1 < len(GROUPS) else 0
        for b in range(3):
            part = slice(b * CH, (b + 1) * CH)
            result = nn(near, wide[here, part])
            if g > 0:
                result += total[:, part]
            if ahead:
                total[:, part] = result
            for r in range(ahead * b // 3, ahead * (b + 1) // 3):
                build(start + r)
            if not ahead:
                for a in range(3):
                    put(result[a * CH : (a + 1) * CH], a, b)

    centre = slice(CH, 2 * CH)
    order_rows(wide[0:COLS, centre], wide[(ROWS - 1) * COLS :, centre], even_ref, odd_ref)
    left_ref[...] = first[1].astype(BF16)
    right_ref[...] = last[1].astype(BF16)


def order_rows(first, last, even_ref, odd_ref):
    odd = is_odd("gy")
    even_ref[0] = jnp.where(odd, first, last)
    odd_ref[0] = jnp.where(odd, last, first)


def back_taps(weight, taps):
    return jnp.concatenate([weight[tap] for tap in taps], axis=1)


def input_blocks(wide, weight, first, prods, finish, send):
    for block in range(BLOCKS + 1):
        if block < BLOCKS:
            at = first + STEP * block
            near = [wide[(at + step) * COLS : (at + step + STEP) * COLS] for step in (1, 0, -1)]
            prods[block % 2][...] = nt(jnp.concatenate(near, axis=1), back_taps(weight, range(9)))
        if block > 0:
            at = first + STEP * (block - 1)
            for j in range(STEP):
                finish(at + j, prods[(block - 1) % 2][j * COLS : (j + 1) * COLS])
            send(at, STEP)


def upper_body(wide, spread, weight, out, kept_ref, raw_ref, prod_a, prod_b, done, sems):
    started = []

    def finish(r, prod):
        value = spread[r % 2] + prod
        done[r] = value.astype(BF16)
        raw_ref[0, r : r + 1] = value[0:1]
        raw_ref[1, r : r + 1] = value[COLS - 1 :]
        kept_ref[0, r] = done[r, 0:16]
        kept_ref[1, r] = done[r, COLS - 16 :]

    def send(first, count):
        here = slice(first, first + count)
        started.append(pltpu.make_async_copy(done.at[here], out.at[here], sems.at[len(started)]))
        started[-1].start()

    input_blocks(wide, weight, 1, (prod_a, prod_b), finish, send)
    for one in started:
        one.wait()


def lower_body(
    wide, top, bot, even, odd, spread, weight, kept, raw, _, out, prod_a, prod_b, side32, added, done, fixed, sems
):
    for i, whole in enumerate(sides(even, odd)):
        side32[...] = whole
        near = [side32[2 - a : 2 - a + ROWS].astype(BF16) for a in range(3)]
        taps = back_taps(weight, [3 * a + 2 - 2 * i for a in range(3)])
        added[i] = nt(jnp.concatenate(near, axis=1), taps)
    started = []

    def start(source, target):
        started.append(pltpu.make_async_copy(source, target, sems.at[len(started)]))
        started[-1].start()

    small = iota((16, CH), 0)
    for i in range(2):
        for r in range(1, HALF):
            value = raw[i, r : r + 1] + added[i, r : r + 1]
            fixed[i, r] = jnp.where(small == 15 * i, value, kept[i, r].astype(F32)).astype(BF16)
        at = (COLS - 16) * i
        start(fixed.at[i, 1:HALF], out.at[1:HALF, at : at + 16])

    pix = iota((COLS, CH), 0)

    def finish(r, prod):
        outer = jnp.where(pix == 0, added[0, r : r + 1], 0.0)
        outer = jnp.where(pix == COLS - 1, added[1, r : r + 1], outer)
        at = r - HALF if r >= HALF else HALF
        done[at] = (spread[(r // HALF) * 2 + r % 2] + (prod + outer)).astype(BF16)

    def send(first, count):
        at = first - HALF if first >= HALF else HALF
        start(done.at[at : at + count], out.at[first : first + count])

    input_blocks(wide, weight, HALF, (prod_a, prod_b), finish, send)

    def row(r):
        return wide[r * COLS : (r + 1) * COLS]

    def outside(one):
        left, right = neighbours(one[0])
        return jnp.concatenate([right, one[0], left], axis=1)

    def pair(one, two):
        return jnp.concatenate([one, two], axis=0)

    near = [pair(row(1), outside(bot)), pair(row(0), row(ROWS - 1)), pair(outside(top), row(ROWS - 2))]
    both = nt(jnp.concatenate(near, axis=1), back_taps(weight, range(9)))
    for i, r in enumerate((0, ROWS - 1)):
        finish(r, both[i * COLS : (i + 1) * COLS])
        send(r, 1)
    for one in started:
        one.wait()


def sum_body(*refs, terms, axis):
    outs, total_ref = refs[terms:-1], refs[-1]
    total = refs[0][...].astype(F32)
    for one in refs[1:terms]:
        total += one[...].astype(F32)
    total_ref[...] = total.astype(BF16)
    size = outs[0].shape[0]
    for k, out in enumerate(outs):
        at = lax.bitwise_xor(lax.axis_index(axis), k) * size
        out[...] = total_ref[pl.ds(pl.multiple_of(at, 16), size)]


def last_sum_body(*refs):
    emb, out = refs[-2:]
    total = refs[0][...].astype(F32)
    for one in refs[1:-2]:
        total += one[...].astype(F32)
    out[0 : total.shape[0]] = total.astype(BF16)
    out[total.shape[0] :] = emb[...]


def stack_body(*refs):
    for i, one in enumerate(refs[:-1]):
        refs[-1][i] = one[...]


def half_of(array, grad_ref, buf, sem, share, half):
    gy, gz = lax.axis_index("gy"), lax.axis_index("gz")
    bands, depth = array.shape[0], array.shape[1]
    for k in range(bands):
        for j in range(depth):
            at = (lax.bitwise_xor(gy, k) * depth + lax.bitwise_xor(gz, j)) * share
            here = pl.ds(pl.multiple_of(at, 16), share)
            buf[here] = array[k, j, 0:share].astype(F32) * (1.0 / loss_scale)
    lanes = pl.ds(pl.multiple_of(half * LANES, LANES), LANES)
    one = pltpu.make_async_copy(buf, grad_ref.at[:, lanes], sem.at[0])
    one.start()
    return one


def mine_body(mine, grad_ref, buf, sem, *, share):
    half_of(mine, grad_ref, buf, sem, share, lax.axis_index("core")).wait()


def other_body(mine, other, _, grad_ref, emb_ref, buf, sem, *, share, norm_scale):
    sent = half_of(other, grad_ref, buf, sem, share, 1 - lax.axis_index("core"))
    gy, gz = lax.axis_index("gy"), lax.axis_index("gz")
    is_one = is_odd("core")
    total = jnp.zeros((16, LANES), F32)
    for band in range(mine.shape[0]):
        k = lax.bitwise_xor(gy, band)
        one, two = (array[k, gz, share : share + 16].astype(F32) for array in (mine, other))
        total += jnp.where(is_one, two, one)
    total = total * norm_scale
    emb_ref[:, 0:LANES] = total[0:1] + total[2:3]
    emb_ref[:, LANES:] = total[1:2] + total[3:4]
    sent.wait()


SMEM = pl.BlockSpec(memory_space=pltpu.SMEM)
VMEM = pl.BlockSpec(memory_space=pltpu.VMEM)
HBM = pl.BlockSpec(memory_space=pltpu.HBM)


def run(body, args, outs, scratch=(), flops=1 << 20, mib=8, far=(), **rest):
    specs = [HBM if i in far else SMEM if a.dtype == jnp.int32 else VMEM for i, a in enumerate(args)]
    return pl.pallas_call(
        body,
        in_specs=specs,
        out_shape=outs,
        scratch_shapes=list(scratch),
        compiler_params=pltpu.CompilerParams(vmem_limit_bytes=mib << 20),
        cost_estimate=pl.CostEstimate(flops=flops, bytes_accessed=1 << 20, transcendentals=0),
        **rest,
    )(*args)


def per_device(features, tissue, owner_map, w_conv, w_stride, w_query, w_key, w_value, cotangent):
    gy_count, gz_count, cores = lax.axis_size("gy"), lax.axis_size("gz"), lax.axis_size("core")
    gx_count, chips = gz_count * cores, gy_count * gz_count
    across = ("gz", "core")
    norm_scale = 1.0 / math.sqrt(16 * gy_count * gx_count)
    swap = [(i, i ^ 1) for i in range(cores)]

    def pairs(value, axis, count, odd):
        low = range(odd, count - 1, 2)
        return lax.ppermute(value, axis, [(i, i + 1) for i in low] + [(i + 1, i) for i in low])

    def others(values, axis, count):
        return [
            lax.ppermute(value, axis, [(i, i ^ k) for i in range(count)])
            for k, value in enumerate(values, 1)
        ]

    column = shape((HALO, CH), BF16)
    line = shape((1, COLS, CH), BF16)

    def row_halos(even, odd):
        return pairs(even, "gy", gy_count, 0), pairs(odd, "gy", gy_count, 1)

    def corners(left, right, even, odd):
        return run(corner_body, (left, right, even, odd), [line, line, column, column], mib=1)

    def column_halos(even, odd):
        return pairs(even, across, gx_count, 0), pairs(odd, across, gx_count, 1)

    conv_flops = 2 * ROWS * COLS * 9 * CH * CH
    prod = pltpu.VMEM((STEP * COLS, CH), F32)
    side32 = pltpu.VMEM((HALO, CH), F32)
    half_block = shape((HALF, COLS, CH), BF16)

    def forward(band, weight):
        return run(
            lambda *refs: forward_body(*refs, band=band),
            (tissue, features, weight),
            [half_block, shape((2, COLS, CH), F32), shape((6, HALF, CH), F32)],
            [pltpu.VMEM(((HALF + 1) * COLS, 3 * CH), BF16), prod, prod, pltpu.VMEM((COLS, CH), F32)],
            flops=conv_flops // 2,
            mib=16,
        )

    rows = run(
        rows_body,
        (features,),
        [line, line],
        [pltpu.SemaphoreType.DMA((2,))],
        flops=conv_flops,
        mib=56,
        far=(0,),
    )
    outer = run(columns_body, (features,), [column, column], mib=2)
    even, odd = row_halos(*rows)
    slope_a, sums_a, cols_a = forward(0, w_conv)
    even, odd, cols_a = lax.optimization_barrier((even, odd, cols_a))
    top, bot, even, odd = corners(*outer, even, odd)
    weight_b, even = lax.optimization_barrier((w_conv, even))
    even, odd = column_halos(even, odd)
    slope_b, sums_b, cols_b = forward(1, weight_b)
    pooled, token, edge, side = run(
        border_body,
        (
            tissue, features, w_conv, sums_a, sums_b, cols_a, cols_b, top, bot, even, odd, w_stride,
            owner_map.reshape(16),
        ),
        [
            shape((16, CH), F32),
            shape((16, CH + LANES), BF16),
            shape((2, COLS, CH), BF16),
            shape((2, ROWS, CH), F32),
        ],
        [side32],
        flops=conv_flops // 8,
        mib=12,
    )
    near, far = token, lax.ppermute(token, "core", swap)
    step = 1
    while step < gz_count:
        near = run(pair_body, (near, far), shape((2 * near.shape[0], CH + LANES), BF16), mib=1)
        far = lax.ppermute(near, "gz", [(i, i ^ step) for i in range(gz_count)])
        step *= 2
    turned, high_w, low_w = run(
        turn_body,
        (features, top, bot, w_query, w_key, w_value, token),
        [shape((CH, (ROWS + 2) * COLS), BF16), shape((CH, 3 * CH), BF16), shape((CH, 3 * CH), BF16)],
        flops=conv_flops // 4,
        mib=12,
    )
    spread, emb = run(
        lambda *refs: attention_body(*refs, seed_scale=loss_scale * norm_scale, pieces=2),
        (near, far, pooled, high_w, low_w, cotangent.reshape(1, CH), w_stride),
        [shape((4, COLS, CH), F32), shape((16, LANES), BF16)],
        flops=1 << 30,
        mib=12,
    )
    border = pltpu.VMEM((3, HALO, CH), F32)
    wide, keep, give, *outer = run(
        weight_body,
        (spread, slope_a, slope_b, edge, side, turned, even, odd),
        [
            shape((ROWS * COLS, 3 * CH), BF16),
            shape((9 * CH, LANES), BF16),
            shape((9 * CH, LANES), BF16),
            line,
            line,
            column,
            column,
        ],
        [pltpu.VMEM((3 * CH, 3 * CH), F32), border, border],
        flops=conv_flops,
        mib=20,
    )

    share = -(-9 * CH // (16 * chips)) * 16
    spare = share * chips - 9 * CH
    taken = lax.ppermute(give, "core", swap)
    if spare:
        keep, taken = (jnp.pad(a, ((0, spare), (0, 0))) for a in (keep, taken))

    def summed(axis, terms, count):
        rows = terms[0].shape[0]
        return run(
            lambda *refs: sum_body(*refs, terms=len(terms), axis=axis),
            terms,
            [shape((rows // count, LANES), BF16)] * count,
            [pltpu.VMEM((rows, LANES), BF16)],
            mib=6,
        )

    def stacked(terms):
        return run(stack_body, terms, shape((len(terms),) + terms[0].shape, BF16), mib=4)

    block = shape((ROWS, COLS, CH), BF16)
    parts = summed("gy", [keep, taken], gy_count)
    *parts, wide_upper = lax.optimization_barrier((*parts, wide))
    upper, kept, raw = run(
        upper_body,
        (wide_upper, spread, w_conv),
        [block, shape((2, HALF, 16, CH), BF16), shape((2, HALF, CH), F32)],
        [prod, prod, pltpu.VMEM((HALF, COLS, CH), BF16), pltpu.SemaphoreType.DMA((BLOCKS,))],
        flops=conv_flops // 2,
        mib=16,
        out_specs=[HBM, VMEM, VMEM],
    )
    raw, *outer = lax.optimization_barrier((raw, *outer))
    parts = [parts[0]] + others(parts[1:], "gy", gy_count)
    even, odd = row_halos(*outer[:2])
    *parts, raw = lax.optimization_barrier((*parts, raw))
    parts = summed("gz", parts, gz_count)
    even, odd, *parts = lax.optimization_barrier((even, odd, *parts))
    parts = [parts[0]] + others(parts[1:], "gz", gz_count)
    top, bot, even, odd = corners(*outer[2:], even, odd)
    even, odd = column_halos(even, odd)
    *parts, even, odd = lax.optimization_barrier((*parts, even, odd))
    mine = run(last_sum_body, (*parts, emb), shape((share + 16, LANES), BF16), mib=2)
    row = stacked([mine] + others([mine] * (gz_count - 1), "gz", gz_count))
    row, wide_lower = lax.optimization_barrier((row, wide))
    input_grad = run(
        lower_body,
        (wide_lower, top, bot, even, odd, spread, w_conv, kept, raw, upper),
        block,
        [
            prod,
            prod,
            side32,
            pltpu.VMEM((2, ROWS, CH), F32),
            pltpu.VMEM((HALF + 1, COLS, CH), BF16),
            pltpu.VMEM((2, HALF, 16, CH), BF16),
            pltpu.SemaphoreType.DMA((BLOCKS + 4,)),
        ],
        flops=conv_flops // 2,
        mib=16,
        far=(9,),
        out_specs=HBM,
        input_output_aliases={9: 0},
    )
    planes = [row] + others([row] * (gy_count - 1), "gy", gy_count)
    *planes, input_grad = lax.optimization_barrier((*planes, input_grad))
    plane = stacked(planes)
    other = lax.ppermute(plane, "core", swap)
    whole = shape((share * chips, CH), F32)
    buffers = [pltpu.VMEM((share * chips, LANES), F32), pltpu.SemaphoreType.DMA((1,))]
    half_grad = run(
        lambda *refs: mine_body(*refs, share=share), (plane,), whole, buffers, mib=4, out_specs=HBM
    )
    conv_grad, embedding = run(
        lambda *refs: other_body(*refs, share=share, norm_scale=norm_scale),
        (plane, other, half_grad),
        [whole, shape((1, CH), F32)],
        buffers,
        mib=4,
        far=(2,),
        out_specs=[HBM, VMEM],
        input_output_aliases={2: 0},
    )
    return embedding.reshape(CH), input_grad, conv_grad[: 9 * CH].reshape(9, CH, CH)


def solution(mesh):
    sizes = mesh.devices.shape
    split = Mesh(mesh.devices.reshape(sizes[0], sizes[1] // 2, 2), ("gy", "gz", "core"))
    gx = ("gz", "core")
    in_specs = (P("gy", gx, None), P("gy", gx), P("gy", gx, None, None), P(), P(), P(), P(), P(), P())
    out_specs = (P(), P("gy", gx, None), P())
    return jax.shard_map(per_device, mesh=split, in_specs=in_specs, out_specs=out_specs, check_vma=False)
```

```python
import math

import jax
import jax.numpy as jnp
from jax import lax
from jax.experimental import pallas as pl
from jax.experimental.pallas import tpu as pltpu
from jax.sharding import Mesh, PartitionSpec as P

HEADS = 4
F32 = jnp.float32
BF16 = jnp.bfloat16

attention_bias = -1.0
loss_scale = 512.0

ROWS = 32
COLS = 128
CH = 256
HALO = 48
LANES = 128
STEP = 5
TILE_CELLS = 64


def shape(dims, dtype):
    return jax.ShapeDtypeStruct(dims, dtype)


def nt(left, right):
    return lax.dot_general(left, right, (((1,), (1,)), ((), ())), preferred_element_type=F32)


def tn(left, right):
    return lax.dot_general(left, right, (((0,), (0,)), ((), ())), preferred_element_type=F32)


def nn(left, right):
    return jnp.dot(left, right, preferred_element_type=F32)


def halves(value):
    high = value.astype(BF16)
    return high, (value - high.astype(F32)).astype(BF16)


def wide_product(product, left, right):
    (a, b), (c, d) = left, right
    return product(a, c) + (product(a, d) + product(b, c))


def iota(dims, axis):
    return lax.broadcasted_iota(jnp.int32, dims, axis)


def gate_of(value):
    return 0.5 * jnp.tanh(0.5 * value) + 0.5


def copies(pairs, sems):
    started = [pltpu.make_async_copy(a, b, sems.at[i]) for i, (a, b) in enumerate(pairs)]
    for one in started:
        one.start()
    return started


def is_odd(axis):
    return lax.axis_index(axis) % 2 == 1


def rows_body(block, even_ref, odd_ref, sems):
    odd = is_odd("gy")
    first, last = jnp.where(odd, 0, ROWS - 1), jnp.where(odd, ROWS - 1, 0)
    started = copies([(block.at[pl.ds(first, 1)], even_ref), (block.at[pl.ds(last, 1)], odd_ref)], sems)
    for one in started:
        one.wait()


def columns_body(block, left_ref, right_ref):
    row, spot = iota((HALO, ROWS * 16), 0), iota((HALO, ROWS * 16), 1)
    for out, at, place in ((left_ref, 0, 0), (right_ref, COLS - 16, 15)):
        pick = (spot == (row - 1) * 16 + place).astype(F32).astype(BF16)
        out[...] = nn(pick, block[:, at : at + 16].reshape(ROWS * 16, CH)).astype(BF16)


def corner_body(left, right, even, odd, top_ref, bot_ref, even_ref, odd_ref):
    low = is_odd("gy")
    top_ref[0] = jnp.where(low, even[0], odd[0])
    bot_ref[0] = jnp.where(low, odd[0], even[0])
    row = iota((HALO, CH), 0)
    whole = []
    for side, at in ((left, 0), (right, COLS - 16)):
        part = slice(0, 1) if at == 0 else slice(15, 16)
        above = top_ref[0, at : at + 16].astype(F32)[part]
        below = bot_ref[0, at : at + 16].astype(F32)[part]
        whole.append(jnp.where(row == 0, above, jnp.where(row == ROWS + 1, below, side[...].astype(F32))))
    high = is_odd("core")
    even_ref[...] = jnp.where(high, whole[0], whole[1]).astype(BF16)
    odd_ref[...] = jnp.where(high, whole[1], whole[0]).astype(BF16)


def sides(even, odd):
    high = is_odd("core")
    one, two = even[...].astype(F32), odd[...].astype(F32)
    return jnp.where(high, one, two), jnp.where(high, two, one)


def forward_taps(weight, b):
    return jnp.concatenate([weight[3 * a + b] for a in range(3)], axis=0)


HALF = ROWS // 2
BLOCKS = (HALF - 1) // STEP
PARTS = (3, 5, 5, 2)


def neighbours(row):
    pix = iota((COLS, CH), 0)
    wide = row.astype(F32)
    left = jnp.where(pix == 0, 0.0, pltpu.roll(wide, 1, 0)).astype(BF16)
    right = jnp.where(pix == COLS - 1, 0.0, pltpu.roll(wide, COLS - 1, 0)).astype(BF16)
    return left, right


def forward_body(flags_ref, feat, weight, slope_ref, sums, cols, wide, prod_a, prod_b, mask, *, band):
    for tile in range(8):
        mask[16 * tile : 16 * tile + 16] = jnp.full((16, CH), flags_ref[band, tile], jnp.int32).astype(F32)
    sums[...] = jnp.zeros_like(sums)
    taps = weight[...].reshape(9 * CH, CH)
    base = (HALF - 1) * band

    def build(i):
        here = slice(i * COLS, (i + 1) * COLS)
        row = feat[base + i]
        wide[here, 0:CH], wide[here, 2 * CH :] = neighbours(row)
        wide[here, CH : 2 * CH] = row

    def finish(r, value):
        at = r - HALF * band
        gate = gate_of(value)
        kept = gate * mask[...]
        pixel = feat[r].astype(F32)
        summed = (pixel + value * kept).astype(BF16).astype(F32)
        slope_ref[at] = (kept * (1.0 + value * (1.0 - gate))).astype(BF16)
        sums[r % 2] += summed
        for i, part in enumerate((value, summed, pixel)):
            cols[2 * i, at : at + 1] = part[0:1]
            cols[2 * i + 1, at : at + 1] = part[COLS - 1 :]

    prods = (prod_a, prod_b)
    built, done = PARTS[0] + 2, 0
    for i in range(built):
        build(i)
    for block in range(len(PARTS) + 1):
        start = sum(PARTS[:block])
        if block < len(PARTS):
            count = PARTS[block]
            near = [slice((start + a) * COLS, (start + count + a) * COLS) for a in range(3)]
            near = jnp.concatenate([wide[part] for part in near], axis=1)
            prods[block % 2][0 : count * COLS] = nn(near, taps)
        ahead = min(HALF + 1, sum(PARTS[: block + 2]) + 2)
        for j in range(STEP):
            if done < start:
                at = (done - sum(PARTS[: block - 1])) * COLS
                finish(base + 1 + done, prods[(block - 1) % 2][at : at + COLS])
                done += 1
            if built < ahead:
                build(built)
                built += 1


def border_body(
    flags_ref, feat, weight, sums_a, sums_b, cols_a, cols_b, top, bot, even, odd, strided, owner_ref,
    pooled_ref, token_ref, edge_ref, side_ref, side32,
):
    added = []
    cols = [jnp.concatenate([cols_a[i], cols_b[i]], axis=0) for i in range(6)]
    for i, whole in enumerate(sides(even, odd)):
        side32[...] = whole
        near = [side32[a : a + ROWS].astype(BF16) for a in range(3)]
        added.append(nn(jnp.concatenate(near, axis=1), forward_taps(weight, 2 * i)))

    def pair(one, two):
        return jnp.concatenate([one, two], axis=0)

    taken = jnp.concatenate(
        [pair(top[0], feat[ROWS - 2]), pair(feat[0], feat[ROWS - 1]), pair(feat[1], bot[0])], axis=1
    )
    low, mid, high = (nn(taken, forward_taps(weight, b)) for b in range(3))
    pix = iota((COLS, CH), 0)
    rows = []
    for i, r in enumerate((0, ROWS - 1)):
        part = slice(i * COLS, (i + 1) * COLS)
        before = jnp.where(pix == 0, added[0][r : r + 1], pltpu.roll(low[part], 1, 0))
        after = jnp.where(pix == COLS - 1, added[1][r : r + 1], pltpu.roll(high[part], COLS - 1, 0))
        value = mid[part] + before + after
        gate = gate_of(value)
        keep = jnp.concatenate(
            [jnp.full((16, CH), flags_ref[i, t], jnp.int32).astype(F32) for t in range(8)], axis=0
        )
        kept = gate * keep
        edge_ref[i] = (kept * (1.0 + value * (1.0 - gate))).astype(BF16)
        rows.append((feat[r].astype(F32) + value * kept).astype(BF16).astype(F32))

    line = iota((ROWS, CH), 0)
    deltas = []
    for i in range(2):
        value = cols[i] + added[i]
        gate = gate_of(value)
        tile = 7 * i
        keep = jnp.where(line < ROWS // 2, flags_ref[0, tile], flags_ref[1, tile]).astype(F32)
        kept = gate * keep
        side_ref[i] = kept * (1.0 + value * (1.0 - gate))
        summed = (cols[4 + i] + value * kept).astype(BF16).astype(F32)
        inside = (line > 0) & (line < ROWS - 1)
        deltas.append(jnp.where(inside, summed - cols[2 + i], 0.0))

    row, spot = iota((16, COLS), 0), iota((16, COLS), 1)
    pick = ((spot // 16 == row % 8) & (spot % 2 == row // 8)).astype(F32).astype(BF16)
    place = iota((16, CH), 0)
    parts = {}
    for band in range(2):
        for a in range(2):
            total = (sums_a, sums_b)[band][a]
            if band == a:
                total += rows[band]
            high, low = halves(total)
            part = nn(pick, high) + nn(pick, low)
            mine = (line // 16 == band) & (line % 2 == a)
            for i in range(2):
                delta = jnp.sum(jnp.where(mine, deltas[i], 0.0), axis=0, keepdims=True)
                part += jnp.where(place == 15 * i, delta, 0.0)
            parts[band, a] = part
    taken = [
        jnp.concatenate([parts[band, a][8 * b : 8 * b + 8] for band in range(2)], axis=0)
        for a in range(2)
        for b in range(2)
    ]
    high, low = halves(jnp.concatenate(taken, axis=1))
    flat = strided[...].reshape(4 * CH, CH)
    pooled = (nn(high, flat) + nn(low, flat)) * (1.0 / TILE_CELLS)
    pooled_ref[...] = pooled
    normed = pooled * lax.rsqrt(jnp.mean(pooled * pooled, axis=-1, keepdims=True) + 1e-05)
    token_ref[:, 0:CH] = normed.astype(BF16)
    owner = jnp.full((16, LANES), -1, jnp.int32)
    for tile in range(16):
        named = jnp.where(flags_ref[tile // 8, tile % 8] != 0, owner_ref[tile], -1)
        owner = jnp.where(iota((16, LANES), 0) == tile, named, owner)
    token_ref[:, CH:] = (owner == iota((16, LANES), 1)).astype(F32).astype(BF16)


def turn_body(feat, top, bot, w_query, w_key, w_value, token, turned_ref, high_ref, low_ref):
    turned_ref[:, 0:COLS] = top[0].T
    turned_ref[:, (ROWS + 1) * COLS :] = bot[0].T

    @pl.loop(0, ROWS // 4)
    def _(i):
        for j in range(4):
            here = pl.multiple_of((4 * i + j + 1) * COLS, COLS)
            turned_ref[:, pl.ds(here, COLS)] = feat[4 * i + j].T

    for i, one in enumerate((w_query, w_key, w_value)):
        high, low = halves(one[...])
        high_ref[:, i * CH : (i + 1) * CH] = high
        low_ref[:, i * CH : (i + 1) * CH] = low


def pair_body(one, two, out_ref):
    out_ref[0:16] = one[...]
    out_ref[16:32] = two[...]


def attention_body(*refs, seed_scale, pieces):
    got = refs[:pieces]
    pooled_ref, high_w, low_w, cot, strided, spread_ref, emb_ref, band, grad_ref = refs[pieces:]
    gz, core = lax.axis_index("gz"), lax.axis_index("core")

    def rows_of(depth, other):
        return pl.ds(pl.multiple_of(depth * 32 + other * 16, 16), 16)

    for k, piece in enumerate(got):
        depth = lax.bitwise_xor(gz, k)
        band[rows_of(depth, core)] = piece[0:16]
        band[rows_of(depth, 1 - core)] = piece[16:32]
    count = band.shape[0]
    tokens, group = band[:, 0:CH], band[:, CH:]
    pair = nt(group, group)
    pairs = jnp.concatenate([pair] * HEADS, axis=0)
    projected = nn(tokens, high_w[...]) + nn(tokens, low_w[...])
    query, key, value = (projected[:, i * CH : (i + 1) * CH] for i in range(3))
    lane = iota((1, CH), 1) // (CH // HEADS)
    scale = 1.0 / math.sqrt(CH // HEADS)

    def by_head(array):
        return jnp.concatenate([jnp.where(lane == h, array, 0.0) for h in range(HEADS)], axis=0)

    queries, keys = halves(by_head(query)), halves(by_head(key))
    gate = gate_of(wide_product(nt, queries, halves(key)) * scale + attention_bias)
    weights = gate * pairs
    seed = cot[...] * seed_scale
    seeds = jnp.where(lane == iota((8, CH), 0), seed, 0.0)
    values = halves(value)
    along = wide_product(nt, halves(seeds), values)
    columns, grads = [], []
    for h in range(HEADS):
        part = slice(h * count, (h + 1) * count)
        columns.append(jnp.sum(weights[part], axis=0, keepdims=True))
        grads.append(weights[part] * (1.0 - gate[part]) * (along[h : h + 1] * scale))
    columns = halves(jnp.concatenate(columns + [jnp.zeros((8 - HEADS, count), F32)], axis=0))
    grad_ref[:, 0:CH] = wide_product(nn, halves(jnp.concatenate(grads, axis=1)), keys)
    grad_ref[:, CH : 2 * CH] = wide_product(tn, halves(jnp.concatenate(grads, axis=0)), queries)
    grad_ref[:, 2 * CH :] = wide_product(tn, columns, halves(seeds))
    mixed = wide_product(nn, columns, values)
    mixed = jnp.sum(jnp.where(lane == iota((8, CH), 0), mixed, 0.0), axis=0, keepdims=True)
    high = mixed.astype(BF16).astype(F32)
    low = mixed - high
    rows = iota((16, LANES), 0)
    packed = jnp.zeros((16, LANES), F32)
    for i, part in enumerate((high[:, :LANES], high[:, LANES:], low[:, :LANES], low[:, LANES:])):
        packed = jnp.where(rows == i, part, packed)
    emb_ref[...] = packed.astype(BF16)

    grads = halves(grad_ref[rows_of(gz, core)])
    grad = wide_product(nt, grads, (high_w[...], low_w[...]))
    grad = grad.astype(BF16).astype(F32)
    pooled = pooled_ref[...]
    inv = lax.rsqrt(jnp.mean(pooled * pooled, axis=-1, keepdims=True) + 1e-05)
    unit = pooled * inv
    back = inv * (grad - unit * jnp.mean(grad * unit, axis=-1, keepdims=True))
    cell = (back * (1.0 / TILE_CELLS)).astype(BF16)
    spot, row = iota((COLS, 16), 0), iota((COLS, 16), 1)
    expand = ((spot // 16 == row % 8) & (spot % 2 == row // 8)).astype(F32).astype(BF16)
    taps = nt(cell, strided[...].reshape(4 * CH, CH))
    for band in range(2):
        here = taps[8 * band : 8 * band + 8]
        both = [
            jnp.concatenate([here[:, (2 * a + b) * CH : (2 * a + b + 1) * CH] for a in range(2)], axis=1)
            for b in range(2)
        ]
        high, low = halves(jnp.concatenate(both, axis=0))
        spread = nn(expand, high) + nn(expand, low)
        for a in range(2):
            spread_ref[band * 2 + a] = spread[:, a * CH : (a + 1) * CH]


GROUPS = (6, 10, 16)


def weight_body(
    spread, slope_a, slope_b, edge, side, turned, even, odd,
    wide, keep_ref, give_ref, even_ref, odd_ref, left_ref, right_ref, total, first, last,
):
    first[...] = jnp.zeros_like(first)
    last[...] = jnp.zeros_like(last)
    pix = iota((COLS, CH), 0)

    def build(r):
        if r in (0, ROWS - 1):
            slope = edge[r // HALF].astype(F32)
        else:
            slope = (slope_a, slope_b)[r // HALF][r % HALF].astype(F32)
            slope = jnp.where(pix == 0, side[0, r : r + 1], slope)
            slope = jnp.where(pix == COLS - 1, side[1, r : r + 1], slope)
        grad = (spread[(r // HALF) * 2 + r % 2] * slope).astype(BF16)
        here = slice(r * COLS, (r + 1) * COLS)
        wide[here, 2 * CH :], wide[here, 0:CH] = neighbours(grad)
        wide[here, CH : 2 * CH] = grad
        full = grad.astype(F32)
        for a in range(3):
            first[a, r + a : r + a + 1] = full[0:1]
            last[a, r + a : r + a + 1] = full[COLS - 1 :]

    is_one = is_odd("core")
    left, right = (part.astype(BF16) for part in sides(even, odd))

    def put(part, a, b):
        if b == 0:
            part += tn(left, first[a].astype(BF16))
        if b == 2:
            part += tn(right, last[a].astype(BF16))
        low, high = part[:, :LANES], part[:, LANES:]
        at = slice((3 * a + b) * CH, (3 * a + b + 1) * CH)
        keep_ref[at] = jnp.where(is_one, high, low).astype(BF16)
        give_ref[at] = jnp.where(is_one, low, high).astype(BF16)

    for r in range(GROUPS[0]):
        build(r)
    start = 0
    for g, count in enumerate(GROUPS):
        here = slice(start * COLS, (start + count) * COLS)
        near = [turned[:, (start + a) * COLS : (start + a + count) * COLS] for a in range(3)]
        near = jnp.concatenate(near, axis=0)
        start += count
        ahead = GROUPS[g + 1] if g + 1 < len(GROUPS) else 0
        for b in range(3):
            part = slice(b * CH, (b + 1) * CH)
            result = nn(near, wide[here, part])
            if g > 0:
                result += total[:, part]
            if ahead:
                total[:, part] = result
            for r in range(ahead * b // 3, ahead * (b + 1) // 3):
                build(start + r)
            if not ahead:
                for a in range(3):
                    put(result[a * CH : (a + 1) * CH], a, b)

    centre = slice(CH, 2 * CH)
    order_rows(wide[0:COLS, centre], wide[(ROWS - 1) * COLS :, centre], even_ref, odd_ref)
    left_ref[...] = first[1].astype(BF16)
    right_ref[...] = last[1].astype(BF16)


def order_rows(first, last, even_ref, odd_ref):
    odd = is_odd("gy")
    even_ref[0] = jnp.where(odd, first, last)
    odd_ref[0] = jnp.where(odd, last, first)


def back_taps(weight, taps):
    return jnp.concatenate([weight[tap] for tap in taps], axis=1)


def input_blocks(wide, weight, first, prods, finish, send):
    for block in range(BLOCKS + 1):
        if block < BLOCKS:
            at = first + STEP * block
            near = [wide[(at + step) * COLS : (at + step + STEP) * COLS] for step in (1, 0, -1)]
            prods[block % 2][...] = nt(jnp.concatenate(near, axis=1), back_taps(weight, range(9)))
        if block > 0:
            at = first + STEP * (block - 1)
            for j in range(STEP):
                finish(at + j, prods[(block - 1) % 2][j * COLS : (j + 1) * COLS])
            send(at, STEP)


def upper_body(wide, spread, weight, out, kept_ref, raw_ref, prod_a, prod_b, done, sems):
    started = []

    def finish(r, prod):
        value = spread[r % 2] + prod
        done[r] = value.astype(BF16)
        raw_ref[0, r : r + 1] = value[0:1]
        raw_ref[1, r : r + 1] = value[COLS - 1 :]
        kept_ref[0, r] = done[r, 0:16]
        kept_ref[1, r] = done[r, COLS - 16 :]

    def send(first, count):
        here = slice(first, first + count)
        started.append(pltpu.make_async_copy(done.at[here], out.at[here], sems.at[len(started)]))
        started[-1].start()

    input_blocks(wide, weight, 1, (prod_a, prod_b), finish, send)
    for one in started:
        one.wait()


def lower_body(
    wide, top, bot, even, odd, spread, weight, kept, raw, _, out, prod_a, prod_b, side32, added, done, fixed, sems
):
    for i, whole in enumerate(sides(even, odd)):
        side32[...] = whole
        near = [side32[2 - a : 2 - a + ROWS].astype(BF16) for a in range(3)]
        taps = back_taps(weight, [3 * a + 2 - 2 * i for a in range(3)])
        added[i] = nt(jnp.concatenate(near, axis=1), taps)
    started = []

    def start(source, target):
        started.append(pltpu.make_async_copy(source, target, sems.at[len(started)]))
        started[-1].start()

    small = iota((16, CH), 0)
    for i in range(2):
        for r in range(1, HALF):
            value = raw[i, r : r + 1] + added[i, r : r + 1]
            fixed[i, r] = jnp.where(small == 15 * i, value, kept[i, r].astype(F32)).astype(BF16)
        at = (COLS - 16) * i
        start(fixed.at[i, 1:HALF], out.at[1:HALF, at : at + 16])

    pix = iota((COLS, CH), 0)

    def finish(r, prod):
        outer = jnp.where(pix == 0, added[0, r : r + 1], 0.0)
        outer = jnp.where(pix == COLS - 1, added[1, r : r + 1], outer)
        at = r - HALF if r >= HALF else HALF
        done[at] = (spread[(r // HALF) * 2 + r % 2] + (prod + outer)).astype(BF16)

    def send(first, count):
        at = first - HALF if first >= HALF else HALF
        start(done.at[at : at + count], out.at[first : first + count])

    input_blocks(wide, weight, HALF, (prod_a, prod_b), finish, send)

    def row(r):
        return wide[r * COLS : (r + 1) * COLS]

    def outside(one):
        left, right = neighbours(one[0])
        return jnp.concatenate([right, one[0], left], axis=1)

    def pair(one, two):
        return jnp.concatenate([one, two], axis=0)

    near = [pair(row(1), outside(bot)), pair(row(0), row(ROWS - 1)), pair(outside(top), row(ROWS - 2))]
    both = nt(jnp.concatenate(near, axis=1), back_taps(weight, range(9)))
    for i, r in enumerate((0, ROWS - 1)):
        finish(r, both[i * COLS : (i + 1) * COLS])
        send(r, 1)
    for one in started:
        one.wait()


def add_up(refs, rows):
    total = refs[0][0:rows].astype(F32)
    for one in refs[1:]:
        total += one[0:rows].astype(F32)
    return total.astype(BF16)


def deal(total_ref, outs, size, axis):
    for k, out in enumerate(reversed(outs)):
        at = lax.bitwise_xor(lax.axis_index(axis), k) * size
        out[0:size] = total_ref[pl.ds(pl.multiple_of(at, 16), size)]


def chip_sum_body(one, two, emb, *refs):
    outs, total_ref = refs[:-1], refs[-1]
    rows = one.shape[0]
    size = rows // len(outs)
    total_ref[...] = add_up((one, two), rows)
    deal(total_ref, outs, size, "gy")
    for out in outs:
        out[size:] = emb[...]


def band_sum_body(*refs, terms, norm_scale):
    outs, emb_ref, total_ref = refs[terms:-2], refs[-2], refs[-1]
    rows = total_ref.shape[0]
    total_ref[...] = add_up(refs[:terms], rows)
    deal(total_ref, outs, rows // len(outs), "gz")
    embs = []
    for one in (refs[0], *refs[terms - 1 : 0 : -1]):
        part = one[rows : rows + 16].astype(F32)
        embs.append(part[0:2] + part[2:4])
    while len(embs) > 1:
        embs = [a + b for a, b in zip(embs[0::2], embs[1::2])]
    emb_ref[:, 0:LANES] = embs[0][0:1] * norm_scale
    emb_ref[:, LANES:] = embs[0][1:2] * norm_scale


def last_sum_body(*refs):
    refs[-1][...] = add_up(refs[:-1], refs[-1].shape[0])


def stack_body(*refs):
    for i, one in enumerate(refs[:-1]):
        refs[-1][i] = one[...]


def half_body(array, *refs, other):
    grad_ref, buf, sems = refs[-3:]
    gy, gz, core = (lax.axis_index(name) for name in ("gy", "gz", "core"))
    bands, depth, share = array.shape[:3]
    half = 1 - core if other else core
    lanes = pl.ds(pl.multiple_of(half * LANES, LANES), LANES)
    started = []
    for k in range(bands):
        first = lax.bitwise_xor(gy, k) * (depth * share)
        for j in range(depth):
            at = first + lax.bitwise_xor(gz, j) * share
            buf[pl.ds(pl.multiple_of(at, 16), share)] = array[k, j].astype(F32) * (1.0 / loss_scale)
        here = pl.ds(pl.multiple_of(first, 16), depth * share)
        started.append(pltpu.make_async_copy(buf.at[here], grad_ref.at[here, lanes], sems.at[k]))
        started[-1].start()
    for one in started:
        one.wait()


SMEM = pl.BlockSpec(memory_space=pltpu.SMEM)
VMEM = pl.BlockSpec(memory_space=pltpu.VMEM)
HBM = pl.BlockSpec(memory_space=pltpu.HBM)


def run(body, args, outs, scratch=(), flops=1 << 20, mib=8, far=(), **rest):
    specs = [HBM if i in far else SMEM if a.dtype == jnp.int32 else VMEM for i, a in enumerate(args)]
    return pl.pallas_call(
        body,
        in_specs=specs,
        out_shape=outs,
        scratch_shapes=list(scratch),
        compiler_params=pltpu.CompilerParams(vmem_limit_bytes=mib << 20),
        cost_estimate=pl.CostEstimate(flops=flops, bytes_accessed=1 << 20, transcendentals=0),
        **rest,
    )(*args)


def per_device(features, tissue, owner_map, w_conv, w_stride, w_query, w_key, w_value, cotangent):
    gy_count, gz_count, cores = lax.axis_size("gy"), lax.axis_size("gz"), lax.axis_size("core")
    gx_count, chips = gz_count * cores, gy_count * gz_count
    across = ("gz", "core")
    norm_scale = 1.0 / math.sqrt(16 * gy_count * gx_count)
    swap = [(i, i ^ 1) for i in range(cores)]

    def pairs(value, axis, count, odd):
        low = range(odd, count - 1, 2)
        return lax.ppermute(value, axis, [(i, i + 1) for i in low] + [(i + 1, i) for i in low])

    def others(values, axis, count):
        got = [
            lax.ppermute(values[k - 1], axis, [(i, i ^ k) for i in range(count)])
            for k in range(count - 1, 0, -1)
        ]
        return got[::-1]

    column = shape((HALO, CH), BF16)
    line = shape((1, COLS, CH), BF16)

    def row_halos(even, odd):
        return pairs(even, "gy", gy_count, 0), pairs(odd, "gy", gy_count, 1)

    def corners(left, right, even, odd):
        return run(corner_body, (left, right, even, odd), [line, line, column, column], mib=1)

    def column_halos(even, odd):
        return pairs(even, across, gx_count, 0), pairs(odd, across, gx_count, 1)

    conv_flops = 2 * ROWS * COLS * 9 * CH * CH
    prod = pltpu.VMEM((STEP * COLS, CH), F32)
    side32 = pltpu.VMEM((HALO, CH), F32)
    half_block = shape((HALF, COLS, CH), BF16)

    def forward(band, weight):
        return run(
            lambda *refs: forward_body(*refs, band=band),
            (tissue, features, weight),
            [half_block, shape((2, COLS, CH), F32), shape((6, HALF, CH), F32)],
            [pltpu.VMEM(((HALF + 1) * COLS, 3 * CH), BF16), prod, prod, pltpu.VMEM((COLS, CH), F32)],
            flops=conv_flops // 2,
            mib=16,
        )

    rows = run(
        rows_body,
        (features,),
        [line, line],
        [pltpu.SemaphoreType.DMA((2,))],
        flops=conv_flops,
        mib=56,
        far=(0,),
    )
    outer = run(columns_body, (features,), [column, column], mib=2)
    even, odd = row_halos(*rows)
    slope_a, sums_a, cols_a = forward(0, w_conv)
    even, odd, cols_a = lax.optimization_barrier((even, odd, cols_a))
    top, bot, even, odd = corners(*outer, even, odd)
    weight_b, even = lax.optimization_barrier((w_conv, even))
    even, odd = column_halos(even, odd)
    slope_b, sums_b, cols_b = forward(1, weight_b)
    pooled, token, edge, side = run(
        border_body,
        (
            tissue, features, w_conv, sums_a, sums_b, cols_a, cols_b, top, bot, even, odd, w_stride,
            owner_map.reshape(16),
        ),
        [
            shape((16, CH), F32),
            shape((16, CH + LANES), BF16),
            shape((2, COLS, CH), BF16),
            shape((2, ROWS, CH), F32),
        ],
        [side32],
        flops=conv_flops // 8,
        mib=12,
    )
    both = run(
        pair_body, (token, lax.ppermute(token, "core", swap)), shape((32, CH + LANES), BF16), mib=1
    )
    pieces = [both] + others([both] * (gz_count - 1), "gz", gz_count)
    turned, high_w, low_w = run(
        turn_body,
        (features, top, bot, w_query, w_key, w_value, token),
        [shape((CH, (ROWS + 2) * COLS), BF16), shape((CH, 3 * CH), BF16), shape((CH, 3 * CH), BF16)],
        flops=conv_flops // 4,
        mib=12,
    )
    count = 16 * gx_count
    spread, emb = run(
        lambda *refs: attention_body(*refs, seed_scale=loss_scale * norm_scale, pieces=gz_count),
        (*pieces, pooled, high_w, low_w, cotangent.reshape(1, CH), w_stride),
        [shape((4, COLS, CH), F32), shape((16, LANES), BF16)],
        [pltpu.VMEM((count, CH + LANES), BF16), pltpu.VMEM((count, 3 * CH), F32)],
        flops=1 << 30,
        mib=12,
    )
    border = pltpu.VMEM((3, HALO, CH), F32)
    wide, keep, give, *outer = run(
        weight_body,
        (spread, slope_a, slope_b, edge, side, turned, even, odd),
        [
            shape((ROWS * COLS, 3 * CH), BF16),
            shape((9 * CH, LANES), BF16),
            shape((9 * CH, LANES), BF16),
            line,
            line,
            column,
            column,
        ],
        [pltpu.VMEM((3 * CH, 3 * CH), F32), border, border],
        flops=conv_flops,
        mib=20,
    )

    share = -(-9 * CH // (16 * chips)) * 16
    spare = share * chips - 9 * CH
    taken = lax.ppermute(give, "core", swap)
    pre_rows = row_halos(*outer[:2])
    if spare:
        keep, taken = (jnp.pad(a, ((0, spare), (0, 0))) for a in (keep, taken))

    def stacked(terms):
        return run(stack_body, terms, shape((len(terms),) + terms[0].shape, BF16), mib=4)

    block = shape((ROWS, COLS, CH), BF16)
    whole_rows = share * chips
    band_rows = share * gz_count
    parts = run(
        chip_sum_body,
        (keep, taken, emb),
        [shape((band_rows + 16, LANES), BF16)] * gy_count,
        [pltpu.VMEM((whole_rows, LANES), BF16)],
        mib=6,
    )[::-1]
    *parts, wide_upper = lax.optimization_barrier((*parts, wide))
    upper, kept, raw = run(
        upper_body,
        (wide_upper, spread, w_conv),
        [block, shape((2, HALF, 16, CH), BF16), shape((2, HALF, CH), F32)],
        [prod, prod, pltpu.VMEM((HALF, COLS, CH), BF16), pltpu.SemaphoreType.DMA((BLOCKS,))],
        flops=conv_flops // 2,
        mib=16,
        out_specs=[HBM, VMEM, VMEM],
    )
    raw, *outer = lax.optimization_barrier((raw, *outer[2:], *pre_rows))
    parts = [parts[0]] + others(parts[1:], "gy", gy_count)[::-1]
    top, bot, even, odd = corners(*outer)
    even, odd = column_halos(even, odd)
    *parts, raw, even, odd = lax.optimization_barrier((*parts, raw, even, odd))
    embedding, *parts = run(
        lambda *refs: band_sum_body(*refs, terms=gy_count, norm_scale=norm_scale),
        parts,
        [shape((share, LANES), BF16)] * gz_count + [shape((1, CH), F32)],
        [pltpu.VMEM((band_rows, LANES), BF16)],
        mib=4,
    )[::-1]
    parts = [parts[0]] + others(parts[1:], "gz", gz_count)[::-1]
    mine = run(last_sum_body, parts, shape((share, LANES), BF16), mib=2)
    row = stacked([mine] + others([mine] * (gz_count - 1), "gz", gz_count))
    row, wide_lower = lax.optimization_barrier((row, wide))
    input_grad = run(
        lower_body,
        (wide_lower, top, bot, even, odd, spread, w_conv, kept, raw, upper),
        block,
        [
            prod,
            prod,
            side32,
            pltpu.VMEM((2, ROWS, CH), F32),
            pltpu.VMEM((HALF + 1, COLS, CH), BF16),
            pltpu.VMEM((2, HALF, 16, CH), BF16),
            pltpu.SemaphoreType.DMA((BLOCKS + 4,)),
        ],
        flops=conv_flops // 2,
        mib=16,
        far=(9,),
        out_specs=HBM,
        input_output_aliases={9: 0},
    )
    planes = [row] + others([row] * (gy_count - 1), "gy", gy_count)
    *planes, input_grad = lax.optimization_barrier((*planes, input_grad))
    plane = stacked(planes)
    other = lax.ppermute(plane, "core", swap)
    whole = shape((whole_rows, CH), F32)
    buffers = [pltpu.VMEM((whole_rows, LANES), F32), pltpu.SemaphoreType.DMA((gy_count,))]
    half_grad = run(
        lambda *refs: half_body(*refs, other=False), (plane,), whole, buffers, mib=4, out_specs=HBM
    )
    conv_grad = run(
        lambda *refs: half_body(*refs, other=True),
        (other, half_grad),
        whole,
        buffers,
        mib=4,
        far=(1,),
        out_specs=HBM,
        input_output_aliases={1: 0},
    )
    return embedding.reshape(CH), input_grad, conv_grad[: 9 * CH].reshape(9, CH, CH)


def solution(mesh):
    sizes = mesh.devices.shape
    split = Mesh(mesh.devices.reshape(sizes[0], sizes[1] // 2, 2), ("gy", "gz", "core"))
    gx = ("gz", "core")
    in_specs = (P("gy", gx, None), P("gy", gx), P("gy", gx, None, None), P(), P(), P(), P(), P(), P())
    out_specs = (P(), P("gy", gx, None), P())
    return jax.shard_map(per_device, mesh=split, in_specs=in_specs, out_specs=out_specs, check_vma=False)
```

```python
import math

import jax
import jax.numpy as jnp
from jax import lax
from jax.experimental import pallas as pl
from jax.experimental.pallas import tpu as pltpu
from jax.sharding import Mesh, PartitionSpec as P

HEADS = 4
F32 = jnp.float32
BF16 = jnp.bfloat16

attention_bias = -1.0
loss_scale = 512.0

ROWS = 32
COLS = 128
CH = 256
HALO = 48
LANES = 128
STEP = 5
TILE_CELLS = 64


def shape(dims, dtype):
    return jax.ShapeDtypeStruct(dims, dtype)


def nt(left, right):
    return lax.dot_general(left, right, (((1,), (1,)), ((), ())), preferred_element_type=F32)


def tn(left, right):
    return lax.dot_general(left, right, (((0,), (0,)), ((), ())), preferred_element_type=F32)


def nn(left, right):
    return jnp.dot(left, right, preferred_element_type=F32)


def halves(value):
    high = value.astype(BF16)
    return high, (value - high.astype(F32)).astype(BF16)


def wide_product(product, left, right):
    (a, b), (c, d) = left, right
    return product(a, c) + (product(a, d) + product(b, c))


def iota(dims, axis):
    return lax.broadcasted_iota(jnp.int32, dims, axis)


def gate_of(value):
    return 0.5 * jnp.tanh(0.5 * value) + 0.5


def copies(pairs, sems):
    started = [pltpu.make_async_copy(a, b, sems.at[i]) for i, (a, b) in enumerate(pairs)]
    for one in started:
        one.start()
    return started


def is_odd(axis):
    return lax.axis_index(axis) % 2 == 1


def rows_body(block, even_ref, odd_ref, sems):
    odd = is_odd("gy")
    first, last = jnp.where(odd, 0, ROWS - 1), jnp.where(odd, ROWS - 1, 0)
    started = copies([(block.at[pl.ds(first, 1)], even_ref), (block.at[pl.ds(last, 1)], odd_ref)], sems)
    for one in started:
        one.wait()


def columns_body(block, left_ref, right_ref):
    row, spot = iota((HALO, ROWS * 16), 0), iota((HALO, ROWS * 16), 1)
    for out, at, place in ((left_ref, 0, 0), (right_ref, COLS - 16, 15)):
        pick = (spot == (row - 1) * 16 + place).astype(F32).astype(BF16)
        out[...] = nn(pick, block[:, at : at + 16].reshape(ROWS * 16, CH)).astype(BF16)


def corner_body(left, right, even, odd, top_ref, bot_ref, even_ref, odd_ref):
    low = is_odd("gy")
    top_ref[0] = jnp.where(low, even[0], odd[0])
    bot_ref[0] = jnp.where(low, odd[0], even[0])
    row = iota((HALO, CH), 0)
    whole = []
    for side, at in ((left, 0), (right, COLS - 16)):
        part = slice(0, 1) if at == 0 else slice(15, 16)
        above = top_ref[0, at : at + 16].astype(F32)[part]
        below = bot_ref[0, at : at + 16].astype(F32)[part]
        whole.append(jnp.where(row == 0, above, jnp.where(row == ROWS + 1, below, side[...].astype(F32))))
    high = is_odd("core")
    even_ref[...] = jnp.where(high, whole[0], whole[1]).astype(BF16)
    odd_ref[...] = jnp.where(high, whole[1], whole[0]).astype(BF16)


def sides(even, odd):
    high = is_odd("core")
    one, two = even[...].astype(F32), odd[...].astype(F32)
    return jnp.where(high, one, two), jnp.where(high, two, one)


def forward_taps(weight, b):
    return jnp.concatenate([weight[3 * a + b] for a in range(3)], axis=0)


HALF = ROWS // 2
BLOCKS = (HALF - 1) // STEP
PARTS = ((3, 5, 5, 2), (2, 2, 2, 2, 2, 2, 2, 1))


def with_first(wide, value):
    start = jnp.where(iota((8, CH), 0) == 0, value, wide[0:8])
    return jnp.concatenate([start, wide[8:]], axis=0)


def with_last(wide, value):
    end = jnp.where(iota((8, CH), 0) == 7, value, wide[COLS - 8 :])
    return jnp.concatenate([wide[: COLS - 8], end], axis=0)


def neighbours(row):
    wide = row.astype(F32)
    left = with_first(pltpu.roll(wide, 1, 0), 0.0)
    right = with_last(pltpu.roll(wide, COLS - 1, 0), 0.0)
    return left.astype(BF16), right.astype(BF16)


def silu_pair(value, half_mask):
    half = 0.5 * value
    bend = jnp.tanh(half)
    kept = (1.0 + bend) * half_mask
    return value * kept, kept * (1.0 + half * (1.0 - bend))


def forward_body(flags_ref, feat, weight, slope_ref, sums, cols, wide, prod_a, prod_b, mask, *, band):
    for tile in range(8):
        mask[16 * tile : 16 * tile + 16] = 0.5 * jnp.full((16, CH), flags_ref[band, tile], jnp.int32).astype(F32)
    sums[...] = jnp.zeros_like(sums)
    taps = weight[...].reshape(9 * CH, CH)
    base = (HALF - 1) * band

    def build(i):
        here = slice(i * COLS, (i + 1) * COLS)
        row = feat[base + i]
        wide[here, 0:CH], wide[here, 2 * CH :] = neighbours(row)
        wide[here, CH : 2 * CH] = row

    def finish(r, value):
        at = r - HALF * band
        pixel = feat[r].astype(F32)
        bent, slope = silu_pair(value, mask[...])
        summed = pixel + bent
        slope_ref[at] = slope.astype(BF16)
        sums[r % 2] += summed
        for i, part in enumerate((value, summed, pixel)):
            cols[2 * i, at : at + 1] = part[0:1]
            cols[2 * i + 1, at : at + 1] = part[COLS - 1 :]

    prods = (prod_a, prod_b)
    parts = PARTS[band]
    built, done = parts[0] + 2, 0
    for i in range(built):
        build(i)
    for block in range(len(parts) + 1):
        start = sum(parts[:block])
        if block < len(parts):
            count = parts[block]
            near = [slice((start + a) * COLS, (start + count + a) * COLS) for a in range(3)]
            near = jnp.concatenate([wide[part] for part in near], axis=1)
            prods[block % 2][0 : count * COLS] = nn(near, taps)
        ahead = min(HALF + 1, sum(parts[: block + 2]) + 2)
        for j in range(STEP):
            if done < start:
                at = (done - sum(parts[: block - 1])) * COLS
                finish(base + 1 + done, prods[(block - 1) % 2][at : at + COLS])
                done += 1
            if built < ahead:
                build(built)
                built += 1


def border_body(
    flags_ref, feat, weight, sums_a, sums_b, cols_a, cols_b, top, bot, even, odd, strided, owner_ref,
    pooled_ref, token_ref, edge_ref, side_ref, side32,
):
    added = []
    cols = [jnp.concatenate([cols_a[i], cols_b[i]], axis=0) for i in range(6)]
    for i, whole in enumerate(sides(even, odd)):
        side32[...] = whole
        near = [side32[a : a + ROWS].astype(BF16) for a in range(3)]
        added.append(nn(jnp.concatenate(near, axis=1), forward_taps(weight, 2 * i)))

    def pair(one, two):
        return jnp.concatenate([one, two], axis=0)

    taken = jnp.concatenate(
        [pair(top[0], feat[ROWS - 2]), pair(feat[0], feat[ROWS - 1]), pair(feat[1], bot[0])], axis=1
    )
    low, mid, high = (nn(taken, forward_taps(weight, b)) for b in range(3))
    rows = []
    for i, r in enumerate((0, ROWS - 1)):
        part = slice(i * COLS, (i + 1) * COLS)
        before = with_first(pltpu.roll(low[part], 1, 0), added[0][r : r + 1])
        after = with_last(pltpu.roll(high[part], COLS - 1, 0), added[1][r : r + 1])
        value = mid[part] + before + after
        keep = jnp.concatenate(
            [0.5 * jnp.full((16, CH), flags_ref[i, t], jnp.int32).astype(F32) for t in range(8)], axis=0
        )
        bent, slope = silu_pair(value, keep)
        edge_ref[i] = slope.astype(BF16)
        rows.append(feat[r].astype(F32) + bent)

    line = iota((ROWS, CH), 0)
    deltas = []
    for i in range(2):
        tile = 7 * i
        keep = 0.5 * jnp.where(line < ROWS // 2, flags_ref[0, tile], flags_ref[1, tile]).astype(F32)
        bent, side_ref[i] = silu_pair(cols[i] + added[i], keep)
        inside = (line > 0) & (line < ROWS - 1)
        deltas.append(jnp.where(inside, cols[4 + i] + bent - cols[2 + i], 0.0))

    row, spot = iota((16, COLS), 0), iota((16, COLS), 1)
    pick = ((spot // 16 == row % 8) & (spot % 2 == row // 8)).astype(F32).astype(BF16)
    place = iota((16, CH), 0)
    parts = {}
    for band in range(2):
        for a in range(2):
            total = (sums_a, sums_b)[band][a]
            if band == a:
                total += rows[band]
            high, low = halves(total)
            part = nn(pick, high) + nn(pick, low)
            mine = (line // 16 == band) & (line % 2 == a)
            for i in range(2):
                delta = jnp.sum(jnp.where(mine, deltas[i], 0.0), axis=0, keepdims=True)
                part += jnp.where(place == 15 * i, delta, 0.0)
            parts[band, a] = part
    taken = [
        jnp.concatenate([parts[band, a][8 * b : 8 * b + 8] for band in range(2)], axis=0)
        for a in range(2)
        for b in range(2)
    ]
    high, low = halves(jnp.concatenate(taken, axis=1))
    flat = strided[...].reshape(4 * CH, CH)
    pooled = (nn(high, flat) + nn(low, flat)) * (1.0 / TILE_CELLS)
    pooled_ref[...] = pooled
    normed = pooled * lax.rsqrt(jnp.mean(pooled * pooled, axis=-1, keepdims=True) + 1e-05)
    token_ref[:, 0:CH] = normed.astype(BF16)
    owner = jnp.full((16, LANES), -1, jnp.int32)
    for tile in range(16):
        named = jnp.where(flags_ref[tile // 8, tile % 8] != 0, owner_ref[tile], -1)
        owner = jnp.where(iota((16, LANES), 0) == tile, named, owner)
    token_ref[:, CH:] = (owner == iota((16, LANES), 1)).astype(F32).astype(BF16)


def turn_body(feat, top, bot, w_query, w_key, w_value, token, turned_ref, high_ref, low_ref):
    turned_ref[:, 0:COLS] = top[0].T
    turned_ref[:, (ROWS + 1) * COLS :] = bot[0].T

    @pl.loop(0, ROWS // 4)
    def _(i):
        for j in range(4):
            here = pl.multiple_of((4 * i + j + 1) * COLS, COLS)
            turned_ref[:, pl.ds(here, COLS)] = feat[4 * i + j].T

    for i, one in enumerate((w_query, w_key, w_value)):
        high, low = halves(one[...])
        high_ref[:, i * CH : (i + 1) * CH] = high
        low_ref[:, i * CH : (i + 1) * CH] = low


def pair_body(one, two, out_ref):
    out_ref[0:16] = one[...]
    out_ref[16:32] = two[...]


def attention_body(*refs, seed_scale, pieces):
    got = refs[:pieces]
    pooled_ref, high_w, low_w, cot, strided, spread_ref, emb_ref, band, grad_ref = refs[pieces:]
    gz, core = lax.axis_index("gz"), lax.axis_index("core")

    def rows_of(depth, other):
        return pl.ds(pl.multiple_of(depth * 32 + other * 16, 16), 16)

    for k, piece in enumerate(got):
        depth = lax.bitwise_xor(gz, k)
        band[rows_of(depth, core)] = piece[0:16]
        band[rows_of(depth, 1 - core)] = piece[16:32]
    count = band.shape[0]
    tokens, group = band[:, 0:CH], band[:, CH:]
    pair = nt(group, group)
    pairs = jnp.concatenate([pair] * HEADS, axis=0)
    projected = nn(tokens, high_w[...]) + nn(tokens, low_w[...])
    query, key, value = (projected[:, i * CH : (i + 1) * CH] for i in range(3))
    lane = iota((1, CH), 1) // (CH // HEADS)
    scale = 1.0 / math.sqrt(CH // HEADS)

    def by_head(array):
        return jnp.concatenate([jnp.where(lane == h, array, 0.0) for h in range(HEADS)], axis=0)

    queries, keys = halves(by_head(query)), halves(by_head(key))
    gate = gate_of(wide_product(nt, queries, halves(key)) * scale + attention_bias)
    weights = gate * pairs
    seed = cot[...] * seed_scale
    seeds = jnp.where(lane == iota((8, CH), 0), seed, 0.0)
    values = halves(value)
    along = wide_product(nt, halves(seeds), values)
    columns, grads = [], []
    for h in range(HEADS):
        part = slice(h * count, (h + 1) * count)
        columns.append(jnp.sum(weights[part], axis=0, keepdims=True))
        grads.append(weights[part] * (1.0 - gate[part]) * (along[h : h + 1] * scale))
    columns = halves(jnp.concatenate(columns + [jnp.zeros((8 - HEADS, count), F32)], axis=0))
    grad_ref[:, 0:CH] = wide_product(nn, halves(jnp.concatenate(grads, axis=1)), keys)
    grad_ref[:, CH : 2 * CH] = wide_product(tn, halves(jnp.concatenate(grads, axis=0)), queries)
    grad_ref[:, 2 * CH :] = wide_product(tn, columns, halves(seeds))
    mixed = wide_product(nn, columns, values)
    mixed = jnp.sum(jnp.where(lane == iota((8, CH), 0), mixed, 0.0), axis=0, keepdims=True)
    high = mixed.astype(BF16).astype(F32)
    low = mixed - high
    rows = iota((16, LANES), 0)
    packed = jnp.zeros((16, LANES), F32)
    for i, part in enumerate((high[:, :LANES], high[:, LANES:], low[:, :LANES], low[:, LANES:])):
        packed = jnp.where(rows == i, part, packed)
    emb_ref[...] = packed.astype(BF16)

    grads = halves(grad_ref[rows_of(gz, core)])
    grad = wide_product(nt, grads, (high_w[...], low_w[...]))
    grad = grad.astype(BF16).astype(F32)
    pooled = pooled_ref[...]
    inv = lax.rsqrt(jnp.mean(pooled * pooled, axis=-1, keepdims=True) + 1e-05)
    unit = pooled * inv
    back = inv * (grad - unit * jnp.mean(grad * unit, axis=-1, keepdims=True))
    cell = (back * (1.0 / TILE_CELLS)).astype(BF16)
    spot, row = iota((COLS, 16), 0), iota((COLS, 16), 1)
    expand = ((spot // 16 == row % 8) & (spot % 2 == row // 8)).astype(F32).astype(BF16)
    taps = nt(cell, strided[...].reshape(4 * CH, CH))
    for band in range(2):
        here = taps[8 * band : 8 * band + 8]
        both = [
            jnp.concatenate([here[:, (2 * a + b) * CH : (2 * a + b + 1) * CH] for a in range(2)], axis=1)
            for b in range(2)
        ]
        high, low = halves(jnp.concatenate(both, axis=0))
        spread = nn(expand, high) + nn(expand, low)
        for a in range(2):
            spread_ref[band * 2 + a] = spread[:, a * CH : (a + 1) * CH]


GROUPS = (6, 10, 16)


def weight_body(
    spread, slope_a, slope_b, edge, side, turned, even, odd,
    wide, keep_ref, give_ref, even_ref, odd_ref, left_ref, right_ref, total, first, last,
):
    first[...] = jnp.zeros_like(first)
    last[...] = jnp.zeros_like(last)

    def build(r):
        if r in (0, ROWS - 1):
            slope = edge[r // HALF].astype(F32)
        else:
            slope = (slope_a, slope_b)[r // HALF][r % HALF].astype(F32)
            slope = with_last(with_first(slope, side[0, r : r + 1]), side[1, r : r + 1])
        grad = (spread[(r // HALF) * 2 + r % 2] * slope).astype(BF16)
        here = slice(r * COLS, (r + 1) * COLS)
        wide[here, 2 * CH :], wide[here, 0:CH] = neighbours(grad)
        wide[here, CH : 2 * CH] = grad
        full = grad.astype(F32)
        for a in range(3):
            first[a, r + a : r + a + 1] = full[0:1]
            last[a, r + a : r + a + 1] = full[COLS - 1 :]

    is_one = is_odd("core")
    left, right = (part.astype(BF16) for part in sides(even, odd))

    def put(part, a, b):
        if b == 0:
            part += tn(left, first[a].astype(BF16))
        if b == 2:
            part += tn(right, last[a].astype(BF16))
        low, high = part[:, :LANES], part[:, LANES:]
        at = slice((3 * a + b) * CH, (3 * a + b + 1) * CH)
        keep_ref[at] = jnp.where(is_one, high, low).astype(BF16)
        give_ref[at] = jnp.where(is_one, low, high).astype(BF16)

    for r in range(GROUPS[0]):
        build(r)
    start = 0
    for g, count in enumerate(GROUPS):
        here = slice(start * COLS, (start + count) * COLS)
        near = [turned[:, (start + a) * COLS : (start + a + count) * COLS] for a in range(3)]
        near = jnp.concatenate(near, axis=0)
        start += count
        ahead = GROUPS[g + 1] if g + 1 < len(GROUPS) else 0
        for b in range(3):
            part = slice(b * CH, (b + 1) * CH)
            result = nn(near, wide[here, part])
            if g > 0:
                result += total[:, part]
            if ahead:
                total[:, part] = result
            for r in range(ahead * b // 3, ahead * (b + 1) // 3):
                build(start + r)
            if not ahead:
                for a in range(3):
                    put(result[a * CH : (a + 1) * CH], a, b)

    centre = slice(CH, 2 * CH)
    order_rows(wide[0:COLS, centre], wide[(ROWS - 1) * COLS :, centre], even_ref, odd_ref)
    left_ref[...] = first[1].astype(BF16)
    right_ref[...] = last[1].astype(BF16)


def order_rows(first, last, even_ref, odd_ref):
    odd = is_odd("gy")
    even_ref[0] = jnp.where(odd, first, last)
    odd_ref[0] = jnp.where(odd, last, first)


def back_taps(weight, taps):
    return jnp.concatenate([weight[tap] for tap in taps], axis=1)


def input_blocks(wide, weight, first, blocks, prods, finish, send=None):
    for block in range(blocks + 1):
        if block < blocks:
            at = first + STEP * block
            near = [wide[(at + step) * COLS : (at + step + STEP) * COLS] for step in (1, 0, -1)]
            prods[block % 2][...] = nt(jnp.concatenate(near, axis=1), back_taps(weight, range(9)))
        if block > 0:
            at = first + STEP * (block - 1)
            for j in range(STEP):
                finish(at + j, prods[(block - 1) % 2][j * COLS : (j + 1) * COLS])
            if send is not None:
                send(at, STEP)


UPPER = 2 * STEP


def upper_body(wide, spread, weight, done, raw_ref, prod_a, prod_b):
    def finish(r, prod):
        value = spread[r % 2] + prod
        done[r - 1] = value.astype(BF16)
        raw_ref[0, r : r + 1] = value[0:1]
        raw_ref[1, r : r + 1] = value[COLS - 1 :]

    input_blocks(wide, weight, 1, UPPER // STEP, (prod_a, prod_b), finish)


def lower_body(
    wide, top, bot, even, odd, spread, weight, upper, raw, out, prod_a, prod_b, side32, added, done, fixed, sems
):
    started = []

    def start(source, target):
        started.append(pltpu.make_async_copy(source, target, sems.at[len(started)]))
        started[-1].start()

    start(upper.at[:, 16 : COLS - 16], out.at[1 : UPPER + 1, 16 : COLS - 16])
    for i, whole in enumerate(sides(even, odd)):
        side32[...] = whole
        near = [side32[2 - a : 2 - a + ROWS].astype(BF16) for a in range(3)]
        taps = back_taps(weight, [3 * a + 2 - 2 * i for a in range(3)])
        added[i] = nt(jnp.concatenate(near, axis=1), taps)

    small = iota((16, CH), 0)
    for i in range(2):
        at = (COLS - 16) * i
        for r in range(1, UPPER + 1):
            value = raw[i, r : r + 1] + added[i, r : r + 1]
            old = upper[r - 1, at : at + 16].astype(F32)
            fixed[i, r - 1] = jnp.where(small == 15 * i, value, old).astype(BF16)
        start(fixed.at[i], out.at[1 : UPPER + 1, at : at + 16])

    def place(r):
        return r - UPPER if r else 0

    def finish(r, prod):
        prod = with_first(prod, prod[0:1] + added[0, r : r + 1])
        prod = with_last(prod, prod[COLS - 1 :] + added[1, r : r + 1])
        done[place(r)] = (spread[(r // HALF) * 2 + r % 2] + prod).astype(BF16)

    def send(first, count):
        start(done.at[place(first) : place(first) + count], out.at[first : first + count])

    input_blocks(wide, weight, UPPER + 1, (ROWS - 2 - UPPER) // STEP, (prod_a, prod_b), finish, send)

    def row(r):
        return wide[r * COLS : (r + 1) * COLS]

    def outside(one):
        left, right = neighbours(one[0])
        return jnp.concatenate([right, one[0], left], axis=1)

    def pair(one, two):
        return jnp.concatenate([one, two], axis=0)

    near = [pair(row(1), outside(bot)), pair(row(0), row(ROWS - 1)), pair(outside(top), row(ROWS - 2))]
    both = nt(jnp.concatenate(near, axis=1), back_taps(weight, range(9)))
    for i, r in enumerate((0, ROWS - 1)):
        finish(r, both[i * COLS : (i + 1) * COLS])
        send(r, 1)
    for one in started:
        one.wait()


def add_up(refs, rows):
    total = refs[0][0:rows].astype(F32)
    for one in refs[1:]:
        total += one[0:rows].astype(F32)
    return total.astype(BF16)


def deal(total_ref, outs, size, axis):
    for k, out in enumerate(reversed(outs)):
        at = lax.bitwise_xor(lax.axis_index(axis), k) * size
        out[0:size] = total_ref[pl.ds(pl.multiple_of(at, 16), size)]


def chip_sum_body(one, two, emb, *refs):
    outs, total_ref = refs[:-1], refs[-1]
    rows = one.shape[0]
    size = rows // len(outs)
    total_ref[...] = add_up((one, two), rows)
    deal(total_ref, outs, size, "gy")
    for out in outs:
        out[size:] = emb[...]


def band_sum_body(*refs, terms, norm_scale):
    outs, emb_ref, total_ref = refs[terms:-2], refs[-2], refs[-1]
    rows = total_ref.shape[0]
    total_ref[...] = add_up(refs[:terms], rows)
    deal(total_ref, outs, rows // len(outs), "gz")
    embs = []
    for one in (refs[0], *refs[terms - 1 : 0 : -1]):
        part = one[rows : rows + 16].astype(F32)
        embs.append(part[0:2] + part[2:4])
    while len(embs) > 1:
        embs = [a + b for a, b in zip(embs[0::2], embs[1::2])]
    emb_ref[:, 0:LANES] = embs[0][0:1] * norm_scale
    emb_ref[:, LANES:] = embs[0][1:2] * norm_scale


def last_sum_body(*refs):
    refs[-1][...] = add_up(refs[:-1], refs[-1].shape[0])


def stack_body(*refs):
    for i, one in enumerate(refs[:-1]):
        refs[-1][i] = one[...]


def half_body(array, *refs, other):
    grad_ref, buf, sems = refs[-3:]
    gy, gz, core = (lax.axis_index(name) for name in ("gy", "gz", "core"))
    bands, depth, share = array.shape[:3]
    half = 1 - core if other else core
    lanes = pl.ds(pl.multiple_of(half * LANES, LANES), LANES)
    started = []
    for k in range(bands):
        first = lax.bitwise_xor(gy, k) * (depth * share)
        for j in range(depth):
            at = first + lax.bitwise_xor(gz, j) * share
            buf[pl.ds(pl.multiple_of(at, 16), share)] = array[k, j].astype(F32) * (1.0 / loss_scale)
        here = pl.ds(pl.multiple_of(first, 16), depth * share)
        started.append(pltpu.make_async_copy(buf.at[here], grad_ref.at[here, lanes], sems.at[k]))
        started[-1].start()
    for one in started:
        one.wait()


SMEM = pl.BlockSpec(memory_space=pltpu.SMEM)
VMEM = pl.BlockSpec(memory_space=pltpu.VMEM)
HBM = pl.BlockSpec(memory_space=pltpu.HBM)


def run(body, args, outs, scratch=(), flops=1 << 20, mib=8, far=(), **rest):
    specs = [HBM if i in far else SMEM if a.dtype == jnp.int32 else VMEM for i, a in enumerate(args)]
    return pl.pallas_call(
        body,
        in_specs=specs,
        out_shape=outs,
        scratch_shapes=list(scratch),
        compiler_params=pltpu.CompilerParams(vmem_limit_bytes=mib << 20),
        cost_estimate=pl.CostEstimate(flops=flops, bytes_accessed=1 << 20, transcendentals=0),
        **rest,
    )(*args)


def per_device(features, tissue, owner_map, w_conv, w_stride, w_query, w_key, w_value, cotangent):
    gy_count, gz_count, cores = lax.axis_size("gy"), lax.axis_size("gz"), lax.axis_size("core")
    gx_count, chips = gz_count * cores, gy_count * gz_count
    across = ("gz", "core")
    norm_scale = 1.0 / math.sqrt(16 * gy_count * gx_count)
    swap = [(i, i ^ 1) for i in range(cores)]

    def pairs(value, axis, count, odd):
        low = range(odd, count - 1, 2)
        return lax.ppermute(value, axis, [(i, i + 1) for i in low] + [(i + 1, i) for i in low])

    def others(values, axis, count):
        got = [
            lax.ppermute(values[k - 1], axis, [(i, i ^ k) for i in range(count)])
            for k in range(count - 1, 0, -1)
        ]
        return got[::-1]

    column = shape((HALO, CH), BF16)
    line = shape((1, COLS, CH), BF16)

    def row_halos(even, odd):
        return pairs(even, "gy", gy_count, 0), pairs(odd, "gy", gy_count, 1)

    def corners(left, right, even, odd):
        return run(corner_body, (left, right, even, odd), [line, line, column, column], mib=1)

    def column_halos(even, odd):
        return pairs(even, across, gx_count, 0), pairs(odd, across, gx_count, 1)

    conv_flops = 2 * ROWS * COLS * 9 * CH * CH
    prod = pltpu.VMEM((STEP * COLS, CH), F32)
    side32 = pltpu.VMEM((HALO, CH), F32)
    half_block = shape((HALF, COLS, CH), BF16)

    def forward(band, weight):
        return run(
            lambda *refs: forward_body(*refs, band=band),
            (tissue, features, weight),
            [half_block, shape((2, COLS, CH), F32), shape((6, HALF, CH), F32)],
            [pltpu.VMEM(((HALF + 1) * COLS, 3 * CH), BF16), prod, prod, pltpu.VMEM((COLS, CH), F32)],
            flops=conv_flops // 2,
            mib=16,
        )

    rows = run(
        rows_body,
        (features,),
        [line, line],
        [pltpu.SemaphoreType.DMA((2,))],
        flops=conv_flops,
        mib=56,
        far=(0,),
    )
    outer = run(columns_body, (features,), [column, column], mib=2)
    even, odd = row_halos(*rows)
    slope_a, sums_a, cols_a = forward(0, w_conv)
    even, odd, cols_a = lax.optimization_barrier((even, odd, cols_a))
    top, bot, even, odd = corners(*outer, even, odd)
    weight_b, even = lax.optimization_barrier((w_conv, even))
    even, odd = column_halos(even, odd)
    slope_b, sums_b, cols_b = forward(1, weight_b)
    pooled, token, edge, side = run(
        border_body,
        (
            tissue, features, w_conv, sums_a, sums_b, cols_a, cols_b, top, bot, even, odd, w_stride,
            owner_map.reshape(16),
        ),
        [
            shape((16, CH), F32),
            shape((16, CH + LANES), BF16),
            shape((2, COLS, CH), BF16),
            shape((2, ROWS, CH), F32),
        ],
        [side32],
        flops=conv_flops // 8,
        mib=12,
    )
    both = run(
        pair_body, (token, lax.ppermute(token, "core", swap)), shape((32, CH + LANES), BF16), mib=1
    )
    pieces = [both] + others([both] * (gz_count - 1), "gz", gz_count)
    turned, high_w, low_w = run(
        turn_body,
        (features, top, bot, w_query, w_key, w_value, token),
        [shape((CH, (ROWS + 2) * COLS), BF16), shape((CH, 3 * CH), BF16), shape((CH, 3 * CH), BF16)],
        flops=conv_flops // 4,
        mib=12,
    )
    count = 16 * gx_count
    spread, emb = run(
        lambda *refs: attention_body(*refs, seed_scale=loss_scale * norm_scale, pieces=gz_count),
        (*pieces, pooled, high_w, low_w, cotangent.reshape(1, CH), w_stride),
        [shape((4, COLS, CH), F32), shape((16, LANES), BF16)],
        [pltpu.VMEM((count, CH + LANES), BF16), pltpu.VMEM((count, 3 * CH), F32)],
        flops=1 << 30,
        mib=12,
    )
    border = pltpu.VMEM((3, HALO, CH), F32)
    wide, keep, give, *outer = run(
        weight_body,
        (spread, slope_a, slope_b, edge, side, turned, even, odd),
        [
            shape((ROWS * COLS, 3 * CH), BF16),
            shape((9 * CH, LANES), BF16),
            shape((9 * CH, LANES), BF16),
            line,
            line,
            column,
            column,
        ],
        [pltpu.VMEM((3 * CH, 3 * CH), F32), border, border],
        flops=conv_flops,
        mib=20,
    )

    share = -(-9 * CH // (16 * chips)) * 16
    spare = share * chips - 9 * CH
    taken = lax.ppermute(give, "core", swap)
    pre_rows = row_halos(*outer[:2])
    if spare:
        keep, taken = (jnp.pad(a, ((0, spare), (0, 0))) for a in (keep, taken))

    def stacked(terms):
        return run(stack_body, terms, shape((len(terms),) + terms[0].shape, BF16), mib=4)

    whole_rows = share * chips
    band_rows = share * gz_count
    parts = run(
        chip_sum_body,
        (keep, taken, emb),
        [shape((band_rows + 16, LANES), BF16)] * gy_count,
        [pltpu.VMEM((whole_rows, LANES), BF16)],
        mib=6,
    )[::-1]
    *parts, wide_upper = lax.optimization_barrier((*parts, wide))
    upper, raw = run(
        upper_body,
        (wide_upper, spread, w_conv),
        [shape((UPPER, COLS, CH), BF16), shape((2, HALF, CH), F32)],
        [prod, prod],
        flops=conv_flops // 3,
        mib=12,
    )
    raw, *outer = lax.optimization_barrier((raw, *outer[2:], *pre_rows))
    parts = [parts[0]] + others(parts[1:], "gy", gy_count)[::-1]
    top, bot, even, odd = corners(*outer)
    even, odd = column_halos(even, odd)
    *parts, raw, even, odd = lax.optimization_barrier((*parts, raw, even, odd))
    embedding, *parts = run(
        lambda *refs: band_sum_body(*refs, terms=gy_count, norm_scale=norm_scale),
        parts,
        [shape((share, LANES), BF16)] * gz_count + [shape((1, CH), F32)],
        [pltpu.VMEM((band_rows, LANES), BF16)],
        mib=4,
    )[::-1]
    parts = [parts[0]] + others(parts[1:], "gz", gz_count)[::-1]
    mine = run(last_sum_body, parts, shape((share, LANES), BF16), mib=2)
    row = stacked([mine] + others([mine] * (gz_count - 1), "gz", gz_count))
    row, wide_lower = lax.optimization_barrier((row, wide))
    input_grad = run(
        lower_body,
        (wide_lower, top, bot, even, odd, spread, w_conv, upper, raw),
        shape((ROWS, COLS, CH), BF16),
        [
            prod,
            prod,
            side32,
            pltpu.VMEM((2, ROWS, CH), F32),
            pltpu.VMEM((ROWS - UPPER, COLS, CH), BF16),
            pltpu.VMEM((2, UPPER, 16, CH), BF16),
            pltpu.SemaphoreType.DMA((BLOCKS + 6,)),
        ],
        flops=conv_flops // 2,
        mib=16,
        out_specs=HBM,
    )
    planes = [row] + others([row] * (gy_count - 1), "gy", gy_count)
    *planes, input_grad = lax.optimization_barrier((*planes, input_grad))
    plane = stacked(planes)
    other = lax.ppermute(plane, "core", swap)
    whole = shape((whole_rows, CH), F32)
    buffers = [pltpu.VMEM((whole_rows, LANES), F32), pltpu.SemaphoreType.DMA((gy_count,))]
    half_grad = run(
        lambda *refs: half_body(*refs, other=False), (plane,), whole, buffers, mib=4, out_specs=HBM
    )
    conv_grad = run(
        lambda *refs: half_body(*refs, other=True),
        (other, half_grad),
        whole,
        buffers,
        mib=4,
        far=(1,),
        out_specs=HBM,
        input_output_aliases={1: 0},
    )
    return embedding.reshape(CH), input_grad, conv_grad[: 9 * CH].reshape(9, CH, CH)


def solution(mesh):
    sizes = mesh.devices.shape
    split = Mesh(mesh.devices.reshape(sizes[0], sizes[1] // 2, 2), ("gy", "gz", "core"))
    gx = ("gz", "core")
    in_specs = (P("gy", gx, None), P("gy", gx), P("gy", gx, None, None), P(), P(), P(), P(), P(), P())
    out_specs = (P(), P("gy", gx, None), P())
    return jax.shard_map(per_device, mesh=split, in_specs=in_specs, out_specs=out_specs, check_vma=False)
```

```python
import math

import jax
import jax.numpy as jnp
from jax import lax
from jax.experimental import pallas as pl
from jax.experimental.pallas import tpu as pltpu
from jax.sharding import Mesh, PartitionSpec as P

HEADS = 4
F32 = jnp.float32
BF16 = jnp.bfloat16

attention_bias = -1.0
loss_scale = 512.0

ROWS = 32
COLS = 128
CH = 256
HALO = 48
LANES = 128
STEP = 5
TILE_CELLS = 64


def shape(dims, dtype):
    return jax.ShapeDtypeStruct(dims, dtype)


def nt(left, right):
    return lax.dot_general(left, right, (((1,), (1,)), ((), ())), preferred_element_type=F32)


def tn(left, right):
    return lax.dot_general(left, right, (((0,), (0,)), ((), ())), preferred_element_type=F32)


def nn(left, right):
    return jnp.dot(left, right, preferred_element_type=F32)


def halves(value):
    high = value.astype(BF16)
    return high, (value - high.astype(F32)).astype(BF16)


def wide_product(product, left, right):
    (a, b), (c, d) = left, right
    return product(a, c) + (product(a, d) + product(b, c))


def iota(dims, axis):
    return lax.broadcasted_iota(jnp.int32, dims, axis)


def gate_of(value):
    return 0.5 * jnp.tanh(0.5 * value) + 0.5


def copies(pairs, sems):
    started = [pltpu.make_async_copy(a, b, sems.at[i]) for i, (a, b) in enumerate(pairs)]
    for one in started:
        one.start()
    return started


def is_odd(axis):
    return lax.axis_index(axis) % 2 == 1


def rows_body(block, even_ref, odd_ref, sems):
    odd = is_odd("gy")
    first, last = jnp.where(odd, 0, ROWS - 1), jnp.where(odd, ROWS - 1, 0)
    started = copies([(block.at[pl.ds(first, 1)], even_ref), (block.at[pl.ds(last, 1)], odd_ref)], sems)
    for one in started:
        one.wait()


def columns_body(block, left_ref, right_ref):
    row, spot = iota((HALO, ROWS * 16), 0), iota((HALO, ROWS * 16), 1)
    for out, at, place in ((left_ref, 0, 0), (right_ref, COLS - 16, 15)):
        pick = (spot == (row - 1) * 16 + place).astype(F32).astype(BF16)
        out[...] = nn(pick, block[:, at : at + 16].reshape(ROWS * 16, CH)).astype(BF16)


def corner_body(left, right, even, odd, top_ref, bot_ref, even_ref, odd_ref):
    low = is_odd("gy")
    top_ref[0] = jnp.where(low, even[0], odd[0])
    bot_ref[0] = jnp.where(low, odd[0], even[0])
    row = iota((HALO, CH), 0)
    whole = []
    for side, at in ((left, 0), (right, COLS - 16)):
        part = slice(0, 1) if at == 0 else slice(15, 16)
        above = top_ref[0, at : at + 16].astype(F32)[part]
        below = bot_ref[0, at : at + 16].astype(F32)[part]
        whole.append(jnp.where(row == 0, above, jnp.where(row == ROWS + 1, below, side[...].astype(F32))))
    high = is_odd("core")
    even_ref[...] = jnp.where(high, whole[0], whole[1]).astype(BF16)
    odd_ref[...] = jnp.where(high, whole[1], whole[0]).astype(BF16)


def sides(even, odd):
    high = is_odd("core")
    one, two = even[...].astype(F32), odd[...].astype(F32)
    return jnp.where(high, one, two), jnp.where(high, two, one)


def forward_taps(weight, b):
    return jnp.concatenate([weight[3 * a + b] for a in range(3)], axis=0)


HALF = ROWS // 2
BLOCKS = (HALF - 1) // STEP
PARTS = ((3, 5, 5, 2), (2, 2, 2, 2, 2, 2, 2, 1))


def with_first(wide, value):
    start = jnp.where(iota((8, wide.shape[1]), 0) == 0, value, wide[0:8])
    return jnp.concatenate([start, wide[8:]], axis=0)


def with_last(wide, value):
    end = jnp.where(iota((8, wide.shape[1]), 0) == 7, value, wide[COLS - 8 :])
    return jnp.concatenate([wide[: COLS - 8], end], axis=0)


def neighbours(row):
    wide = row.astype(F32)
    left = with_first(pltpu.roll(wide, 1, 0), 0.0)
    right = with_last(pltpu.roll(wide, COLS - 1, 0), 0.0)
    return left.astype(BF16), right.astype(BF16)


HALVES = (slice(0, LANES), slice(LANES, CH))


def silu_pair(value, half_mask):
    half = 0.5 * value
    bend = jnp.tanh(half)
    kept = (1.0 + bend) * half_mask
    return value * kept, kept * (1.0 + half * (1.0 - bend))


def forward_body(flags_ref, feat, weight, slope_ref, sums, cols, wide, prod_a, prod_b, *, band):
    sums[...] = jnp.zeros_like(sums)
    taps = weight[...].reshape(9 * CH, CH)
    base = (HALF - 1) * band
    halves_of_mask = [0.5 * flags_ref[band, tile].astype(F32) for tile in range(8)]

    def build(i):
        here = slice(i * COLS, (i + 1) * COLS)
        for lanes in HALVES:
            left, right = neighbours(feat[base + i, :, lanes])
            wide[here, lanes] = left
            wide[here, lanes.start + CH : lanes.stop + CH] = right

    def around(start, count):
        taken = []
        for a in range(3):
            here = slice((start + a) * COLS, (start + a + count) * COLS)
            rows = feat[base + start + a : base + start + a + count].reshape(count * COLS, CH)
            taken += [wide[here, 0:CH], rows, wide[here, CH:]]
        return jnp.concatenate(taken, axis=1)

    def finish(r, prod, first):
        at = r - HALF * band
        for tile in range(8):
            here = slice(16 * tile, 16 * tile + 16)
            value = prod[first + 16 * tile : first + 16 * tile + 16]
            pixel = feat[r, here].astype(F32)
            bent, slope = silu_pair(value, halves_of_mask[tile])
            summed = pixel + bent
            slope_ref[at, here] = slope.astype(BF16)
            sums[r % 2, here] += summed
            if tile in (0, 7):
                edge = slice(0, 1) if tile == 0 else slice(15, 16)
                for i, part in enumerate((value, summed, pixel)):
                    cols[2 * i + tile // 7, at : at + 1] = part[edge]

    prods = (prod_a, prod_b)
    parts = PARTS[band]
    built, done = parts[0] + 2, 0
    for i in range(built):
        build(i)
    for block in range(len(parts) + 1):
        start = sum(parts[:block])
        if block < len(parts):
            prods[block % 2][0 : parts[block] * COLS] = nn(around(start, parts[block]), taps)
        ahead = min(HALF + 1, sum(parts[: block + 2]) + 2)
        for j in range(STEP):
            if done < start:
                finish(base + 1 + done, prods[(block - 1) % 2], (done - sum(parts[: block - 1])) * COLS)
                done += 1
            if built < ahead:
                build(built)
                built += 1


def border_body(
    flags_ref, feat, weight, sums_a, sums_b, cols_a, cols_b, top, bot, even, odd, strided, owner_ref,
    pooled_ref, token_ref, edge_ref, side_ref, side32,
):
    added = []
    cols = [jnp.concatenate([cols_a[i], cols_b[i]], axis=0) for i in range(6)]
    for i, whole in enumerate(sides(even, odd)):
        side32[...] = whole
        near = [side32[a : a + ROWS].astype(BF16) for a in range(3)]
        added.append(nn(jnp.concatenate(near, axis=1), forward_taps(weight, 2 * i)))

    def pair(one, two):
        return jnp.concatenate([one, two], axis=0)

    taken = jnp.concatenate(
        [pair(top[0], feat[ROWS - 2]), pair(feat[0], feat[ROWS - 1]), pair(feat[1], bot[0])], axis=1
    )
    low, mid, high = (nn(taken, forward_taps(weight, b)) for b in range(3))
    rows = []
    for i, r in enumerate((0, ROWS - 1)):
        part = slice(i * COLS, (i + 1) * COLS)
        before = with_first(pltpu.roll(low[part], 1, 0), added[0][r : r + 1])
        after = with_last(pltpu.roll(high[part], COLS - 1, 0), added[1][r : r + 1])
        value = mid[part] + before + after
        keep = jnp.concatenate(
            [0.5 * jnp.full((16, CH), flags_ref[i, t], jnp.int32).astype(F32) for t in range(8)], axis=0
        )
        bent, slope = silu_pair(value, keep)
        edge_ref[i] = slope.astype(BF16)
        rows.append(feat[r].astype(F32) + bent)

    line = iota((ROWS, CH), 0)
    deltas = []
    for i in range(2):
        tile = 7 * i
        keep = 0.5 * jnp.where(line < ROWS // 2, flags_ref[0, tile], flags_ref[1, tile]).astype(F32)
        bent, side_ref[i] = silu_pair(cols[i] + added[i], keep)
        inside = (line > 0) & (line < ROWS - 1)
        deltas.append(jnp.where(inside, cols[4 + i] + bent - cols[2 + i], 0.0))

    row, spot = iota((16, COLS), 0), iota((16, COLS), 1)
    pick = ((spot // 16 == row % 8) & (spot % 2 == row // 8)).astype(F32).astype(BF16)
    place = iota((16, CH), 0)
    parts = {}
    for band in range(2):
        for a in range(2):
            total = (sums_a, sums_b)[band][a]
            if band == a:
                total += rows[band]
            high, low = halves(total)
            part = nn(pick, high) + nn(pick, low)
            mine = (line // 16 == band) & (line % 2 == a)
            for i in range(2):
                delta = jnp.sum(jnp.where(mine, deltas[i], 0.0), axis=0, keepdims=True)
                part += jnp.where(place == 15 * i, delta, 0.0)
            parts[band, a] = part
    taken = [
        jnp.concatenate([parts[band, a][8 * b : 8 * b + 8] for band in range(2)], axis=0)
        for a in range(2)
        for b in range(2)
    ]
    high, low = halves(jnp.concatenate(taken, axis=1))
    flat = strided[...].reshape(4 * CH, CH)
    pooled = (nn(high, flat) + nn(low, flat)) * (1.0 / TILE_CELLS)
    pooled_ref[...] = pooled
    normed = pooled * lax.rsqrt(jnp.mean(pooled * pooled, axis=-1, keepdims=True) + 1e-05)
    token_ref[:, 0:CH] = normed.astype(BF16)
    owner = jnp.full((16, LANES), -1, jnp.int32)
    for tile in range(16):
        named = jnp.where(flags_ref[tile // 8, tile % 8] != 0, owner_ref[tile], -1)
        owner = jnp.where(iota((16, LANES), 0) == tile, named, owner)
    token_ref[:, CH:] = (owner == iota((16, LANES), 1)).astype(F32).astype(BF16)


def turn_body(feat, top, bot, w_query, w_key, w_value, token, turned_ref, high_ref, low_ref):
    turned_ref[:, 0:COLS] = top[0].T
    turned_ref[:, (ROWS + 1) * COLS :] = bot[0].T

    @pl.loop(0, ROWS // 4)
    def _(i):
        for j in range(4):
            here = pl.multiple_of((4 * i + j + 1) * COLS, COLS)
            turned_ref[:, pl.ds(here, COLS)] = feat[4 * i + j].T

    for i, one in enumerate((w_query, w_key, w_value)):
        high, low = halves(one[...])
        high_ref[:, i * CH : (i + 1) * CH] = high
        low_ref[:, i * CH : (i + 1) * CH] = low


def attention_body(
    mine, other, pooled_ref, high_w, low_w, cot, strided, spread_ref, emb_ref, band, grad_ref, *, seed_scale
):
    gz, core = lax.axis_index("gz"), lax.axis_index("core")

    def rows_of(depth, other):
        return pl.ds(pl.multiple_of(depth * 32 + other * 16, 16), 16)

    for k in range(mine.shape[0]):
        depth = lax.bitwise_xor(gz, k)
        band[rows_of(depth, core)] = mine[k]
        band[rows_of(depth, 1 - core)] = other[k]
    count = band.shape[0]
    tokens, group = band[:, 0:CH], band[:, CH:]
    pair = nt(group, group)
    pairs = jnp.concatenate([pair] * HEADS, axis=0)
    projected = nn(tokens, high_w[...]) + nn(tokens, low_w[...])
    query, key, value = (projected[:, i * CH : (i + 1) * CH] for i in range(3))
    lane = iota((1, CH), 1) // (CH // HEADS)
    scale = 1.0 / math.sqrt(CH // HEADS)

    def by_head(array):
        return jnp.concatenate([jnp.where(lane == h, array, 0.0) for h in range(HEADS)], axis=0)

    queries, keys = halves(by_head(query)), halves(by_head(key))
    gate = gate_of(wide_product(nt, queries, halves(key)) * scale + attention_bias)
    weights = gate * pairs
    seed = cot[...] * seed_scale
    seeds = jnp.where(lane == iota((8, CH), 0), seed, 0.0)
    values = halves(value)
    along = wide_product(nt, halves(seeds), values)
    columns, grads = [], []
    for h in range(HEADS):
        part = slice(h * count, (h + 1) * count)
        columns.append(jnp.sum(weights[part], axis=0, keepdims=True))
        grads.append(weights[part] * (1.0 - gate[part]) * (along[h : h + 1] * scale))
    columns = halves(jnp.concatenate(columns + [jnp.zeros((8 - HEADS, count), F32)], axis=0))
    grad_ref[:, 0:CH] = wide_product(nn, halves(jnp.concatenate(grads, axis=1)), keys)
    grad_ref[:, CH : 2 * CH] = wide_product(tn, halves(jnp.concatenate(grads, axis=0)), queries)
    grad_ref[:, 2 * CH :] = wide_product(tn, columns, halves(seeds))
    mixed = wide_product(nn, columns, values)
    mixed = jnp.sum(jnp.where(lane == iota((8, CH), 0), mixed, 0.0), axis=0, keepdims=True)
    high = mixed.astype(BF16).astype(F32)
    low = mixed - high
    rows = iota((16, LANES), 0)
    packed = jnp.zeros((16, LANES), F32)
    for i, part in enumerate((high[:, :LANES], high[:, LANES:], low[:, :LANES], low[:, LANES:])):
        packed = jnp.where(rows == i, part, packed)
    emb_ref[...] = packed.astype(BF16)

    grads = halves(grad_ref[rows_of(gz, core)])
    grad = wide_product(nt, grads, (high_w[...], low_w[...]))
    grad = grad.astype(BF16).astype(F32)
    pooled = pooled_ref[...]
    inv = lax.rsqrt(jnp.mean(pooled * pooled, axis=-1, keepdims=True) + 1e-05)
    unit = pooled * inv
    back = inv * (grad - unit * jnp.mean(grad * unit, axis=-1, keepdims=True))
    cell = (back * (1.0 / TILE_CELLS)).astype(BF16)
    spot, row = iota((COLS, 16), 0), iota((COLS, 16), 1)
    expand = ((spot // 16 == row % 8) & (spot % 2 == row // 8)).astype(F32).astype(BF16)
    taps = nt(cell, strided[...].reshape(4 * CH, CH))
    for band in range(2):
        here = taps[8 * band : 8 * band + 8]
        both = [
            jnp.concatenate([here[:, (2 * a + b) * CH : (2 * a + b + 1) * CH] for a in range(2)], axis=1)
            for b in range(2)
        ]
        high, low = halves(jnp.concatenate(both, axis=0))
        spread = nn(expand, high) + nn(expand, low)
        for a in range(2):
            spread_ref[band * 2 + a] = spread[:, a * CH : (a + 1) * CH]


GROUPS = (6, 10, 16)


def weight_body(
    spread, slope_a, slope_b, edge, side, turned, even, odd,
    wide, keep_ref, give_ref, even_ref, odd_ref, left_ref, right_ref, total, first, last,
):
    first[...] = jnp.zeros_like(first)
    last[...] = jnp.zeros_like(last)

    def build(r):
        here = slice(r * COLS, (r + 1) * COLS)
        for lanes in HALVES:
            if r in (0, ROWS - 1):
                slope = edge[r // HALF, :, lanes].astype(F32)
            else:
                slope = (slope_a, slope_b)[r // HALF][r % HALF, :, lanes].astype(F32)
                slope = with_last(with_first(slope, side[0, r : r + 1, lanes]), side[1, r : r + 1, lanes])
            grad = (spread[(r // HALF) * 2 + r % 2, :, lanes] * slope).astype(BF16)
            before, after = neighbours(grad)
            wide[here, lanes] = after
            wide[here, lanes.start + CH : lanes.stop + CH] = grad
            wide[here, lanes.start + 2 * CH : lanes.stop + 2 * CH] = before
            for a in range(3):
                first[a, r + a : r + a + 1, lanes] = grad[0:16].astype(F32)[0:1]
                last[a, r + a : r + a + 1, lanes] = grad[COLS - 16 :].astype(F32)[15:16]

    is_one = is_odd("core")
    left, right = (part.astype(BF16) for part in sides(even, odd))

    def put(part, a, b):
        if b == 0:
            part += tn(left, first[a].astype(BF16))
        if b == 2:
            part += tn(right, last[a].astype(BF16))
        low, high = part[:, :LANES], part[:, LANES:]
        at = slice((3 * a + b) * CH, (3 * a + b + 1) * CH)
        keep_ref[at] = jnp.where(is_one, high, low).astype(BF16)
        give_ref[at] = jnp.where(is_one, low, high).astype(BF16)

    for r in range(GROUPS[0]):
        build(r)
    start = 0
    for g, count in enumerate(GROUPS):
        here = slice(start * COLS, (start + count) * COLS)
        near = [turned[:, (start + a) * COLS : (start + a + count) * COLS] for a in range(3)]
        near = jnp.concatenate(near, axis=0)
        start += count
        ahead = GROUPS[g + 1] if g + 1 < len(GROUPS) else 0
        for b in range(3):
            part = slice(b * CH, (b + 1) * CH)
            result = nn(near, wide[here, part])
            if g > 0:
                result += total[:, part]
            if ahead:
                total[:, part] = result
            for r in range(ahead * b // 3, ahead * (b + 1) // 3):
                build(start + r)
            if not ahead:
                for a in range(3):
                    put(result[a * CH : (a + 1) * CH], a, b)

    centre = slice(CH, 2 * CH)
    order_rows(wide[0:COLS, centre], wide[(ROWS - 1) * COLS :, centre], even_ref, odd_ref)
    left_ref[...] = first[1].astype(BF16)
    right_ref[...] = last[1].astype(BF16)


def order_rows(first, last, even_ref, odd_ref):
    odd = is_odd("gy")
    even_ref[0] = jnp.where(odd, first, last)
    odd_ref[0] = jnp.where(odd, last, first)


def back_taps(weight, taps):
    return jnp.concatenate([weight[tap] for tap in taps], axis=1)


def input_blocks(wide, weight, first, blocks, prods, finish, send=None):
    for block in range(blocks + 1):
        if block < blocks:
            at = first + STEP * block
            near = [wide[(at + step) * COLS : (at + step + STEP) * COLS] for step in (1, 0, -1)]
            prods[block % 2][...] = nt(jnp.concatenate(near, axis=1), back_taps(weight, range(9)))
        if block > 0:
            at = first + STEP * (block - 1)
            for j in range(STEP):
                finish(at + j, prods[(block - 1) % 2][j * COLS : (j + 1) * COLS])
            if send is not None:
                send(at, STEP)


UPPER = 2 * STEP


def upper_body(wide, spread, weight, done, raw_ref, prod_a, prod_b):
    def finish(r, prod):
        value = spread[r % 2] + prod
        done[r - 1] = value.astype(BF16)
        raw_ref[0, r : r + 1] = value[0:1]
        raw_ref[1, r : r + 1] = value[COLS - 1 :]

    input_blocks(wide, weight, 1, UPPER // STEP, (prod_a, prod_b), finish)


def lower_body(
    wide, top, bot, even, odd, spread, weight, upper, raw, out, prod_a, prod_b, side32, added, done, fixed, sems
):
    started = []

    def start(source, target):
        started.append(pltpu.make_async_copy(source, target, sems.at[len(started)]))
        started[-1].start()

    start(upper.at[:, 16 : COLS - 16], out.at[1 : UPPER + 1, 16 : COLS - 16])
    for i, whole in enumerate(sides(even, odd)):
        side32[...] = whole
        near = [side32[2 - a : 2 - a + ROWS].astype(BF16) for a in range(3)]
        taps = back_taps(weight, [3 * a + 2 - 2 * i for a in range(3)])
        added[i] = nt(jnp.concatenate(near, axis=1), taps)

    small = iota((16, CH), 0)
    for i in range(2):
        at = (COLS - 16) * i
        for r in range(1, UPPER + 1):
            value = raw[i, r : r + 1] + added[i, r : r + 1]
            old = upper[r - 1, at : at + 16].astype(F32)
            fixed[i, r - 1] = jnp.where(small == 15 * i, value, old).astype(BF16)
        start(fixed.at[i], out.at[1 : UPPER + 1, at : at + 16])

    def place(r):
        return r - UPPER if r else 0

    def finish(r, prod):
        prod = with_first(prod, prod[0:1] + added[0, r : r + 1])
        prod = with_last(prod, prod[COLS - 1 :] + added[1, r : r + 1])
        done[place(r)] = (spread[(r // HALF) * 2 + r % 2] + prod).astype(BF16)

    def send(first, count):
        start(done.at[place(first) : place(first) + count], out.at[first : first + count])

    input_blocks(wide, weight, UPPER + 1, (ROWS - 2 - UPPER) // STEP, (prod_a, prod_b), finish, send)

    def row(r):
        return wide[r * COLS : (r + 1) * COLS]

    def outside(one):
        left, right = neighbours(one[0])
        return jnp.concatenate([right, one[0], left], axis=1)

    def pair(one, two):
        return jnp.concatenate([one, two], axis=0)

    near = [pair(row(1), outside(bot)), pair(row(0), row(ROWS - 1)), pair(outside(top), row(ROWS - 2))]
    both = nt(jnp.concatenate(near, axis=1), back_taps(weight, range(9)))
    for i, r in enumerate((0, ROWS - 1)):
        finish(r, both[i * COLS : (i + 1) * COLS])
        send(r, 1)
    for one in started:
        one.wait()


def add_up(refs, rows):
    total = refs[0][0:rows].astype(F32)
    for one in refs[1:]:
        total += one[0:rows].astype(F32)
    return total.astype(BF16)


def deal(total_ref, outs, size, axis):
    for k, out in enumerate(reversed(outs)):
        at = lax.bitwise_xor(lax.axis_index(axis), k) * size
        out[0:size] = total_ref[pl.ds(pl.multiple_of(at, 16), size)]


def chip_sum_body(one, two, emb, *refs):
    outs, total_ref = refs[:-1], refs[-1]
    rows = one.shape[0]
    size = rows // len(outs)
    total_ref[...] = add_up((one, two), rows)
    deal(total_ref, outs, size, "gy")
    for out in outs:
        out[size:] = emb[...]


def band_sum_body(*refs, terms, norm_scale):
    outs, emb_ref, total_ref = refs[terms:-2], refs[-2], refs[-1]
    rows = total_ref.shape[0]
    total_ref[...] = add_up(refs[:terms], rows)
    deal(total_ref, outs, rows // len(outs), "gz")
    embs = []
    for one in (refs[0], *refs[terms - 1 : 0 : -1]):
        part = one[rows : rows + 16].astype(F32)
        embs.append(part[0:2] + part[2:4])
    while len(embs) > 1:
        embs = [a + b for a, b in zip(embs[0::2], embs[1::2])]
    emb_ref[:, 0:LANES] = embs[0][0:1] * norm_scale
    emb_ref[:, LANES:] = embs[0][1:2] * norm_scale


def last_sum_body(*refs):
    refs[-1][...] = add_up(refs[:-1], refs[-1].shape[0])


def stack_body(*refs):
    for i, one in enumerate(refs[:-1]):
        refs[-1][i] = one[...]


def half_body(array, *refs, other):
    grad_ref, buf, sems = refs[-3:]
    gy, gz, core = (lax.axis_index(name) for name in ("gy", "gz", "core"))
    bands, depth, share = array.shape[:3]
    half = 1 - core if other else core
    lanes = pl.ds(pl.multiple_of(half * LANES, LANES), LANES)
    started = []
    for k in range(bands):
        first = lax.bitwise_xor(gy, k) * (depth * share)
        for j in range(depth):
            at = first + lax.bitwise_xor(gz, j) * share
            buf[pl.ds(pl.multiple_of(at, 16), share)] = array[k, j].astype(F32) * (1.0 / loss_scale)
        here = pl.ds(pl.multiple_of(first, 16), depth * share)
        started.append(pltpu.make_async_copy(buf.at[here], grad_ref.at[here, lanes], sems.at[k]))
        started[-1].start()
    for one in started:
        one.wait()


SMEM = pl.BlockSpec(memory_space=pltpu.SMEM)
VMEM = pl.BlockSpec(memory_space=pltpu.VMEM)
HBM = pl.BlockSpec(memory_space=pltpu.HBM)


def run(body, args, outs, scratch=(), flops=1 << 20, mib=8, far=(), **rest):
    specs = [HBM if i in far else SMEM if a.dtype == jnp.int32 else VMEM for i, a in enumerate(args)]
    return pl.pallas_call(
        body,
        in_specs=specs,
        out_shape=outs,
        scratch_shapes=list(scratch),
        compiler_params=pltpu.CompilerParams(vmem_limit_bytes=mib << 20),
        cost_estimate=pl.CostEstimate(flops=flops, bytes_accessed=1 << 20, transcendentals=0),
        **rest,
    )(*args)


def per_device(features, tissue, owner_map, w_conv, w_stride, w_query, w_key, w_value, cotangent):
    gy_count, gz_count, cores = lax.axis_size("gy"), lax.axis_size("gz"), lax.axis_size("core")
    gx_count, chips = gz_count * cores, gy_count * gz_count
    across = ("gz", "core")
    norm_scale = 1.0 / math.sqrt(16 * gy_count * gx_count)
    swap = [(i, i ^ 1) for i in range(cores)]

    def pairs(value, axis, count, odd):
        low = range(odd, count - 1, 2)
        return lax.ppermute(value, axis, [(i, i + 1) for i in low] + [(i + 1, i) for i in low])

    def others(values, axis, count):
        got = [
            lax.ppermute(values[k - 1], axis, [(i, i ^ k) for i in range(count)])
            for k in range(count - 1, 0, -1)
        ]
        return got[::-1]

    column = shape((HALO, CH), BF16)
    line = shape((1, COLS, CH), BF16)

    def row_halos(even, odd):
        return pairs(even, "gy", gy_count, 0), pairs(odd, "gy", gy_count, 1)

    def corners(left, right, even, odd):
        return run(corner_body, (left, right, even, odd), [line, line, column, column], mib=1)

    def column_halos(even, odd):
        return pairs(even, across, gx_count, 0), pairs(odd, across, gx_count, 1)

    conv_flops = 2 * ROWS * COLS * 9 * CH * CH
    prod = pltpu.VMEM((STEP * COLS, CH), F32)
    side32 = pltpu.VMEM((HALO, CH), F32)
    half_block = shape((HALF, COLS, CH), BF16)

    def forward(band, weight):
        return run(
            lambda *refs: forward_body(*refs, band=band),
            (tissue, features, weight),
            [half_block, shape((2, COLS, CH), F32), shape((6, HALF, CH), F32)],
            [pltpu.VMEM(((HALF + 1) * COLS, 2 * CH), BF16), prod, prod],
            flops=conv_flops // 2,
            mib=16,
        )

    rows = run(
        rows_body,
        (features,),
        [line, line],
        [pltpu.SemaphoreType.DMA((2,))],
        flops=conv_flops,
        mib=56,
        far=(0,),
    )
    outer = run(columns_body, (features,), [column, column], mib=2)
    even, odd = row_halos(*rows)
    slope_a, sums_a, cols_a = forward(0, w_conv)
    even, odd, cols_a = lax.optimization_barrier((even, odd, cols_a))
    top, bot, even, odd = corners(*outer, even, odd)
    weight_b, even = lax.optimization_barrier((w_conv, even))
    even, odd = column_halos(even, odd)
    slope_b, sums_b, cols_b = forward(1, weight_b)
    pooled, token, edge, side = run(
        border_body,
        (
            tissue, features, w_conv, sums_a, sums_b, cols_a, cols_b, top, bot, even, odd, w_stride,
            owner_map.reshape(16),
        ),
        [
            shape((16, CH), F32),
            shape((16, CH + LANES), BF16),
            shape((2, COLS, CH), BF16),
            shape((2, ROWS, CH), F32),
        ],
        [side32],
        flops=conv_flops // 8,
        mib=12,
    )
    def stacked(terms):
        return run(stack_body, terms, shape((len(terms),) + terms[0].shape, BF16), mib=4)

    turned, high_w, low_w = run(
        turn_body,
        (features, top, bot, w_query, w_key, w_value, token),
        [shape((CH, (ROWS + 2) * COLS), BF16), shape((CH, 3 * CH), BF16), shape((CH, 3 * CH), BF16)],
        flops=conv_flops // 4,
        mib=12,
    )
    tokens = stacked([token] + others([token] * (gz_count - 1), "gz", gz_count))
    tokens, high_w = lax.optimization_barrier((tokens, high_w))
    count = 16 * gx_count
    spread, emb = run(
        lambda *refs: attention_body(*refs, seed_scale=loss_scale * norm_scale),
        (tokens, lax.ppermute(tokens, "core", swap), pooled, high_w, low_w, cotangent.reshape(1, CH), w_stride),
        [shape((4, COLS, CH), F32), shape((16, LANES), BF16)],
        [pltpu.VMEM((count, CH + LANES), BF16), pltpu.VMEM((count, 3 * CH), F32)],
        flops=1 << 30,
        mib=12,
    )
    border = pltpu.VMEM((3, HALO, CH), F32)
    wide, keep, give, *outer = run(
        weight_body,
        (spread, slope_a, slope_b, edge, side, turned, even, odd),
        [
            shape((ROWS * COLS, 3 * CH), BF16),
            shape((9 * CH, LANES), BF16),
            shape((9 * CH, LANES), BF16),
            line,
            line,
            column,
            column,
        ],
        [pltpu.VMEM((3 * CH, 3 * CH), F32), border, border],
        flops=conv_flops,
        mib=20,
    )

    share = -(-9 * CH // (16 * chips)) * 16
    spare = share * chips - 9 * CH
    taken = lax.ppermute(give, "core", swap)
    pre_rows = row_halos(*outer[:2])
    if spare:
        keep, taken = (jnp.pad(a, ((0, spare), (0, 0))) for a in (keep, taken))

    whole_rows = share * chips
    band_rows = share * gz_count
    parts = run(
        chip_sum_body,
        (keep, taken, emb),
        [shape((band_rows + 16, LANES), BF16)] * gy_count,
        [pltpu.VMEM((whole_rows, LANES), BF16)],
        mib=6,
    )[::-1]
    *parts, wide_upper = lax.optimization_barrier((*parts, wide))
    upper, raw = run(
        upper_body,
        (wide_upper, spread, w_conv),
        [shape((UPPER, COLS, CH), BF16), shape((2, HALF, CH), F32)],
        [prod, prod],
        flops=conv_flops // 3,
        mib=12,
    )
    raw, *outer = lax.optimization_barrier((raw, *outer[2:], *pre_rows))
    parts = [parts[0]] + others(parts[1:], "gy", gy_count)[::-1]
    top, bot, even, odd = corners(*outer)
    even, odd = column_halos(even, odd)
    *parts, raw, even, odd = lax.optimization_barrier((*parts, raw, even, odd))
    embedding, *parts = run(
        lambda *refs: band_sum_body(*refs, terms=gy_count, norm_scale=norm_scale),
        parts,
        [shape((share, LANES), BF16)] * gz_count + [shape((1, CH), F32)],
        [pltpu.VMEM((band_rows, LANES), BF16)],
        mib=4,
    )[::-1]
    parts = [parts[0]] + others(parts[1:], "gz", gz_count)[::-1]
    mine = run(last_sum_body, parts, shape((share, LANES), BF16), mib=2)
    row = stacked([mine] + others([mine] * (gz_count - 1), "gz", gz_count))
    row, wide_lower = lax.optimization_barrier((row, wide))
    input_grad = run(
        lower_body,
        (wide_lower, top, bot, even, odd, spread, w_conv, upper, raw),
        shape((ROWS, COLS, CH), BF16),
        [
            prod,
            prod,
            side32,
            pltpu.VMEM((2, ROWS, CH), F32),
            pltpu.VMEM((ROWS - UPPER, COLS, CH), BF16),
            pltpu.VMEM((2, UPPER, 16, CH), BF16),
            pltpu.SemaphoreType.DMA((BLOCKS + 6,)),
        ],
        flops=conv_flops // 2,
        mib=16,
        out_specs=HBM,
    )
    planes = [row] + others([row] * (gy_count - 1), "gy", gy_count)
    *planes, input_grad = lax.optimization_barrier((*planes, input_grad))
    plane = stacked(planes)
    other = lax.ppermute(plane, "core", swap)
    whole = shape((whole_rows, CH), F32)
    buffers = [pltpu.VMEM((whole_rows, LANES), F32), pltpu.SemaphoreType.DMA((gy_count,))]
    half_grad = run(
        lambda *refs: half_body(*refs, other=False), (plane,), whole, buffers, mib=4, out_specs=HBM
    )
    conv_grad = run(
        lambda *refs: half_body(*refs, other=True),
        (other, half_grad),
        whole,
        buffers,
        mib=4,
        far=(1,),
        out_specs=HBM,
        input_output_aliases={1: 0},
    )
    return embedding.reshape(CH), input_grad, conv_grad[: 9 * CH].reshape(9, CH, CH)


def solution(mesh):
    sizes = mesh.devices.shape
    split = Mesh(mesh.devices.reshape(sizes[0], sizes[1] // 2, 2), ("gy", "gz", "core"))
    gx = ("gz", "core")
    in_specs = (P("gy", gx, None), P("gy", gx), P("gy", gx, None, None), P(), P(), P(), P(), P(), P())
    out_specs = (P(), P("gy", gx, None), P())
    return jax.shard_map(per_device, mesh=split, in_specs=in_specs, out_specs=out_specs, check_vma=False)
```

```python
import math

import jax
import jax.numpy as jnp
from jax import lax
from jax.experimental import pallas as pl
from jax.experimental.pallas import tpu as pltpu
from jax.sharding import Mesh, PartitionSpec as P

HEADS = 4
F32 = jnp.float32
BF16 = jnp.bfloat16

attention_bias = -1.0
loss_scale = 512.0

ROWS = 32
COLS = 128
CH = 256
HALO = 48
LANES = 128
STEP = 5
TILE_CELLS = 64


def shape(dims, dtype):
    return jax.ShapeDtypeStruct(dims, dtype)


def nt(left, right):
    return lax.dot_general(left, right, (((1,), (1,)), ((), ())), preferred_element_type=F32)


def tn(left, right):
    return lax.dot_general(left, right, (((0,), (0,)), ((), ())), preferred_element_type=F32)


def nn(left, right):
    return jnp.dot(left, right, preferred_element_type=F32)


def halves(value):
    high = value.astype(BF16)
    return high, (value - high.astype(F32)).astype(BF16)


def wide_product(product, left, right):
    (a, b), (c, d) = left, right
    return product(a, c) + (product(a, d) + product(b, c))


def iota(dims, axis):
    return lax.broadcasted_iota(jnp.int32, dims, axis)


def gate_of(value):
    return 0.5 * jnp.tanh(0.5 * value) + 0.5


def is_odd(axis):
    return lax.axis_index(axis) % 2 == 1


def order_body(first_ref, last_ref, even_ref, odd_ref):
    order_rows(first_ref[0], last_ref[0], even_ref, odd_ref)


def columns_body(block, left_ref, right_ref):
    row, spot = iota((HALO, ROWS * 16), 0), iota((HALO, ROWS * 16), 1)
    for out, at, place in ((left_ref, 0, 0), (right_ref, COLS - 16, 15)):
        pick = (spot == (row - 1) * 16 + place).astype(F32).astype(BF16)
        out[...] = nn(pick, block[:, at : at + 16].reshape(ROWS * 16, CH)).astype(BF16)


def corner_body(left, right, even, odd, top_ref, bot_ref, even_ref, odd_ref):
    low = is_odd("gy")
    top_ref[0] = jnp.where(low, even[0], odd[0])
    bot_ref[0] = jnp.where(low, odd[0], even[0])
    row = iota((HALO, CH), 0)
    whole = []
    for side, at in ((left, 0), (right, COLS - 16)):
        part = slice(0, 1) if at == 0 else slice(15, 16)
        above = top_ref[0, at : at + 16].astype(F32)[part]
        below = bot_ref[0, at : at + 16].astype(F32)[part]
        whole.append(jnp.where(row == 0, above, jnp.where(row == ROWS + 1, below, side[...].astype(F32))))
    high = is_odd("core")
    even_ref[...] = jnp.where(high, whole[0], whole[1]).astype(BF16)
    odd_ref[...] = jnp.where(high, whole[1], whole[0]).astype(BF16)


def sides(even, odd):
    high = is_odd("core")
    one, two = even[...].astype(F32), odd[...].astype(F32)
    return jnp.where(high, one, two), jnp.where(high, two, one)


def silu_pair_exp(value, half_mask):
    gate = pl.reciprocal(1.0 + jnp.exp(-value), approx=True)
    kept = gate * (2.0 * half_mask)
    return value * kept, kept * (1.0 + value * (1.0 - gate))


def forward_taps(weight, b):
    return jnp.concatenate([weight[3 * a + b] for a in range(3)], axis=0)


HALF = ROWS // 2
BLOCKS = (HALF - 1) // STEP
PARTS = ((3, 5, 5, 2), (2, 2, 2, 2, 2, 2, 2, 1))


def with_first(wide, value):
    start = jnp.where(iota((8, wide.shape[1]), 0) == 0, value, wide[0:8])
    return jnp.concatenate([start, wide[8:]], axis=0)


def with_last(wide, value):
    end = jnp.where(iota((8, wide.shape[1]), 0) == 7, value, wide[COLS - 8 :])
    return jnp.concatenate([wide[: COLS - 8], end], axis=0)


def neighbours(row):
    wide = row.astype(F32)
    left = with_first(pltpu.roll(wide, 1, 0), 0.0)
    right = with_last(pltpu.roll(wide, COLS - 1, 0), 0.0)
    return left.astype(BF16), right.astype(BF16)


HALVES = (slice(0, LANES), slice(LANES, CH))


def silu_pair(value, half_mask):
    half = 0.5 * value
    bend = jnp.tanh(half)
    kept = (1.0 + bend) * half_mask
    return value * kept, kept * (1.0 + half * (1.0 - bend))


def forward_body(flags_ref, feat, weight, slope_ref, sums, cols, wide, prod_a, prod_b, *, band):
    sums[...] = jnp.zeros_like(sums)
    base = (HALF - 1) * band
    halves_of_mask = [0.5 * flags_ref[band, tile].astype(F32) for tile in range(8)]

    def build(i):
        here = slice(i * COLS, (i + 1) * COLS)
        for lanes in HALVES:
            left, right = neighbours(feat[base + i, :, lanes])
            wide[here, lanes] = left
            wide[here, lanes.start + CH : lanes.stop + CH] = right

    def around(start, count):
        taken = []
        for a in range(3):
            here = slice((start + a) * COLS, (start + a + count) * COLS)
            rows = feat[base + start + a : base + start + a + count].reshape(count * COLS, CH)
            taken += [wide[here, 0:CH], rows, wide[here, CH:]]
        return jnp.concatenate(taken, axis=1)

    def finish(r, prod, first):
        at = r - HALF * band
        for tile in range(8):
            here = slice(16 * tile, 16 * tile + 16)
            value = prod[first + 16 * tile : first + 16 * tile + 16]
            pixel = feat[r, here].astype(F32)
            bent, slope = (silu_pair, silu_pair_exp)[band](value, halves_of_mask[tile])
            summed = pixel + bent
            slope_ref[at, here] = slope.astype(BF16)
            sums[r % 2, here] += summed
            if tile in (0, 7):
                edge = slice(0, 1) if tile == 0 else slice(15, 16)
                for i, part in enumerate((value, summed, pixel)):
                    cols[2 * i + tile // 7, at : at + 1] = part[edge]

    prods = (prod_a, prod_b)
    parts = PARTS[band]
    built, done = parts[0] + 2, 0
    for i in range(built):
        build(i)
    for block in range(len(parts) + 1):
        start = sum(parts[:block])
        if block < len(parts):
            prods[block % 2][0 : parts[block] * COLS] = nn(
                around(start, parts[block]), weight[...].reshape(9 * CH, CH)
            )
        ahead = min(HALF + 1, sum(parts[: block + 2]) + 2)
        for j in range(STEP):
            if done < start:
                finish(base + 1 + done, prods[(block - 1) % 2], (done - sum(parts[: block - 1])) * COLS)
                done += 1
            if built < ahead:
                build(built)
                built += 1


def border_body(
    flags_ref, feat, weight, sums_a, sums_b, cols_a, cols_b, top, bot, even, odd, strided, owner_ref,
    pooled_ref, token_ref, edge_ref, side_ref, side32,
):
    added = []
    cols = [jnp.concatenate([cols_a[i], cols_b[i]], axis=0) for i in range(6)]
    for i, whole in enumerate(sides(even, odd)):
        side32[...] = whole
        near = [side32[a : a + ROWS].astype(BF16) for a in range(3)]
        added.append(nn(jnp.concatenate(near, axis=1), forward_taps(weight, 2 * i)))

    def pair(one, two):
        return jnp.concatenate([one, two], axis=0)

    taken = jnp.concatenate(
        [pair(top[0], feat[ROWS - 2]), pair(feat[0], feat[ROWS - 1]), pair(feat[1], bot[0])], axis=1
    )
    low, mid, high = (nn(taken, forward_taps(weight, b)) for b in range(3))
    rows = []
    for i, r in enumerate((0, ROWS - 1)):
        part = slice(i * COLS, (i + 1) * COLS)
        before = with_first(pltpu.roll(low[part], 1, 0), added[0][r : r + 1])
        after = with_last(pltpu.roll(high[part], COLS - 1, 0), added[1][r : r + 1])
        value = mid[part] + before + after
        keep = jnp.concatenate(
            [0.5 * jnp.full((16, CH), flags_ref[i, t], jnp.int32).astype(F32) for t in range(8)], axis=0
        )
        bent, slope = silu_pair(value, keep)
        edge_ref[i] = slope.astype(BF16)
        rows.append(feat[r].astype(F32) + bent)

    line = iota((ROWS, CH), 0)
    deltas = []
    for i in range(2):
        tile = 7 * i
        keep = 0.5 * jnp.where(line < ROWS // 2, flags_ref[0, tile], flags_ref[1, tile]).astype(F32)
        bent, side_ref[i] = silu_pair(cols[i] + added[i], keep)
        inside = (line > 0) & (line < ROWS - 1)
        deltas.append(jnp.where(inside, cols[4 + i] + bent - cols[2 + i], 0.0))

    row, spot = iota((16, COLS), 0), iota((16, COLS), 1)
    pick = ((spot // 16 == row % 8) & (spot % 2 == row // 8)).astype(F32).astype(BF16)
    place = iota((16, CH), 0)
    parts = {}
    for band in range(2):
        for a in range(2):
            total = (sums_a, sums_b)[band][a]
            if band == a:
                total += rows[band]
            high, low = halves(total)
            part = nn(pick, high) + nn(pick, low)
            mine = (line // 16 == band) & (line % 2 == a)
            for i in range(2):
                delta = jnp.sum(jnp.where(mine, deltas[i], 0.0), axis=0, keepdims=True)
                part += jnp.where(place == 15 * i, delta, 0.0)
            parts[band, a] = part
    taken = [
        jnp.concatenate([parts[band, a][8 * b : 8 * b + 8] for band in range(2)], axis=0)
        for a in range(2)
        for b in range(2)
    ]
    high, low = halves(jnp.concatenate(taken, axis=1))
    flat = strided[...].reshape(4 * CH, CH)
    pooled = (nn(high, flat) + nn(low, flat)) * (1.0 / TILE_CELLS)
    pooled_ref[...] = pooled
    normed = pooled * lax.rsqrt(jnp.mean(pooled * pooled, axis=-1, keepdims=True) + 1e-05)
    token_ref[:, 0:CH] = normed.astype(BF16)
    owner = jnp.full((16, LANES), -1, jnp.int32)
    for tile in range(16):
        named = jnp.where(flags_ref[tile // 8, tile % 8] != 0, owner_ref[tile], -1)
        owner = jnp.where(iota((16, LANES), 0) == tile, named, owner)
    token_ref[:, CH:] = (owner == iota((16, LANES), 1)).astype(F32).astype(BF16)


def turn_body(feat, top, bot, w_query, w_key, w_value, token, turned_ref, high_ref, low_ref):
    turned_ref[:, 0:COLS] = top[0].T
    turned_ref[:, (ROWS + 1) * COLS :] = bot[0].T

    @pl.loop(0, ROWS // 4)
    def _(i):
        for j in range(4):
            here = pl.multiple_of((4 * i + j + 1) * COLS, COLS)
            turned_ref[:, pl.ds(here, COLS)] = feat[4 * i + j].T

    for i, one in enumerate((w_query, w_key, w_value)):
        high, low = halves(one[...])
        high_ref[:, i * CH : (i + 1) * CH] = high
        low_ref[:, i * CH : (i + 1) * CH] = low


def attention_body(
    mine, other, pooled_ref, high_w, low_w, cot, strided, spread_ref, emb_ref, band, grad_ref, *, seed_scale
):
    gz, core = lax.axis_index("gz"), lax.axis_index("core")

    def rows_of(depth, other):
        return pl.ds(pl.multiple_of(depth * 32 + other * 16, 16), 16)

    for k in range(mine.shape[0]):
        depth = lax.bitwise_xor(gz, k)
        band[rows_of(depth, core)] = mine[k]
        band[rows_of(depth, 1 - core)] = other[k]
    count = band.shape[0]
    tokens, group = band[:, 0:CH], band[:, CH:]
    pair = nt(group, group)
    pairs = jnp.concatenate([pair] * HEADS, axis=0)
    projected = nn(tokens, high_w[...]) + nn(tokens, low_w[...])
    query, key, value = (projected[:, i * CH : (i + 1) * CH] for i in range(3))
    lane = iota((1, CH), 1) // (CH // HEADS)
    scale = 1.0 / math.sqrt(CH // HEADS)

    def by_head(array):
        return jnp.concatenate([jnp.where(lane == h, array, 0.0) for h in range(HEADS)], axis=0)

    queries, keys = halves(by_head(query)), halves(by_head(key))
    gate = gate_of(wide_product(nt, queries, halves(key)) * scale + attention_bias)
    weights = gate * pairs
    seed = cot[...] * seed_scale
    seeds = jnp.where(lane == iota((8, CH), 0), seed, 0.0)
    values = halves(value)
    along = wide_product(nt, halves(seeds), values)
    columns, grads = [], []
    for h in range(HEADS):
        part = slice(h * count, (h + 1) * count)
        columns.append(jnp.sum(weights[part], axis=0, keepdims=True))
        grads.append(weights[part] * (1.0 - gate[part]) * (along[h : h + 1] * scale))
    columns = halves(jnp.concatenate(columns + [jnp.zeros((8 - HEADS, count), F32)], axis=0))
    grad_ref[:, 0:CH] = wide_product(nn, halves(jnp.concatenate(grads, axis=1)), keys)
    grad_ref[:, CH : 2 * CH] = wide_product(tn, halves(jnp.concatenate(grads, axis=0)), queries)
    grad_ref[:, 2 * CH :] = wide_product(tn, columns, halves(seeds))
    mixed = wide_product(nn, columns, values)
    mixed = jnp.sum(jnp.where(lane == iota((8, CH), 0), mixed, 0.0), axis=0, keepdims=True)
    high = mixed.astype(BF16).astype(F32)
    low = mixed - high
    rows = iota((16, LANES), 0)
    packed = jnp.zeros((16, LANES), F32)
    for i, part in enumerate((high[:, :LANES], high[:, LANES:], low[:, :LANES], low[:, LANES:])):
        packed = jnp.where(rows == i, part, packed)
    emb_ref[...] = packed.astype(BF16)

    grads = halves(grad_ref[rows_of(gz, core)])
    grad = wide_product(nt, grads, (high_w[...], low_w[...]))
    grad = grad.astype(BF16).astype(F32)
    pooled = pooled_ref[...]
    inv = lax.rsqrt(jnp.mean(pooled * pooled, axis=-1, keepdims=True) + 1e-05)
    unit = pooled * inv
    back = inv * (grad - unit * jnp.mean(grad * unit, axis=-1, keepdims=True))
    cell = (back * (1.0 / TILE_CELLS)).astype(BF16)
    spot, row = iota((COLS, 16), 0), iota((COLS, 16), 1)
    expand = ((spot // 16 == row % 8) & (spot % 2 == row // 8)).astype(F32).astype(BF16)
    taps = nt(cell, strided[...].reshape(4 * CH, CH))
    for band in range(2):
        here = taps[8 * band : 8 * band + 8]
        both = [
            jnp.concatenate([here[:, (2 * a + b) * CH : (2 * a + b + 1) * CH] for a in range(2)], axis=1)
            for b in range(2)
        ]
        high, low = halves(jnp.concatenate(both, axis=0))
        spread = nn(expand, high) + nn(expand, low)
        for a in range(2):
            spread_ref[band * 2 + a] = spread[:, a * CH : (a + 1) * CH]


GROUPS = (6, 10, 16)


def weight_body(
    spread, slope_a, slope_b, edge, side, turned, even, odd,
    wide, keep_ref, give_ref, even_ref, odd_ref, left_ref, right_ref, total, first, last,
):
    first[...] = jnp.zeros_like(first)
    last[...] = jnp.zeros_like(last)

    def build(r):
        if r in (0, ROWS - 1):
            slope = edge[r // HALF].astype(F32)
        else:
            slope = (slope_a, slope_b)[r // HALF][r % HALF].astype(F32)
            slope = with_last(with_first(slope, side[0, r : r + 1]), side[1, r : r + 1])
        grad = (spread[(r // HALF) * 2 + r % 2] * slope).astype(BF16)
        here = slice(r * COLS, (r + 1) * COLS)
        wide[here, 2 * CH :], wide[here, 0:CH] = neighbours(grad)
        wide[here, CH : 2 * CH] = grad
        full = grad.astype(F32)
        for a in range(3):
            first[a, r + a : r + a + 1] = full[0:1]
            last[a, r + a : r + a + 1] = full[COLS - 1 :]

    is_one = is_odd("core")
    left, right = (part.astype(BF16) for part in sides(even, odd))

    def put(part, a, b):
        if b == 0:
            part += tn(left, first[a].astype(BF16))
        if b == 2:
            part += tn(right, last[a].astype(BF16))
        low, high = part[:, :LANES], part[:, LANES:]
        at = slice((3 * a + b) * CH, (3 * a + b + 1) * CH)
        keep_ref[at] = jnp.where(is_one, high, low).astype(BF16)
        give_ref[at] = jnp.where(is_one, low, high).astype(BF16)

    for r in range(GROUPS[0]):
        build(r)
    start = 0
    for g, count in enumerate(GROUPS):
        here = slice(start * COLS, (start + count) * COLS)
        near = [turned[:, (start + a) * COLS : (start + a + count) * COLS] for a in range(3)]
        near = jnp.concatenate(near, axis=0)
        start += count
        ahead = GROUPS[g + 1] if g + 1 < len(GROUPS) else 0
        for b in range(3):
            part = slice(b * CH, (b + 1) * CH)
            result = nn(near, wide[here, part])
            if g > 0:
                result += total[:, part]
            if ahead:
                total[:, part] = result
            for r in range(ahead * b // 3, ahead * (b + 1) // 3):
                build(start + r)
            if not ahead:
                for a in range(3):
                    put(result[a * CH : (a + 1) * CH], a, b)

    centre = slice(CH, 2 * CH)
    order_rows(wide[0:COLS, centre], wide[(ROWS - 1) * COLS :, centre], even_ref, odd_ref)
    left_ref[...] = first[1].astype(BF16)
    right_ref[...] = last[1].astype(BF16)


def order_rows(first, last, even_ref, odd_ref):
    odd = is_odd("gy")
    even_ref[0] = jnp.where(odd, first, last)
    odd_ref[0] = jnp.where(odd, last, first)


def back_taps(weight, taps):
    return jnp.concatenate([weight[tap] for tap in taps], axis=1)


def input_blocks(wide, weight, first, blocks, prods, finish, send=None):
    for block in range(blocks + 1):
        if block < blocks:
            at = first + STEP * block
            near = [wide[(at + step) * COLS : (at + step + STEP) * COLS] for step in (1, 0, -1)]
            prods[block % 2][...] = nt(jnp.concatenate(near, axis=1), back_taps(weight, range(9)))
        if block > 0:
            at = first + STEP * (block - 1)
            for j in range(STEP):
                finish(at + j, prods[(block - 1) % 2][j * COLS : (j + 1) * COLS])
            if send is not None:
                send(at, STEP)


UPPER = 2 * STEP


def upper_body(wide, spread, weight, done, raw_ref, prod_a, prod_b):
    def finish(r, prod):
        value = spread[r % 2] + prod
        done[r - 1] = value.astype(BF16)
        raw_ref[0, r : r + 1] = value[0:1]
        raw_ref[1, r : r + 1] = value[COLS - 1 :]

    input_blocks(wide, weight, 1, UPPER // STEP, (prod_a, prod_b), finish)


def lower_body(
    wide, top, bot, even, odd, spread, weight, upper, raw, out, prod_a, prod_b, side32, added, done, fixed, sems
):
    started = []

    def start(source, target):
        started.append(pltpu.make_async_copy(source, target, sems.at[len(started)]))
        started[-1].start()

    start(upper.at[:, 16 : COLS - 16], out.at[1 : UPPER + 1, 16 : COLS - 16])
    for i, whole in enumerate(sides(even, odd)):
        side32[...] = whole
        near = [side32[2 - a : 2 - a + ROWS].astype(BF16) for a in range(3)]
        taps = back_taps(weight, [3 * a + 2 - 2 * i for a in range(3)])
        added[i] = nt(jnp.concatenate(near, axis=1), taps)

    small = iota((16, CH), 0)
    for i in range(2):
        at = (COLS - 16) * i
        for r in range(1, UPPER + 1):
            value = raw[i, r : r + 1] + added[i, r : r + 1]
            old = upper[r - 1, at : at + 16].astype(F32)
            fixed[i, r - 1] = jnp.where(small == 15 * i, value, old).astype(BF16)
        start(fixed.at[i], out.at[1 : UPPER + 1, at : at + 16])

    def place(r):
        return r - UPPER if r else 0

    def finish(r, prod):
        prod = with_first(prod, prod[0:1] + added[0, r : r + 1])
        prod = with_last(prod, prod[COLS - 1 :] + added[1, r : r + 1])
        done[place(r)] = (spread[(r // HALF) * 2 + r % 2] + prod).astype(BF16)

    def send(first, count):
        start(done.at[place(first) : place(first) + count], out.at[first : first + count])

    input_blocks(wide, weight, UPPER + 1, (ROWS - 2 - UPPER) // STEP, (prod_a, prod_b), finish, send)

    def row(r):
        return wide[r * COLS : (r + 1) * COLS]

    def outside(one):
        left, right = neighbours(one[0])
        return jnp.concatenate([right, one[0], left], axis=1)

    def pair(one, two):
        return jnp.concatenate([one, two], axis=0)

    near = [pair(row(1), outside(bot)), pair(row(0), row(ROWS - 1)), pair(outside(top), row(ROWS - 2))]
    both = nt(jnp.concatenate(near, axis=1), back_taps(weight, range(9)))
    for i, r in enumerate((0, ROWS - 1)):
        finish(r, both[i * COLS : (i + 1) * COLS])
        send(r, 1)
    for one in started:
        one.wait()


def add_up(refs, rows):
    total = refs[0][0:rows].astype(F32)
    for one in refs[1:]:
        total += one[0:rows].astype(F32)
    return total.astype(BF16)


def deal(total_ref, outs, size, axis):
    for k, out in enumerate(reversed(outs)):
        at = lax.bitwise_xor(lax.axis_index(axis), k) * size
        out[0:size] = total_ref[pl.ds(pl.multiple_of(at, 16), size)]


def chip_sum_body(one, two, emb, *refs):
    outs, total_ref = refs[:-1], refs[-1]
    rows = one.shape[0]
    size = rows // len(outs)
    total_ref[...] = add_up((one, two), rows)
    deal(total_ref, outs, size, "gy")
    for out in outs:
        out[size:] = emb[...]


def band_sum_body(*refs, terms, norm_scale):
    outs, emb_ref, total_ref = refs[terms:-2], refs[-2], refs[-1]
    rows = total_ref.shape[0]
    total_ref[...] = add_up(refs[:terms], rows)
    deal(total_ref, outs, rows // len(outs), "gz")
    embs = []
    for one in (refs[0], *refs[terms - 1 : 0 : -1]):
        part = one[rows : rows + 16].astype(F32)
        embs.append(part[0:2] + part[2:4])
    while len(embs) > 1:
        embs = [a + b for a, b in zip(embs[0::2], embs[1::2])]
    emb_ref[:, 0:LANES] = embs[0][0:1] * norm_scale
    emb_ref[:, LANES:] = embs[0][1:2] * norm_scale


def last_sum_body(*refs):
    refs[-1][...] = add_up(refs[:-1], refs[-1].shape[0])


def stack_body(*refs):
    for i, one in enumerate(refs[:-1]):
        refs[-1][i] = one[...]


def half_body(array, *refs, other):
    grad_ref, buf, sems = refs[-3:]
    gy, gz, core = (lax.axis_index(name) for name in ("gy", "gz", "core"))
    bands, depth, share = array.shape[:3]
    half = 1 - core if other else core
    lanes = pl.ds(pl.multiple_of(half * LANES, LANES), LANES)
    started = []
    for k in range(bands):
        first = lax.bitwise_xor(gy, k) * (depth * share)
        for j in range(depth):
            at = first + lax.bitwise_xor(gz, j) * share
            buf[pl.ds(pl.multiple_of(at, 16), share)] = array[k, j].astype(F32) * (1.0 / loss_scale)
        here = pl.ds(pl.multiple_of(first, 16), depth * share)
        started.append(pltpu.make_async_copy(buf.at[here], grad_ref.at[here, lanes], sems.at[k]))
        started[-1].start()
    for one in started:
        one.wait()


SMEM = pl.BlockSpec(memory_space=pltpu.SMEM)
VMEM = pl.BlockSpec(memory_space=pltpu.VMEM)
HBM = pl.BlockSpec(memory_space=pltpu.HBM)


def run(body, args, outs, scratch=(), flops=1 << 20, mib=8, far=(), **rest):
    specs = [HBM if i in far else SMEM if a.dtype == jnp.int32 else VMEM for i, a in enumerate(args)]
    return pl.pallas_call(
        body,
        in_specs=specs,
        out_shape=outs,
        scratch_shapes=list(scratch),
        compiler_params=pltpu.CompilerParams(vmem_limit_bytes=mib << 20),
        cost_estimate=pl.CostEstimate(flops=flops, bytes_accessed=1 << 20, transcendentals=0),
        **rest,
    )(*args)


def per_device(features, tissue, owner_map, w_conv, w_stride, w_query, w_key, w_value, cotangent):
    gy_count, gz_count, cores = lax.axis_size("gy"), lax.axis_size("gz"), lax.axis_size("core")
    gx_count, chips = gz_count * cores, gy_count * gz_count
    across = ("gz", "core")
    norm_scale = 1.0 / math.sqrt(16 * gy_count * gx_count)
    swap = [(i, i ^ 1) for i in range(cores)]

    def pairs(value, axis, count, odd):
        low = range(odd, count - 1, 2)
        return lax.ppermute(value, axis, [(i, i + 1) for i in low] + [(i + 1, i) for i in low])

    def others(values, axis, count):
        got = [
            lax.ppermute(values[k - 1], axis, [(i, i ^ k) for i in range(count)])
            for k in range(count - 1, 0, -1)
        ]
        return got[::-1]

    column = shape((HALO, CH), BF16)
    line = shape((1, COLS, CH), BF16)

    def row_halos(even, odd):
        return pairs(even, "gy", gy_count, 0), pairs(odd, "gy", gy_count, 1)

    def corners(left, right, even, odd):
        return run(corner_body, (left, right, even, odd), [line, line, column, column], mib=1)

    def column_halos(even, odd):
        return pairs(even, across, gx_count, 0), pairs(odd, across, gx_count, 1)

    conv_flops = 2 * ROWS * COLS * 9 * CH * CH
    prod = pltpu.VMEM((STEP * COLS, CH), F32)
    side32 = pltpu.VMEM((HALO, CH), F32)
    half_block = shape((HALF, COLS, CH), BF16)

    def forward(band, weight):
        return run(
            lambda *refs: forward_body(*refs, band=band),
            (tissue, features, weight),
            [half_block, shape((2, COLS, CH), F32), shape((6, HALF, CH), F32)],
            [pltpu.VMEM(((HALF + 1) * COLS, 2 * CH), BF16), prod, prod],
            flops=conv_flops // 2,
            mib=16,
        )

    rows = run(
        order_body, (features[:1], features[ROWS - 1 :]), [line, line], flops=conv_flops, mib=2
    )
    outer = run(columns_body, (features,), [column, column], mib=2)
    even, odd = row_halos(*rows)
    slope_a, sums_a, cols_a = forward(0, w_conv)
    even, odd, cols_a = lax.optimization_barrier((even, odd, cols_a))
    top, bot, even, odd = corners(*outer, even, odd)
    weight_b, even = lax.optimization_barrier((w_conv, even))
    even, odd = column_halos(even, odd)
    slope_b, sums_b, cols_b = forward(1, weight_b)
    pooled, token, edge, side = run(
        border_body,
        (
            tissue, features, w_conv, sums_a, sums_b, cols_a, cols_b, top, bot, even, odd, w_stride,
            owner_map.reshape(16),
        ),
        [
            shape((16, CH), F32),
            shape((16, CH + LANES), BF16),
            shape((2, COLS, CH), BF16),
            shape((2, ROWS, CH), F32),
        ],
        [side32],
        flops=conv_flops // 8,
        mib=12,
    )
    def stacked(terms):
        return run(stack_body, terms, shape((len(terms),) + terms[0].shape, BF16), mib=4)

    turned, high_w, low_w = run(
        turn_body,
        (features, top, bot, w_query, w_key, w_value, token),
        [shape((CH, (ROWS + 2) * COLS), BF16), shape((CH, 3 * CH), BF16), shape((CH, 3 * CH), BF16)],
        flops=conv_flops // 4,
        mib=12,
    )
    tokens = stacked([token] + others([token] * (gz_count - 1), "gz", gz_count))
    tokens, high_w = lax.optimization_barrier((tokens, high_w))
    count = 16 * gx_count
    spread, emb = run(
        lambda *refs: attention_body(*refs, seed_scale=loss_scale * norm_scale),
        (tokens, lax.ppermute(tokens, "core", swap), pooled, high_w, low_w, cotangent.reshape(1, CH), w_stride),
        [shape((4, COLS, CH), F32), shape((16, LANES), BF16)],
        [pltpu.VMEM((count, CH + LANES), BF16), pltpu.VMEM((count, 3 * CH), F32)],
        flops=1 << 30,
        mib=12,
    )
    border = pltpu.VMEM((3, HALO, CH), F32)
    wide, keep, give, *outer = run(
        weight_body,
        (spread, slope_a, slope_b, edge, side, turned, even, odd),
        [
            shape((ROWS * COLS, 3 * CH), BF16),
            shape((9 * CH, LANES), BF16),
            shape((9 * CH, LANES), BF16),
            line,
            line,
            column,
            column,
        ],
        [pltpu.VMEM((3 * CH, 3 * CH), F32), border, border],
        flops=conv_flops,
        mib=20,
    )

    share = -(-9 * CH // (16 * chips)) * 16
    spare = share * chips - 9 * CH
    taken = lax.ppermute(give, "core", swap)
    pre_rows = row_halos(*outer[:2])
    if spare:
        keep, taken = (jnp.pad(a, ((0, spare), (0, 0))) for a in (keep, taken))

    whole_rows = share * chips
    band_rows = share * gz_count
    parts = run(
        chip_sum_body,
        (keep, taken, emb),
        [shape((band_rows + 16, LANES), BF16)] * gy_count,
        [pltpu.VMEM((whole_rows, LANES), BF16)],
        mib=6,
    )[::-1]
    *parts, wide_upper = lax.optimization_barrier((*parts, wide))
    upper, raw = run(
        upper_body,
        (wide_upper, spread, w_conv),
        [shape((UPPER, COLS, CH), BF16), shape((2, HALF, CH), F32)],
        [prod, prod],
        flops=conv_flops // 3,
        mib=12,
    )
    raw, *outer = lax.optimization_barrier((raw, *outer[2:], *pre_rows))
    parts = [parts[0]] + others(parts[1:], "gy", gy_count)[::-1]
    top, bot, even, odd = corners(*outer)
    even, odd = column_halos(even, odd)
    *parts, raw, even, odd = lax.optimization_barrier((*parts, raw, even, odd))
    embedding, *parts = run(
        lambda *refs: band_sum_body(*refs, terms=gy_count, norm_scale=norm_scale),
        parts,
        [shape((share, LANES), BF16)] * gz_count + [shape((1, CH), F32)],
        [pltpu.VMEM((band_rows, LANES), BF16)],
        mib=4,
    )[::-1]
    parts = [parts[0]] + others(parts[1:], "gz", gz_count)[::-1]
    mine = run(last_sum_body, parts, shape((share, LANES), BF16), mib=2)
    row = stacked([mine] + others([mine] * (gz_count - 1), "gz", gz_count))
    row, wide_lower = lax.optimization_barrier((row, wide))
    input_grad = run(
        lower_body,
        (wide_lower, top, bot, even, odd, spread, w_conv, upper, raw),
        shape((ROWS, COLS, CH), BF16),
        [
            prod,
            prod,
            side32,
            pltpu.VMEM((2, ROWS, CH), F32),
            pltpu.VMEM((ROWS - UPPER, COLS, CH), BF16),
            pltpu.VMEM((2, UPPER, 16, CH), BF16),
            pltpu.SemaphoreType.DMA((BLOCKS + 6,)),
        ],
        flops=conv_flops // 2,
        mib=16,
        out_specs=HBM,
    )
    planes = [row] + others([row] * (gy_count - 1), "gy", gy_count)
    *planes, input_grad = lax.optimization_barrier((*planes, input_grad))
    plane = stacked(planes)
    other = lax.ppermute(plane, "core", swap)
    whole = shape((whole_rows, CH), F32)
    buffers = [pltpu.VMEM((whole_rows, LANES), F32), pltpu.SemaphoreType.DMA((gy_count,))]
    half_grad = run(
        lambda *refs: half_body(*refs, other=False), (plane,), whole, buffers, mib=4, out_specs=HBM
    )
    conv_grad = run(
        lambda *refs: half_body(*refs, other=True),
        (other, half_grad),
        whole,
        buffers,
        mib=4,
        far=(1,),
        out_specs=HBM,
        input_output_aliases={1: 0},
    )
    return embedding.reshape(CH), input_grad, conv_grad[: 9 * CH].reshape(9, CH, CH)


def solution(mesh):
    sizes = mesh.devices.shape
    split = Mesh(mesh.devices.reshape(sizes[0], sizes[1] // 2, 2), ("gy", "gz", "core"))
    gx = ("gz", "core")
    in_specs = (P("gy", gx, None), P("gy", gx), P("gy", gx, None, None), P(), P(), P(), P(), P(), P())
    out_specs = (P(), P("gy", gx, None), P())
    return jax.shard_map(per_device, mesh=split, in_specs=in_specs, out_specs=out_specs, check_vma=False)
```

```python
import math

import jax
import jax.numpy as jnp
from jax import lax
from jax.experimental import pallas as pl
from jax.experimental.pallas import tpu as pltpu
from jax.sharding import Mesh, PartitionSpec as P

HEADS = 4
F32 = jnp.float32
BF16 = jnp.bfloat16

attention_bias = -1.0
loss_scale = 512.0

ROWS = 32
COLS = 128
CH = 256
HALO = 48
LANES = 128
STEP = 5
TILE_CELLS = 64


def shape(dims, dtype):
    return jax.ShapeDtypeStruct(dims, dtype)


def nt(left, right):
    return lax.dot_general(left, right, (((1,), (1,)), ((), ())), preferred_element_type=F32)


def tn(left, right):
    return lax.dot_general(left, right, (((0,), (0,)), ((), ())), preferred_element_type=F32)


def nn(left, right):
    return jnp.dot(left, right, preferred_element_type=F32)


def halves(value):
    high = value.astype(BF16)
    return high, (value - high.astype(F32)).astype(BF16)


def wide_product(product, left, right):
    (a, b), (c, d) = left, right
    return product(a, c) + (product(a, d) + product(b, c))


def iota(dims, axis):
    return lax.broadcasted_iota(jnp.int32, dims, axis)


def gate_of(value):
    return 0.5 * jnp.tanh(0.5 * value) + 0.5


def is_odd(axis):
    return lax.axis_index(axis) % 2 == 1


def order_body(first_ref, last_ref, even_ref, odd_ref):
    order_rows(first_ref[0], last_ref[0], even_ref, odd_ref)


def columns_body(block, left_ref, right_ref):
    row, spot = iota((HALO, ROWS * 16), 0), iota((HALO, ROWS * 16), 1)
    for out, at, place in ((left_ref, 0, 0), (right_ref, COLS - 16, 15)):
        pick = (spot == (row - 1) * 16 + place).astype(F32).astype(BF16)
        out[...] = nn(pick, block[:, at : at + 16].reshape(ROWS * 16, CH)).astype(BF16)


def corner_body(left, right, even, odd, top_ref, bot_ref, even_ref, odd_ref):
    low = is_odd("gy")
    top_ref[0] = jnp.where(low, even[0], odd[0])
    bot_ref[0] = jnp.where(low, odd[0], even[0])
    row = iota((HALO, CH), 0)
    whole = []
    for side, at in ((left, 0), (right, COLS - 16)):
        part = slice(0, 1) if at == 0 else slice(15, 16)
        above = top_ref[0, at : at + 16].astype(F32)[part]
        below = bot_ref[0, at : at + 16].astype(F32)[part]
        whole.append(jnp.where(row == 0, above, jnp.where(row == ROWS + 1, below, side[...].astype(F32))))
    high = is_odd("core")
    even_ref[...] = jnp.where(high, whole[0], whole[1]).astype(BF16)
    odd_ref[...] = jnp.where(high, whole[1], whole[0]).astype(BF16)


def sides(even, odd):
    high = is_odd("core")
    one, two = even[...].astype(F32), odd[...].astype(F32)
    return jnp.where(high, one, two), jnp.where(high, two, one)


def forward_taps(weight, b):
    return jnp.concatenate([weight[3 * a + b] for a in range(3)], axis=0)


HALF = ROWS // 2
BLOCKS = (HALF - 1) // STEP
PARTS = ((3, 5, 5, 2), (2, 2, 2, 2, 2, 2, 2, 1))


def with_first(wide, value):
    start = jnp.where(iota((8, wide.shape[1]), 0) == 0, value, wide[0:8])
    return jnp.concatenate([start, wide[8:]], axis=0)


def with_last(wide, value):
    end = jnp.where(iota((8, wide.shape[1]), 0) == 7, value, wide[COLS - 8 :])
    return jnp.concatenate([wide[: COLS - 8], end], axis=0)


def neighbours(row):
    wide = row.astype(F32)
    left = with_first(pltpu.roll(wide, 1, 0), 0.0)
    right = with_last(pltpu.roll(wide, COLS - 1, 0), 0.0)
    return left.astype(BF16), right.astype(BF16)


HALVES = (slice(0, LANES), slice(LANES, CH))


def silu_pair(value, half_mask):
    half = 0.5 * value
    bend = jnp.tanh(half)
    kept = (1.0 + bend) * half_mask
    return value * kept, kept * (1.0 + half * (1.0 - bend))


def forward_body(flags_ref, feat, weight, slope_ref, sums, cols, wide, prod_a, prod_b, *, band):
    sums[...] = jnp.zeros_like(sums)
    base = (HALF - 1) * band
    halves_of_mask = [0.5 * flags_ref[band, tile].astype(F32) for tile in range(8)]

    def build(i):
        here = slice(i * COLS, (i + 1) * COLS)
        for lanes in HALVES:
            left, right = neighbours(feat[base + i, :, lanes])
            wide[here, lanes] = left
            wide[here, lanes.start + CH : lanes.stop + CH] = right

    def around(start, count):
        taken = []
        for a in range(3):
            here = slice((start + a) * COLS, (start + a + count) * COLS)
            rows = feat[base + start + a : base + start + a + count].reshape(count * COLS, CH)
            taken += [wide[here, 0:CH], rows, wide[here, CH:]]
        return jnp.concatenate(taken, axis=1)

    def finish(r, prod, first):
        at = r - HALF * band
        for tile in range(8):
            here = slice(16 * tile, 16 * tile + 16)
            value = prod[first + 16 * tile : first + 16 * tile + 16]
            pixel = feat[r, here].astype(F32)
            bent, slope = silu_pair(value, halves_of_mask[tile])
            summed = pixel + bent
            slope_ref[at, here] = slope.astype(BF16)
            sums[r % 2, here] += summed
            if tile in (0, 7):
                edge = slice(0, 1) if tile == 0 else slice(15, 16)
                for i, part in enumerate((value, summed, pixel)):
                    cols[2 * i + tile // 7, at : at + 1] = part[edge]

    prods = (prod_a, prod_b)
    parts = PARTS[band]
    built, done = parts[0] + 2, 0
    for i in range(built):
        build(i)
    for block in range(len(parts) + 1):
        start = sum(parts[:block])
        if block < len(parts):
            prods[block % 2][0 : parts[block] * COLS] = nn(
                around(start, parts[block]), weight[...].reshape(9 * CH, CH)
            )
        ahead = min(HALF + 1, sum(parts[: block + 2]) + 2)
        for j in range(STEP):
            if done < start:
                finish(base + 1 + done, prods[(block - 1) % 2], (done - sum(parts[: block - 1])) * COLS)
                done += 1
            if built < ahead:
                build(built)
                built += 1


def border_body(
    flags_ref, feat, weight, sums_a, sums_b, cols_a, cols_b, top, bot, even, odd, strided, owner_ref,
    pooled_ref, token_ref, edge_ref, side_ref, side32,
):
    added = []
    cols = [jnp.concatenate([cols_a[i], cols_b[i]], axis=0) for i in range(6)]
    for i, whole in enumerate(sides(even, odd)):
        side32[...] = whole
        near = [side32[a : a + ROWS].astype(BF16) for a in range(3)]
        added.append(nn(jnp.concatenate(near, axis=1), forward_taps(weight, 2 * i)))

    def pair(one, two):
        return jnp.concatenate([one, two], axis=0)

    taken = jnp.concatenate(
        [pair(top[0], feat[ROWS - 2]), pair(feat[0], feat[ROWS - 1]), pair(feat[1], bot[0])], axis=1
    )
    low, mid, high = (nn(taken, forward_taps(weight, b)) for b in range(3))
    rows = []
    for i, r in enumerate((0, ROWS - 1)):
        part = slice(i * COLS, (i + 1) * COLS)
        before = with_first(pltpu.roll(low[part], 1, 0), added[0][r : r + 1])
        after = with_last(pltpu.roll(high[part], COLS - 1, 0), added[1][r : r + 1])
        value = mid[part] + before + after
        keep = jnp.concatenate(
            [0.5 * jnp.full((16, CH), flags_ref[i, t], jnp.int32).astype(F32) for t in range(8)], axis=0
        )
        bent, slope = silu_pair(value, keep)
        edge_ref[i] = slope.astype(BF16)
        rows.append(feat[r].astype(F32) + bent)

    line = iota((ROWS, CH), 0)
    deltas = []
    for i in range(2):
        tile = 7 * i
        keep = 0.5 * jnp.where(line < ROWS // 2, flags_ref[0, tile], flags_ref[1, tile]).astype(F32)
        bent, side_ref[i] = silu_pair(cols[i] + added[i], keep)
        inside = (line > 0) & (line < ROWS - 1)
        deltas.append(jnp.where(inside, cols[4 + i] + bent - cols[2 + i], 0.0))

    row, spot = iota((16, COLS), 0), iota((16, COLS), 1)
    pick = ((spot // 16 == row % 8) & (spot % 2 == row // 8)).astype(F32).astype(BF16)
    place = iota((16, CH), 0)
    parts = {}
    for band in range(2):
        for a in range(2):
            total = (sums_a, sums_b)[band][a]
            if band == a:
                total += rows[band]
            high, low = halves(total)
            part = nn(pick, high) + nn(pick, low)
            mine = (line // 16 == band) & (line % 2 == a)
            for i in range(2):
                delta = jnp.sum(jnp.where(mine, deltas[i], 0.0), axis=0, keepdims=True)
                part += jnp.where(place == 15 * i, delta, 0.0)
            parts[band, a] = part
    taken = [
        jnp.concatenate([parts[band, a][8 * b : 8 * b + 8] for band in range(2)], axis=0)
        for a in range(2)
        for b in range(2)
    ]
    high, low = halves(jnp.concatenate(taken, axis=1))
    flat = strided[...].reshape(4 * CH, CH)
    pooled = (nn(high, flat) + nn(low, flat)) * (1.0 / TILE_CELLS)
    pooled_ref[...] = pooled
    normed = pooled * lax.rsqrt(jnp.mean(pooled * pooled, axis=-1, keepdims=True) + 1e-05)
    token_ref[:, 0:CH] = normed.astype(BF16)
    owner = jnp.full((16, LANES), -1, jnp.int32)
    for tile in range(16):
        named = jnp.where(flags_ref[tile // 8, tile % 8] != 0, owner_ref[tile], -1)
        owner = jnp.where(iota((16, LANES), 0) == tile, named, owner)
    token_ref[:, CH:] = (owner == iota((16, LANES), 1)).astype(F32).astype(BF16)


def turn_body(feat, top, bot, w_query, w_key, w_value, token, turned_ref, high_ref, low_ref):
    turned_ref[:, 0:COLS] = top[0].T
    turned_ref[:, (ROWS + 1) * COLS :] = bot[0].T

    @pl.loop(0, ROWS // 4)
    def _(i):
        for j in range(4):
            here = pl.multiple_of((4 * i + j + 1) * COLS, COLS)
            turned_ref[:, pl.ds(here, COLS)] = feat[4 * i + j].T

    for i, one in enumerate((w_query, w_key, w_value)):
        high, low = halves(one[...])
        high_ref[:, i * CH : (i + 1) * CH] = high
        low_ref[:, i * CH : (i + 1) * CH] = low


def attention_body(
    mine, other, pooled_ref, high_w, low_w, cot, strided, spread_ref, emb_ref, band, grad_ref, *, seed_scale
):
    gz, core = lax.axis_index("gz"), lax.axis_index("core")

    def rows_of(depth, other):
        return pl.ds(pl.multiple_of(depth * 32 + other * 16, 16), 16)

    for k in range(mine.shape[0]):
        depth = lax.bitwise_xor(gz, k)
        band[rows_of(depth, core)] = mine[k]
        band[rows_of(depth, 1 - core)] = other[k]
    count = band.shape[0]
    tokens, group = band[:, 0:CH], band[:, CH:]
    pair = nt(group, group)
    pairs = jnp.concatenate([pair] * HEADS, axis=0)
    projected = nn(tokens, high_w[...]) + nn(tokens, low_w[...])
    query, key, value = (projected[:, i * CH : (i + 1) * CH] for i in range(3))
    lane = iota((1, CH), 1) // (CH // HEADS)
    scale = 1.0 / math.sqrt(CH // HEADS)

    def by_head(array):
        return jnp.concatenate([jnp.where(lane == h, array, 0.0) for h in range(HEADS)], axis=0)

    queries, keys = halves(by_head(query)), halves(by_head(key))
    gate = gate_of(wide_product(nt, queries, halves(key)) * scale + attention_bias)
    weights = gate * pairs
    seed = cot[...] * seed_scale
    seeds = jnp.where(lane == iota((8, CH), 0), seed, 0.0)
    values = halves(value)
    along = wide_product(nt, halves(seeds), values)
    columns, grads = [], []
    for h in range(HEADS):
        part = slice(h * count, (h + 1) * count)
        columns.append(jnp.sum(weights[part], axis=0, keepdims=True))
        grads.append(weights[part] * (1.0 - gate[part]) * (along[h : h + 1] * scale))
    columns = halves(jnp.concatenate(columns + [jnp.zeros((8 - HEADS, count), F32)], axis=0))
    grad_ref[:, 0:CH] = wide_product(nn, halves(jnp.concatenate(grads, axis=1)), keys)
    grad_ref[:, CH : 2 * CH] = wide_product(tn, halves(jnp.concatenate(grads, axis=0)), queries)
    grad_ref[:, 2 * CH :] = wide_product(tn, columns, halves(seeds))
    mixed = wide_product(nn, columns, values)
    mixed = jnp.sum(jnp.where(lane == iota((8, CH), 0), mixed, 0.0), axis=0, keepdims=True)
    high = mixed.astype(BF16).astype(F32)
    low = mixed - high
    rows = iota((16, LANES), 0)
    packed = jnp.zeros((16, LANES), F32)
    for i, part in enumerate((high[:, :LANES], high[:, LANES:], low[:, :LANES], low[:, LANES:])):
        packed = jnp.where(rows == i, part, packed)
    emb_ref[...] = packed.astype(BF16)

    grads = halves(grad_ref[rows_of(gz, core)])
    grad = wide_product(nt, grads, (high_w[...], low_w[...]))
    grad = grad.astype(BF16).astype(F32)
    pooled = pooled_ref[...]
    inv = lax.rsqrt(jnp.mean(pooled * pooled, axis=-1, keepdims=True) + 1e-05)
    unit = pooled * inv
    back = inv * (grad - unit * jnp.mean(grad * unit, axis=-1, keepdims=True))
    cell = (back * (1.0 / TILE_CELLS)).astype(BF16)
    spot, row = iota((COLS, 16), 0), iota((COLS, 16), 1)
    expand = ((spot // 16 == row % 8) & (spot % 2 == row // 8)).astype(F32).astype(BF16)
    taps = nt(cell, strided[...].reshape(4 * CH, CH))
    for band in range(2):
        here = taps[8 * band : 8 * band + 8]
        both = [
            jnp.concatenate([here[:, (2 * a + b) * CH : (2 * a + b + 1) * CH] for a in range(2)], axis=1)
            for b in range(2)
        ]
        high, low = halves(jnp.concatenate(both, axis=0))
        spread = nn(expand, high) + nn(expand, low)
        for a in range(2):
            spread_ref[band * 2 + a] = spread[:, a * CH : (a + 1) * CH]


GROUPS = (6, 10, 16)


def weight_body(
    spread, slope_a, slope_b, edge, side, turned, even, odd,
    wide, keep_ref, give_ref, even_ref, odd_ref, left_ref, right_ref, total, first, last,
):
    first[...] = jnp.zeros_like(first)
    last[...] = jnp.zeros_like(last)

    def build(r):
        if r in (0, ROWS - 1):
            slope = edge[r // HALF].astype(F32)
        else:
            slope = (slope_a, slope_b)[r // HALF][r % HALF].astype(F32)
            slope = with_last(with_first(slope, side[0, r : r + 1]), side[1, r : r + 1])
        grad = (spread[(r // HALF) * 2 + r % 2] * slope).astype(BF16)
        here = slice(r * COLS, (r + 1) * COLS)
        wide[here, 2 * CH :], wide[here, 0:CH] = neighbours(grad)
        wide[here, CH : 2 * CH] = grad
        full = grad.astype(F32)
        for a in range(3):
            first[a, r + a : r + a + 1] = full[0:1]
            last[a, r + a : r + a + 1] = full[COLS - 1 :]

    is_one = is_odd("core")
    left, right = (part.astype(BF16) for part in sides(even, odd))

    def put(part, a, b):
        if b == 0:
            part += tn(left, first[a].astype(BF16))
        if b == 2:
            part += tn(right, last[a].astype(BF16))
        low, high = part[:, :LANES], part[:, LANES:]
        at = slice((3 * a + b) * CH, (3 * a + b + 1) * CH)
        keep_ref[at] = jnp.where(is_one, high, low).astype(BF16)
        give_ref[at] = jnp.where(is_one, low, high).astype(BF16)

    for r in range(GROUPS[0]):
        build(r)
    start = 0
    for g, count in enumerate(GROUPS):
        here = slice(start * COLS, (start + count) * COLS)
        near = [turned[:, (start + a) * COLS : (start + a + count) * COLS] for a in range(3)]
        near = jnp.concatenate(near, axis=0)
        start += count
        ahead = GROUPS[g + 1] if g + 1 < len(GROUPS) else 0
        for b in range(3):
            part = slice(b * CH, (b + 1) * CH)
            result = nn(near, wide[here, part])
            if g > 0:
                result += total[:, part]
            if ahead:
                total[:, part] = result
            for r in range(ahead * b // 3, ahead * (b + 1) // 3):
                build(start + r)
            if not ahead:
                for a in range(3):
                    put(result[a * CH : (a + 1) * CH], a, b)

    centre = slice(CH, 2 * CH)
    order_rows(wide[0:COLS, centre], wide[(ROWS - 1) * COLS :, centre], even_ref, odd_ref)
    left_ref[...] = first[1].astype(BF16)
    right_ref[...] = last[1].astype(BF16)


def order_rows(first, last, even_ref, odd_ref):
    odd = is_odd("gy")
    even_ref[0] = jnp.where(odd, first, last)
    odd_ref[0] = jnp.where(odd, last, first)


def back_taps(weight, taps):
    return jnp.concatenate([weight[tap] for tap in taps], axis=1)


def input_blocks(wide, weight, first, blocks, prods, finish, send=None):
    for block in range(blocks + 1):
        if block < blocks:
            at = first + STEP * block
            near = [wide[(at + step) * COLS : (at + step + STEP) * COLS] for step in (1, 0, -1)]
            prods[block % 2][...] = nt(jnp.concatenate(near, axis=1), back_taps(weight, range(9)))
        if block > 0:
            at = first + STEP * (block - 1)
            for j in range(STEP):
                finish(at + j, prods[(block - 1) % 2][j * COLS : (j + 1) * COLS])
            if send is not None:
                send(at, STEP)


UPPER = 2 * STEP


def upper_body(wide, spread, weight, done, raw_ref, prod_a, prod_b):
    def finish(r, prod):
        value = spread[r % 2] + prod
        done[r - 1] = value.astype(BF16)
        raw_ref[0, r : r + 1] = value[0:1]
        raw_ref[1, r : r + 1] = value[COLS - 1 :]

    input_blocks(wide, weight, 1, UPPER // STEP, (prod_a, prod_b), finish)


def lower_body(
    wide, top, bot, even, odd, spread, weight, upper, raw, out, prod_a, prod_b, side32, added, done, fixed, sems
):
    started = []

    def start(source, target):
        started.append(pltpu.make_async_copy(source, target, sems.at[len(started)]))
        started[-1].start()

    start(upper.at[:, 16 : COLS - 16], out.at[1 : UPPER + 1, 16 : COLS - 16])
    for i, whole in enumerate(sides(even, odd)):
        side32[...] = whole
        near = [side32[2 - a : 2 - a + ROWS].astype(BF16) for a in range(3)]
        taps = back_taps(weight, [3 * a + 2 - 2 * i for a in range(3)])
        added[i] = nt(jnp.concatenate(near, axis=1), taps)

    small = iota((16, CH), 0)
    for i in range(2):
        at = (COLS - 16) * i
        for r in range(1, UPPER + 1):
            value = raw[i, r : r + 1] + added[i, r : r + 1]
            old = upper[r - 1, at : at + 16].astype(F32)
            fixed[i, r - 1] = jnp.where(small == 15 * i, value, old).astype(BF16)
        start(fixed.at[i], out.at[1 : UPPER + 1, at : at + 16])

    def place(r):
        return r - UPPER if r else 0

    def finish(r, prod):
        prod = with_first(prod, prod[0:1] + added[0, r : r + 1])
        prod = with_last(prod, prod[COLS - 1 :] + added[1, r : r + 1])
        done[place(r)] = (spread[(r // HALF) * 2 + r % 2] + prod).astype(BF16)

    def send(first, count):
        start(done.at[place(first) : place(first) + count], out.at[first : first + count])

    input_blocks(wide, weight, UPPER + 1, (ROWS - 2 - UPPER) // STEP, (prod_a, prod_b), finish, send)

    def row(r):
        return wide[r * COLS : (r + 1) * COLS]

    def outside(one):
        left, right = neighbours(one[0])
        return jnp.concatenate([right, one[0], left], axis=1)

    def pair(one, two):
        return jnp.concatenate([one, two], axis=0)

    near = [pair(row(1), outside(bot)), pair(row(0), row(ROWS - 1)), pair(outside(top), row(ROWS - 2))]
    both = nt(jnp.concatenate(near, axis=1), back_taps(weight, range(9)))
    for i, r in enumerate((0, ROWS - 1)):
        finish(r, both[i * COLS : (i + 1) * COLS])
        send(r, 1)
    for one in started:
        one.wait()


def add_up(refs, rows):
    total = refs[0][0:rows].astype(F32)
    for one in refs[1:]:
        total += one[0:rows].astype(F32)
    return total.astype(BF16)


def deal(total_ref, outs, size, axis):
    for k, out in enumerate(reversed(outs)):
        at = lax.bitwise_xor(lax.axis_index(axis), k) * size
        out[0:size] = total_ref[pl.ds(pl.multiple_of(at, 16), size)]


def chip_sum_body(one, two, emb, *refs):
    outs, total_ref = refs[:-1], refs[-1]
    rows = one.shape[0]
    size = rows // len(outs)
    total_ref[...] = add_up((one, two), rows)
    deal(total_ref, outs, size, "gy")
    for out in outs:
        out[size:] = emb[...]


def band_sum_body(*refs, terms, norm_scale):
    outs, emb_ref, total_ref = refs[terms:-2], refs[-2], refs[-1]
    rows = total_ref.shape[0]
    total_ref[...] = add_up(refs[:terms], rows)
    deal(total_ref, outs, rows // len(outs), "gz")
    embs = []
    for one in (refs[0], *refs[terms - 1 : 0 : -1]):
        part = one[rows : rows + 16].astype(F32)
        embs.append(part[0:2] + part[2:4])
    while len(embs) > 1:
        embs = [a + b for a, b in zip(embs[0::2], embs[1::2])]
    emb_ref[:, 0:LANES] = embs[0][0:1] * norm_scale
    emb_ref[:, LANES:] = embs[0][1:2] * norm_scale


def last_sum_body(*refs):
    refs[-1][...] = add_up(refs[:-1], refs[-1].shape[0])


def stack_body(*refs):
    for i, one in enumerate(refs[:-1]):
        refs[-1][i] = one[...]


def half_body(array, *refs, other):
    grad_ref, buf, sems = refs[-3:]
    gy, gz, core = (lax.axis_index(name) for name in ("gy", "gz", "core"))
    bands, depth, share = array.shape[:3]
    half = 1 - core if other else core
    lanes = pl.ds(pl.multiple_of(half * LANES, LANES), LANES)
    started = []
    for k in range(bands):
        first = lax.bitwise_xor(gy, k) * (depth * share)
        for j in range(depth):
            at = first + lax.bitwise_xor(gz, j) * share
            buf[pl.ds(pl.multiple_of(at, 16), share)] = array[k, j].astype(F32) * (1.0 / loss_scale)
        here = pl.ds(pl.multiple_of(first, 16), depth * share)
        started.append(pltpu.make_async_copy(buf.at[here], grad_ref.at[here, lanes], sems.at[k]))
        started[-1].start()
    for one in started:
        one.wait()


SMEM = pl.BlockSpec(memory_space=pltpu.SMEM)
VMEM = pl.BlockSpec(memory_space=pltpu.VMEM)
HBM = pl.BlockSpec(memory_space=pltpu.HBM)


def run(body, args, outs, scratch=(), flops=1 << 20, mib=8, far=(), **rest):
    specs = [HBM if i in far else SMEM if a.dtype == jnp.int32 else VMEM for i, a in enumerate(args)]
    return pl.pallas_call(
        body,
        in_specs=specs,
        out_shape=outs,
        scratch_shapes=list(scratch),
        compiler_params=pltpu.CompilerParams(vmem_limit_bytes=mib << 20),
        cost_estimate=pl.CostEstimate(flops=flops, bytes_accessed=1 << 20, transcendentals=0),
        **rest,
    )(*args)


def per_device(features, tissue, owner_map, w_conv, w_stride, w_query, w_key, w_value, cotangent):
    gy_count, gz_count, cores = lax.axis_size("gy"), lax.axis_size("gz"), lax.axis_size("core")
    gx_count, chips = gz_count * cores, gy_count * gz_count
    across = ("gz", "core")
    norm_scale = 1.0 / math.sqrt(16 * gy_count * gx_count)
    swap = [(i, i ^ 1) for i in range(cores)]

    def pairs(value, axis, count, odd):
        low = range(odd, count - 1, 2)
        return lax.ppermute(value, axis, [(i, i + 1) for i in low] + [(i + 1, i) for i in low])

    def others(values, axis, count):
        got = [
            lax.ppermute(values[k - 1], axis, [(i, i ^ k) for i in range(count)])
            for k in range(count - 1, 0, -1)
        ]
        return got[::-1]

    column = shape((HALO, CH), BF16)
    line = shape((1, COLS, CH), BF16)

    def row_halos(even, odd):
        return pairs(even, "gy", gy_count, 0), pairs(odd, "gy", gy_count, 1)

    def corners(left, right, even, odd):
        return run(corner_body, (left, right, even, odd), [line, line, column, column], mib=1)

    def column_halos(even, odd):
        return pairs(even, across, gx_count, 0), pairs(odd, across, gx_count, 1)

    conv_flops = 2 * ROWS * COLS * 9 * CH * CH
    prod = pltpu.VMEM((STEP * COLS, CH), F32)
    side32 = pltpu.VMEM((HALO, CH), F32)
    half_block = shape((HALF, COLS, CH), BF16)

    def forward(band, weight):
        return run(
            lambda *refs: forward_body(*refs, band=band),
            (tissue, features, weight),
            [half_block, shape((2, COLS, CH), F32), shape((6, HALF, CH), F32)],
            [pltpu.VMEM(((HALF + 1) * COLS, 2 * CH), BF16), prod, prod],
            flops=conv_flops // 2,
            mib=16,
        )

    rows = run(
        order_body, (features[:1], features[ROWS - 1 :]), [line, line], flops=conv_flops, mib=2
    )
    outer = run(columns_body, (features,), [column, column], mib=2)
    even, odd = row_halos(*rows)
    slope_a, sums_a, cols_a = forward(0, w_conv)
    even, odd, cols_a = lax.optimization_barrier((even, odd, cols_a))
    top, bot, even, odd = corners(*outer, even, odd)
    weight_b, even = lax.optimization_barrier((w_conv, even))
    even, odd = column_halos(even, odd)
    slope_b, sums_b, cols_b = forward(1, weight_b)
    pooled, token, edge, side = run(
        border_body,
        (
            tissue, features, w_conv, sums_a, sums_b, cols_a, cols_b, top, bot, even, odd, w_stride,
            owner_map.reshape(16),
        ),
        [
            shape((16, CH), F32),
            shape((16, CH + LANES), BF16),
            shape((2, COLS, CH), BF16),
            shape((2, ROWS, CH), F32),
        ],
        [side32],
        flops=conv_flops // 8,
        mib=12,
    )
    def stacked(terms):
        return run(stack_body, terms, shape((len(terms),) + terms[0].shape, BF16), mib=4)

    turned, high_w, low_w = run(
        turn_body,
        (features, top, bot, w_query, w_key, w_value, token),
        [shape((CH, (ROWS + 2) * COLS), BF16), shape((CH, 3 * CH), BF16), shape((CH, 3 * CH), BF16)],
        flops=conv_flops // 4,
        mib=12,
    )
    tokens = stacked([token] + others([token] * (gz_count - 1), "gz", gz_count))
    tokens, high_w = lax.optimization_barrier((tokens, high_w))
    count = 16 * gx_count
    spread, emb = run(
        lambda *refs: attention_body(*refs, seed_scale=loss_scale * norm_scale),
        (tokens, lax.ppermute(tokens, "core", swap), pooled, high_w, low_w, cotangent.reshape(1, CH), w_stride),
        [shape((4, COLS, CH), F32), shape((16, LANES), BF16)],
        [pltpu.VMEM((count, CH + LANES), BF16), pltpu.VMEM((count, 3 * CH), F32)],
        flops=1 << 30,
        mib=12,
    )
    border = pltpu.VMEM((3, HALO, CH), F32)
    wide, keep, give, *outer = run(
        weight_body,
        (spread, slope_a, slope_b, edge, side, turned, even, odd),
        [
            shape((ROWS * COLS, 3 * CH), BF16),
            shape((9 * CH, LANES), BF16),
            shape((9 * CH, LANES), BF16),
            line,
            line,
            column,
            column,
        ],
        [pltpu.VMEM((3 * CH, 3 * CH), F32), border, border],
        flops=conv_flops,
        mib=20,
    )

    share = -(-9 * CH // (16 * chips)) * 16
    spare = share * chips - 9 * CH
    taken = lax.ppermute(give, "core", swap)
    upper, raw = run(
        upper_body,
        (wide, spread, w_conv),
        [shape((UPPER, COLS, CH), BF16), shape((2, HALF, CH), F32)],
        [prod, prod],
        flops=conv_flops // 3,
        mib=12,
    )
    keep, raw = lax.optimization_barrier((keep, raw))
    if spare:
        keep, taken = (jnp.pad(a, ((0, spare), (0, 0))) for a in (keep, taken))

    whole_rows = share * chips
    band_rows = share * gz_count
    parts = run(
        chip_sum_body,
        (keep, taken, emb),
        [shape((band_rows + 16, LANES), BF16)] * gy_count,
        [pltpu.VMEM((whole_rows, LANES), BF16)],
        mib=6,
    )[::-1]
    *parts, even, odd = lax.optimization_barrier((*parts, *outer[:2]))
    parts = [parts[0]] + others(parts[1:], "gy", gy_count)[::-1]
    even, odd = row_halos(even, odd)
    embedding, *parts = run(
        lambda *refs: band_sum_body(*refs, terms=gy_count, norm_scale=norm_scale),
        parts,
        [shape((share, LANES), BF16)] * gz_count + [shape((1, CH), F32)],
        [pltpu.VMEM((band_rows, LANES), BF16)],
        mib=4,
    )[::-1]
    *parts, even, odd = lax.optimization_barrier((*parts, even, odd))
    parts = [parts[0]] + others(parts[1:], "gz", gz_count)[::-1]
    top, bot, even, odd = corners(*outer[2:], even, odd)
    even = pairs(even, across, gx_count, 0)
    *parts, even, odd = lax.optimization_barrier((*parts, even, odd))
    mine = run(last_sum_body, parts, shape((share, LANES), BF16), mib=2)
    mine, odd = lax.optimization_barrier((mine, odd))
    row = stacked([mine] + others([mine] * (gz_count - 1), "gz", gz_count))
    odd = pairs(odd, across, gx_count, 1)
    row, wide_lower = lax.optimization_barrier((row, wide))
    input_grad = run(
        lower_body,
        (wide_lower, top, bot, even, odd, spread, w_conv, upper, raw),
        shape((ROWS, COLS, CH), BF16),
        [
            prod,
            prod,
            side32,
            pltpu.VMEM((2, ROWS, CH), F32),
            pltpu.VMEM((ROWS - UPPER, COLS, CH), BF16),
            pltpu.VMEM((2, UPPER, 16, CH), BF16),
            pltpu.SemaphoreType.DMA((BLOCKS + 6,)),
        ],
        flops=conv_flops // 2,
        mib=16,
        out_specs=HBM,
    )
    planes = [row] + others([row] * (gy_count - 1), "gy", gy_count)
    *planes, input_grad = lax.optimization_barrier((*planes, input_grad))
    plane = stacked(planes)
    other = lax.ppermute(plane, "core", swap)
    whole = shape((whole_rows, CH), F32)
    buffers = [pltpu.VMEM((whole_rows, LANES), F32), pltpu.SemaphoreType.DMA((gy_count,))]
    half_grad = run(
        lambda *refs: half_body(*refs, other=False), (plane,), whole, buffers, mib=4, out_specs=HBM
    )
    conv_grad = run(
        lambda *refs: half_body(*refs, other=True),
        (other, half_grad),
        whole,
        buffers,
        mib=4,
        far=(1,),
        out_specs=HBM,
        input_output_aliases={1: 0},
    )
    return embedding.reshape(CH), input_grad, conv_grad[: 9 * CH].reshape(9, CH, CH)


def solution(mesh):
    sizes = mesh.devices.shape
    split = Mesh(mesh.devices.reshape(sizes[0], sizes[1] // 2, 2), ("gy", "gz", "core"))
    gx = ("gz", "core")
    in_specs = (P("gy", gx, None), P("gy", gx), P("gy", gx, None, None), P(), P(), P(), P(), P(), P())
    out_specs = (P(), P("gy", gx, None), P())
    return jax.shard_map(per_device, mesh=split, in_specs=in_specs, out_specs=out_specs, check_vma=False)
```

```python
import math

import jax
import jax.numpy as jnp
from jax import lax
from jax.experimental import pallas as pl
from jax.experimental.pallas import tpu as pltpu
from jax.sharding import Mesh, PartitionSpec as P

HEADS = 4
F32 = jnp.float32
BF16 = jnp.bfloat16

attention_bias = -1.0
loss_scale = 512.0

ROWS = 32
COLS = 128
CH = 256
HALO = 48
LANES = 128
STEP = 5
TILE_CELLS = 64


def shape(dims, dtype):
    return jax.ShapeDtypeStruct(dims, dtype)


def nt(left, right):
    return lax.dot_general(left, right, (((1,), (1,)), ((), ())), preferred_element_type=F32)


def tn(left, right):
    return lax.dot_general(left, right, (((0,), (0,)), ((), ())), preferred_element_type=F32)


def nn(left, right):
    return jnp.dot(left, right, preferred_element_type=F32)


def halves(value):
    high = value.astype(BF16)
    return high, (value - high.astype(F32)).astype(BF16)


def wide_product(product, left, right):
    (a, b), (c, d) = left, right
    return product(a, c) + (product(a, d) + product(b, c))


def iota(dims, axis):
    return lax.broadcasted_iota(jnp.int32, dims, axis)


def gate_of(value):
    return 0.5 * jnp.tanh(0.5 * value) + 0.5


def is_odd(axis):
    return lax.axis_index(axis) % 2 == 1


def order_body(first_ref, last_ref, even_ref, odd_ref):
    order_rows(first_ref[0], last_ref[0], even_ref, odd_ref)


def columns_body(block, left_ref, right_ref):
    row, spot = iota((HALO, ROWS * 16), 0), iota((HALO, ROWS * 16), 1)
    for out, at, place in ((left_ref, 0, 0), (right_ref, COLS - 16, 15)):
        pick = (spot == (row - 1) * 16 + place).astype(F32).astype(BF16)
        out[...] = nn(pick, block[:, at : at + 16].reshape(ROWS * 16, CH)).astype(BF16)


def corner_body(left, right, even, odd, top_ref, bot_ref, even_ref, odd_ref):
    low = is_odd("gy")
    top_ref[0] = jnp.where(low, even[0], odd[0])
    bot_ref[0] = jnp.where(low, odd[0], even[0])
    row = iota((HALO, CH), 0)
    whole = []
    for side, at in ((left, 0), (right, COLS - 16)):
        part = slice(0, 1) if at == 0 else slice(15, 16)
        above = top_ref[0, at : at + 16].astype(F32)[part]
        below = bot_ref[0, at : at + 16].astype(F32)[part]
        whole.append(jnp.where(row == 0, above, jnp.where(row == ROWS + 1, below, side[...].astype(F32))))
    high = is_odd("core")
    even_ref[...] = jnp.where(high, whole[0], whole[1]).astype(BF16)
    odd_ref[...] = jnp.where(high, whole[1], whole[0]).astype(BF16)


def sides(even, odd):
    high = is_odd("core")
    one, two = even[...].astype(F32), odd[...].astype(F32)
    return jnp.where(high, one, two), jnp.where(high, two, one)


def forward_taps(weight, b):
    return jnp.concatenate([weight[3 * a + b] for a in range(3)], axis=0)


HALF = ROWS // 2
BLOCKS = (HALF - 1) // STEP
PARTS = ((3, 5, 5, 2), (2, 2, 2, 2, 2, 2, 2, 1))


def with_first(wide, value):
    start = jnp.where(iota((8, wide.shape[1]), 0) == 0, value, wide[0:8])
    return jnp.concatenate([start, wide[8:]], axis=0)


def with_last(wide, value):
    end = jnp.where(iota((8, wide.shape[1]), 0) == 7, value, wide[COLS - 8 :])
    return jnp.concatenate([wide[: COLS - 8], end], axis=0)


def neighbours(row):
    wide = row.astype(F32)
    left = with_first(pltpu.roll(wide, 1, 0), 0.0)
    right = with_last(pltpu.roll(wide, COLS - 1, 0), 0.0)
    return left.astype(BF16), right.astype(BF16)


HALVES = (slice(0, LANES), slice(LANES, CH))


def silu_pair(value, half_mask, narrow=False):
    half = 0.5 * value
    bend = jnp.tanh(half.astype(BF16)).astype(F32) if narrow else jnp.tanh(half)
    kept = (1.0 + bend) * half_mask
    return value * kept, kept * (1.0 + half * (1.0 - bend))


def forward_body(flags_ref, feat, weight, slope_ref, sums, cols, wide, prod_a, prod_b, *, band):
    sums[...] = jnp.zeros_like(sums)
    base = (HALF - 1) * band
    halves_of_mask = [0.5 * flags_ref[band, tile].astype(F32) for tile in range(8)]

    def build(i):
        here = slice(i * COLS, (i + 1) * COLS)
        for lanes in HALVES:
            left, right = neighbours(feat[base + i, :, lanes])
            wide[here, lanes] = left
            wide[here, lanes.start + CH : lanes.stop + CH] = right

    def around(start, count):
        taken = []
        for a in range(3):
            here = slice((start + a) * COLS, (start + a + count) * COLS)
            rows = feat[base + start + a : base + start + a + count].reshape(count * COLS, CH)
            taken += [wide[here, 0:CH], rows, wide[here, CH:]]
        return jnp.concatenate(taken, axis=1)

    def finish(r, prod, first):
        at = r - HALF * band
        for tile in range(8):
            here = slice(16 * tile, 16 * tile + 16)
            value = prod[first + 16 * tile : first + 16 * tile + 16]
            pixel = feat[r, here].astype(F32)
            bent, slope = silu_pair(value, halves_of_mask[tile], narrow=True)
            summed = pixel + bent
            slope_ref[at, here] = slope.astype(BF16)
            sums[r % 2, here] += summed
            if tile in (0, 7):
                edge = slice(0, 1) if tile == 0 else slice(15, 16)
                for i, part in enumerate((value, summed, pixel)):
                    cols[2 * i + tile // 7, at : at + 1] = part[edge]

    prods = (prod_a, prod_b)
    parts = PARTS[band]
    built, done = parts[0] + 2, 0
    for i in range(built):
        build(i)
    for block in range(len(parts) + 1):
        start = sum(parts[:block])
        if block < len(parts):
            prods[block % 2][0 : parts[block] * COLS] = nn(
                around(start, parts[block]), weight[...].reshape(9 * CH, CH)
            )
        ahead = min(HALF + 1, sum(parts[: block + 2]) + 2)
        for j in range(STEP):
            if done < start:
                finish(base + 1 + done, prods[(block - 1) % 2], (done - sum(parts[: block - 1])) * COLS)
                done += 1
            if built < ahead:
                build(built)
                built += 1


def border_body(
    flags_ref, feat, weight, sums_a, sums_b, cols_a, cols_b, top, bot, even, odd, strided, owner_ref,
    pooled_ref, token_ref, edge_ref, side_ref, side32,
):
    added = []
    cols = [jnp.concatenate([cols_a[i], cols_b[i]], axis=0) for i in range(6)]
    for i, whole in enumerate(sides(even, odd)):
        side32[...] = whole
        near = [side32[a : a + ROWS].astype(BF16) for a in range(3)]
        added.append(nn(jnp.concatenate(near, axis=1), forward_taps(weight, 2 * i)))

    def pair(one, two):
        return jnp.concatenate([one, two], axis=0)

    taken = jnp.concatenate(
        [pair(top[0], feat[ROWS - 2]), pair(feat[0], feat[ROWS - 1]), pair(feat[1], bot[0])], axis=1
    )
    low, mid, high = (nn(taken, forward_taps(weight, b)) for b in range(3))
    rows = []
    for i, r in enumerate((0, ROWS - 1)):
        part = slice(i * COLS, (i + 1) * COLS)
        before = with_first(pltpu.roll(low[part], 1, 0), added[0][r : r + 1])
        after = with_last(pltpu.roll(high[part], COLS - 1, 0), added[1][r : r + 1])
        value = mid[part] + before + after
        keep = jnp.concatenate(
            [0.5 * jnp.full((16, CH), flags_ref[i, t], jnp.int32).astype(F32) for t in range(8)], axis=0
        )
        bent, slope = silu_pair(value, keep)
        edge_ref[i] = slope.astype(BF16)
        rows.append(feat[r].astype(F32) + bent)

    line = iota((ROWS, CH), 0)
    deltas = []
    for i in range(2):
        tile = 7 * i
        keep = 0.5 * jnp.where(line < ROWS // 2, flags_ref[0, tile], flags_ref[1, tile]).astype(F32)
        bent, side_ref[i] = silu_pair(cols[i] + added[i], keep)
        inside = (line > 0) & (line < ROWS - 1)
        deltas.append(jnp.where(inside, cols[4 + i] + bent - cols[2 + i], 0.0))

    row, spot = iota((16, COLS), 0), iota((16, COLS), 1)
    pick = ((spot // 16 == row % 8) & (spot % 2 == row // 8)).astype(F32).astype(BF16)
    place = iota((16, CH), 0)
    parts = {}
    for band in range(2):
        for a in range(2):
            total = (sums_a, sums_b)[band][a]
            if band == a:
                total += rows[band]
            high, low = halves(total)
            part = nn(pick, high) + nn(pick, low)
            mine = (line // 16 == band) & (line % 2 == a)
            for i in range(2):
                delta = jnp.sum(jnp.where(mine, deltas[i], 0.0), axis=0, keepdims=True)
                part += jnp.where(place == 15 * i, delta, 0.0)
            parts[band, a] = part
    taken = [
        jnp.concatenate([parts[band, a][8 * b : 8 * b + 8] for band in range(2)], axis=0)
        for a in range(2)
        for b in range(2)
    ]
    high, low = halves(jnp.concatenate(taken, axis=1))
    flat = strided[...].reshape(4 * CH, CH)
    pooled = (nn(high, flat) + nn(low, flat)) * (1.0 / TILE_CELLS)
    pooled_ref[...] = pooled
    normed = pooled * lax.rsqrt(jnp.mean(pooled * pooled, axis=-1, keepdims=True) + 1e-05)
    token_ref[:, 0:CH] = normed.astype(BF16)
    owner = jnp.full((16, LANES), -1, jnp.int32)
    for tile in range(16):
        named = jnp.where(flags_ref[tile // 8, tile % 8] != 0, owner_ref[tile], -1)
        owner = jnp.where(iota((16, LANES), 0) == tile, named, owner)
    token_ref[:, CH:] = (owner == iota((16, LANES), 1)).astype(F32).astype(BF16)


def turn_body(feat, top, bot, w_query, w_key, w_value, token, turned_ref, high_ref, low_ref):
    turned_ref[:, 0:COLS] = top[0].T
    turned_ref[:, (ROWS + 1) * COLS :] = bot[0].T

    @pl.loop(0, ROWS // 4)
    def _(i):
        for j in range(4):
            here = pl.multiple_of((4 * i + j + 1) * COLS, COLS)
            turned_ref[:, pl.ds(here, COLS)] = feat[4 * i + j].T

    for i, one in enumerate((w_query, w_key, w_value)):
        high, low = halves(one[...])
        high_ref[:, i * CH : (i + 1) * CH] = high
        low_ref[:, i * CH : (i + 1) * CH] = low


def attention_body(
    mine, other, pooled_ref, high_w, low_w, cot, strided, spread_ref, emb_ref, band, grad_ref, *, seed_scale
):
    gz, core = lax.axis_index("gz"), lax.axis_index("core")

    def rows_of(depth, other):
        return pl.ds(pl.multiple_of(depth * 32 + other * 16, 16), 16)

    for k in range(mine.shape[0]):
        depth = lax.bitwise_xor(gz, k)
        band[rows_of(depth, core)] = mine[k]
        band[rows_of(depth, 1 - core)] = other[k]
    count = band.shape[0]
    tokens, group = band[:, 0:CH], band[:, CH:]
    pair = nt(group, group)
    pairs = jnp.concatenate([pair] * HEADS, axis=0)
    projected = nn(tokens, high_w[...]) + nn(tokens, low_w[...])
    query, key, value = (projected[:, i * CH : (i + 1) * CH] for i in range(3))
    lane = iota((1, CH), 1) // (CH // HEADS)
    scale = 1.0 / math.sqrt(CH // HEADS)

    def by_head(array):
        return jnp.concatenate([jnp.where(lane == h, array, 0.0) for h in range(HEADS)], axis=0)

    queries, keys = halves(by_head(query)), halves(by_head(key))
    gate = gate_of(wide_product(nt, queries, halves(key)) * scale + attention_bias)
    weights = gate * pairs
    seed = cot[...] * seed_scale
    seeds = jnp.where(lane == iota((8, CH), 0), seed, 0.0)
    values = halves(value)
    along = wide_product(nt, halves(seeds), values)
    columns, grads = [], []
    for h in range(HEADS):
        part = slice(h * count, (h + 1) * count)
        columns.append(jnp.sum(weights[part], axis=0, keepdims=True))
        grads.append(weights[part] * (1.0 - gate[part]) * (along[h : h + 1] * scale))
    columns = halves(jnp.concatenate(columns + [jnp.zeros((8 - HEADS, count), F32)], axis=0))
    grad_ref[:, 0:CH] = wide_product(nn, halves(jnp.concatenate(grads, axis=1)), keys)
    grad_ref[:, CH : 2 * CH] = wide_product(tn, halves(jnp.concatenate(grads, axis=0)), queries)
    grad_ref[:, 2 * CH :] = wide_product(tn, columns, halves(seeds))
    mixed = wide_product(nn, columns, values)
    mixed = jnp.sum(jnp.where(lane == iota((8, CH), 0), mixed, 0.0), axis=0, keepdims=True)
    high = mixed.astype(BF16).astype(F32)
    low = mixed - high
    rows = iota((16, LANES), 0)
    packed = jnp.zeros((16, LANES), F32)
    for i, part in enumerate((high[:, :LANES], high[:, LANES:], low[:, :LANES], low[:, LANES:])):
        packed = jnp.where(rows == i, part, packed)
    emb_ref[...] = packed.astype(BF16)

    grads = halves(grad_ref[rows_of(gz, core)])
    grad = wide_product(nt, grads, (high_w[...], low_w[...]))
    grad = grad.astype(BF16).astype(F32)
    pooled = pooled_ref[...]
    inv = lax.rsqrt(jnp.mean(pooled * pooled, axis=-1, keepdims=True) + 1e-05)
    unit = pooled * inv
    back = inv * (grad - unit * jnp.mean(grad * unit, axis=-1, keepdims=True))
    cell = (back * (1.0 / TILE_CELLS)).astype(BF16)
    spot, row = iota((COLS, 16), 0), iota((COLS, 16), 1)
    expand = ((spot // 16 == row % 8) & (spot % 2 == row // 8)).astype(F32).astype(BF16)
    taps = nt(cell, strided[...].reshape(4 * CH, CH))
    for band in range(2):
        here = taps[8 * band : 8 * band + 8]
        both = [
            jnp.concatenate([here[:, (2 * a + b) * CH : (2 * a + b + 1) * CH] for a in range(2)], axis=1)
            for b in range(2)
        ]
        high, low = halves(jnp.concatenate(both, axis=0))
        spread = nn(expand, high) + nn(expand, low)
        for a in range(2):
            spread_ref[band * 2 + a] = spread[:, a * CH : (a + 1) * CH]


GROUPS = (6, 10, 16)


def weight_body(
    spread, slope_a, slope_b, edge, side, turned, even, odd,
    wide, keep_ref, give_ref, even_ref, odd_ref, left_ref, right_ref, total, first, last,
):
    first[...] = jnp.zeros_like(first)
    last[...] = jnp.zeros_like(last)

    def build(r):
        if r in (0, ROWS - 1):
            slope = edge[r // HALF].astype(F32)
        else:
            slope = (slope_a, slope_b)[r // HALF][r % HALF].astype(F32)
            slope = with_last(with_first(slope, side[0, r : r + 1]), side[1, r : r + 1])
        grad = (spread[(r // HALF) * 2 + r % 2] * slope).astype(BF16)
        here = slice(r * COLS, (r + 1) * COLS)
        wide[here, 2 * CH :], wide[here, 0:CH] = neighbours(grad)
        wide[here, CH : 2 * CH] = grad
        full = grad.astype(F32)
        for a in range(3):
            first[a, r + a : r + a + 1] = full[0:1]
            last[a, r + a : r + a + 1] = full[COLS - 1 :]

    is_one = is_odd("core")
    left, right = (part.astype(BF16) for part in sides(even, odd))

    def put(part, a, b):
        if b == 0:
            part += tn(left, first[a].astype(BF16))
        if b == 2:
            part += tn(right, last[a].astype(BF16))
        low, high = part[:, :LANES], part[:, LANES:]
        at = slice((3 * a + b) * CH, (3 * a + b + 1) * CH)
        keep_ref[at] = jnp.where(is_one, high, low).astype(BF16)
        give_ref[at] = jnp.where(is_one, low, high).astype(BF16)

    for r in range(GROUPS[0]):
        build(r)
    start = 0
    for g, count in enumerate(GROUPS):
        here = slice(start * COLS, (start + count) * COLS)
        near = [turned[:, (start + a) * COLS : (start + a + count) * COLS] for a in range(3)]
        near = jnp.concatenate(near, axis=0)
        start += count
        ahead = GROUPS[g + 1] if g + 1 < len(GROUPS) else 0
        for b in range(3):
            part = slice(b * CH, (b + 1) * CH)
            result = nn(near, wide[here, part])
            if g > 0:
                result += total[:, part]
            if ahead:
                total[:, part] = result
            for r in range(ahead * b // 3, ahead * (b + 1) // 3):
                build(start + r)
            if not ahead:
                for a in range(3):
                    put(result[a * CH : (a + 1) * CH], a, b)

    centre = slice(CH, 2 * CH)
    order_rows(wide[0:COLS, centre], wide[(ROWS - 1) * COLS :, centre], even_ref, odd_ref)
    left_ref[...] = first[1].astype(BF16)
    right_ref[...] = last[1].astype(BF16)


def order_rows(first, last, even_ref, odd_ref):
    odd = is_odd("gy")
    even_ref[0] = jnp.where(odd, first, last)
    odd_ref[0] = jnp.where(odd, last, first)


def back_taps(weight, taps):
    return jnp.concatenate([weight[tap] for tap in taps], axis=1)


def input_blocks(wide, weight, first, blocks, prods, finish, send=None):
    for block in range(blocks + 1):
        if block < blocks:
            at = first + STEP * block
            near = [wide[(at + step) * COLS : (at + step + STEP) * COLS] for step in (1, 0, -1)]
            prods[block % 2][...] = nt(jnp.concatenate(near, axis=1), back_taps(weight, range(9)))
        if block > 0:
            at = first + STEP * (block - 1)
            for j in range(STEP):
                finish(at + j, prods[(block - 1) % 2][j * COLS : (j + 1) * COLS])
            if send is not None:
                send(at, STEP)


UPPER = 2 * STEP


def upper_body(wide, spread, weight, done, raw_ref, prod_a, prod_b):
    def finish(r, prod):
        value = spread[r % 2] + prod
        done[r - 1] = value.astype(BF16)
        raw_ref[0, r : r + 1] = value[0:1]
        raw_ref[1, r : r + 1] = value[COLS - 1 :]

    input_blocks(wide, weight, 1, UPPER // STEP, (prod_a, prod_b), finish)


def lower_body(
    wide, top, bot, even, odd, spread, weight, upper, raw, out, prod_a, prod_b, side32, added, done, fixed, sems
):
    started = []

    def start(source, target):
        started.append(pltpu.make_async_copy(source, target, sems.at[len(started)]))
        started[-1].start()

    start(upper.at[:, 16 : COLS - 16], out.at[1 : UPPER + 1, 16 : COLS - 16])
    for i, whole in enumerate(sides(even, odd)):
        side32[...] = whole
        near = [side32[2 - a : 2 - a + ROWS].astype(BF16) for a in range(3)]
        taps = back_taps(weight, [3 * a + 2 - 2 * i for a in range(3)])
        added[i] = nt(jnp.concatenate(near, axis=1), taps)

    small = iota((16, CH), 0)
    for i in range(2):
        at = (COLS - 16) * i
        for r in range(1, UPPER + 1):
            value = raw[i, r : r + 1] + added[i, r : r + 1]
            old = upper[r - 1, at : at + 16].astype(F32)
            fixed[i, r - 1] = jnp.where(small == 15 * i, value, old).astype(BF16)
        start(fixed.at[i], out.at[1 : UPPER + 1, at : at + 16])

    def place(r):
        return r - UPPER if r else 0

    def finish(r, prod):
        prod = with_first(prod, prod[0:1] + added[0, r : r + 1])
        prod = with_last(prod, prod[COLS - 1 :] + added[1, r : r + 1])
        done[place(r)] = (spread[(r // HALF) * 2 + r % 2] + prod).astype(BF16)

    def send(first, count):
        start(done.at[place(first) : place(first) + count], out.at[first : first + count])

    input_blocks(wide, weight, UPPER + 1, (ROWS - 2 - UPPER) // STEP, (prod_a, prod_b), finish, send)

    def row(r):
        return wide[r * COLS : (r + 1) * COLS]

    def outside(one):
        left, right = neighbours(one[0])
        return jnp.concatenate([right, one[0], left], axis=1)

    def pair(one, two):
        return jnp.concatenate([one, two], axis=0)

    near = [pair(row(1), outside(bot)), pair(row(0), row(ROWS - 1)), pair(outside(top), row(ROWS - 2))]
    both = nt(jnp.concatenate(near, axis=1), back_taps(weight, range(9)))
    for i, r in enumerate((0, ROWS - 1)):
        finish(r, both[i * COLS : (i + 1) * COLS])
        send(r, 1)
    for one in started:
        one.wait()


def add_up(refs, rows):
    total = refs[0][0:rows].astype(F32)
    for one in refs[1:]:
        total += one[0:rows].astype(F32)
    return total.astype(BF16)


def deal(total_ref, outs, size, axis):
    for k, out in enumerate(reversed(outs)):
        at = lax.bitwise_xor(lax.axis_index(axis), k) * size
        out[0:size] = total_ref[pl.ds(pl.multiple_of(at, 16), size)]


def chip_sum_body(one, two, emb, *refs):
    outs, total_ref = refs[:-1], refs[-1]
    rows = one.shape[0]
    size = rows // len(outs)
    total_ref[...] = add_up((one, two), rows)
    deal(total_ref, outs, size, "gy")
    for out in outs:
        out[size:] = emb[...]


def band_sum_body(*refs, terms, norm_scale):
    outs, emb_ref, total_ref = refs[terms:-2], refs[-2], refs[-1]
    rows = total_ref.shape[0]
    total_ref[...] = add_up(refs[:terms], rows)
    deal(total_ref, outs, rows // len(outs), "gz")
    embs = []
    for one in (refs[0], *refs[terms - 1 : 0 : -1]):
        part = one[rows : rows + 16].astype(F32)
        embs.append(part[0:2] + part[2:4])
    while len(embs) > 1:
        embs = [a + b for a, b in zip(embs[0::2], embs[1::2])]
    emb_ref[:, 0:LANES] = embs[0][0:1] * norm_scale
    emb_ref[:, LANES:] = embs[0][1:2] * norm_scale


def last_sum_body(*refs):
    refs[-1][...] = add_up(refs[:-1], refs[-1].shape[0])


def stack_body(*refs):
    for i, one in enumerate(refs[:-1]):
        refs[-1][i] = one[...]


def half_body(array, *refs, other):
    grad_ref, buf, sems = refs[-3:]
    gy, gz, core = (lax.axis_index(name) for name in ("gy", "gz", "core"))
    bands, depth, share = array.shape[:3]
    half = 1 - core if other else core
    lanes = pl.ds(pl.multiple_of(half * LANES, LANES), LANES)
    started = []
    for k in range(bands):
        first = lax.bitwise_xor(gy, k) * (depth * share)
        for j in range(depth):
            at = first + lax.bitwise_xor(gz, j) * share
            buf[pl.ds(pl.multiple_of(at, 16), share)] = array[k, j].astype(F32) * (1.0 / loss_scale)
        here = pl.ds(pl.multiple_of(first, 16), depth * share)
        started.append(pltpu.make_async_copy(buf.at[here], grad_ref.at[here, lanes], sems.at[k]))
        started[-1].start()
    for one in started:
        one.wait()


SMEM = pl.BlockSpec(memory_space=pltpu.SMEM)
VMEM = pl.BlockSpec(memory_space=pltpu.VMEM)
HBM = pl.BlockSpec(memory_space=pltpu.HBM)


def run(body, args, outs, scratch=(), flops=1 << 20, mib=8, far=(), **rest):
    specs = [HBM if i in far else SMEM if a.dtype == jnp.int32 else VMEM for i, a in enumerate(args)]
    return pl.pallas_call(
        body,
        in_specs=specs,
        out_shape=outs,
        scratch_shapes=list(scratch),
        compiler_params=pltpu.CompilerParams(vmem_limit_bytes=mib << 20),
        cost_estimate=pl.CostEstimate(flops=flops, bytes_accessed=1 << 20, transcendentals=0),
        **rest,
    )(*args)


def per_device(features, tissue, owner_map, w_conv, w_stride, w_query, w_key, w_value, cotangent):
    gy_count, gz_count, cores = lax.axis_size("gy"), lax.axis_size("gz"), lax.axis_size("core")
    gx_count, chips = gz_count * cores, gy_count * gz_count
    across = ("gz", "core")
    norm_scale = 1.0 / math.sqrt(16 * gy_count * gx_count)
    swap = [(i, i ^ 1) for i in range(cores)]

    def pairs(value, axis, count, odd):
        low = range(odd, count - 1, 2)
        return lax.ppermute(value, axis, [(i, i + 1) for i in low] + [(i + 1, i) for i in low])

    def others(values, axis, count):
        got = [
            lax.ppermute(values[k - 1], axis, [(i, i ^ k) for i in range(count)])
            for k in range(count - 1, 0, -1)
        ]
        return got[::-1]

    column = shape((HALO, CH), BF16)
    line = shape((1, COLS, CH), BF16)

    def row_halos(even, odd):
        return pairs(even, "gy", gy_count, 0), pairs(odd, "gy", gy_count, 1)

    def corners(left, right, even, odd):
        return run(corner_body, (left, right, even, odd), [line, line, column, column], mib=1)

    def column_halos(even, odd):
        return pairs(even, across, gx_count, 0), pairs(odd, across, gx_count, 1)

    conv_flops = 2 * ROWS * COLS * 9 * CH * CH
    prod = pltpu.VMEM((STEP * COLS, CH), F32)
    side32 = pltpu.VMEM((HALO, CH), F32)
    half_block = shape((HALF, COLS, CH), BF16)

    def forward(band, weight):
        return run(
            lambda *refs: forward_body(*refs, band=band),
            (tissue, features, weight),
            [half_block, shape((2, COLS, CH), F32), shape((6, HALF, CH), F32)],
            [pltpu.VMEM(((HALF + 1) * COLS, 2 * CH), BF16), prod, prod],
            flops=conv_flops // 2,
            mib=16,
        )

    rows = run(
        order_body, (features[:1], features[ROWS - 1 :]), [line, line], flops=conv_flops, mib=2
    )
    outer = run(columns_body, (features,), [column, column], mib=2)
    even, odd = row_halos(*rows)
    slope_a, sums_a, cols_a = forward(0, w_conv)
    even, odd, cols_a = lax.optimization_barrier((even, odd, cols_a))
    top, bot, even, odd = corners(*outer, even, odd)
    weight_b, even = lax.optimization_barrier((w_conv, even))
    even, odd = column_halos(even, odd)
    slope_b, sums_b, cols_b = forward(1, weight_b)
    pooled, token, edge, side = run(
        border_body,
        (
            tissue, features, w_conv, sums_a, sums_b, cols_a, cols_b, top, bot, even, odd, w_stride,
            owner_map.reshape(16),
        ),
        [
            shape((16, CH), F32),
            shape((16, CH + LANES), BF16),
            shape((2, COLS, CH), BF16),
            shape((2, ROWS, CH), F32),
        ],
        [side32],
        flops=conv_flops // 8,
        mib=12,
    )
    def stacked(terms):
        return run(stack_body, terms, shape((len(terms),) + terms[0].shape, BF16), mib=4)

    turned, high_w, low_w = run(
        turn_body,
        (features, top, bot, w_query, w_key, w_value, token),
        [shape((CH, (ROWS + 2) * COLS), BF16), shape((CH, 3 * CH), BF16), shape((CH, 3 * CH), BF16)],
        flops=conv_flops // 4,
        mib=12,
    )
    tokens = stacked([token] + others([token] * (gz_count - 1), "gz", gz_count))
    tokens, high_w = lax.optimization_barrier((tokens, high_w))
    count = 16 * gx_count
    spread, emb = run(
        lambda *refs: attention_body(*refs, seed_scale=loss_scale * norm_scale),
        (tokens, lax.ppermute(tokens, "core", swap), pooled, high_w, low_w, cotangent.reshape(1, CH), w_stride),
        [shape((4, COLS, CH), F32), shape((16, LANES), BF16)],
        [pltpu.VMEM((count, CH + LANES), BF16), pltpu.VMEM((count, 3 * CH), F32)],
        flops=1 << 30,
        mib=12,
    )
    border = pltpu.VMEM((3, HALO, CH), F32)
    wide, keep, give, *outer = run(
        weight_body,
        (spread, slope_a, slope_b, edge, side, turned, even, odd),
        [
            shape((ROWS * COLS, 3 * CH), BF16),
            shape((9 * CH, LANES), BF16),
            shape((9 * CH, LANES), BF16),
            line,
            line,
            column,
            column,
        ],
        [pltpu.VMEM((3 * CH, 3 * CH), F32), border, border],
        flops=conv_flops,
        mib=20,
    )

    share = -(-9 * CH // (16 * chips)) * 16
    spare = share * chips - 9 * CH
    taken = lax.ppermute(give, "core", swap)
    pre_rows = row_halos(*outer[:2])
    if spare:
        keep, taken = (jnp.pad(a, ((0, spare), (0, 0))) for a in (keep, taken))

    whole_rows = share * chips
    band_rows = share * gz_count
    parts = run(
        chip_sum_body,
        (keep, taken, emb),
        [shape((band_rows + 16, LANES), BF16)] * gy_count,
        [pltpu.VMEM((whole_rows, LANES), BF16)],
        mib=6,
    )[::-1]
    *parts, wide_upper = lax.optimization_barrier((*parts, wide))
    upper, raw = run(
        upper_body,
        (wide_upper, spread, w_conv),
        [shape((UPPER, COLS, CH), BF16), shape((2, HALF, CH), F32)],
        [prod, prod],
        flops=conv_flops // 3,
        mib=12,
    )
    raw, *outer = lax.optimization_barrier((raw, *outer[2:], *pre_rows))
    parts = [parts[0]] + others(parts[1:], "gy", gy_count)[::-1]
    top, bot, even, odd = corners(*outer)
    even, odd = column_halos(even, odd)
    *parts, raw = lax.optimization_barrier((*parts, raw))
    embedding, *parts = run(
        lambda *refs: band_sum_body(*refs, terms=gy_count, norm_scale=norm_scale),
        parts,
        [shape((share, LANES), BF16)] * gz_count + [shape((1, CH), F32)],
        [pltpu.VMEM((band_rows, LANES), BF16)],
        mib=4,
    )[::-1]
    *parts, even, odd = lax.optimization_barrier((*parts, even, odd))
    parts = [parts[0]] + others(parts[1:], "gz", gz_count)[::-1]
    mine = run(last_sum_body, parts, shape((share, LANES), BF16), mib=2)
    row = stacked([mine] + others([mine] * (gz_count - 1), "gz", gz_count))
    row, wide_lower = lax.optimization_barrier((row, wide))
    input_grad = run(
        lower_body,
        (wide_lower, top, bot, even, odd, spread, w_conv, upper, raw),
        shape((ROWS, COLS, CH), BF16),
        [
            prod,
            prod,
            side32,
            pltpu.VMEM((2, ROWS, CH), F32),
            pltpu.VMEM((ROWS - UPPER, COLS, CH), BF16),
            pltpu.VMEM((2, UPPER, 16, CH), BF16),
            pltpu.SemaphoreType.DMA((BLOCKS + 6,)),
        ],
        flops=conv_flops // 2,
        mib=16,
        out_specs=HBM,
    )
    planes = [row] + others([row] * (gy_count - 1), "gy", gy_count)
    *planes, input_grad = lax.optimization_barrier((*planes, input_grad))
    plane = stacked(planes)
    other = lax.ppermute(plane, "core", swap)
    whole = shape((whole_rows, CH), F32)
    buffers = [pltpu.VMEM((whole_rows, LANES), F32), pltpu.SemaphoreType.DMA((gy_count,))]
    half_grad = run(
        lambda *refs: half_body(*refs, other=False), (plane,), whole, buffers, mib=4, out_specs=HBM
    )
    conv_grad = run(
        lambda *refs: half_body(*refs, other=True),
        (other, half_grad),
        whole,
        buffers,
        mib=4,
        far=(1,),
        out_specs=HBM,
        input_output_aliases={1: 0},
    )
    return embedding.reshape(CH), input_grad, conv_grad[: 9 * CH].reshape(9, CH, CH)


def solution(mesh):
    sizes = mesh.devices.shape
    split = Mesh(mesh.devices.reshape(sizes[0], sizes[1] // 2, 2), ("gy", "gz", "core"))
    gx = ("gz", "core")
    in_specs = (P("gy", gx, None), P("gy", gx), P("gy", gx, None, None), P(), P(), P(), P(), P(), P())
    out_specs = (P(), P("gy", gx, None), P())
    return jax.shard_map(per_device, mesh=split, in_specs=in_specs, out_specs=out_specs, check_vma=False)
```

```python
import math

import jax
import jax.numpy as jnp
from jax import lax
from jax.experimental import pallas as pl
from jax.experimental.pallas import tpu as pltpu
from jax.sharding import Mesh, PartitionSpec as P

HEADS = 4
F32 = jnp.float32
BF16 = jnp.bfloat16

attention_bias = -1.0
loss_scale = 512.0

ROWS = 32
COLS = 128
CH = 256
HALO = 48
LANES = 128
STEP = 5
TILE_CELLS = 64


def shape(dims, dtype):
    return jax.ShapeDtypeStruct(dims, dtype)


def nt(left, right):
    return lax.dot_general(left, right, (((1,), (1,)), ((), ())), preferred_element_type=F32)


def tn(left, right):
    return lax.dot_general(left, right, (((0,), (0,)), ((), ())), preferred_element_type=F32)


def nn(left, right):
    return jnp.dot(left, right, preferred_element_type=F32)


def halves(value):
    high = value.astype(BF16)
    return high, (value - high.astype(F32)).astype(BF16)


def wide_product(product, left, right):
    (a, b), (c, d) = left, right
    return product(a, c) + (product(a, d) + product(b, c))


def half_product(product, left, right):
    left = left.astype(BF16)
    return product(left, right[0]) + product(left, right[1])


def iota(dims, axis):
    return lax.broadcasted_iota(jnp.int32, dims, axis)


def gate_of(value):
    return 0.5 * jnp.tanh(0.5 * value) + 0.5


def is_odd(axis):
    return lax.axis_index(axis) % 2 == 1


def order_body(first_ref, last_ref, even_ref, odd_ref):
    order_rows(first_ref[0], last_ref[0], even_ref, odd_ref)


def columns_body(block, left_ref, right_ref):
    row, spot = iota((HALO, ROWS * 16), 0), iota((HALO, ROWS * 16), 1)
    for out, at, place in ((left_ref, 0, 0), (right_ref, COLS - 16, 15)):
        pick = (spot == (row - 1) * 16 + place).astype(F32).astype(BF16)
        out[...] = nn(pick, block[:, at : at + 16].reshape(ROWS * 16, CH)).astype(BF16)


def corner_body(left, right, even, odd, top_ref, bot_ref, even_ref, odd_ref):
    low = is_odd("gy")
    top_ref[0] = jnp.where(low, even[0], odd[0])
    bot_ref[0] = jnp.where(low, odd[0], even[0])
    row = iota((HALO, CH), 0)
    whole = []
    for side, at in ((left, 0), (right, COLS - 16)):
        part = slice(0, 1) if at == 0 else slice(15, 16)
        above = top_ref[0, at : at + 16].astype(F32)[part]
        below = bot_ref[0, at : at + 16].astype(F32)[part]
        whole.append(jnp.where(row == 0, above, jnp.where(row == ROWS + 1, below, side[...].astype(F32))))
    high = is_odd("core")
    even_ref[...] = jnp.where(high, whole[0], whole[1]).astype(BF16)
    odd_ref[...] = jnp.where(high, whole[1], whole[0]).astype(BF16)


def sides(even, odd):
    high = is_odd("core")
    one, two = even[...].astype(F32), odd[...].astype(F32)
    return jnp.where(high, one, two), jnp.where(high, two, one)


def forward_taps(weight, b):
    return jnp.concatenate([weight[3 * a + b] for a in range(3)], axis=0)


HALF = ROWS // 2
BLOCKS = (HALF - 1) // STEP
PARTS = (2, 2, 2, 2, 2, 2, 2, 1)


def with_first(wide, value):
    start = jnp.where(iota((8, wide.shape[1]), 0) == 0, value, wide[0:8])
    return jnp.concatenate([start, wide[8:]], axis=0)


def with_last(wide, value):
    end = jnp.where(iota((8, wide.shape[1]), 0) == 7, value, wide[COLS - 8 :])
    return jnp.concatenate([wide[: COLS - 8], end], axis=0)


def neighbours(row):
    wide = row.astype(F32)
    left = with_first(pltpu.roll(wide, 1, 0), 0.0)
    right = with_last(pltpu.roll(wide, COLS - 1, 0), 0.0)
    return left.astype(BF16), right.astype(BF16)


HALVES = (slice(0, LANES), slice(LANES, CH))


def silu_pair(value, half_mask):
    half = 0.5 * value
    bend = jnp.tanh(half)
    kept = (1.0 + bend) * half_mask
    return value * kept, kept * (1.0 + half * (1.0 - bend))


def forward_body(flags_ref, feat, weight, slope_ref, sums, cols, wide, prod_a, prod_b, *, band):
    sums[...] = jnp.zeros_like(sums)
    base = (HALF - 1) * band
    halves_of_mask = [0.5 * flags_ref[band, tile].astype(F32) for tile in range(8)]

    def build(i):
        here = slice(i * COLS, (i + 1) * COLS)
        for lanes in HALVES:
            left, right = neighbours(feat[base + i, :, lanes])
            wide[here, lanes] = left
            wide[here, lanes.start + CH : lanes.stop + CH] = right

    def around(start, count):
        taken = []
        for a in range(3):
            here = slice((start + a) * COLS, (start + a + count) * COLS)
            rows = feat[base + start + a : base + start + a + count].reshape(count * COLS, CH)
            taken += [wide[here, 0:CH], rows, wide[here, CH:]]
        return jnp.concatenate(taken, axis=1)

    def finish(r, prod, first):
        at = r - HALF * band
        for tile in range(8):
            here = slice(16 * tile, 16 * tile + 16)
            value = prod[first + 16 * tile : first + 16 * tile + 16]
            pixel = feat[r, here].astype(F32)
            bent, slope = silu_pair(value, halves_of_mask[tile])
            summed = pixel + bent
            slope_ref[at, here] = slope.astype(BF16)
            sums[r % 2, here] += summed
            if tile in (0, 7):
                edge = slice(0, 1) if tile == 0 else slice(15, 16)
                for i, part in enumerate((value, summed, pixel)):
                    cols[2 * i + tile // 7, at : at + 1] = part[edge]

    prods = (prod_a, prod_b)
    parts = PARTS
    built, done = parts[0] + 2, 0
    for i in range(built):
        build(i)
    for block in range(len(parts) + 1):
        start = sum(parts[:block])
        if block < len(parts):
            prods[block % 2][0 : parts[block] * COLS] = nn(
                around(start, parts[block]), weight[...].reshape(9 * CH, CH)
            )
        ahead = min(HALF + 1, sum(parts[: block + 2]) + 2)
        for j in range(STEP):
            if done < start:
                finish(base + 1 + done, prods[(block - 1) % 2], (done - sum(parts[: block - 1])) * COLS)
                done += 1
            if built < ahead:
                build(built)
                built += 1


def border_body(
    flags_ref, feat, weight, sums_a, sums_b, cols_a, cols_b, top, bot, even, odd, strided, owner_ref,
    pooled_ref, token_ref, edge_ref, side_ref, side32,
):
    added = []
    cols = [jnp.concatenate([cols_a[i], cols_b[i]], axis=0) for i in range(6)]
    for i, whole in enumerate(sides(even, odd)):
        side32[...] = whole
        near = [side32[a : a + ROWS].astype(BF16) for a in range(3)]
        added.append(nn(jnp.concatenate(near, axis=1), forward_taps(weight, 2 * i)))

    def pair(one, two):
        return jnp.concatenate([one, two], axis=0)

    taken = jnp.concatenate(
        [pair(top[0], feat[ROWS - 2]), pair(feat[0], feat[ROWS - 1]), pair(feat[1], bot[0])], axis=1
    )
    low, mid, high = (nn(taken, forward_taps(weight, b)) for b in range(3))
    rows = []
    for i, r in enumerate((0, ROWS - 1)):
        part = slice(i * COLS, (i + 1) * COLS)
        before = with_first(pltpu.roll(low[part], 1, 0), added[0][r : r + 1])
        after = with_last(pltpu.roll(high[part], COLS - 1, 0), added[1][r : r + 1])
        value = mid[part] + before + after
        keep = jnp.concatenate(
            [0.5 * jnp.full((16, CH), flags_ref[i, t], jnp.int32).astype(F32) for t in range(8)], axis=0
        )
        bent, slope = silu_pair(value, keep)
        edge_ref[i] = slope.astype(BF16)
        rows.append(feat[r].astype(F32) + bent)

    line = iota((ROWS, CH), 0)
    deltas = []
    for i in range(2):
        tile = 7 * i
        keep = 0.5 * jnp.where(line < ROWS // 2, flags_ref[0, tile], flags_ref[1, tile]).astype(F32)
        bent, side_ref[i] = silu_pair(cols[i] + added[i], keep)
        inside = (line > 0) & (line < ROWS - 1)
        deltas.append(jnp.where(inside, cols[4 + i] + bent - cols[2 + i], 0.0))

    row, spot = iota((16, COLS), 0), iota((16, COLS), 1)
    pick = ((spot // 16 == row % 8) & (spot % 2 == row // 8)).astype(F32).astype(BF16)
    place = iota((16, CH), 0)
    parts = {}
    for band in range(2):
        for a in range(2):
            total = (sums_a, sums_b)[band][a]
            if band == a:
                total += rows[band]
            high, low = halves(total)
            part = nn(pick, high) + nn(pick, low)
            mine = (line // 16 == band) & (line % 2 == a)
            for i in range(2):
                delta = jnp.sum(jnp.where(mine, deltas[i], 0.0), axis=0, keepdims=True)
                part += jnp.where(place == 15 * i, delta, 0.0)
            parts[band, a] = part
    taken = [
        jnp.concatenate([parts[band, a][8 * b : 8 * b + 8] for band in range(2)], axis=0)
        for a in range(2)
        for b in range(2)
    ]
    high, low = halves(jnp.concatenate(taken, axis=1))
    flat = strided[...].reshape(4 * CH, CH)
    pooled = (nn(high, flat) + nn(low, flat)) * (1.0 / TILE_CELLS)
    pooled_ref[...] = pooled
    normed = pooled * lax.rsqrt(jnp.mean(pooled * pooled, axis=-1, keepdims=True) + 1e-05)
    token_ref[:, 0:CH] = normed.astype(BF16)
    owner = jnp.full((16, LANES), -1, jnp.int32)
    for tile in range(16):
        named = jnp.where(flags_ref[tile // 8, tile % 8] != 0, owner_ref[tile], -1)
        owner = jnp.where(iota((16, LANES), 0) == tile, named, owner)
    token_ref[:, CH:] = (owner == iota((16, LANES), 1)).astype(F32).astype(BF16)


def turn_body(feat, top, bot, w_query, w_key, w_value, token, turned_ref, high_ref, low_ref):
    turned_ref[:, 0:COLS] = top[0].T
    turned_ref[:, (ROWS + 1) * COLS :] = bot[0].T

    @pl.loop(0, ROWS // 4)
    def _(i):
        for j in range(4):
            here = pl.multiple_of((4 * i + j + 1) * COLS, COLS)
            turned_ref[:, pl.ds(here, COLS)] = feat[4 * i + j].T

    for i, one in enumerate((w_query, w_key, w_value)):
        high, low = halves(one[...])
        high_ref[:, i * CH : (i + 1) * CH] = high
        low_ref[:, i * CH : (i + 1) * CH] = low


def attention_body(
    mine, other, pooled_ref, high_w, low_w, cot, strided, spread_ref, emb_ref, band, grad_ref, *, seed_scale
):
    gz, core = lax.axis_index("gz"), lax.axis_index("core")

    def rows_of(depth, other):
        return pl.ds(pl.multiple_of(depth * 32 + other * 16, 16), 16)

    for k in range(mine.shape[0]):
        depth = lax.bitwise_xor(gz, k)
        band[rows_of(depth, core)] = mine[k]
        band[rows_of(depth, 1 - core)] = other[k]
    count = band.shape[0]
    tokens, group = band[:, 0:CH], band[:, CH:]
    pair = nt(group, group)
    pairs = jnp.concatenate([pair] * HEADS, axis=0)
    projected = nn(tokens, high_w[...]) + nn(tokens, low_w[...])
    query, key, value = (projected[:, i * CH : (i + 1) * CH] for i in range(3))
    lane = iota((1, CH), 1) // (CH // HEADS)
    scale = 1.0 / math.sqrt(CH // HEADS)

    def by_head(array):
        return jnp.concatenate([jnp.where(lane == h, array, 0.0) for h in range(HEADS)], axis=0)

    queries, keys = halves(by_head(query)), halves(by_head(key))
    gate = gate_of(wide_product(nt, queries, halves(key)) * scale + attention_bias)
    weights = gate * pairs
    seed = cot[...] * seed_scale
    seeds = jnp.where(lane == iota((8, CH), 0), seed, 0.0)
    values = halves(value)
    along = wide_product(nt, halves(seeds), values)
    columns, grads = [], []
    for h in range(HEADS):
        part = slice(h * count, (h + 1) * count)
        columns.append(jnp.sum(weights[part], axis=0, keepdims=True))
        grads.append(weights[part] * (1.0 - gate[part]) * (along[h : h + 1] * scale))
    columns = halves(jnp.concatenate(columns + [jnp.zeros((8 - HEADS, count), F32)], axis=0))
    grad_ref[:, 0:CH] = half_product(nn, jnp.concatenate(grads, axis=1), keys)
    grad_ref[:, CH : 2 * CH] = half_product(tn, jnp.concatenate(grads, axis=0), queries)
    grad_ref[:, 2 * CH :] = half_product(tn, columns[0], halves(seeds))
    mixed = wide_product(nn, columns, values)
    mixed = jnp.sum(jnp.where(lane == iota((8, CH), 0), mixed, 0.0), axis=0, keepdims=True)
    high = mixed.astype(BF16).astype(F32)
    low = mixed - high
    rows = iota((16, LANES), 0)
    packed = jnp.zeros((16, LANES), F32)
    for i, part in enumerate((high[:, :LANES], high[:, LANES:], low[:, :LANES], low[:, LANES:])):
        packed = jnp.where(rows == i, part, packed)
    emb_ref[...] = packed.astype(BF16)

    grad = half_product(nt, grad_ref[rows_of(gz, core)], (high_w[...], low_w[...]))
    grad = grad.astype(BF16).astype(F32)
    pooled = pooled_ref[...]
    inv = lax.rsqrt(jnp.mean(pooled * pooled, axis=-1, keepdims=True) + 1e-05)
    unit = pooled * inv
    back = inv * (grad - unit * jnp.mean(grad * unit, axis=-1, keepdims=True))
    cell = (back * (1.0 / TILE_CELLS)).astype(BF16)
    spot, row = iota((COLS, 16), 0), iota((COLS, 16), 1)
    expand = ((spot // 16 == row % 8) & (spot % 2 == row // 8)).astype(F32).astype(BF16)
    taps = nt(cell, strided[...].reshape(4 * CH, CH))
    for band in range(2):
        here = taps[8 * band : 8 * band + 8]
        both = [
            jnp.concatenate([here[:, (2 * a + b) * CH : (2 * a + b + 1) * CH] for a in range(2)], axis=1)
            for b in range(2)
        ]
        high, low = halves(jnp.concatenate(both, axis=0))
        spread = nn(expand, high) + nn(expand, low)
        for a in range(2):
            spread_ref[band * 2 + a] = spread[:, a * CH : (a + 1) * CH]


GROUPS = (4, 12, 16)


def weight_body(
    spread, slope_a, slope_b, edge, side, turned, even, odd,
    wide, keep_ref, give_ref, even_ref, odd_ref, left_ref, right_ref, total, first, last,
):
    first[...] = jnp.zeros_like(first)
    last[...] = jnp.zeros_like(last)

    def build(r):
        if r in (0, ROWS - 1):
            slope = edge[r // HALF].astype(F32)
        else:
            slope = (slope_a, slope_b)[r // HALF][r % HALF].astype(F32)
            slope = with_last(with_first(slope, side[0, r : r + 1]), side[1, r : r + 1])
        grad = (spread[(r // HALF) * 2 + r % 2] * slope).astype(BF16)
        here = slice(r * COLS, (r + 1) * COLS)
        wide[here, 2 * CH :], wide[here, 0:CH] = neighbours(grad)
        wide[here, CH : 2 * CH] = grad
        full = grad.astype(F32)
        for a in range(3):
            first[a, r + a : r + a + 1] = full[0:1]
            last[a, r + a : r + a + 1] = full[COLS - 1 :]

    is_one = is_odd("core")
    left, right = (part.astype(BF16) for part in sides(even, odd))

    def put(part, a, b):
        if b == 0:
            part += tn(left, first[a].astype(BF16))
        if b == 2:
            part += tn(right, last[a].astype(BF16))
        low, high = part[:, :LANES], part[:, LANES:]
        at = slice((3 * a + b) * CH, (3 * a + b + 1) * CH)
        keep_ref[at] = jnp.where(is_one, high, low).astype(BF16)
        give_ref[at] = jnp.where(is_one, low, high).astype(BF16)

    for r in range(GROUPS[0]):
        build(r)
    start = 0
    for g, count in enumerate(GROUPS):
        here = slice(start * COLS, (start + count) * COLS)
        near = [turned[:, (start + a) * COLS : (start + a + count) * COLS] for a in range(3)]
        near = jnp.concatenate(near, axis=0)
        start += count
        ahead = GROUPS[g + 1] if g + 1 < len(GROUPS) else 0
        for b in range(3):
            part = slice(b * CH, (b + 1) * CH)
            result = nn(near, wide[here, part])
            if g > 0:
                result += total[:, part]
            if ahead:
                total[:, part] = result
            for r in range(ahead * b // 3, ahead * (b + 1) // 3):
                build(start + r)
            if not ahead:
                for a in range(3):
                    put(result[a * CH : (a + 1) * CH], a, b)

    centre = slice(CH, 2 * CH)
    order_rows(wide[0:COLS, centre], wide[(ROWS - 1) * COLS :, centre], even_ref, odd_ref)
    left_ref[...] = first[1].astype(BF16)
    right_ref[...] = last[1].astype(BF16)


def order_rows(first, last, even_ref, odd_ref):
    odd = is_odd("gy")
    even_ref[0] = jnp.where(odd, first, last)
    odd_ref[0] = jnp.where(odd, last, first)


def back_taps(weight, taps):
    return jnp.concatenate([weight[tap] for tap in taps], axis=1)


def input_blocks(wide, weight, first, blocks, prods, finish, send=None):
    for block in range(blocks + 1):
        if block < blocks:
            at = first + STEP * block
            near = [wide[(at + step) * COLS : (at + step + STEP) * COLS] for step in (1, 0, -1)]
            prods[block % 2][...] = nt(jnp.concatenate(near, axis=1), back_taps(weight, range(9)))
        if block > 0:
            at = first + STEP * (block - 1)
            for j in range(STEP):
                finish(at + j, prods[(block - 1) % 2][j * COLS : (j + 1) * COLS])
            if send is not None:
                send(at, STEP)


UPPER = 2 * STEP


def upper_body(wide, spread, weight, done, raw_ref, prod_a, prod_b):
    def finish(r, prod):
        value = spread[r % 2] + prod
        done[r - 1] = value.astype(BF16)
        raw_ref[0, r : r + 1] = value[0:1]
        raw_ref[1, r : r + 1] = value[COLS - 1 :]

    input_blocks(wide, weight, 1, UPPER // STEP, (prod_a, prod_b), finish)


def lower_body(
    wide, top, bot, even, odd, spread, weight, upper, raw, out, prod_a, prod_b, side32, added, done, fixed, sems
):
    started = []

    def start(source, target):
        started.append(pltpu.make_async_copy(source, target, sems.at[len(started)]))
        started[-1].start()

    start(upper.at[:, 16 : COLS - 16], out.at[1 : UPPER + 1, 16 : COLS - 16])
    for i, whole in enumerate(sides(even, odd)):
        side32[...] = whole
        near = [side32[2 - a : 2 - a + ROWS].astype(BF16) for a in range(3)]
        taps = back_taps(weight, [3 * a + 2 - 2 * i for a in range(3)])
        added[i] = nt(jnp.concatenate(near, axis=1), taps)

    small = iota((16, CH), 0)
    for i in range(2):
        at = (COLS - 16) * i
        for r in range(1, UPPER + 1):
            value = raw[i, r : r + 1] + added[i, r : r + 1]
            old = upper[r - 1, at : at + 16].astype(F32)
            fixed[i, r - 1] = jnp.where(small == 15 * i, value, old).astype(BF16)
        start(fixed.at[i], out.at[1 : UPPER + 1, at : at + 16])

    def place(r):
        return r - UPPER if r else 0

    def finish(r, prod):
        prod = with_first(prod, prod[0:1] + added[0, r : r + 1])
        prod = with_last(prod, prod[COLS - 1 :] + added[1, r : r + 1])
        done[place(r)] = (spread[(r // HALF) * 2 + r % 2] + prod).astype(BF16)

    def send(first, count):
        start(done.at[place(first) : place(first) + count], out.at[first : first + count])

    input_blocks(wide, weight, UPPER + 1, (ROWS - 2 - UPPER) // STEP, (prod_a, prod_b), finish, send)

    def row(r):
        return wide[r * COLS : (r + 1) * COLS]

    def outside(one):
        left, right = neighbours(one[0])
        return jnp.concatenate([right, one[0], left], axis=1)

    def pair(one, two):
        return jnp.concatenate([one, two], axis=0)

    near = [pair(row(1), outside(bot)), pair(row(0), row(ROWS - 1)), pair(outside(top), row(ROWS - 2))]
    both = nt(jnp.concatenate(near, axis=1), back_taps(weight, range(9)))
    for i, r in enumerate((0, ROWS - 1)):
        finish(r, both[i * COLS : (i + 1) * COLS])
        send(r, 1)
    for one in started:
        one.wait()


def add_up(refs, rows):
    total = refs[0][0:rows].astype(F32)
    for one in refs[1:]:
        total += one[0:rows].astype(F32)
    return total.astype(BF16)


def deal(total_ref, outs, size, axis):
    for k, out in enumerate(reversed(outs)):
        at = lax.bitwise_xor(lax.axis_index(axis), k) * size
        out[0:size] = total_ref[pl.ds(pl.multiple_of(at, 16), size)]


def chip_sum_body(one, two, emb, *refs):
    outs, total_ref = refs[:-1], refs[-1]
    rows = one.shape[0]
    size = rows // len(outs)
    total_ref[...] = add_up((one, two), rows)
    deal(total_ref, outs, size, "gy")
    for out in outs:
        out[size:] = emb[...]


def band_sum_body(*refs, terms, norm_scale):
    outs, emb_ref, total_ref = refs[terms:-2], refs[-2], refs[-1]
    rows = total_ref.shape[0]
    total_ref[...] = add_up(refs[:terms], rows)
    deal(total_ref, outs, rows // len(outs), "gz")
    embs = []
    for one in (refs[0], *refs[terms - 1 : 0 : -1]):
        part = one[rows : rows + 16].astype(F32)
        embs.append(part[0:2] + part[2:4])
    while len(embs) > 1:
        embs = [a + b for a, b in zip(embs[0::2], embs[1::2])]
    emb_ref[:, 0:LANES] = embs[0][0:1] * norm_scale
    emb_ref[:, LANES:] = embs[0][1:2] * norm_scale


def last_sum_body(*refs):
    refs[-1][...] = add_up(refs[:-1], refs[-1].shape[0])


def stack_body(*refs):
    for i, one in enumerate(refs[:-1]):
        refs[-1][i] = one[...]


def half_body(array, *refs, other):
    grad_ref, buf, sems = refs[-3:]
    gy, gz, core = (lax.axis_index(name) for name in ("gy", "gz", "core"))
    bands, depth, share = array.shape[:3]
    half = 1 - core if other else core
    lanes = pl.ds(pl.multiple_of(half * LANES, LANES), LANES)
    started = []
    for k in range(bands):
        first = lax.bitwise_xor(gy, k) * (depth * share)
        for j in range(depth):
            at = first + lax.bitwise_xor(gz, j) * share
            buf[pl.ds(pl.multiple_of(at, 16), share)] = array[k, j].astype(F32) * (1.0 / loss_scale)
        here = pl.ds(pl.multiple_of(first, 16), depth * share)
        started.append(pltpu.make_async_copy(buf.at[here], grad_ref.at[here, lanes], sems.at[k]))
        started[-1].start()
    for one in started:
        one.wait()


SMEM = pl.BlockSpec(memory_space=pltpu.SMEM)
VMEM = pl.BlockSpec(memory_space=pltpu.VMEM)
HBM = pl.BlockSpec(memory_space=pltpu.HBM)


def run(body, args, outs, scratch=(), flops=1 << 20, mib=8, far=(), **rest):
    specs = [HBM if i in far else SMEM if a.dtype == jnp.int32 else VMEM for i, a in enumerate(args)]
    return pl.pallas_call(
        body,
        in_specs=specs,
        out_shape=outs,
        scratch_shapes=list(scratch),
        compiler_params=pltpu.CompilerParams(vmem_limit_bytes=mib << 20),
        cost_estimate=pl.CostEstimate(flops=flops, bytes_accessed=1 << 20, transcendentals=0),
        **rest,
    )(*args)


def per_device(features, tissue, owner_map, w_conv, w_stride, w_query, w_key, w_value, cotangent):
    gy_count, gz_count, cores = lax.axis_size("gy"), lax.axis_size("gz"), lax.axis_size("core")
    gx_count, chips = gz_count * cores, gy_count * gz_count
    across = ("gz", "core")
    norm_scale = 1.0 / math.sqrt(16 * gy_count * gx_count)
    swap = [(i, i ^ 1) for i in range(cores)]

    def pairs(value, axis, count, odd):
        low = range(odd, count - 1, 2)
        return lax.ppermute(value, axis, [(i, i + 1) for i in low] + [(i + 1, i) for i in low])

    def others(values, axis, count):
        got = [
            lax.ppermute(values[k - 1], axis, [(i, i ^ k) for i in range(count)])
            for k in range(count - 1, 0, -1)
        ]
        return got[::-1]

    column = shape((HALO, CH), BF16)
    line = shape((1, COLS, CH), BF16)

    def row_halos(even, odd):
        return pairs(even, "gy", gy_count, 0), pairs(odd, "gy", gy_count, 1)

    def corners(left, right, even, odd):
        return run(corner_body, (left, right, even, odd), [line, line, column, column], mib=1)

    def column_halos(even, odd):
        return pairs(even, across, gx_count, 0), pairs(odd, across, gx_count, 1)

    conv_flops = 2 * ROWS * COLS * 9 * CH * CH
    prod = pltpu.VMEM((STEP * COLS, CH), F32)
    side32 = pltpu.VMEM((HALO, CH), F32)
    half_block = shape((HALF, COLS, CH), BF16)

    def forward(band, weight):
        return run(
            lambda *refs: forward_body(*refs, band=band),
            (tissue, features, weight),
            [half_block, shape((2, COLS, CH), F32), shape((6, HALF, CH), F32)],
            [pltpu.VMEM(((HALF + 1) * COLS, 2 * CH), BF16), prod, prod],
            flops=conv_flops // 2,
            mib=16,
        )

    rows = run(
        order_body, (features[:1], features[ROWS - 1 :]), [line, line], flops=conv_flops, mib=2
    )
    outer = run(columns_body, (features,), [column, column], mib=2)
    even, odd = row_halos(*rows)
    slope_a, sums_a, cols_a = forward(0, w_conv)
    even, odd, cols_a = lax.optimization_barrier((even, odd, cols_a))
    top, bot, even, odd = corners(*outer, even, odd)
    weight_b, even = lax.optimization_barrier((w_conv, even))
    even, odd = column_halos(even, odd)
    slope_b, sums_b, cols_b = forward(1, weight_b)
    pooled, token, edge, side = run(
        border_body,
        (
            tissue, features, w_conv, sums_a, sums_b, cols_a, cols_b, top, bot, even, odd, w_stride,
            owner_map.reshape(16),
        ),
        [
            shape((16, CH), F32),
            shape((16, CH + LANES), BF16),
            shape((2, COLS, CH), BF16),
            shape((2, ROWS, CH), F32),
        ],
        [side32],
        flops=conv_flops // 8,
        mib=12,
    )
    def stacked(terms):
        return run(stack_body, terms, shape((len(terms),) + terms[0].shape, BF16), mib=4)

    turned, high_w, low_w = run(
        turn_body,
        (features, top, bot, w_query, w_key, w_value, token),
        [shape((CH, (ROWS + 2) * COLS), BF16), shape((CH, 3 * CH), BF16), shape((CH, 3 * CH), BF16)],
        flops=conv_flops // 4,
        mib=12,
    )
    tokens = stacked([token] + others([token] * (gz_count - 1), "gz", gz_count))
    tokens, high_w = lax.optimization_barrier((tokens, high_w))
    count = 16 * gx_count
    spread, emb = run(
        lambda *refs: attention_body(*refs, seed_scale=loss_scale * norm_scale),
        (tokens, lax.ppermute(tokens, "core", swap), pooled, high_w, low_w, cotangent.reshape(1, CH), w_stride),
        [shape((4, COLS, CH), F32), shape((16, LANES), BF16)],
        [pltpu.VMEM((count, CH + LANES), BF16), pltpu.VMEM((count, 3 * CH), F32)],
        flops=1 << 30,
        mib=12,
    )
    border = pltpu.VMEM((3, HALO, CH), F32)
    wide, keep, give, *outer = run(
        weight_body,
        (spread, slope_a, slope_b, edge, side, turned, even, odd),
        [
            shape((ROWS * COLS, 3 * CH), BF16),
            shape((9 * CH, LANES), BF16),
            shape((9 * CH, LANES), BF16),
            line,
            line,
            column,
            column,
        ],
        [pltpu.VMEM((3 * CH, 3 * CH), F32), border, border],
        flops=conv_flops,
        mib=20,
    )

    share = -(-9 * CH // (16 * chips)) * 16
    spare = share * chips - 9 * CH
    taken = lax.ppermute(give, "core", swap)
    pre_rows = row_halos(*outer[:2])
    if spare:
        keep, taken = (jnp.pad(a, ((0, spare), (0, 0))) for a in (keep, taken))

    whole_rows = share * chips
    band_rows = share * gz_count
    parts = run(
        chip_sum_body,
        (keep, taken, emb),
        [shape((band_rows + 16, LANES), BF16)] * gy_count,
        [pltpu.VMEM((whole_rows, LANES), BF16)],
        mib=6,
    )[::-1]
    *parts, wide_upper = lax.optimization_barrier((*parts, wide))
    upper, raw = run(
        upper_body,
        (wide_upper, spread, w_conv),
        [shape((UPPER, COLS, CH), BF16), shape((2, HALF, CH), F32)],
        [prod, prod],
        flops=conv_flops // 3,
        mib=12,
    )
    raw, *outer = lax.optimization_barrier((raw, *outer[2:], *pre_rows))
    parts = [parts[0]] + others(parts[1:], "gy", gy_count)[::-1]
    top, bot, even, odd = corners(*outer)
    even, odd = column_halos(even, odd)
    *parts, raw = lax.optimization_barrier((*parts, raw))
    embedding, *parts = run(
        lambda *refs: band_sum_body(*refs, terms=gy_count, norm_scale=norm_scale),
        parts,
        [shape((share, LANES), BF16)] * gz_count + [shape((1, CH), F32)],
        [pltpu.VMEM((band_rows, LANES), BF16)],
        mib=4,
    )[::-1]
    *parts, even, odd = lax.optimization_barrier((*parts, even, odd))
    parts = [parts[0]] + others(parts[1:], "gz", gz_count)[::-1]
    mine = run(last_sum_body, parts, shape((share, LANES), BF16), mib=2)
    row = stacked([mine] + others([mine] * (gz_count - 1), "gz", gz_count))
    row, wide_lower = lax.optimization_barrier((row, wide))
    input_grad = run(
        lower_body,
        (wide_lower, top, bot, even, odd, spread, w_conv, upper, raw),
        shape((ROWS, COLS, CH), BF16),
        [
            prod,
            prod,
            side32,
            pltpu.VMEM((2, ROWS, CH), F32),
            pltpu.VMEM((ROWS - UPPER, COLS, CH), BF16),
            pltpu.VMEM((2, UPPER, 16, CH), BF16),
            pltpu.SemaphoreType.DMA((BLOCKS + 6,)),
        ],
        flops=conv_flops // 2,
        mib=16,
        out_specs=HBM,
    )
    planes = [row] + others([row] * (gy_count - 1), "gy", gy_count)
    *planes, input_grad = lax.optimization_barrier((*planes, input_grad))
    plane = stacked(planes)
    other = lax.ppermute(plane, "core", swap)
    whole = shape((whole_rows, CH), F32)
    buffers = [pltpu.VMEM((whole_rows, LANES), F32), pltpu.SemaphoreType.DMA((gy_count,))]
    half_grad = run(
        lambda *refs: half_body(*refs, other=False), (plane,), whole, buffers, mib=4, out_specs=HBM
    )
    conv_grad = run(
        lambda *refs: half_body(*refs, other=True),
        (other, half_grad),
        whole,
        buffers,
        mib=4,
        far=(1,),
        out_specs=HBM,
        input_output_aliases={1: 0},
    )
    return embedding.reshape(CH), input_grad, conv_grad[: 9 * CH].reshape(9, CH, CH)


def solution(mesh):
    sizes = mesh.devices.shape
    split = Mesh(mesh.devices.reshape(sizes[0], sizes[1] // 2, 2), ("gy", "gz", "core"))
    gx = ("gz", "core")
    in_specs = (P("gy", gx, None), P("gy", gx), P("gy", gx, None, None), P(), P(), P(), P(), P(), P())
    out_specs = (P(), P("gy", gx, None), P())
    return jax.shard_map(per_device, mesh=split, in_specs=in_specs, out_specs=out_specs, check_vma=False)
```

```python
import math

import jax
import jax.numpy as jnp
from jax import lax
from jax.experimental import pallas as pl
from jax.experimental.pallas import tpu as pltpu
from jax.sharding import Mesh, PartitionSpec as P

HEADS = 4
F32 = jnp.float32
BF16 = jnp.bfloat16

attention_bias = -1.0
loss_scale = 512.0

ROWS = 32
COLS = 128
CH = 256
HALO = 48
LANES = 128
STEP = 5
TILE_CELLS = 64


def shape(dims, dtype):
    return jax.ShapeDtypeStruct(dims, dtype)


def nt(left, right):
    return lax.dot_general(left, right, (((1,), (1,)), ((), ())), preferred_element_type=F32)


def tn(left, right):
    return lax.dot_general(left, right, (((0,), (0,)), ((), ())), preferred_element_type=F32)


def nn(left, right):
    return jnp.dot(left, right, preferred_element_type=F32)


def halves(value):
    high = value.astype(BF16)
    return high, (value - high.astype(F32)).astype(BF16)


def wide_product(product, left, right):
    (a, b), (c, d) = left, right
    return product(a, c) + (product(a, d) + product(b, c))


def half_product(product, left, right):
    left = left.astype(BF16)
    return product(left, right[0]) + product(left, right[1])


def iota(dims, axis):
    return lax.broadcasted_iota(jnp.int32, dims, axis)


def gate_of(value):
    return 0.5 * jnp.tanh(0.5 * value) + 0.5


def is_odd(axis):
    return lax.axis_index(axis) % 2 == 1


def order_body(first_ref, last_ref, even_ref, odd_ref):
    order_rows(first_ref[0], last_ref[0], even_ref, odd_ref)


def columns_body(block, left_ref, right_ref):
    row, spot = iota((HALO, ROWS * 16), 0), iota((HALO, ROWS * 16), 1)
    for out, at, place in ((left_ref, 0, 0), (right_ref, COLS - 16, 15)):
        pick = (spot == (row - 1) * 16 + place).astype(F32).astype(BF16)
        out[...] = nn(pick, block[:, at : at + 16].reshape(ROWS * 16, CH)).astype(BF16)


def corner_body(left, right, even, odd, top_ref, bot_ref, even_ref, odd_ref):
    low = is_odd("gy")
    top_ref[0] = jnp.where(low, even[0], odd[0])
    bot_ref[0] = jnp.where(low, odd[0], even[0])
    row = iota((HALO, CH), 0)
    whole = []
    for side, at in ((left, 0), (right, COLS - 16)):
        part = slice(0, 1) if at == 0 else slice(15, 16)
        above = top_ref[0, at : at + 16].astype(F32)[part]
        below = bot_ref[0, at : at + 16].astype(F32)[part]
        whole.append(jnp.where(row == 0, above, jnp.where(row == ROWS + 1, below, side[...].astype(F32))))
    high = is_odd("core")
    even_ref[...] = jnp.where(high, whole[0], whole[1]).astype(BF16)
    odd_ref[...] = jnp.where(high, whole[1], whole[0]).astype(BF16)


def sides(even, odd):
    high = is_odd("core")
    one, two = even[...].astype(F32), odd[...].astype(F32)
    return jnp.where(high, one, two), jnp.where(high, two, one)


def forward_taps(weight, b):
    return jnp.concatenate([weight[3 * a + b] for a in range(3)], axis=0)


HALF = ROWS // 2
BLOCKS = (HALF - 1) // STEP
PARTS = (2, 2, 2, 2, 2, 2, 2, 1)


def with_first(wide, value):
    start = jnp.where(iota((8, wide.shape[1]), 0) == 0, value, wide[0:8])
    return jnp.concatenate([start, wide[8:]], axis=0)


def with_last(wide, value):
    end = jnp.where(iota((8, wide.shape[1]), 0) == 7, value, wide[COLS - 8 :])
    return jnp.concatenate([wide[: COLS - 8], end], axis=0)


def neighbours(row):
    wide = row.astype(F32)
    left = with_first(pltpu.roll(wide, 1, 0), 0.0)
    right = with_last(pltpu.roll(wide, COLS - 1, 0), 0.0)
    return left.astype(BF16), right.astype(BF16)


HALVES = (slice(0, LANES), slice(LANES, CH))


def silu_pair(value, half_mask):
    half = 0.5 * value
    bend = jnp.tanh(half)
    kept = (1.0 + bend) * half_mask
    return value * kept, kept * (1.0 + half * (1.0 - bend))


def forward_body(flags_ref, feat, weight, slope_ref, sums, cols, wide, prod_a, prod_b, *, band):
    sums[...] = jnp.zeros_like(sums)
    base = (HALF - 1) * band
    halves_of_mask = [0.5 * flags_ref[band, tile].astype(F32) for tile in range(8)]

    def build(i):
        here = slice(i * COLS, (i + 1) * COLS)
        for lanes in HALVES:
            left, right = neighbours(feat[base + i, :, lanes])
            wide[here, lanes] = left
            wide[here, lanes.start + CH : lanes.stop + CH] = right

    def around(start, count):
        taken = []
        for a in range(3):
            here = slice((start + a) * COLS, (start + a + count) * COLS)
            rows = feat[base + start + a : base + start + a + count].reshape(count * COLS, CH)
            taken += [wide[here, 0:CH], rows, wide[here, CH:]]
        return jnp.concatenate(taken, axis=1)

    def finish(r, prod, first):
        at = r - HALF * band
        for tile in range(8):
            here = slice(16 * tile, 16 * tile + 16)
            value = prod[first + 16 * tile : first + 16 * tile + 16]
            pixel = feat[r, here].astype(F32)
            bent, slope = silu_pair(value, halves_of_mask[tile])
            summed = pixel + bent
            slope_ref[at, here] = slope.astype(BF16)
            sums[r % 2, here] += summed
            if tile in (0, 7):
                edge = slice(0, 1) if tile == 0 else slice(15, 16)
                for i, part in enumerate((value, summed, pixel)):
                    cols[2 * i + tile // 7, at : at + 1] = part[edge]

    prods = (prod_a, prod_b)
    parts = PARTS
    built, done = parts[0] + 2, 0
    for i in range(built):
        build(i)
    for block in range(len(parts) + 1):
        start = sum(parts[:block])
        if block < len(parts):
            prods[block % 2][0 : parts[block] * COLS] = nn(
                around(start, parts[block]), weight[...].reshape(9 * CH, CH)
            )
        ahead = min(HALF + 1, sum(parts[: block + 2]) + 2)
        for j in range(STEP):
            if done < start:
                finish(base + 1 + done, prods[(block - 1) % 2], (done - sum(parts[: block - 1])) * COLS)
                done += 1
            if built < ahead:
                build(built)
                built += 1


def border_body(
    flags_ref, feat, weight, sums_a, sums_b, cols_a, cols_b, top, bot, even, odd, strided, owner_ref,
    pooled_ref, token_ref, edge_ref, side_ref, side32,
):
    added = []
    cols = [jnp.concatenate([cols_a[i], cols_b[i]], axis=0) for i in range(6)]
    for i, whole in enumerate(sides(even, odd)):
        side32[...] = whole
        near = [side32[a : a + ROWS].astype(BF16) for a in range(3)]
        added.append(nn(jnp.concatenate(near, axis=1), forward_taps(weight, 2 * i)))

    def pair(one, two):
        return jnp.concatenate([one, two], axis=0)

    taken = jnp.concatenate(
        [pair(top[0], feat[ROWS - 2]), pair(feat[0], feat[ROWS - 1]), pair(feat[1], bot[0])], axis=1
    )
    low, mid, high = (nn(taken, forward_taps(weight, b)) for b in range(3))
    rows = []
    for i, r in enumerate((0, ROWS - 1)):
        part = slice(i * COLS, (i + 1) * COLS)
        before = with_first(pltpu.roll(low[part], 1, 0), added[0][r : r + 1])
        after = with_last(pltpu.roll(high[part], COLS - 1, 0), added[1][r : r + 1])
        value = mid[part] + before + after
        keep = jnp.concatenate(
            [0.5 * jnp.full((16, CH), flags_ref[i, t], jnp.int32).astype(F32) for t in range(8)], axis=0
        )
        bent, slope = silu_pair(value, keep)
        edge_ref[i] = slope.astype(BF16)
        rows.append(feat[r].astype(F32) + bent)

    line = iota((ROWS, CH), 0)
    deltas = []
    for i in range(2):
        tile = 7 * i
        keep = 0.5 * jnp.where(line < ROWS // 2, flags_ref[0, tile], flags_ref[1, tile]).astype(F32)
        bent, side_ref[i] = silu_pair(cols[i] + added[i], keep)
        inside = (line > 0) & (line < ROWS - 1)
        deltas.append(jnp.where(inside, cols[4 + i] + bent - cols[2 + i], 0.0))

    row, spot = iota((16, COLS), 0), iota((16, COLS), 1)
    pick = ((spot // 16 == row % 8) & (spot % 2 == row // 8)).astype(F32).astype(BF16)
    place = iota((16, CH), 0)
    parts = {}
    for band in range(2):
        for a in range(2):
            total = (sums_a, sums_b)[band][a]
            if band == a:
                total += rows[band]
            high, low = halves(total)
            part = nn(pick, high) + nn(pick, low)
            mine = (line // 16 == band) & (line % 2 == a)
            for i in range(2):
                delta = jnp.sum(jnp.where(mine, deltas[i], 0.0), axis=0, keepdims=True)
                part += jnp.where(place == 15 * i, delta, 0.0)
            parts[band, a] = part
    taken = [
        jnp.concatenate([parts[band, a][8 * b : 8 * b + 8] for band in range(2)], axis=0)
        for a in range(2)
        for b in range(2)
    ]
    high, low = halves(jnp.concatenate(taken, axis=1))
    flat = strided[...].reshape(4 * CH, CH)
    pooled = (nn(high, flat) + nn(low, flat)) * (1.0 / TILE_CELLS)
    pooled_ref[...] = pooled
    normed = pooled * lax.rsqrt(jnp.mean(pooled * pooled, axis=-1, keepdims=True) + 1e-05)
    token_ref[:, 0:CH] = normed.astype(BF16)
    owner = jnp.full((16, LANES), -1, jnp.int32)
    for tile in range(16):
        named = jnp.where(flags_ref[tile // 8, tile % 8] != 0, owner_ref[tile], -1)
        owner = jnp.where(iota((16, LANES), 0) == tile, named, owner)
    token_ref[:, CH:] = (owner == iota((16, LANES), 1)).astype(F32).astype(BF16)


def turn_body(feat, top, bot, w_query, w_key, w_value, token, turned_ref, high_ref, low_ref):
    turned_ref[:, 0:COLS] = top[0].T
    turned_ref[:, (ROWS + 1) * COLS :] = bot[0].T

    @pl.loop(0, ROWS // 4)
    def _(i):
        for j in range(4):
            here = pl.multiple_of((4 * i + j + 1) * COLS, COLS)
            turned_ref[:, pl.ds(here, COLS)] = feat[4 * i + j].T

    for i, one in enumerate((w_query, w_key, w_value)):
        high, low = halves(one[...])
        high_ref[:, i * CH : (i + 1) * CH] = high
        low_ref[:, i * CH : (i + 1) * CH] = low


def pair_body(one, two, out_ref):
    out_ref[0:16] = one[...]
    out_ref[16:32] = two[...]


def attention_body(*refs, seed_scale):
    *got, pooled_ref, high_w, low_w, cot, strided, spread_ref, emb_ref, band, grad_ref = refs
    gz, core = lax.axis_index("gz"), lax.axis_index("core")

    def rows_of(depth, other):
        return pl.ds(pl.multiple_of(depth * 32 + other * 16, 16), 16)

    for k, piece in enumerate(got):
        depth = lax.bitwise_xor(gz, k)
        band[rows_of(depth, core)] = piece[0:16]
        band[rows_of(depth, 1 - core)] = piece[16:32]
    count = band.shape[0]
    tokens, group = band[:, 0:CH], band[:, CH:]
    pair = nt(group, group)
    pairs = jnp.concatenate([pair] * HEADS, axis=0)
    projected = nn(tokens, high_w[...]) + nn(tokens, low_w[...])
    query, key, value = (projected[:, i * CH : (i + 1) * CH] for i in range(3))
    lane = iota((1, CH), 1) // (CH // HEADS)
    scale = 1.0 / math.sqrt(CH // HEADS)

    def by_head(array):
        return jnp.concatenate([jnp.where(lane == h, array, 0.0) for h in range(HEADS)], axis=0)

    queries, keys = halves(by_head(query)), halves(by_head(key))
    gate = gate_of(wide_product(nt, queries, halves(key)) * scale + attention_bias)
    weights = gate * pairs
    seed = cot[...] * seed_scale
    seeds = jnp.where(lane == iota((8, CH), 0), seed, 0.0)
    values = halves(value)
    along = wide_product(nt, halves(seeds), values)
    columns, grads = [], []
    for h in range(HEADS):
        part = slice(h * count, (h + 1) * count)
        columns.append(jnp.sum(weights[part], axis=0, keepdims=True))
        grads.append(weights[part] * (1.0 - gate[part]) * (along[h : h + 1] * scale))
    columns = halves(jnp.concatenate(columns + [jnp.zeros((8 - HEADS, count), F32)], axis=0))
    grad_ref[:, 0:CH] = half_product(nn, jnp.concatenate(grads, axis=1), keys)
    grad_ref[:, CH : 2 * CH] = half_product(tn, jnp.concatenate(grads, axis=0), queries)
    grad_ref[:, 2 * CH :] = half_product(tn, columns[0], halves(seeds))
    mixed = wide_product(nn, columns, values)
    mixed = jnp.sum(jnp.where(lane == iota((8, CH), 0), mixed, 0.0), axis=0, keepdims=True)
    high = mixed.astype(BF16).astype(F32)
    low = mixed - high
    rows = iota((16, LANES), 0)
    packed = jnp.zeros((16, LANES), F32)
    for i, part in enumerate((high[:, :LANES], high[:, LANES:], low[:, :LANES], low[:, LANES:])):
        packed = jnp.where(rows == i, part, packed)
    emb_ref[...] = packed.astype(BF16)

    grad = half_product(nt, grad_ref[rows_of(gz, core)], (high_w[...], low_w[...]))
    grad = grad.astype(BF16).astype(F32)
    pooled = pooled_ref[...]
    inv = lax.rsqrt(jnp.mean(pooled * pooled, axis=-1, keepdims=True) + 1e-05)
    unit = pooled * inv
    back = inv * (grad - unit * jnp.mean(grad * unit, axis=-1, keepdims=True))
    cell = (back * (1.0 / TILE_CELLS)).astype(BF16)
    spot, row = iota((COLS, 16), 0), iota((COLS, 16), 1)
    expand = ((spot // 16 == row % 8) & (spot % 2 == row // 8)).astype(F32).astype(BF16)
    taps = nt(cell, strided[...].reshape(4 * CH, CH))
    for band in range(2):
        here = taps[8 * band : 8 * band + 8]
        both = [
            jnp.concatenate([here[:, (2 * a + b) * CH : (2 * a + b + 1) * CH] for a in range(2)], axis=1)
            for b in range(2)
        ]
        high, low = halves(jnp.concatenate(both, axis=0))
        spread = nn(expand, high) + nn(expand, low)
        for a in range(2):
            spread_ref[band * 2 + a] = spread[:, a * CH : (a + 1) * CH]


GROUPS = (6, 10, 16)


def weight_body(
    spread, slope_a, slope_b, edge, side, turned, even, odd,
    wide, keep_ref, give_ref, even_ref, odd_ref, left_ref, right_ref, total, first, last,
):
    first[...] = jnp.zeros_like(first)
    last[...] = jnp.zeros_like(last)

    def build(r):
        if r in (0, ROWS - 1):
            slope = edge[r // HALF].astype(F32)
        else:
            slope = (slope_a, slope_b)[r // HALF][r % HALF].astype(F32)
            slope = with_last(with_first(slope, side[0, r : r + 1]), side[1, r : r + 1])
        grad = (spread[(r // HALF) * 2 + r % 2] * slope).astype(BF16)
        here = slice(r * COLS, (r + 1) * COLS)
        wide[here, 2 * CH :], wide[here, 0:CH] = neighbours(grad)
        wide[here, CH : 2 * CH] = grad
        full = grad.astype(F32)
        for a in range(3):
            first[a, r + a : r + a + 1] = full[0:1]
            last[a, r + a : r + a + 1] = full[COLS - 1 :]

    is_one = is_odd("core")
    left, right = (part.astype(BF16) for part in sides(even, odd))

    def put(part, a, b):
        if b == 0:
            part += tn(left, first[a].astype(BF16))
        if b == 2:
            part += tn(right, last[a].astype(BF16))
        low, high = part[:, :LANES], part[:, LANES:]
        at = slice((3 * a + b) * CH, (3 * a + b + 1) * CH)
        keep_ref[at] = jnp.where(is_one, high, low).astype(BF16)
        give_ref[at] = jnp.where(is_one, low, high).astype(BF16)

    for r in range(GROUPS[0]):
        build(r)
    start = 0
    for g, count in enumerate(GROUPS):
        here = slice(start * COLS, (start + count) * COLS)
        near = [turned[:, (start + a) * COLS : (start + a + count) * COLS] for a in range(3)]
        near = jnp.concatenate(near, axis=0)
        start += count
        ahead = GROUPS[g + 1] if g + 1 < len(GROUPS) else 0
        for b in range(3):
            part = slice(b * CH, (b + 1) * CH)
            result = nn(near, wide[here, part])
            if g > 0:
                result += total[:, part]
            if ahead:
                total[:, part] = result
            for r in range(ahead * b // 3, ahead * (b + 1) // 3):
                build(start + r)
            if not ahead:
                for a in range(3):
                    put(result[a * CH : (a + 1) * CH], a, b)

    centre = slice(CH, 2 * CH)
    order_rows(wide[0:COLS, centre], wide[(ROWS - 1) * COLS :, centre], even_ref, odd_ref)
    left_ref[...] = first[1].astype(BF16)
    right_ref[...] = last[1].astype(BF16)


def order_rows(first, last, even_ref, odd_ref):
    odd = is_odd("gy")
    even_ref[0] = jnp.where(odd, first, last)
    odd_ref[0] = jnp.where(odd, last, first)


def back_taps(weight, taps):
    return jnp.concatenate([weight[tap] for tap in taps], axis=1)


def input_blocks(wide, weight, first, blocks, prods, finish, send=None):
    for block in range(blocks + 1):
        if block < blocks:
            at = first + STEP * block
            near = [wide[(at + step) * COLS : (at + step + STEP) * COLS] for step in (1, 0, -1)]
            prods[block % 2][...] = nt(jnp.concatenate(near, axis=1), back_taps(weight, range(9)))
        if block > 0:
            at = first + STEP * (block - 1)
            for j in range(STEP):
                finish(at + j, prods[(block - 1) % 2][j * COLS : (j + 1) * COLS])
            if send is not None:
                send(at, STEP)


UPPER = 2 * STEP


def upper_body(wide, spread, weight, done, raw_ref, prod_a, prod_b):
    def finish(r, prod):
        value = spread[r % 2] + prod
        done[r - 1] = value.astype(BF16)
        raw_ref[0, r : r + 1] = value[0:1]
        raw_ref[1, r : r + 1] = value[COLS - 1 :]

    input_blocks(wide, weight, 1, UPPER // STEP, (prod_a, prod_b), finish)


def lower_body(
    wide, top, bot, even, odd, spread, weight, upper, raw, out, prod_a, prod_b, side32, added, done, fixed, sems
):
    started = []

    def start(source, target):
        started.append(pltpu.make_async_copy(source, target, sems.at[len(started)]))
        started[-1].start()

    start(upper.at[:, 16 : COLS - 16], out.at[1 : UPPER + 1, 16 : COLS - 16])
    for i, whole in enumerate(sides(even, odd)):
        side32[...] = whole
        near = [side32[2 - a : 2 - a + ROWS].astype(BF16) for a in range(3)]
        taps = back_taps(weight, [3 * a + 2 - 2 * i for a in range(3)])
        added[i] = nt(jnp.concatenate(near, axis=1), taps)

    small = iota((16, CH), 0)
    for i in range(2):
        at = (COLS - 16) * i
        for r in range(1, UPPER + 1):
            value = raw[i, r : r + 1] + added[i, r : r + 1]
            old = upper[r - 1, at : at + 16].astype(F32)
            fixed[i, r - 1] = jnp.where(small == 15 * i, value, old).astype(BF16)
        start(fixed.at[i], out.at[1 : UPPER + 1, at : at + 16])

    def place(r):
        return r - UPPER if r else 0

    def finish(r, prod):
        prod = with_first(prod, prod[0:1] + added[0, r : r + 1])
        prod = with_last(prod, prod[COLS - 1 :] + added[1, r : r + 1])
        done[place(r)] = (spread[(r // HALF) * 2 + r % 2] + prod).astype(BF16)

    def send(first, count):
        start(done.at[place(first) : place(first) + count], out.at[first : first + count])

    input_blocks(wide, weight, UPPER + 1, (ROWS - 2 - UPPER) // STEP, (prod_a, prod_b), finish, send)

    def row(r):
        return wide[r * COLS : (r + 1) * COLS]

    def outside(one):
        left, right = neighbours(one[0])
        return jnp.concatenate([right, one[0], left], axis=1)

    def pair(one, two):
        return jnp.concatenate([one, two], axis=0)

    near = [pair(row(1), outside(bot)), pair(row(0), row(ROWS - 1)), pair(outside(top), row(ROWS - 2))]
    both = nt(jnp.concatenate(near, axis=1), back_taps(weight, range(9)))
    for i, r in enumerate((0, ROWS - 1)):
        finish(r, both[i * COLS : (i + 1) * COLS])
        send(r, 1)
    for one in started:
        one.wait()


def add_up(refs, rows):
    total = refs[0][0:rows].astype(F32)
    for one in refs[1:]:
        total += one[0:rows].astype(F32)
    return total.astype(BF16)


def deal(total_ref, outs, size, axis):
    for k, out in enumerate(reversed(outs)):
        at = lax.bitwise_xor(lax.axis_index(axis), k) * size
        out[0:size] = total_ref[pl.ds(pl.multiple_of(at, 16), size)]


def chip_sum_body(one, two, emb, *refs):
    outs, total_ref = refs[:-1], refs[-1]
    rows = one.shape[0]
    size = rows // len(outs)
    total_ref[...] = add_up((one, two), rows)
    deal(total_ref, outs, size, "gy")
    for out in outs:
        out[size:] = emb[...]


def band_sum_body(*refs, terms, norm_scale):
    outs, emb_ref, total_ref = refs[terms:-2], refs[-2], refs[-1]
    rows = total_ref.shape[0]
    total_ref[...] = add_up(refs[:terms], rows)
    deal(total_ref, outs, rows // len(outs), "gz")
    embs = []
    for one in (refs[0], *refs[terms - 1 : 0 : -1]):
        part = one[rows : rows + 16].astype(F32)
        embs.append(part[0:2] + part[2:4])
    while len(embs) > 1:
        embs = [a + b for a, b in zip(embs[0::2], embs[1::2])]
    emb_ref[:, 0:LANES] = embs[0][0:1] * norm_scale
    emb_ref[:, LANES:] = embs[0][1:2] * norm_scale


def last_sum_body(*refs):
    refs[-1][...] = add_up(refs[:-1], refs[-1].shape[0])


def stack_body(*refs):
    for i, one in enumerate(refs[:-1]):
        refs[-1][i] = one[...]


def half_body(array, *refs, other):
    grad_ref, buf, sems = refs[-3:]
    gy, gz, core = (lax.axis_index(name) for name in ("gy", "gz", "core"))
    bands, depth, share = array.shape[:3]
    half = 1 - core if other else core
    lanes = pl.ds(pl.multiple_of(half * LANES, LANES), LANES)
    started = []
    for k in range(bands):
        first = lax.bitwise_xor(gy, k) * (depth * share)
        for j in range(depth):
            at = first + lax.bitwise_xor(gz, j) * share
            buf[pl.ds(pl.multiple_of(at, 16), share)] = array[k, j].astype(F32) * (1.0 / loss_scale)
        here = pl.ds(pl.multiple_of(first, 16), depth * share)
        started.append(pltpu.make_async_copy(buf.at[here], grad_ref.at[here, lanes], sems.at[k]))
        started[-1].start()
    for one in started:
        one.wait()


SMEM = pl.BlockSpec(memory_space=pltpu.SMEM)
VMEM = pl.BlockSpec(memory_space=pltpu.VMEM)
HBM = pl.BlockSpec(memory_space=pltpu.HBM)


def run(body, args, outs, scratch=(), flops=1 << 20, mib=8, far=(), **rest):
    specs = [HBM if i in far else SMEM if a.dtype == jnp.int32 else VMEM for i, a in enumerate(args)]
    return pl.pallas_call(
        body,
        in_specs=specs,
        out_shape=outs,
        scratch_shapes=list(scratch),
        compiler_params=pltpu.CompilerParams(vmem_limit_bytes=mib << 20),
        cost_estimate=pl.CostEstimate(flops=flops, bytes_accessed=1 << 20, transcendentals=0),
        **rest,
    )(*args)


def per_device(features, tissue, owner_map, w_conv, w_stride, w_query, w_key, w_value, cotangent):
    gy_count, gz_count, cores = lax.axis_size("gy"), lax.axis_size("gz"), lax.axis_size("core")
    gx_count, chips = gz_count * cores, gy_count * gz_count
    across = ("gz", "core")
    norm_scale = 1.0 / math.sqrt(16 * gy_count * gx_count)
    swap = [(i, i ^ 1) for i in range(cores)]

    def pairs(value, axis, count, odd):
        low = range(odd, count - 1, 2)
        return lax.ppermute(value, axis, [(i, i + 1) for i in low] + [(i + 1, i) for i in low])

    def others(values, axis, count):
        got = [
            lax.ppermute(values[k - 1], axis, [(i, i ^ k) for i in range(count)])
            for k in range(count - 1, 0, -1)
        ]
        return got[::-1]

    column = shape((HALO, CH), BF16)
    line = shape((1, COLS, CH), BF16)

    def row_halos(even, odd):
        return pairs(even, "gy", gy_count, 0), pairs(odd, "gy", gy_count, 1)

    def corners(left, right, even, odd):
        return run(corner_body, (left, right, even, odd), [line, line, column, column], mib=1)

    def column_halos(even, odd):
        return pairs(even, across, gx_count, 0), pairs(odd, across, gx_count, 1)

    conv_flops = 2 * ROWS * COLS * 9 * CH * CH
    prod = pltpu.VMEM((STEP * COLS, CH), F32)
    side32 = pltpu.VMEM((HALO, CH), F32)
    half_block = shape((HALF, COLS, CH), BF16)

    def forward(band, weight):
        return run(
            lambda *refs: forward_body(*refs, band=band),
            (tissue, features, weight),
            [half_block, shape((2, COLS, CH), F32), shape((6, HALF, CH), F32)],
            [pltpu.VMEM(((HALF + 1) * COLS, 2 * CH), BF16), prod, prod],
            flops=conv_flops // 2,
            mib=16,
        )

    rows = run(
        order_body, (features[:1], features[ROWS - 1 :]), [line, line], flops=conv_flops, mib=2
    )
    outer = run(columns_body, (features,), [column, column], mib=2)
    even, odd = row_halos(*rows)
    slope_a, sums_a, cols_a = forward(0, w_conv)
    even, odd, cols_a = lax.optimization_barrier((even, odd, cols_a))
    top, bot, even, odd = corners(*outer, even, odd)
    weight_b, even = lax.optimization_barrier((w_conv, even))
    even, odd = column_halos(even, odd)
    slope_b, sums_b, cols_b = forward(1, weight_b)
    pooled, token, edge, side = run(
        border_body,
        (
            tissue, features, w_conv, sums_a, sums_b, cols_a, cols_b, top, bot, even, odd, w_stride,
            owner_map.reshape(16),
        ),
        [
            shape((16, CH), F32),
            shape((16, CH + LANES), BF16),
            shape((2, COLS, CH), BF16),
            shape((2, ROWS, CH), F32),
        ],
        [side32],
        flops=conv_flops // 8,
        mib=12,
    )
    def stacked(terms):
        return run(stack_body, terms, shape((len(terms),) + terms[0].shape, BF16), mib=4)

    both = run(
        pair_body, (token, lax.ppermute(token, "core", swap)), shape((32, CH + LANES), BF16), mib=1
    )
    pieces = [both] + others([both] * (gz_count - 1), "gz", gz_count)
    turned, high_w, low_w = run(
        turn_body,
        (features, top, bot, w_query, w_key, w_value, token),
        [shape((CH, (ROWS + 2) * COLS), BF16), shape((CH, 3 * CH), BF16), shape((CH, 3 * CH), BF16)],
        flops=conv_flops // 4,
        mib=12,
    )
    count = 16 * gx_count
    spread, emb = run(
        lambda *refs: attention_body(*refs, seed_scale=loss_scale * norm_scale),
        (*pieces, pooled, high_w, low_w, cotangent.reshape(1, CH), w_stride),
        [shape((4, COLS, CH), F32), shape((16, LANES), BF16)],
        [pltpu.VMEM((count, CH + LANES), BF16), pltpu.VMEM((count, 3 * CH), F32)],
        flops=1 << 30,
        mib=12,
    )
    border = pltpu.VMEM((3, HALO, CH), F32)
    wide, keep, give, *outer = run(
        weight_body,
        (spread, slope_a, slope_b, edge, side, turned, even, odd),
        [
            shape((ROWS * COLS, 3 * CH), BF16),
            shape((9 * CH, LANES), BF16),
            shape((9 * CH, LANES), BF16),
            line,
            line,
            column,
            column,
        ],
        [pltpu.VMEM((3 * CH, 3 * CH), F32), border, border],
        flops=conv_flops,
        mib=20,
    )

    share = -(-9 * CH // (16 * chips)) * 16
    spare = share * chips - 9 * CH
    taken = lax.ppermute(give, "core", swap)
    pre_rows = row_halos(*outer[:2])
    if spare:
        keep, taken = (jnp.pad(a, ((0, spare), (0, 0))) for a in (keep, taken))

    whole_rows = share * chips
    band_rows = share * gz_count
    parts = run(
        chip_sum_body,
        (keep, taken, emb),
        [shape((band_rows + 16, LANES), BF16)] * gy_count,
        [pltpu.VMEM((whole_rows, LANES), BF16)],
        mib=6,
    )[::-1]
    *parts, wide_upper = lax.optimization_barrier((*parts, wide))
    upper, raw = run(
        upper_body,
        (wide_upper, spread, w_conv),
        [shape((UPPER, COLS, CH), BF16), shape((2, HALF, CH), F32)],
        [prod, prod],
        flops=conv_flops // 3,
        mib=12,
    )
    raw, *outer = lax.optimization_barrier((raw, *outer[2:], *pre_rows))
    parts = [parts[0]] + others(parts[1:], "gy", gy_count)[::-1]
    top, bot, even, odd = corners(*outer)
    even, odd = column_halos(even, odd)
    *parts, raw = lax.optimization_barrier((*parts, raw))
    embedding, *parts = run(
        lambda *refs: band_sum_body(*refs, terms=gy_count, norm_scale=norm_scale),
        parts,
        [shape((share, LANES), BF16)] * gz_count + [shape((1, CH), F32)],
        [pltpu.VMEM((band_rows, LANES), BF16)],
        mib=4,
    )[::-1]
    *parts, even, odd = lax.optimization_barrier((*parts, even, odd))
    parts = [parts[0]] + others(parts[1:], "gz", gz_count)[::-1]
    mine = run(last_sum_body, parts, shape((share, LANES), BF16), mib=2)
    row = stacked([mine] + others([mine] * (gz_count - 1), "gz", gz_count))
    row, wide_lower = lax.optimization_barrier((row, wide))
    input_grad = run(
        lower_body,
        (wide_lower, top, bot, even, odd, spread, w_conv, upper, raw),
        shape((ROWS, COLS, CH), BF16),
        [
            prod,
            prod,
            side32,
            pltpu.VMEM((2, ROWS, CH), F32),
            pltpu.VMEM((ROWS - UPPER, COLS, CH), BF16),
            pltpu.VMEM((2, UPPER, 16, CH), BF16),
            pltpu.SemaphoreType.DMA((BLOCKS + 6,)),
        ],
        flops=conv_flops // 2,
        mib=16,
        out_specs=HBM,
    )
    planes = [row] + others([row] * (gy_count - 1), "gy", gy_count)
    *planes, input_grad = lax.optimization_barrier((*planes, input_grad))
    plane = stacked(planes)
    other = lax.ppermute(plane, "core", swap)
    whole = shape((whole_rows, CH), F32)
    buffers = [pltpu.VMEM((whole_rows, LANES), F32), pltpu.SemaphoreType.DMA((gy_count,))]
    half_grad = run(
        lambda *refs: half_body(*refs, other=False), (plane,), whole, buffers, mib=4, out_specs=HBM
    )
    conv_grad = run(
        lambda *refs: half_body(*refs, other=True),
        (other, half_grad),
        whole,
        buffers,
        mib=4,
        far=(1,),
        out_specs=HBM,
        input_output_aliases={1: 0},
    )
    return embedding.reshape(CH), input_grad, conv_grad[: 9 * CH].reshape(9, CH, CH)


def solution(mesh):
    sizes = mesh.devices.shape
    split = Mesh(mesh.devices.reshape(sizes[0], sizes[1] // 2, 2), ("gy", "gz", "core"))
    gx = ("gz", "core")
    in_specs = (P("gy", gx, None), P("gy", gx), P("gy", gx, None, None), P(), P(), P(), P(), P(), P())
    out_specs = (P(), P("gy", gx, None), P())
    return jax.shard_map(per_device, mesh=split, in_specs=in_specs, out_specs=out_specs, check_vma=False)
```

```python
import math

import jax
import jax.numpy as jnp
from jax import lax
from jax.experimental import pallas as pl
from jax.experimental.pallas import tpu as pltpu
from jax.sharding import Mesh, PartitionSpec as P

HEADS = 4
F32 = jnp.float32
BF16 = jnp.bfloat16

attention_bias = -1.0
loss_scale = 512.0

ROWS = 32
COLS = 128
CH = 256
HALO = 48
LANES = 128
STEP = 5
TILE_CELLS = 64


def shape(dims, dtype):
    return jax.ShapeDtypeStruct(dims, dtype)


def nt(left, right):
    return lax.dot_general(left, right, (((1,), (1,)), ((), ())), preferred_element_type=F32)


def tn(left, right):
    return lax.dot_general(left, right, (((0,), (0,)), ((), ())), preferred_element_type=F32)


def nn(left, right):
    return jnp.dot(left, right, preferred_element_type=F32)


def halves(value):
    high = value.astype(BF16)
    return high, (value - high.astype(F32)).astype(BF16)


def wide_product(product, left, right):
    (a, b), (c, d) = left, right
    return product(a, c) + (product(a, d) + product(b, c))


def half_product(product, left, right):
    left = left.astype(BF16)
    return product(left, right[0]) + product(left, right[1])


def iota(dims, axis):
    return lax.broadcasted_iota(jnp.int32, dims, axis)


def gate_of(value):
    return 0.5 * jnp.tanh(0.5 * value) + 0.5


def is_odd(axis):
    return lax.axis_index(axis) % 2 == 1


def order_body(first_ref, last_ref, even_ref, odd_ref):
    order_rows(first_ref[0], last_ref[0], even_ref, odd_ref)


def columns_body(block, left_ref, right_ref):
    row, spot = iota((HALO, ROWS * 16), 0), iota((HALO, ROWS * 16), 1)
    for out, at, place in ((left_ref, 0, 0), (right_ref, COLS - 16, 15)):
        pick = (spot == (row - 1) * 16 + place).astype(F32).astype(BF16)
        out[...] = nn(pick, block[:, at : at + 16].reshape(ROWS * 16, CH)).astype(BF16)


def corner_body(left, right, even, odd, top_ref, bot_ref, even_ref, odd_ref):
    low = is_odd("gy")
    top_ref[0] = jnp.where(low, even[0], odd[0])
    bot_ref[0] = jnp.where(low, odd[0], even[0])
    row = iota((HALO, CH), 0)
    whole = []
    for side, at in ((left, 0), (right, COLS - 16)):
        part = slice(0, 1) if at == 0 else slice(15, 16)
        above = top_ref[0, at : at + 16].astype(F32)[part]
        below = bot_ref[0, at : at + 16].astype(F32)[part]
        whole.append(jnp.where(row == 0, above, jnp.where(row == ROWS + 1, below, side[...].astype(F32))))
    high = is_odd("core")
    even_ref[...] = jnp.where(high, whole[0], whole[1]).astype(BF16)
    odd_ref[...] = jnp.where(high, whole[1], whole[0]).astype(BF16)


def sides(even, odd):
    high = is_odd("core")
    one, two = even[...].astype(F32), odd[...].astype(F32)
    return jnp.where(high, one, two), jnp.where(high, two, one)


def forward_taps(weight, b):
    return jnp.concatenate([weight[3 * a + b] for a in range(3)], axis=0)


HALF = ROWS // 2
BLOCKS = (HALF - 1) // STEP
PARTS = (2, 2, 2, 2, 2, 2, 2, 1)


def with_first(wide, value):
    start = jnp.where(iota((8, wide.shape[1]), 0) == 0, value, wide[0:8])
    return jnp.concatenate([start, wide[8:]], axis=0)


def with_last(wide, value):
    end = jnp.where(iota((8, wide.shape[1]), 0) == 7, value, wide[COLS - 8 :])
    return jnp.concatenate([wide[: COLS - 8], end], axis=0)


def neighbours(row):
    wide = row.astype(F32)
    left = with_first(pltpu.roll(wide, 1, 0), 0.0)
    right = with_last(pltpu.roll(wide, COLS - 1, 0), 0.0)
    return left.astype(BF16), right.astype(BF16)


HALVES = (slice(0, LANES), slice(LANES, CH))


def silu_pair(value, half_mask):
    half = 0.5 * value
    bend = jnp.tanh(half)
    kept = (1.0 + bend) * half_mask
    return value * kept, kept * (1.0 + half * (1.0 - bend))


def forward_body(flags_ref, feat, weight, slope_ref, sums, cols, wide, prod_a, prod_b, *, band):
    sums[...] = jnp.zeros_like(sums)
    base = (HALF - 1) * band
    halves_of_mask = [0.5 * flags_ref[band, tile].astype(F32) for tile in range(8)]

    def build(i):
        here = slice(i * COLS, (i + 1) * COLS)
        for lanes in HALVES:
            left, right = neighbours(feat[base + i, :, lanes])
            wide[here, lanes] = left
            wide[here, lanes.start + CH : lanes.stop + CH] = right

    def around(start, count):
        taken = []
        for a in range(3):
            here = slice((start + a) * COLS, (start + a + count) * COLS)
            rows = feat[base + start + a : base + start + a + count].reshape(count * COLS, CH)
            taken += [wide[here, 0:CH], rows, wide[here, CH:]]
        return jnp.concatenate(taken, axis=1)

    def finish(r, prod, first):
        at = r - HALF * band
        for tile in range(8):
            here = slice(16 * tile, 16 * tile + 16)
            value = prod[first + 16 * tile : first + 16 * tile + 16]
            pixel = feat[r, here].astype(F32)
            bent, slope = silu_pair(value, halves_of_mask[tile])
            summed = pixel + bent
            slope_ref[at, here] = slope.astype(BF16)
            sums[r % 2, here] += summed
            if tile in (0, 7):
                edge = slice(0, 1) if tile == 0 else slice(15, 16)
                for i, part in enumerate((value, summed, pixel)):
                    cols[2 * i + tile // 7, at : at + 1] = part[edge]

    prods = (prod_a, prod_b)
    parts = PARTS
    built, done = parts[0] + 2, 0
    for i in range(built):
        build(i)
    for block in range(len(parts) + 1):
        start = sum(parts[:block])
        if block < len(parts):
            prods[block % 2][0 : parts[block] * COLS] = nn(
                around(start, parts[block]), weight[...].reshape(9 * CH, CH)
            )
        ahead = min(HALF + 1, sum(parts[: block + 2]) + 2)
        for j in range(STEP):
            if done < start:
                finish(base + 1 + done, prods[(block - 1) % 2], (done - sum(parts[: block - 1])) * COLS)
                done += 1
            if built < ahead:
                build(built)
                built += 1


def border_body(
    flags_ref, feat, weight, sums_a, sums_b, cols_a, cols_b, top, bot, even, odd, strided, owner_ref,
    pooled_ref, token_ref, edge_ref, side_ref, side32,
):
    added = []
    cols = [jnp.concatenate([cols_a[i], cols_b[i]], axis=0) for i in range(6)]
    for i, whole in enumerate(sides(even, odd)):
        side32[...] = whole
        near = [side32[a : a + ROWS].astype(BF16) for a in range(3)]
        added.append(jnp.concatenate(near, axis=1))

    def pair(one, two):
        return jnp.concatenate([one, two], axis=0)

    taken = jnp.concatenate(
        [pair(top[0], feat[ROWS - 2]), pair(feat[0], feat[ROWS - 1]), pair(feat[1], bot[0])], axis=1
    )
    mid = nn(taken, forward_taps(weight, 1))
    low, high = (nn(pair(taken, added[i]), forward_taps(weight, 2 * i)) for i in range(2))
    added = [part[2 * COLS :] for part in (low, high)]
    rows = []
    for i, r in enumerate((0, ROWS - 1)):
        part = slice(i * COLS, (i + 1) * COLS)
        before = with_first(pltpu.roll(low[part], 1, 0), added[0][r : r + 1])
        after = with_last(pltpu.roll(high[part], COLS - 1, 0), added[1][r : r + 1])
        value = mid[part] + before + after
        keep = jnp.concatenate(
            [0.5 * jnp.full((16, CH), flags_ref[i, t], jnp.int32).astype(F32) for t in range(8)], axis=0
        )
        bent, slope = silu_pair(value, keep)
        edge_ref[i] = slope.astype(BF16)
        rows.append(feat[r].astype(F32) + bent)

    line = iota((ROWS, CH), 0)
    deltas = []
    for i in range(2):
        tile = 7 * i
        keep = 0.5 * jnp.where(line < ROWS // 2, flags_ref[0, tile], flags_ref[1, tile]).astype(F32)
        bent, side_ref[i] = silu_pair(cols[i] + added[i], keep)
        inside = (line > 0) & (line < ROWS - 1)
        deltas.append(jnp.where(inside, cols[4 + i] + bent - cols[2 + i], 0.0))

    row, spot = iota((16, COLS), 0), iota((16, COLS), 1)
    pick = ((spot // 16 == row % 8) & (spot % 2 == row // 8)).astype(F32).astype(BF16)
    pick = jnp.concatenate([pick, pick], axis=1)
    place = iota((16, CH), 0)
    parts = {}
    for band in range(2):
        for a in range(2):
            total = (sums_a, sums_b)[band][a]
            if band == a:
                total += rows[band]
            part = nn(pick, jnp.concatenate(halves(total), axis=0))
            mine = (line // 16 == band) & (line % 2 == a)
            for i in range(2):
                delta = jnp.sum(jnp.where(mine, deltas[i], 0.0), axis=0, keepdims=True)
                part += jnp.where(place == 15 * i, delta, 0.0)
            parts[band, a] = part
    taken = [
        jnp.concatenate([parts[band, a][8 * b : 8 * b + 8] for band in range(2)], axis=0)
        for a in range(2)
        for b in range(2)
    ]
    both = nn(pair(*halves(jnp.concatenate(taken, axis=1))), strided[...].reshape(4 * CH, CH))
    pooled = (both[0:16] + both[16:32]) * (1.0 / TILE_CELLS)
    pooled_ref[...] = pooled
    normed = pooled * lax.rsqrt(jnp.mean(pooled * pooled, axis=-1, keepdims=True) + 1e-05)
    token_ref[:, 0:CH] = normed.astype(BF16)
    owner = jnp.full((16, LANES), -1, jnp.int32)
    for tile in range(16):
        named = jnp.where(flags_ref[tile // 8, tile % 8] != 0, owner_ref[tile], -1)
        owner = jnp.where(iota((16, LANES), 0) == tile, named, owner)
    token_ref[:, CH:] = (owner == iota((16, LANES), 1)).astype(F32).astype(BF16)


def turn_body(feat, top, bot, w_query, w_key, w_value, token, turned_ref, high_ref, low_ref):
    turned_ref[:, 0:COLS] = top[0].T
    turned_ref[:, (ROWS + 1) * COLS :] = bot[0].T

    @pl.loop(0, ROWS // 4)
    def _(i):
        for j in range(4):
            here = pl.multiple_of((4 * i + j + 1) * COLS, COLS)
            turned_ref[:, pl.ds(here, COLS)] = feat[4 * i + j].T

    for i, one in enumerate((w_query, w_key, w_value)):
        high, low = halves(one[...])
        high_ref[:, i * CH : (i + 1) * CH] = high
        low_ref[:, i * CH : (i + 1) * CH] = low


def pair_body(one, two, out_ref):
    out_ref[0:16] = one[...]
    out_ref[16:32] = two[...]


def attention_body(*refs, seed_scale):
    *got, pooled_ref, high_w, low_w, cot, strided, spread_ref, emb_ref, band, grad_ref = refs
    gz, core = lax.axis_index("gz"), lax.axis_index("core")

    def rows_of(depth, other):
        return pl.ds(pl.multiple_of(depth * 32 + other * 16, 16), 16)

    for k, piece in enumerate(got):
        depth = lax.bitwise_xor(gz, k)
        band[rows_of(depth, core)] = piece[0:16]
        band[rows_of(depth, 1 - core)] = piece[16:32]
    count = band.shape[0]
    tokens, group = band[:, 0:CH], band[:, CH:]
    pair = nt(group, group)
    pairs = jnp.concatenate([pair] * HEADS, axis=0)
    projected = nn(tokens, high_w[...]) + nn(tokens, low_w[...])
    query, key, value = (projected[:, i * CH : (i + 1) * CH] for i in range(3))
    lane = iota((1, CH), 1) // (CH // HEADS)
    scale = 1.0 / math.sqrt(CH // HEADS)

    def by_head(array):
        return jnp.concatenate([jnp.where(lane == h, array, 0.0) for h in range(HEADS)], axis=0)

    queries, keys = halves(by_head(query)), halves(by_head(key))
    gate = gate_of(wide_product(nt, queries, halves(key)) * scale + attention_bias)
    weights = gate * pairs
    seed = cot[...] * seed_scale
    seeds = jnp.where(lane == iota((8, CH), 0), seed, 0.0)
    values = halves(value)
    along = wide_product(nt, halves(seeds), values)
    columns, grads = [], []
    for h in range(HEADS):
        part = slice(h * count, (h + 1) * count)
        columns.append(jnp.sum(weights[part], axis=0, keepdims=True))
        grads.append(weights[part] * (1.0 - gate[part]) * (along[h : h + 1] * scale))
    columns = halves(jnp.concatenate(columns + [jnp.zeros((8 - HEADS, count), F32)], axis=0))
    grad_ref[:, 0:CH] = half_product(nn, jnp.concatenate(grads, axis=1), keys)
    grad_ref[:, CH : 2 * CH] = half_product(tn, jnp.concatenate(grads, axis=0), queries)
    grad_ref[:, 2 * CH :] = half_product(tn, columns[0], halves(seeds))
    mixed = wide_product(nn, columns, values)
    mixed = jnp.sum(jnp.where(lane == iota((8, CH), 0), mixed, 0.0), axis=0, keepdims=True)
    high = mixed.astype(BF16).astype(F32)
    low = mixed - high
    rows = iota((16, LANES), 0)
    packed = jnp.zeros((16, LANES), F32)
    for i, part in enumerate((high[:, :LANES], high[:, LANES:], low[:, :LANES], low[:, LANES:])):
        packed = jnp.where(rows == i, part, packed)
    emb_ref[...] = packed.astype(BF16)

    grad = half_product(nt, grad_ref[rows_of(gz, core)], (high_w[...], low_w[...]))
    grad = grad.astype(BF16).astype(F32)
    pooled = pooled_ref[...]
    inv = lax.rsqrt(jnp.mean(pooled * pooled, axis=-1, keepdims=True) + 1e-05)
    unit = pooled * inv
    back = inv * (grad - unit * jnp.mean(grad * unit, axis=-1, keepdims=True))
    cell = (back * (1.0 / TILE_CELLS)).astype(BF16)
    spot, row = iota((COLS, 16), 0), iota((COLS, 16), 1)
    expand = ((spot // 16 == row % 8) & (spot % 2 == row // 8)).astype(F32).astype(BF16)
    expand = jnp.concatenate([expand, expand], axis=1)
    taps = nt(cell, strided[...].reshape(4 * CH, CH))
    for band in range(2):
        here = taps[8 * band : 8 * band + 8]
        both = [
            jnp.concatenate([here[:, (2 * a + b) * CH : (2 * a + b + 1) * CH] for a in range(2)], axis=1)
            for b in range(2)
        ]
        spread = nn(expand, jnp.concatenate(halves(jnp.concatenate(both, axis=0)), axis=0))
        for a in range(2):
            spread_ref[band * 2 + a] = spread[:, a * CH : (a + 1) * CH]


GROUPS = (6, 10, 16)


def weight_body(
    spread, slope_a, slope_b, edge, side, turned, even, odd,
    wide, keep_ref, give_ref, even_ref, odd_ref, left_ref, right_ref, total, first, last,
):
    first[...] = jnp.zeros_like(first)
    last[...] = jnp.zeros_like(last)

    def build(r):
        if r in (0, ROWS - 1):
            slope = edge[r // HALF].astype(F32)
        else:
            slope = (slope_a, slope_b)[r // HALF][r % HALF].astype(F32)
            slope = with_last(with_first(slope, side[0, r : r + 1]), side[1, r : r + 1])
        grad = (spread[(r // HALF) * 2 + r % 2] * slope).astype(BF16)
        here = slice(r * COLS, (r + 1) * COLS)
        wide[here, 2 * CH :], wide[here, 0:CH] = neighbours(grad)
        wide[here, CH : 2 * CH] = grad
        full = grad.astype(F32)
        for a in range(3):
            first[a, r + a : r + a + 1] = full[0:1]
            last[a, r + a : r + a + 1] = full[COLS - 1 :]

    is_one = is_odd("core")
    left, right = (part.astype(BF16) for part in sides(even, odd))

    def put(part, a, b):
        if b == 0:
            part += tn(left, first[a].astype(BF16))
        if b == 2:
            part += tn(right, last[a].astype(BF16))
        low, high = part[:, :LANES], part[:, LANES:]
        at = slice((3 * a + b) * CH, (3 * a + b + 1) * CH)
        keep_ref[at] = jnp.where(is_one, high, low).astype(BF16)
        give_ref[at] = jnp.where(is_one, low, high).astype(BF16)

    for r in range(GROUPS[0]):
        build(r)
    start = 0
    for g, count in enumerate(GROUPS):
        here = slice(start * COLS, (start + count) * COLS)
        near = [turned[:, (start + a) * COLS : (start + a + count) * COLS] for a in range(3)]
        near = jnp.concatenate(near, axis=0)
        start += count
        ahead = GROUPS[g + 1] if g + 1 < len(GROUPS) else 0
        for b in range(3):
            part = slice(b * CH, (b + 1) * CH)
            result = nn(near, wide[here, part])
            if g > 0:
                result += total[:, part]
            if ahead:
                total[:, part] = result
            for r in range(ahead * b // 3, ahead * (b + 1) // 3):
                build(start + r)
            if not ahead:
                for a in range(3):
                    put(result[a * CH : (a + 1) * CH], a, b)

    centre = slice(CH, 2 * CH)
    order_rows(wide[0:COLS, centre], wide[(ROWS - 1) * COLS :, centre], even_ref, odd_ref)
    left_ref[...] = first[1].astype(BF16)
    right_ref[...] = last[1].astype(BF16)


def order_rows(first, last, even_ref, odd_ref):
    odd = is_odd("gy")
    even_ref[0] = jnp.where(odd, first, last)
    odd_ref[0] = jnp.where(odd, last, first)


def back_taps(weight, taps):
    return jnp.concatenate([weight[tap] for tap in taps], axis=1)


def input_blocks(wide, weight, first, blocks, prods, finish, send=None):
    for block in range(blocks + 1):
        if block < blocks:
            at = first + STEP * block
            near = [wide[(at + step) * COLS : (at + step + STEP) * COLS] for step in (1, 0, -1)]
            prods[block % 2][...] = nt(jnp.concatenate(near, axis=1), back_taps(weight, range(9)))
        if block > 0:
            at = first + STEP * (block - 1)
            for j in range(STEP):
                finish(at + j, prods[(block - 1) % 2][j * COLS : (j + 1) * COLS])
            if send is not None:
                send(at, STEP)


UPPER = 2 * STEP


def upper_body(wide, spread, weight, done, raw_ref, prod_a, prod_b):
    def finish(r, prod):
        value = spread[r % 2] + prod
        done[r - 1] = value.astype(BF16)
        raw_ref[0, r : r + 1] = value[0:1]
        raw_ref[1, r : r + 1] = value[COLS - 1 :]

    input_blocks(wide, weight, 1, UPPER // STEP, (prod_a, prod_b), finish)


def lower_body(
    wide, top, bot, even, odd, spread, weight, upper, raw, out, prod_a, prod_b, side32, added, done, fixed, sems
):
    started = []

    def start(source, target):
        started.append(pltpu.make_async_copy(source, target, sems.at[len(started)]))
        started[-1].start()

    start(upper.at[:, 16 : COLS - 16], out.at[1 : UPPER + 1, 16 : COLS - 16])
    for i, whole in enumerate(sides(even, odd)):
        side32[...] = whole
        near = [side32[2 - a : 2 - a + ROWS].astype(BF16) for a in range(3)]
        taps = back_taps(weight, [3 * a + 2 - 2 * i for a in range(3)])
        added[i] = nt(jnp.concatenate(near, axis=1), taps)

    small = iota((16, CH), 0)
    for i in range(2):
        at = (COLS - 16) * i
        for r in range(1, UPPER + 1):
            value = raw[i, r : r + 1] + added[i, r : r + 1]
            old = upper[r - 1, at : at + 16].astype(F32)
            fixed[i, r - 1] = jnp.where(small == 15 * i, value, old).astype(BF16)
        start(fixed.at[i], out.at[1 : UPPER + 1, at : at + 16])

    def place(r):
        return r - UPPER if r else 0

    def finish(r, prod):
        prod = with_first(prod, prod[0:1] + added[0, r : r + 1])
        prod = with_last(prod, prod[COLS - 1 :] + added[1, r : r + 1])
        done[place(r)] = (spread[(r // HALF) * 2 + r % 2] + prod).astype(BF16)

    def send(first, count):
        start(done.at[place(first) : place(first) + count], out.at[first : first + count])

    input_blocks(wide, weight, UPPER + 1, (ROWS - 2 - UPPER) // STEP, (prod_a, prod_b), finish, send)

    def row(r):
        return wide[r * COLS : (r + 1) * COLS]

    def outside(one):
        left, right = neighbours(one[0])
        return jnp.concatenate([right, one[0], left], axis=1)

    def pair(one, two):
        return jnp.concatenate([one, two], axis=0)

    near = [pair(row(1), outside(bot)), pair(row(0), row(ROWS - 1)), pair(outside(top), row(ROWS - 2))]
    both = nt(jnp.concatenate(near, axis=1), back_taps(weight, range(9)))
    for i, r in enumerate((0, ROWS - 1)):
        finish(r, both[i * COLS : (i + 1) * COLS])
        send(r, 1)
    for one in started:
        one.wait()


def add_up(refs, rows):
    total = refs[0][0:rows].astype(F32)
    for one in refs[1:]:
        total += one[0:rows].astype(F32)
    return total.astype(BF16)


def deal(total_ref, outs, size, axis):
    for k, out in enumerate(reversed(outs)):
        at = lax.bitwise_xor(lax.axis_index(axis), k) * size
        out[0:size] = total_ref[pl.ds(pl.multiple_of(at, 16), size)]


def chip_sum_body(one, two, emb, *refs):
    outs, total_ref = refs[:-1], refs[-1]
    rows = one.shape[0]
    size = rows // len(outs)
    total_ref[...] = add_up((one, two), rows)
    deal(total_ref, outs, size, "gy")
    for out in outs:
        out[size:] = emb[...]


def band_sum_body(*refs, terms, norm_scale):
    outs, emb_ref, total_ref = refs[terms:-2], refs[-2], refs[-1]
    rows = total_ref.shape[0]
    total_ref[...] = add_up(refs[:terms], rows)
    deal(total_ref, outs, rows // len(outs), "gz")
    embs = []
    for one in (refs[0], *refs[terms - 1 : 0 : -1]):
        part = one[rows : rows + 16].astype(F32)
        embs.append(part[0:2] + part[2:4])
    while len(embs) > 1:
        embs = [a + b for a, b in zip(embs[0::2], embs[1::2])]
    emb_ref[:, 0:LANES] = embs[0][0:1] * norm_scale
    emb_ref[:, LANES:] = embs[0][1:2] * norm_scale


def last_sum_body(*refs):
    refs[-1][...] = add_up(refs[:-1], refs[-1].shape[0])


def stack_body(*refs):
    for i, one in enumerate(refs[:-1]):
        refs[-1][i] = one[...]


def half_body(array, *refs, other):
    grad_ref, buf, sems = refs[-3:]
    gy, gz, core = (lax.axis_index(name) for name in ("gy", "gz", "core"))
    bands, depth, share = array.shape[:3]
    half = 1 - core if other else core
    lanes = pl.ds(pl.multiple_of(half * LANES, LANES), LANES)
    started = []
    for k in range(bands):
        first = lax.bitwise_xor(gy, k) * (depth * share)
        for j in range(depth):
            at = first + lax.bitwise_xor(gz, j) * share
            buf[pl.ds(pl.multiple_of(at, 16), share)] = array[k, j].astype(F32) * (1.0 / loss_scale)
        here = pl.ds(pl.multiple_of(first, 16), depth * share)
        started.append(pltpu.make_async_copy(buf.at[here], grad_ref.at[here, lanes], sems.at[k]))
        started[-1].start()
    for one in started:
        one.wait()


SMEM = pl.BlockSpec(memory_space=pltpu.SMEM)
VMEM = pl.BlockSpec(memory_space=pltpu.VMEM)
HBM = pl.BlockSpec(memory_space=pltpu.HBM)


def run(body, args, outs, scratch=(), flops=1 << 20, mib=8, far=(), **rest):
    specs = [HBM if i in far else SMEM if a.dtype == jnp.int32 else VMEM for i, a in enumerate(args)]
    return pl.pallas_call(
        body,
        in_specs=specs,
        out_shape=outs,
        scratch_shapes=list(scratch),
        compiler_params=pltpu.CompilerParams(vmem_limit_bytes=mib << 20),
        cost_estimate=pl.CostEstimate(flops=flops, bytes_accessed=1 << 20, transcendentals=0),
        **rest,
    )(*args)


def per_device(features, tissue, owner_map, w_conv, w_stride, w_query, w_key, w_value, cotangent):
    gy_count, gz_count, cores = lax.axis_size("gy"), lax.axis_size("gz"), lax.axis_size("core")
    gx_count, chips = gz_count * cores, gy_count * gz_count
    across = ("gz", "core")
    norm_scale = 1.0 / math.sqrt(16 * gy_count * gx_count)
    swap = [(i, i ^ 1) for i in range(cores)]

    def pairs(value, axis, count, odd):
        low = range(odd, count - 1, 2)
        return lax.ppermute(value, axis, [(i, i + 1) for i in low] + [(i + 1, i) for i in low])

    def others(values, axis, count):
        got = [
            lax.ppermute(values[k - 1], axis, [(i, i ^ k) for i in range(count)])
            for k in range(count - 1, 0, -1)
        ]
        return got[::-1]

    column = shape((HALO, CH), BF16)
    line = shape((1, COLS, CH), BF16)

    def row_halos(even, odd):
        return pairs(even, "gy", gy_count, 0), pairs(odd, "gy", gy_count, 1)

    def corners(left, right, even, odd):
        return run(corner_body, (left, right, even, odd), [line, line, column, column], mib=1)

    def column_halos(even, odd):
        return pairs(even, across, gx_count, 0), pairs(odd, across, gx_count, 1)

    conv_flops = 2 * ROWS * COLS * 9 * CH * CH
    prod = pltpu.VMEM((STEP * COLS, CH), F32)
    side32 = pltpu.VMEM((HALO, CH), F32)
    half_block = shape((HALF, COLS, CH), BF16)

    def forward(band, weight):
        return run(
            lambda *refs: forward_body(*refs, band=band),
            (tissue, features, weight),
            [half_block, shape((2, COLS, CH), F32), shape((6, HALF, CH), F32)],
            [pltpu.VMEM(((HALF + 1) * COLS, 2 * CH), BF16), prod, prod],
            flops=conv_flops // 2,
            mib=16,
        )

    rows = run(
        order_body, (features[:1], features[ROWS - 1 :]), [line, line], flops=conv_flops, mib=2
    )
    outer = run(columns_body, (features,), [column, column], mib=2)
    even, odd = row_halos(*rows)
    slope_a, sums_a, cols_a = forward(0, w_conv)
    even, odd, cols_a = lax.optimization_barrier((even, odd, cols_a))
    top, bot, even, odd = corners(*outer, even, odd)
    weight_b, even = lax.optimization_barrier((w_conv, even))
    even, odd = column_halos(even, odd)
    slope_b, sums_b, cols_b = forward(1, weight_b)
    pooled, token, edge, side = run(
        border_body,
        (
            tissue, features, w_conv, sums_a, sums_b, cols_a, cols_b, top, bot, even, odd, w_stride,
            owner_map.reshape(16),
        ),
        [
            shape((16, CH), F32),
            shape((16, CH + LANES), BF16),
            shape((2, COLS, CH), BF16),
            shape((2, ROWS, CH), F32),
        ],
        [side32],
        flops=conv_flops // 8,
        mib=12,
    )
    def stacked(terms):
        return run(stack_body, terms, shape((len(terms),) + terms[0].shape, BF16), mib=4)

    both = run(
        pair_body, (token, lax.ppermute(token, "core", swap)), shape((32, CH + LANES), BF16), mib=1
    )
    pieces = [both] + others([both] * (gz_count - 1), "gz", gz_count)
    turned, high_w, low_w = run(
        turn_body,
        (features, top, bot, w_query, w_key, w_value, token),
        [shape((CH, (ROWS + 2) * COLS), BF16), shape((CH, 3 * CH), BF16), shape((CH, 3 * CH), BF16)],
        flops=conv_flops // 4,
        mib=12,
    )
    count = 16 * gx_count
    spread, emb = run(
        lambda *refs: attention_body(*refs, seed_scale=loss_scale * norm_scale),
        (*pieces, pooled, high_w, low_w, cotangent.reshape(1, CH), w_stride),
        [shape((4, COLS, CH), F32), shape((16, LANES), BF16)],
        [pltpu.VMEM((count, CH + LANES), BF16), pltpu.VMEM((count, 3 * CH), F32)],
        flops=1 << 30,
        mib=12,
    )
    border = pltpu.VMEM((3, HALO, CH), F32)
    wide, keep, give, *outer = run(
        weight_body,
        (spread, slope_a, slope_b, edge, side, turned, even, odd),
        [
            shape((ROWS * COLS, 3 * CH), BF16),
            shape((9 * CH, LANES), BF16),
            shape((9 * CH, LANES), BF16),
            line,
            line,
            column,
            column,
        ],
        [pltpu.VMEM((3 * CH, 3 * CH), F32), border, border],
        flops=conv_flops,
        mib=20,
    )

    share = -(-9 * CH // (16 * chips)) * 16
    spare = share * chips - 9 * CH
    taken = lax.ppermute(give, "core", swap)
    pre_rows = row_halos(*outer[:2])
    if spare:
        keep, taken = (jnp.pad(a, ((0, spare), (0, 0))) for a in (keep, taken))

    whole_rows = share * chips
    band_rows = share * gz_count
    parts = run(
        chip_sum_body,
        (keep, taken, emb),
        [shape((band_rows + 16, LANES), BF16)] * gy_count,
        [pltpu.VMEM((whole_rows, LANES), BF16)],
        mib=6,
    )[::-1]
    *parts, wide_upper = lax.optimization_barrier((*parts, wide))
    upper, raw = run(
        upper_body,
        (wide_upper, spread, w_conv),
        [shape((UPPER, COLS, CH), BF16), shape((2, HALF, CH), F32)],
        [prod, prod],
        flops=conv_flops // 3,
        mib=12,
    )
    raw, *outer = lax.optimization_barrier((raw, *outer[2:], *pre_rows))
    parts = [parts[0]] + others(parts[1:], "gy", gy_count)[::-1]
    top, bot, even, odd = corners(*outer)
    even, odd = column_halos(even, odd)
    *parts, raw = lax.optimization_barrier((*parts, raw))
    embedding, *parts = run(
        lambda *refs: band_sum_body(*refs, terms=gy_count, norm_scale=norm_scale),
        parts,
        [shape((share, LANES), BF16)] * gz_count + [shape((1, CH), F32)],
        [pltpu.VMEM((band_rows, LANES), BF16)],
        mib=4,
    )[::-1]
    *parts, even, odd = lax.optimization_barrier((*parts, even, odd))
    parts = [parts[0]] + others(parts[1:], "gz", gz_count)[::-1]
    mine = run(last_sum_body, parts, shape((share, LANES), BF16), mib=2)
    row = stacked([mine] + others([mine] * (gz_count - 1), "gz", gz_count))
    row, wide_lower = lax.optimization_barrier((row, wide))
    input_grad = run(
        lower_body,
        (wide_lower, top, bot, even, odd, spread, w_conv, upper, raw),
        shape((ROWS, COLS, CH), BF16),
        [
            prod,
            prod,
            side32,
            pltpu.VMEM((2, ROWS, CH), F32),
            pltpu.VMEM((ROWS - UPPER, COLS, CH), BF16),
            pltpu.VMEM((2, UPPER, 16, CH), BF16),
            pltpu.SemaphoreType.DMA((BLOCKS + 6,)),
        ],
        flops=conv_flops // 2,
        mib=16,
        out_specs=HBM,
    )
    planes = [row] + others([row] * (gy_count - 1), "gy", gy_count)
    *planes, input_grad = lax.optimization_barrier((*planes, input_grad))
    plane = stacked(planes)
    other = lax.ppermute(plane, "core", swap)
    whole = shape((whole_rows, CH), F32)
    buffers = [pltpu.VMEM((whole_rows, LANES), F32), pltpu.SemaphoreType.DMA((gy_count,))]
    half_grad = run(
        lambda *refs: half_body(*refs, other=False), (plane,), whole, buffers, mib=4, out_specs=HBM
    )
    conv_grad = run(
        lambda *refs: half_body(*refs, other=True),
        (other, half_grad),
        whole,
        buffers,
        mib=4,
        far=(1,),
        out_specs=HBM,
        input_output_aliases={1: 0},
    )
    return embedding.reshape(CH), input_grad, conv_grad[: 9 * CH].reshape(9, CH, CH)


def solution(mesh):
    sizes = mesh.devices.shape
    split = Mesh(mesh.devices.reshape(sizes[0], sizes[1] // 2, 2), ("gy", "gz", "core"))
    gx = ("gz", "core")
    in_specs = (P("gy", gx, None), P("gy", gx), P("gy", gx, None, None), P(), P(), P(), P(), P(), P())
    out_specs = (P(), P("gy", gx, None), P())
    return jax.shard_map(per_device, mesh=split, in_specs=in_specs, out_specs=out_specs, check_vma=False)
```

```python
import math

import jax
import jax.numpy as jnp
from jax import lax
from jax.experimental import pallas as pl
from jax.experimental.pallas import tpu as pltpu
from jax.sharding import Mesh, PartitionSpec as P

HEADS = 4
F32 = jnp.float32
BF16 = jnp.bfloat16

attention_bias = -1.0
loss_scale = 512.0

ROWS = 32
COLS = 128
CH = 256
HALO = 48
LANES = 128
STEP = 5
TILE_CELLS = 64


def shape(dims, dtype):
    return jax.ShapeDtypeStruct(dims, dtype)


def nt(left, right):
    return lax.dot_general(left, right, (((1,), (1,)), ((), ())), preferred_element_type=F32)


def tn(left, right):
    return lax.dot_general(left, right, (((0,), (0,)), ((), ())), preferred_element_type=F32)


def nn(left, right):
    return jnp.dot(left, right, preferred_element_type=F32)


def halves(value):
    high = value.astype(BF16)
    return high, (value - high.astype(F32)).astype(BF16)


def wide_product(product, left, right):
    (a, b), (c, d) = left, right
    return product(a, c) + (product(a, d) + product(b, c))


def half_product(product, left, right):
    left = left.astype(BF16)
    return product(left, right[0]) + product(left, right[1])


def iota(dims, axis):
    return lax.broadcasted_iota(jnp.int32, dims, axis)


def gate_of(value):
    return 0.5 * jnp.tanh(0.5 * value) + 0.5


def is_odd(axis):
    return lax.axis_index(axis) % 2 == 1


def order_body(first_ref, last_ref, even_ref, odd_ref):
    order_rows(first_ref[0], last_ref[0], even_ref, odd_ref)


def columns_body(block, left_ref, right_ref):
    row, spot = iota((HALO, ROWS * 16), 0), iota((HALO, ROWS * 16), 1)
    for out, at, place in ((left_ref, 0, 0), (right_ref, COLS - 16, 15)):
        pick = (spot == (row - 1) * 16 + place).astype(F32).astype(BF16)
        out[...] = nn(pick, block[:, at : at + 16].reshape(ROWS * 16, CH)).astype(BF16)


def corner_body(left, right, even, odd, top_ref, bot_ref, even_ref, odd_ref):
    low = is_odd("gy")
    top_ref[0] = jnp.where(low, even[0], odd[0])
    bot_ref[0] = jnp.where(low, odd[0], even[0])
    row = iota((HALO, CH), 0)
    whole = []
    for side, at in ((left, 0), (right, COLS - 16)):
        part = slice(0, 1) if at == 0 else slice(15, 16)
        above = top_ref[0, at : at + 16].astype(F32)[part]
        below = bot_ref[0, at : at + 16].astype(F32)[part]
        whole.append(jnp.where(row == 0, above, jnp.where(row == ROWS + 1, below, side[...].astype(F32))))
    high = is_odd("core")
    even_ref[...] = jnp.where(high, whole[0], whole[1]).astype(BF16)
    odd_ref[...] = jnp.where(high, whole[1], whole[0]).astype(BF16)


def sides(even, odd):
    high = is_odd("core")
    one, two = even[...].astype(F32), odd[...].astype(F32)
    return jnp.where(high, one, two), jnp.where(high, two, one)


def forward_taps(weight, b):
    return jnp.concatenate([weight[3 * a + b] for a in range(3)], axis=0)


HALF = ROWS // 2
BLOCKS = (HALF - 1) // STEP
PARTS = (2, 2, 2, 2, 2, 2, 2, 1)


def with_first(wide, value):
    start = jnp.where(iota((8, wide.shape[1]), 0) == 0, value, wide[0:8])
    return jnp.concatenate([start, wide[8:]], axis=0)


def with_last(wide, value):
    end = jnp.where(iota((8, wide.shape[1]), 0) == 7, value, wide[COLS - 8 :])
    return jnp.concatenate([wide[: COLS - 8], end], axis=0)


def neighbours(row):
    wide = row.astype(F32)
    left = with_first(pltpu.roll(wide, 1, 0), 0.0)
    right = with_last(pltpu.roll(wide, COLS - 1, 0), 0.0)
    return left.astype(BF16), right.astype(BF16)


HALVES = (slice(0, LANES), slice(LANES, CH))


def silu_pair(value, half_mask):
    half = 0.5 * value
    bend = jnp.tanh(half)
    kept = (1.0 + bend) * half_mask
    return value * kept, kept * (1.0 + half * (1.0 - bend))


def forward_body(flags_ref, feat, weight, slope_ref, sums, cols, wide, prod_a, prod_b, *, band):
    sums[...] = jnp.zeros_like(sums)
    base = (HALF - 1) * band
    halves_of_mask = [0.5 * flags_ref[band, tile].astype(F32) for tile in range(8)]

    def build(i):
        here = slice(i * COLS, (i + 1) * COLS)
        for lanes in HALVES:
            left, right = neighbours(feat[base + i, :, lanes])
            wide[here, lanes] = left
            wide[here, lanes.start + CH : lanes.stop + CH] = right

    def around(start, count):
        taken = []
        for a in range(3):
            here = slice((start + a) * COLS, (start + a + count) * COLS)
            rows = feat[base + start + a : base + start + a + count].reshape(count * COLS, CH)
            taken += [wide[here, 0:CH], rows, wide[here, CH:]]
        return jnp.concatenate(taken, axis=1)

    def finish(r, prod, first):
        at = r - HALF * band
        for tile in range(8):
            here = slice(16 * tile, 16 * tile + 16)
            value = prod[first + 16 * tile : first + 16 * tile + 16]
            pixel = feat[r, here].astype(F32)
            bent, slope = silu_pair(value, halves_of_mask[tile])
            summed = pixel + bent
            slope_ref[at, here] = slope.astype(BF16)
            sums[r % 2, here] += summed
            if tile in (0, 7):
                edge = slice(0, 1) if tile == 0 else slice(15, 16)
                for i, part in enumerate((value, summed, pixel)):
                    cols[2 * i + tile // 7, at : at + 1] = part[edge]

    prods = (prod_a, prod_b)
    parts = PARTS
    built, done = parts[0] + 2, 0
    for i in range(built):
        build(i)
    for block in range(len(parts) + 1):
        start = sum(parts[:block])
        if block < len(parts):
            prods[block % 2][0 : parts[block] * COLS] = nn(
                around(start, parts[block]), weight[...].reshape(9 * CH, CH)
            )
        ahead = min(HALF + 1, sum(parts[: block + 2]) + 2)
        for j in range(STEP):
            if done < start:
                finish(base + 1 + done, prods[(block - 1) % 2], (done - sum(parts[: block - 1])) * COLS)
                done += 1
            if built < ahead:
                build(built)
                built += 1


def border_body(
    flags_ref, feat, weight, sums_a, sums_b, cols_a, cols_b, top, bot, even, odd, strided, owner_ref,
    pooled_ref, token_ref, edge_ref, side_ref, side32,
):
    added = []
    cols = [jnp.concatenate([cols_a[i], cols_b[i]], axis=0) for i in range(6)]
    for i, whole in enumerate(sides(even, odd)):
        side32[...] = whole
        near = [side32[a : a + ROWS].astype(BF16) for a in range(3)]
        added.append(jnp.concatenate(near, axis=1))

    def pair(one, two):
        return jnp.concatenate([one, two], axis=0)

    taken = jnp.concatenate(
        [pair(top[0], feat[ROWS - 2]), pair(feat[0], feat[ROWS - 1]), pair(feat[1], bot[0])], axis=1
    )
    mid = nn(taken, forward_taps(weight, 1))
    low, high = (nn(pair(taken, added[i]), forward_taps(weight, 2 * i)) for i in range(2))
    added = [part[2 * COLS :] for part in (low, high)]
    rows = []
    for i, r in enumerate((0, ROWS - 1)):
        part = slice(i * COLS, (i + 1) * COLS)
        before = with_first(pltpu.roll(low[part], 1, 0), added[0][r : r + 1])
        after = with_last(pltpu.roll(high[part], COLS - 1, 0), added[1][r : r + 1])
        value = mid[part] + before + after
        keep = jnp.concatenate(
            [0.5 * jnp.full((16, CH), flags_ref[i, t], jnp.int32).astype(F32) for t in range(8)], axis=0
        )
        bent, slope = silu_pair(value, keep)
        edge_ref[i] = slope.astype(BF16)
        rows.append(feat[r].astype(F32) + bent)

    line = iota((ROWS, CH), 0)
    deltas = []
    for i in range(2):
        tile = 7 * i
        keep = 0.5 * jnp.where(line < ROWS // 2, flags_ref[0, tile], flags_ref[1, tile]).astype(F32)
        bent, side_ref[i] = silu_pair(cols[i] + added[i], keep)
        inside = (line > 0) & (line < ROWS - 1)
        deltas.append(jnp.where(inside, cols[4 + i] + bent - cols[2 + i], 0.0))

    row, spot = iota((16, COLS), 0), iota((16, COLS), 1)
    pick = ((spot // 16 == row % 8) & (spot % 2 == row // 8)).astype(F32).astype(BF16)
    pick = jnp.concatenate([pick, pick], axis=1)
    place = iota((16, CH), 0)
    parts = {}
    for band in range(2):
        for a in range(2):
            total = (sums_a, sums_b)[band][a]
            if band == a:
                total += rows[band]
            part = nn(pick, jnp.concatenate(halves(total), axis=0))
            mine = (line // 16 == band) & (line % 2 == a)
            for i in range(2):
                delta = jnp.sum(jnp.where(mine, deltas[i], 0.0), axis=0, keepdims=True)
                part += jnp.where(place == 15 * i, delta, 0.0)
            parts[band, a] = part
    taken = [
        jnp.concatenate([parts[band, a][8 * b : 8 * b + 8] for band in range(2)], axis=0)
        for a in range(2)
        for b in range(2)
    ]
    both = nn(pair(*halves(jnp.concatenate(taken, axis=1))), strided[...].reshape(4 * CH, CH))
    pooled = (both[0:16] + both[16:32]) * (1.0 / TILE_CELLS)
    pooled_ref[...] = pooled
    normed = pooled * lax.rsqrt(jnp.mean(pooled * pooled, axis=-1, keepdims=True) + 1e-05)
    token_ref[:, 0:CH] = normed.astype(BF16)
    owner = jnp.full((16, LANES), -1, jnp.int32)
    for tile in range(16):
        named = jnp.where(flags_ref[tile // 8, tile % 8] != 0, owner_ref[tile], -1)
        owner = jnp.where(iota((16, LANES), 0) == tile, named, owner)
    token_ref[:, CH:] = (owner == iota((16, LANES), 1)).astype(F32).astype(BF16)


def turn_body(feat, top, bot, w_query, w_key, w_value, token, turned_ref, high_ref, low_ref):
    turned_ref[:, 0:COLS] = top[0].T
    turned_ref[:, (ROWS + 1) * COLS :] = bot[0].T

    @pl.loop(0, ROWS // 4)
    def _(i):
        for j in range(4):
            here = pl.multiple_of((4 * i + j + 1) * COLS, COLS)
            turned_ref[:, pl.ds(here, COLS)] = feat[4 * i + j].T

    for i, one in enumerate((w_query, w_key, w_value)):
        high, low = halves(one[...])
        high_ref[:, i * CH : (i + 1) * CH] = high
        low_ref[:, i * CH : (i + 1) * CH] = low


def pair_body(one, two, out_ref):
    out_ref[0:16] = one[...]
    out_ref[16:32] = two[...]


def attention_body(*refs, seed_scale):
    *got, pooled_ref, high_w, low_w, cot, strided, spread_ref, emb_ref, band, grad_ref = refs
    gz, core = lax.axis_index("gz"), lax.axis_index("core")

    def rows_of(depth, other):
        return pl.ds(pl.multiple_of(depth * 32 + other * 16, 16), 16)

    for k, piece in enumerate(got):
        depth = lax.bitwise_xor(gz, k)
        band[rows_of(depth, core)] = piece[0:16]
        band[rows_of(depth, 1 - core)] = piece[16:32]
    count = band.shape[0]
    tokens, group = band[:, 0:CH], band[:, CH:]
    pair = nt(group, group)
    pairs = jnp.concatenate([pair] * HEADS, axis=0)
    projected = nn(tokens, high_w[...]) + nn(tokens, low_w[...])
    query, key, value = (projected[:, i * CH : (i + 1) * CH] for i in range(3))
    lane = iota((1, CH), 1) // (CH // HEADS)
    scale = 1.0 / math.sqrt(CH // HEADS)

    def by_head(array):
        return jnp.concatenate([jnp.where(lane == h, array, 0.0) for h in range(HEADS)], axis=0)

    queries, keys = halves(by_head(query)), halves(by_head(key))
    gate = gate_of(wide_product(nt, queries, halves(key)) * scale + attention_bias)
    weights = gate * pairs
    seed = cot[...] * seed_scale
    seeds = jnp.where(lane == iota((8, CH), 0), seed, 0.0)
    values = halves(value)
    along = wide_product(nt, halves(seeds), values)
    columns, grads = [], []
    for h in range(HEADS):
        part = slice(h * count, (h + 1) * count)
        columns.append(jnp.sum(weights[part], axis=0, keepdims=True))
        grads.append(weights[part] * (1.0 - gate[part]) * (along[h : h + 1] * scale))
    columns = halves(jnp.concatenate(columns + [jnp.zeros((8 - HEADS, count), F32)], axis=0))
    grad_ref[:, 0:CH] = half_product(nn, jnp.concatenate(grads, axis=1), keys)
    grad_ref[:, CH : 2 * CH] = half_product(tn, jnp.concatenate(grads, axis=0), queries)
    grad_ref[:, 2 * CH :] = half_product(tn, columns[0], halves(seeds))
    mixed = wide_product(nn, columns, values)
    mixed = jnp.sum(jnp.where(lane == iota((8, CH), 0), mixed, 0.0), axis=0, keepdims=True)
    high = mixed.astype(BF16).astype(F32)
    low = mixed - high
    rows = iota((16, LANES), 0)
    packed = jnp.zeros((16, LANES), F32)
    for i, part in enumerate((high[:, :LANES], high[:, LANES:], low[:, :LANES], low[:, LANES:])):
        packed = jnp.where(rows == i, part, packed)
    emb_ref[...] = packed.astype(BF16)

    grad = half_product(nt, grad_ref[rows_of(gz, core)], (high_w[...], low_w[...]))
    grad = grad.astype(BF16).astype(F32)
    pooled = pooled_ref[...]
    inv = lax.rsqrt(jnp.mean(pooled * pooled, axis=-1, keepdims=True) + 1e-05)
    unit = pooled * inv
    back = inv * (grad - unit * jnp.mean(grad * unit, axis=-1, keepdims=True))
    cell = (back * (1.0 / TILE_CELLS)).astype(BF16)
    spot, row = iota((COLS, 16), 0), iota((COLS, 16), 1)
    expand = ((spot // 16 == row % 8) & (spot % 2 == row // 8)).astype(F32).astype(BF16)
    expand = jnp.concatenate([expand, expand], axis=1)
    taps = nt(cell, strided[...].reshape(4 * CH, CH))
    for band in range(2):
        here = taps[8 * band : 8 * band + 8]
        both = [
            jnp.concatenate([here[:, (2 * a + b) * CH : (2 * a + b + 1) * CH] for a in range(2)], axis=1)
            for b in range(2)
        ]
        spread = nn(expand, jnp.concatenate(halves(jnp.concatenate(both, axis=0)), axis=0))
        for a in range(2):
            spread_ref[band * 2 + a] = spread[:, a * CH : (a + 1) * CH]


GROUPS = (6, 10, 16)


def weight_body(
    spread, slope_a, slope_b, edge, side, turned, even, odd,
    wide, keep_ref, give_ref, even_ref, odd_ref, left_ref, right_ref, total, first, last,
):
    first[...] = jnp.zeros_like(first)
    last[...] = jnp.zeros_like(last)

    def build(r):
        if r in (0, ROWS - 1):
            slope = edge[r // HALF].astype(F32)
        else:
            slope = (slope_a, slope_b)[r // HALF][r % HALF].astype(F32)
            slope = with_last(with_first(slope, side[0, r : r + 1]), side[1, r : r + 1])
        grad = (spread[(r // HALF) * 2 + r % 2] * slope).astype(BF16)
        here = slice(r * COLS, (r + 1) * COLS)
        wide[here, 2 * CH :], wide[here, 0:CH] = neighbours(grad)
        wide[here, CH : 2 * CH] = grad
        full = grad.astype(F32)
        for a in range(3):
            first[a, r + a : r + a + 1] = full[0:1]
            last[a, r + a : r + a + 1] = full[COLS - 1 :]

    is_one = is_odd("core")
    left, right = (part.astype(BF16) for part in sides(even, odd))

    def put(part, a, b):
        if b == 0:
            part += tn(left, first[a].astype(BF16))
        if b == 2:
            part += tn(right, last[a].astype(BF16))
        low, high = part[:, :LANES], part[:, LANES:]
        at = slice((3 * a + b) * CH, (3 * a + b + 1) * CH)
        keep_ref[at] = jnp.where(is_one, high, low).astype(BF16)
        give_ref[at] = jnp.where(is_one, low, high).astype(BF16)

    for r in range(GROUPS[0]):
        build(r)
    start = 0
    for g, count in enumerate(GROUPS):
        here = slice(start * COLS, (start + count) * COLS)
        near = [turned[:, (start + a) * COLS : (start + a + count) * COLS] for a in range(3)]
        near = jnp.concatenate(near, axis=0)
        start += count
        ahead = GROUPS[g + 1] if g + 1 < len(GROUPS) else 0
        for b in range(3):
            part = slice(b * CH, (b + 1) * CH)
            result = nn(near, wide[here, part])
            if g > 0:
                result += total[:, part]
            if ahead:
                total[:, part] = result
            for r in range(ahead * b // 3, ahead * (b + 1) // 3):
                build(start + r)
            if not ahead:
                for a in range(3):
                    put(result[a * CH : (a + 1) * CH], a, b)

    centre = slice(CH, 2 * CH)
    order_rows(wide[0:COLS, centre], wide[(ROWS - 1) * COLS :, centre], even_ref, odd_ref)
    left_ref[...] = first[1].astype(BF16)
    right_ref[...] = last[1].astype(BF16)


def order_rows(first, last, even_ref, odd_ref):
    odd = is_odd("gy")
    even_ref[0] = jnp.where(odd, first, last)
    odd_ref[0] = jnp.where(odd, last, first)


def back_taps(weight, taps):
    return jnp.concatenate([weight[tap] for tap in taps], axis=1)


def input_blocks(wide, weight, first, blocks, prods, finish, send=None):
    for block in range(blocks + 1):
        if block < blocks:
            at = first + STEP * block
            near = [wide[(at + step) * COLS : (at + step + STEP) * COLS] for step in (1, 0, -1)]
            prods[block % 2][...] = nt(jnp.concatenate(near, axis=1), back_taps(weight, range(9)))
        if block > 0:
            at = first + STEP * (block - 1)
            for j in range(STEP):
                finish(at + j, prods[(block - 1) % 2][j * COLS : (j + 1) * COLS])
            if send is not None:
                send(at, STEP)


UPPER = 2 * STEP


def upper_body(wide, spread, weight, done, raw_ref, prod_a, prod_b):
    def finish(r, prod):
        value = spread[r % 2] + prod
        done[r - 1] = value.astype(BF16)
        raw_ref[0, r : r + 1] = value[0:1]
        raw_ref[1, r : r + 1] = value[COLS - 1 :]

    input_blocks(wide, weight, 1, UPPER // STEP, (prod_a, prod_b), finish)


def lower_body(
    wide, top, bot, even, odd, spread, weight, upper, raw, out, prod_a, prod_b, side32, added, done, fixed, sems
):
    started = []

    def start(source, target):
        started.append(pltpu.make_async_copy(source, target, sems.at[len(started)]))
        started[-1].start()

    start(upper.at[:, 16 : COLS - 16], out.at[1 : UPPER + 1, 16 : COLS - 16])
    for i, whole in enumerate(sides(even, odd)):
        side32[...] = whole
        near = [side32[2 - a : 2 - a + ROWS].astype(BF16) for a in range(3)]
        taps = back_taps(weight, [3 * a + 2 - 2 * i for a in range(3)])
        added[i] = nt(jnp.concatenate(near, axis=1), taps)

    small = iota((16, CH), 0)
    for i in range(2):
        at = (COLS - 16) * i
        for r in range(1, UPPER + 1):
            value = raw[i, r : r + 1] + added[i, r : r + 1]
            old = upper[r - 1, at : at + 16].astype(F32)
            fixed[i, r - 1] = jnp.where(small == 15 * i, value, old).astype(BF16)
        start(fixed.at[i], out.at[1 : UPPER + 1, at : at + 16])

    def place(r):
        return r - UPPER if r else 0

    def finish(r, prod):
        prod = with_first(prod, prod[0:1] + added[0, r : r + 1])
        prod = with_last(prod, prod[COLS - 1 :] + added[1, r : r + 1])
        done[place(r)] = (spread[(r // HALF) * 2 + r % 2] + prod).astype(BF16)

    def send(first, count):
        start(done.at[place(first) : place(first) + count], out.at[first : first + count])

    input_blocks(wide, weight, UPPER + 1, (ROWS - 2 - UPPER) // STEP, (prod_a, prod_b), finish, send)

    def row(r):
        return wide[r * COLS : (r + 1) * COLS]

    def outside(one):
        left, right = neighbours(one[0])
        return jnp.concatenate([right, one[0], left], axis=1)

    def pair(one, two):
        return jnp.concatenate([one, two], axis=0)

    near = [pair(row(1), outside(bot)), pair(row(0), row(ROWS - 1)), pair(outside(top), row(ROWS - 2))]
    both = nt(jnp.concatenate(near, axis=1), back_taps(weight, range(9)))
    for i, r in enumerate((0, ROWS - 1)):
        finish(r, both[i * COLS : (i + 1) * COLS])
        send(r, 1)
    for one in started:
        one.wait()


def add_up(refs, rows):
    total = refs[0][0:rows].astype(F32)
    for one in refs[1:]:
        total += one[0:rows].astype(F32)
    return total.astype(BF16)


def deal(refs, outs, size, axis):
    for k, out in enumerate(reversed(outs)):
        at = lax.bitwise_xor(lax.axis_index(axis), k) * size
        here = pl.ds(pl.multiple_of(at, 16), size)
        total = refs[0][here].astype(F32)
        for one in refs[1:]:
            total += one[here].astype(F32)
        out[0:size] = total.astype(BF16)


def chip_sum_body(one, two, emb, *outs):
    size = one.shape[0] // len(outs)
    deal((one, two), outs, size, "gy")
    for out in outs:
        out[size:] = emb[...]


def band_sum_body(*refs, terms, norm_scale):
    outs, emb_ref = refs[terms:-1], refs[-1]
    rows = refs[0].shape[0] - 16
    deal(refs[:terms], outs, rows // len(outs), "gz")
    embs = []
    for one in (refs[0], *refs[terms - 1 : 0 : -1]):
        part = one[rows : rows + 16].astype(F32)
        embs.append(part[0:2] + part[2:4])
    while len(embs) > 1:
        embs = [a + b for a, b in zip(embs[0::2], embs[1::2])]
    emb_ref[:, 0:LANES] = embs[0][0:1] * norm_scale
    emb_ref[:, LANES:] = embs[0][1:2] * norm_scale


def last_sum_body(*refs):
    refs[-1][...] = add_up(refs[:-1], refs[-1].shape[0])


def stack_body(*refs):
    for i, one in enumerate(refs[:-1]):
        refs[-1][i] = one[...]


def half_body(array, *refs, other):
    grad_ref, buf, sems = refs[-3:]
    gy, gz, core = (lax.axis_index(name) for name in ("gy", "gz", "core"))
    bands, depth, share = array.shape[:3]
    half = 1 - core if other else core
    lanes = pl.ds(pl.multiple_of(half * LANES, LANES), LANES)
    started = []
    for k in range(bands):
        first = lax.bitwise_xor(gy, k) * (depth * share)
        for j in range(depth):
            at = first + lax.bitwise_xor(gz, j) * share
            buf[pl.ds(pl.multiple_of(at, 16), share)] = array[k, j].astype(F32) * (1.0 / loss_scale)
        here = pl.ds(pl.multiple_of(first, 16), depth * share)
        started.append(pltpu.make_async_copy(buf.at[here], grad_ref.at[here, lanes], sems.at[k]))
        started[-1].start()
    for one in started:
        one.wait()


SMEM = pl.BlockSpec(memory_space=pltpu.SMEM)
VMEM = pl.BlockSpec(memory_space=pltpu.VMEM)
HBM = pl.BlockSpec(memory_space=pltpu.HBM)


def run(body, args, outs, scratch=(), flops=1 << 20, mib=8, far=(), **rest):
    specs = [HBM if i in far else SMEM if a.dtype == jnp.int32 else VMEM for i, a in enumerate(args)]
    return pl.pallas_call(
        body,
        in_specs=specs,
        out_shape=outs,
        scratch_shapes=list(scratch),
        compiler_params=pltpu.CompilerParams(vmem_limit_bytes=mib << 20),
        cost_estimate=pl.CostEstimate(flops=flops, bytes_accessed=1 << 20, transcendentals=0),
        **rest,
    )(*args)


def per_device(features, tissue, owner_map, w_conv, w_stride, w_query, w_key, w_value, cotangent):
    gy_count, gz_count, cores = lax.axis_size("gy"), lax.axis_size("gz"), lax.axis_size("core")
    gx_count, chips = gz_count * cores, gy_count * gz_count
    across = ("gz", "core")
    norm_scale = 1.0 / math.sqrt(16 * gy_count * gx_count)
    swap = [(i, i ^ 1) for i in range(cores)]

    def pairs(value, axis, count, odd):
        low = range(odd, count - 1, 2)
        return lax.ppermute(value, axis, [(i, i + 1) for i in low] + [(i + 1, i) for i in low])

    def others(values, axis, count):
        got = [
            lax.ppermute(values[k - 1], axis, [(i, i ^ k) for i in range(count)])
            for k in range(count - 1, 0, -1)
        ]
        return got[::-1]

    column = shape((HALO, CH), BF16)
    line = shape((1, COLS, CH), BF16)

    def row_halos(even, odd):
        return pairs(even, "gy", gy_count, 0), pairs(odd, "gy", gy_count, 1)

    def corners(left, right, even, odd):
        return run(corner_body, (left, right, even, odd), [line, line, column, column], mib=1)

    def column_halos(even, odd):
        return pairs(even, across, gx_count, 0), pairs(odd, across, gx_count, 1)

    conv_flops = 2 * ROWS * COLS * 9 * CH * CH
    prod = pltpu.VMEM((STEP * COLS, CH), F32)
    side32 = pltpu.VMEM((HALO, CH), F32)
    half_block = shape((HALF, COLS, CH), BF16)

    def forward(band, weight):
        return run(
            lambda *refs: forward_body(*refs, band=band),
            (tissue, features, weight),
            [half_block, shape((2, COLS, CH), F32), shape((6, HALF, CH), F32)],
            [pltpu.VMEM(((HALF + 1) * COLS, 2 * CH), BF16), prod, prod],
            flops=conv_flops // 2,
            mib=16,
        )

    rows = run(
        order_body, (features[:1], features[ROWS - 1 :]), [line, line], flops=conv_flops, mib=2
    )
    outer = run(columns_body, (features,), [column, column], mib=2)
    even, odd = row_halos(*rows)
    slope_a, sums_a, cols_a = forward(0, w_conv)
    even, odd, cols_a = lax.optimization_barrier((even, odd, cols_a))
    top, bot, even, odd = corners(*outer, even, odd)
    weight_b, even = lax.optimization_barrier((w_conv, even))
    even, odd = column_halos(even, odd)
    slope_b, sums_b, cols_b = forward(1, weight_b)
    pooled, token, edge, side = run(
        border_body,
        (
            tissue, features, w_conv, sums_a, sums_b, cols_a, cols_b, top, bot, even, odd, w_stride,
            owner_map.reshape(16),
        ),
        [
            shape((16, CH), F32),
            shape((16, CH + LANES), BF16),
            shape((2, COLS, CH), BF16),
            shape((2, ROWS, CH), F32),
        ],
        [side32],
        flops=conv_flops // 8,
        mib=12,
    )
    def stacked(terms):
        return run(stack_body, terms, shape((len(terms),) + terms[0].shape, BF16), mib=4)

    both = run(
        pair_body, (token, lax.ppermute(token, "core", swap)), shape((32, CH + LANES), BF16), mib=1
    )
    pieces = [both] + others([both] * (gz_count - 1), "gz", gz_count)
    turned, high_w, low_w = run(
        turn_body,
        (features, top, bot, w_query, w_key, w_value, token),
        [shape((CH, (ROWS + 2) * COLS), BF16), shape((CH, 3 * CH), BF16), shape((CH, 3 * CH), BF16)],
        flops=conv_flops // 4,
        mib=12,
    )
    count = 16 * gx_count
    spread, emb = run(
        lambda *refs: attention_body(*refs, seed_scale=loss_scale * norm_scale),
        (*pieces, pooled, high_w, low_w, cotangent.reshape(1, CH), w_stride),
        [shape((4, COLS, CH), F32), shape((16, LANES), BF16)],
        [pltpu.VMEM((count, CH + LANES), BF16), pltpu.VMEM((count, 3 * CH), F32)],
        flops=1 << 30,
        mib=12,
    )
    border = pltpu.VMEM((3, HALO, CH), F32)
    wide, keep, give, *outer = run(
        weight_body,
        (spread, slope_a, slope_b, edge, side, turned, even, odd),
        [
            shape((ROWS * COLS, 3 * CH), BF16),
            shape((9 * CH, LANES), BF16),
            shape((9 * CH, LANES), BF16),
            line,
            line,
            column,
            column,
        ],
        [pltpu.VMEM((3 * CH, 3 * CH), F32), border, border],
        flops=conv_flops,
        mib=20,
    )

    share = -(-9 * CH // (16 * chips)) * 16
    spare = share * chips - 9 * CH
    taken = lax.ppermute(give, "core", swap)
    pre_rows = row_halos(*outer[:2])
    if spare:
        keep, taken = (jnp.pad(a, ((0, spare), (0, 0))) for a in (keep, taken))

    whole_rows = share * chips
    band_rows = share * gz_count
    parts = run(
        chip_sum_body,
        (keep, taken, emb),
        [shape((band_rows + 16, LANES), BF16)] * gy_count,
        mib=6,
    )[::-1]
    *parts, wide_upper = lax.optimization_barrier((*parts, wide))
    upper, raw = run(
        upper_body,
        (wide_upper, spread, w_conv),
        [shape((UPPER, COLS, CH), BF16), shape((2, HALF, CH), F32)],
        [prod, prod],
        flops=conv_flops // 3,
        mib=12,
    )
    raw, *outer = lax.optimization_barrier((raw, *outer[2:], *pre_rows))
    parts = [parts[0]] + others(parts[1:], "gy", gy_count)[::-1]
    top, bot, even, odd = corners(*outer)
    even, odd = column_halos(even, odd)
    *parts, raw = lax.optimization_barrier((*parts, raw))
    embedding, *parts = run(
        lambda *refs: band_sum_body(*refs, terms=gy_count, norm_scale=norm_scale),
        parts,
        [shape((share, LANES), BF16)] * gz_count + [shape((1, CH), F32)],
        mib=4,
    )[::-1]
    *parts, even, odd = lax.optimization_barrier((*parts, even, odd))
    parts = [parts[0]] + others(parts[1:], "gz", gz_count)[::-1]
    mine = run(last_sum_body, parts, shape((share, LANES), BF16), mib=2)
    row = stacked([mine] + others([mine] * (gz_count - 1), "gz", gz_count))
    row, wide_lower = lax.optimization_barrier((row, wide))
    input_grad = run(
        lower_body,
        (wide_lower, top, bot, even, odd, spread, w_conv, upper, raw),
        shape((ROWS, COLS, CH), BF16),
        [
            prod,
            prod,
            side32,
            pltpu.VMEM((2, ROWS, CH), F32),
            pltpu.VMEM((ROWS - UPPER, COLS, CH), BF16),
            pltpu.VMEM((2, UPPER, 16, CH), BF16),
            pltpu.SemaphoreType.DMA((BLOCKS + 6,)),
        ],
        flops=conv_flops // 2,
        mib=16,
        out_specs=HBM,
    )
    planes = [row] + others([row] * (gy_count - 1), "gy", gy_count)
    *planes, input_grad = lax.optimization_barrier((*planes, input_grad))
    plane = stacked(planes)
    other = lax.ppermute(plane, "core", swap)
    whole = shape((whole_rows, CH), F32)
    buffers = [pltpu.VMEM((whole_rows, LANES), F32), pltpu.SemaphoreType.DMA((gy_count,))]
    half_grad = run(
        lambda *refs: half_body(*refs, other=False), (plane,), whole, buffers, mib=4, out_specs=HBM
    )
    conv_grad = run(
        lambda *refs: half_body(*refs, other=True),
        (other, half_grad),
        whole,
        buffers,
        mib=4,
        far=(1,),
        out_specs=HBM,
        input_output_aliases={1: 0},
    )
    return embedding.reshape(CH), input_grad, conv_grad[: 9 * CH].reshape(9, CH, CH)


def solution(mesh):
    sizes = mesh.devices.shape
    split = Mesh(mesh.devices.reshape(sizes[0], sizes[1] // 2, 2), ("gy", "gz", "core"))
    gx = ("gz", "core")
    in_specs = (P("gy", gx, None), P("gy", gx), P("gy", gx, None, None), P(), P(), P(), P(), P(), P())
    out_specs = (P(), P("gy", gx, None), P())
    return jax.shard_map(per_device, mesh=split, in_specs=in_specs, out_specs=out_specs, check_vma=False)
```
